32 devices in a mesh: parts: 2 (over x), group: 8 (over z, y), tensor: 2 (over core).
Axes of the slice: x: 2, y: 2, z: 4, core: 2. Of those that a mesh axis runs over, the one named last changes fastest.
Arguments:
- normed_inputs: bfloat16 [2048, 8192], P(('parts', 'group'), 'tensor'), parts along dimension 0, may hold values from -6 to 6
- value_matrix: bfloat16 [8192, 1024], P('group', 'tensor'), may hold values from -0.0625 to 0.0625
- adapter_down_weight: bfloat16 [16, 16, 8192], P('group'), may hold values from -0.0625 to 0.0625
- adapter_up_weight: bfloat16 [16, 16, 1024], P('group', None, 'tensor'), may hold values from -1.5 to 1.5
- adapter_position: int32 [16], replicated, may hold values from 0 to 15, each once
- span_adapter_index: int32 [32], P('parts'), parts along dimension 0, may hold values from 0 to 15
- queries: bfloat16 [2048, 8192], P(('parts', 'group'), 'tensor'), parts along dimension 0, may hold values from -150 to 150, as said below
- incoming_keys: bfloat16 [2048, 1024], P(('parts', 'group'), 'tensor'), parts along dimension 0, may hold values from -6 to 6
- stored_keys: bfloat16 [32, 2048, 1024], P(('parts', 'group'), None, 'tensor'), parts along dimension 0, may hold values from -5 to 5
- stored_values: bfloat16 [32, 2048, 1024], P(('parts', 'group'), None, 'tensor'), parts along dimension 0, may hold values from -6 to 6
- cache_length: int32 [32], P(('parts', 'group')), parts along dimension 0, may hold values from 256 to 2048, as said below
Outputs:
- attended: bfloat16 [2048, 8192], P(('parts', 'group'), 'tensor'), parts along dimension 0
- incoming_values: bfloat16 [2048, 1024], P(('parts', 'group'), 'tensor'), parts along dimension 0
The draws below stay inside these ranges and needn't reach their ends.
There are 2 independent parts, one for each index of `parts`. The reference program is written for one: setup_inputs(seed, part) draws one part's arguments, and reference() takes and returns one part's arrays. A program takes and returns all parts, laid end to end along the dimension named above; an argument that names none is the same for every part. Nothing has to cross between parts.
Inputs may be any that keep to these rules, and one draw needn't show every extreme that they name: `queries`: in the shown draw twice a truncated standard normal. `cache_length`: some span has a full cache in every draw.
All inputs are finite; a program needn't handle non-finite values.
Results may differ from the reference program's by a relative error of at most 0.014.
Values may be sent and summed in bfloat16 or wider, within the bound.
No kernel may reach another device: no remote copies, remote signals or barrier semaphores. Data moves between devices by JAX's collectives and lax.ppermute only.
A program may use at most 128 MiB of HBM per device.

```python
import math
import jax
import jax.numpy as jnp
import numpy as np
from jax import lax

MODEL_WIDTH = 8192
QH = 64
KVH = 8
HD = 128
ADAPTER_RANK = 16
SPAN = 64
CACHE = 2048
VALUE_WIDTH = 1024
SPAN_TOTAL = 16
TOKENS = 1024
ADAPTER_TOTAL = 16
N_GROUP = 8


def draw_queries(key, part):
    key = jax.random.fold_in(key, 3)
    result = 2.0 * jax.random.truncated_normal(key, -5.0, 5.0, (TOKENS, QH * HD), jnp.float32)
    return result.astype(jnp.bfloat16)


def draw_stored_keys(key, part):
    key = jax.random.fold_in(key, 5)
    result = jax.random.truncated_normal(key, -5.0, 5.0, (SPAN_TOTAL, CACHE, VALUE_WIDTH), jnp.float32)
    return result.astype(jnp.bfloat16)


def draw_cache_length(key, part):
    key = jax.random.fold_in(key, 9)
    first, second = jax.random.split(key)
    lengths = jax.random.randint(first, (SPAN_TOTAL,), CACHE // 8, CACHE + 1)
    chosen = jax.random.randint(second, (), 0, SPAN_TOTAL)
    return jnp.where(jnp.arange(SPAN_TOTAL) == chosen, CACHE, lengths).astype(jnp.int32)


def with_ends(drawn, own_key, least, largest):
    place = [jax.random.randint(jax.random.fold_in(own_key, axis), (), 0, length) for axis, length in enumerate(drawn.shape)]
    main_axis = drawn.shape.index(max(drawn.shape))
    next_to = place[:main_axis] + [(place[main_axis] + 1) % drawn.shape[main_axis]] + place[main_axis + 1:]
    return drawn.at[tuple(place)].set(least).at[tuple(next_to)].set(largest)


def steps_of(key, shape, cuts, smallest, top_value):
    factor_of, own = 1.0, jax.random.fold_in(key, 6)
    for dim, shards_of in cuts:
        steps = jnp.exp(jax.random.uniform(jax.random.fold_in(own, dim), (shards_of,), jnp.float32, smallest / len(cuts), top_value / len(cuts)))
        factor_of = factor_of * jnp.repeat(steps, shape[dim] // shards_of).reshape([-1 if axis == dim else 1 for axis in range(len(shape))])
    return factor_of


def rank_table(amount, slope):
    loads = [(1 << 20) // math.isqrt(standing ** slope) + 1 for standing in range(1, amount + 1)]
    deviation = 1 + sum(loads) // (1 << 30)
    return np.cumsum(np.array([max(1, weight // deviation) for weight in loads]))


def ranked_ids(stream_key, dims, number_of, slope):
    table = rank_table(number_of, slope)
    lot = jax.random.randint(jax.random.fold_in(stream_key, 1), dims, 0, int(table[number_of - 1]))
    rank = jnp.searchsorted(jnp.asarray(table, jnp.int32), lot, side="right")
    return jax.random.permutation(jax.random.fold_in(stream_key, 2), number_of)[rank].astype(jnp.int32)


def normal_values(key, extent, width, bound, cuts=(), kind=jnp.bfloat16):
    values = jax.random.normal(key, extent, jnp.float32) * width
    if len(cuts) > 0:
        values = steps_of(key, extent, cuts, -0.22, 0.18) * values
    return jnp.clip(values, min=-bound, max=bound).astype(kind)


def setup_inputs(seed: int = 0, part: int = 0) -> dict:
    splits = jax.random.split(jax.random.key(seed), 12)
    part_keys = jax.random.split(jax.random.fold_in(splits[11], part), 12)
    normed_inputs = normal_values(part_keys[0], (TOKENS, MODEL_WIDTH), 1.0, 6.0, ((0, 8), (1, 2)))
    value_matrix = normal_values(splits[1], (MODEL_WIDTH, VALUE_WIDTH), MODEL_WIDTH ** -0.5, 0.0625, ((0, 8), (1, 2)))
    adapter_down_weight = normal_values(splits[2], (ADAPTER_TOTAL, ADAPTER_RANK, MODEL_WIDTH), MODEL_WIDTH ** -0.5, 0.0625, ((0, 8),))
    adapter_up_weight = normal_values(splits[3], (ADAPTER_TOTAL, ADAPTER_RANK, VALUE_WIDTH), ADAPTER_RANK ** -0.5, 1.5, ((0, 8), (2, 2)))
    adapter_position = jax.random.permutation(splits[4], ADAPTER_TOTAL).astype(jnp.int32)
    span_adapter_index = with_ends(ranked_ids(part_keys[5], (SPAN_TOTAL,), ADAPTER_TOTAL, 2), jax.random.fold_in(part_keys[5], 3), 0, ADAPTER_TOTAL - 1).astype(jnp.int32)
    queries = draw_queries(jax.random.fold_in(jax.random.fold_in(splits[11], part), 71), part)
    incoming_keys = normal_values(part_keys[7], (TOKENS, VALUE_WIDTH), 1.0, 6.0, ((0, 8), (1, 2)))
    stored_keys = draw_stored_keys(jax.random.fold_in(jax.random.fold_in(splits[11], part), 71), part)
    stored_values = normal_values(part_keys[9], (SPAN_TOTAL, CACHE, VALUE_WIDTH), 1.0, 6.0, ((0, 8), (2, 2)))
    cache_length = draw_cache_length(jax.random.fold_in(jax.random.fold_in(splits[11], part), 71), part)
    return {"normed_inputs": normed_inputs, "value_matrix": value_matrix, "adapter_down_weight": adapter_down_weight, "adapter_up_weight": adapter_up_weight, "adapter_position": adapter_position, "span_adapter_index": span_adapter_index, "queries": queries, "incoming_keys": incoming_keys, "stored_keys": stored_keys, "stored_values": stored_values, "cache_length": cache_length}


adapter_scale = 2.0

def attend_span(inputs):
    query_rows, fresh_keys, fresh_values, cache_keys, cache_values, length = inputs
    keys = jnp.concatenate([cache_keys, fresh_keys], 0).astype(jnp.float32).reshape(CACHE + SPAN, KVH, HD)
    values = jnp.concatenate([cache_values, fresh_values], 0).astype(jnp.float32).reshape(CACHE + SPAN, KVH, HD)
    query_four = query_rows.astype(jnp.float32).reshape(SPAN, KVH, QH // KVH, HD)
    scores = jnp.einsum('nkgd,mkd->kgnm', query_four, keys) * (1.0 / math.sqrt(HD))
    where_key = jnp.arange(CACHE + SPAN, dtype=jnp.int32)[None, :]
    where_row = jnp.arange(SPAN, dtype=jnp.int32)[:, None]
    live = jnp.where(where_key < CACHE, where_key < length, where_key - CACHE <= where_row)
    scores = jnp.where(live, scores, -1e+30)
    top = lax.optimization_barrier(jnp.max(scores, axis=-1, keepdims=True))
    probs = jnp.where(live, jnp.exp(scores - top), 0.0)
    total = lax.optimization_barrier(jnp.sum(probs, axis=-1))
    rounded = lax.optimization_barrier(probs.astype(jnp.bfloat16)).astype(jnp.float32)
    summed = jnp.einsum('kgnm,mkd->nkgd', rounded, values)
    result = summed / jnp.transpose(total, (2, 0, 1))[..., None]
    return result.reshape(SPAN, QH * HD).astype(jnp.bfloat16)

def reference(normed_inputs, value_matrix, adapter_down_weight, adapter_up_weight, adapter_position, span_adapter_index, queries, incoming_keys, stored_keys, stored_values, cache_length):
    feature_width = MODEL_WIDTH // N_GROUP
    span_position = adapter_position[span_adapter_index]
    down_selected = adapter_down_weight[span_position].reshape(SPAN_TOTAL, ADAPTER_RANK, N_GROUP, feature_width)
    token_slices = normed_inputs.reshape(SPAN_TOTAL, SPAN, N_GROUP, feature_width)
    weight_slices = value_matrix.reshape(N_GROUP, feature_width, VALUE_WIDTH)

    def add_slice(carry, index):
        value_sum, shrink_sum = carry
        tokens_here = lax.dynamic_index_in_dim(token_slices, index, 2, keepdims=False)
        weight_here = lax.dynamic_index_in_dim(weight_slices, index, 0, keepdims=False)
        down_here = lax.dynamic_index_in_dim(down_selected, index, 2, keepdims=False)
        part = jnp.dot(tokens_here.reshape(TOKENS, feature_width), weight_here, preferred_element_type=jnp.float32)
        down_part = jnp.einsum('cns,crs->cnr', tokens_here.astype(jnp.float32), down_here.astype(jnp.float32)).reshape(TOKENS, ADAPTER_RANK)
        part = lax.optimization_barrier(part.astype(jnp.bfloat16)).astype(jnp.float32)
        down_part = lax.optimization_barrier(down_part.astype(jnp.bfloat16)).astype(jnp.float32)
        return ((value_sum + part, shrink_sum + down_part), None)
    start = (jnp.zeros((TOKENS, VALUE_WIDTH), jnp.float32), jnp.zeros((TOKENS, ADAPTER_RANK), jnp.float32))
    (plain_values, shrink_sum), unused = lax.scan(add_slice, start, jnp.arange(N_GROUP, dtype=jnp.int32))
    shrink = shrink_sum.astype(jnp.bfloat16)
    up_selected = adapter_up_weight[span_position]
    adapter_update = jnp.einsum('cnr,crk->cnk', shrink.reshape(SPAN_TOTAL, SPAN, ADAPTER_RANK).astype(jnp.float32), up_selected.astype(jnp.float32)).reshape(TOKENS, VALUE_WIDTH)
    incoming_values = (plain_values + adapter_scale * adapter_update).astype(jnp.bfloat16)
    attended = lax.map(attend_span, (queries.reshape(SPAN_TOTAL, SPAN, QH * HD), incoming_keys.reshape(SPAN_TOTAL, SPAN, VALUE_WIDTH), incoming_values.reshape(SPAN_TOTAL, SPAN, VALUE_WIDTH), stored_keys, stored_values, cache_length))
    return (attended.reshape(TOKENS, QH * HD), incoming_values)
```

```python
import functools
import math

import jax
import jax.numpy as jnp
from jax import lax
from jax.experimental import pallas as pl
from jax.experimental.pallas import tpu as pltpu
from jax.sharding import PartitionSpec as P

HD = 128
RANK = 16
SPAN = 64
CHUNK = 512
ADAPTER_SCALE = 2.0
EXP2_SCALE = math.log2(math.e) / math.sqrt(HD)
DEAD = -1e30
BOTH = ("group", "tensor")
VMEM_LIMIT = 56 * 1024 * 1024


def dot_last(a, b):
    return lax.dot_general(a, b, (((1,), (1,)), ((), ())), preferred_element_type=jnp.float32)


def dot(a, b):
    return jnp.dot(a, b, preferred_element_type=jnp.float32)


def cache_kernel(kv_heads, group_size, lens, q_ref, fk_ref, k_ref, v_ref, out_ref, pf_ref, qs, m_s, l_s, acc):
    span, step = pl.program_id(0), pl.program_id(1)
    length = lens[span]
    rows = group_size * SPAN
    chunk = k_ref.shape[1]

    def fresh_scores(k):
        s = dot_last(qs[k], fk_ref[:, k * HD : (k + 1) * HD])
        token = lax.broadcasted_iota(jnp.int32, (group_size, SPAN, SPAN), 1).reshape(rows, SPAN)
        key = lax.broadcasted_iota(jnp.int32, (rows, SPAN), 1)
        return jnp.where(key <= token, s, DEAD)

    @pl.when(step == 0)
    def _():
        for k in range(kv_heads):
            for h in range(group_size):
                col = (k * group_size + h) * HD
                qs[k, h * SPAN : (h + 1) * SPAN, :] = q_ref[:, col : col + HD]
            s = fresh_scores(k)
            top = jnp.max(s, axis=1, keepdims=True)
            p = jnp.exp2((s - top) * EXP2_SCALE)
            m_s[k] = jnp.broadcast_to(top, (rows, HD))
            l_s[k] = jnp.broadcast_to(jnp.sum(p, axis=1, keepdims=True), (rows, HD))
            acc[k] = jnp.zeros((rows, HD), jnp.float32)

    def add_chunk(masked):
        for k in range(kv_heads):
            s = dot_last(qs[k], k_ref[0, :, k * HD : (k + 1) * HD])
            if masked:
                slot = step * chunk + lax.broadcasted_iota(jnp.int32, (1, chunk), 1)
                s = jnp.where(slot < length, s, DEAD)
            before = m_s[k][:, :1]
            top = jnp.maximum(before, jnp.max(s, axis=1, keepdims=True))
            alpha = jnp.exp2((before - top) * EXP2_SCALE)
            p = jnp.exp2((s - top) * EXP2_SCALE)
            m_s[k] = jnp.broadcast_to(top, (rows, HD))
            l_s[k] = l_s[k] * alpha + jnp.sum(p, axis=1, keepdims=True)
            acc[k] = acc[k] * alpha + dot(p.astype(jnp.bfloat16), v_ref[0, :, k * HD : (k + 1) * HD])

    @pl.when((step + 1) * chunk <= length)
    def _():
        add_chunk(False)

    @pl.when((step * chunk < length) & ((step + 1) * chunk > length))
    def _():
        add_chunk(True)

    @pl.when(step == pl.num_programs(1) - 1)
    def _():
        for k in range(kv_heads):
            inverse = 1.0 / l_s[k]
            p = jnp.exp2((fresh_scores(k) - m_s[k][:, :1]) * EXP2_SCALE) * inverse[:, :SPAN]
            pf_ref[k * rows : (k + 1) * rows, :] = p.astype(jnp.bfloat16)
            mixed = acc[k] * inverse
            for h in range(group_size):
                col = (k * group_size + h) * HD
                out_ref[:, col : col + HD] = mixed[h * SPAN : (h + 1) * SPAN, :]


def cache_attention(queries, fresh_keys, keys, values, lengths):
    spans, slots, width = keys.shape
    kv_heads = width // HD
    q_width = queries.shape[1]
    group_size = q_width // width
    rows = group_size * SPAN
    chunk = min(CHUNK, slots)
    steps = slots // chunk

    def kv_index(s, i, lens):
        return (s, jnp.minimum(i, (lens[s] - 1) // chunk), 0)

    return pl.pallas_call(
        functools.partial(cache_kernel, kv_heads, group_size),
        grid_spec=pltpu.PrefetchScalarGridSpec(
            num_scalar_prefetch=1,
            grid=(spans, steps),
            in_specs=[
                pl.BlockSpec((SPAN, q_width), lambda s, i, lens: (s, 0)),
                pl.BlockSpec((SPAN, width), lambda s, i, lens: (s, 0)),
                pl.BlockSpec((1, chunk, width), kv_index),
                pl.BlockSpec((1, chunk, width), kv_index),
            ],
            out_specs=[
                pl.BlockSpec((SPAN, q_width), lambda s, i, lens: (s, 0)),
                pl.BlockSpec((kv_heads * rows, SPAN), lambda s, i, lens: (s, 0)),
            ],
            scratch_shapes=[
                pltpu.VMEM((kv_heads, rows, HD), jnp.bfloat16),
                pltpu.VMEM((kv_heads, rows, HD), jnp.float32),
                pltpu.VMEM((kv_heads, rows, HD), jnp.float32),
                pltpu.VMEM((kv_heads, rows, HD), jnp.float32),
            ],
        ),
        out_shape=[
            jax.ShapeDtypeStruct((spans * SPAN, q_width), jnp.float32),
            jax.ShapeDtypeStruct((spans * kv_heads * rows, SPAN), jnp.bfloat16),
        ],
        compiler_params=pltpu.CompilerParams(vmem_limit_bytes=VMEM_LIMIT),
        cost_estimate=pl.CostEstimate(
            flops=4 * spans * kv_heads * rows * slots * HD,
            bytes_accessed=2 * spans * slots * width * 2,
            transcendentals=spans * kv_heads * rows * slots,
        ),
        name="cache_attention",
    )(lengths, queries, fresh_keys, keys, values)


def pack_kernel(half, x_ref, d_ref, *outs):
    group, tensor = lax.axis_index("group"), lax.axis_index("tensor")
    a, b = group // half, group % half
    width = outs[0].shape[1]
    features = x_ref.shape[1]
    for r, out in enumerate(outs):
        r1, r2 = r // half, r % half
        piece = (b + r2) % half
        row = pl.multiple_of(((a + r1) % 2) * SPAN, SPAN)
        col = pl.multiple_of(piece * width, width)
        d_col = pl.multiple_of(tensor * features + piece * width, width)
        out[:SPAN, :] = x_ref[pl.ds(row, SPAN), pl.ds(col, width)]
        out[SPAN:, :] = d_ref[:, pl.ds(d_col, width)]


def pack(normed_inputs, downs, width, half):
    rounds = 2 * half
    shape = jax.ShapeDtypeStruct((SPAN + downs.shape[0], width), jnp.bfloat16)
    vmem = pl.BlockSpec(memory_space=pltpu.VMEM)
    return pl.pallas_call(
        functools.partial(pack_kernel, half),
        in_specs=[vmem, vmem],
        out_specs=[vmem] * rounds,
        out_shape=[shape] * rounds,
        compiler_params=pltpu.CompilerParams(vmem_limit_bytes=VMEM_LIMIT),
        name="pack_tokens",
    )(normed_inputs, downs)


def slice_kernel(half, rounds, position, adapter, u_ref, own_ref, other_ref, *refs):
    blocks, outs = refs[:rounds], refs[rounds : 3 * rounds]
    xs, ds, us, ps = refs[3 * rounds :]
    group, core = lax.axis_index("group"), lax.axis_index("tensor")
    home_half, place = group // half, group % half
    slots_here = blocks[0].shape[0] - SPAN
    groups = 2 * half
    ranks = groups * slots_here
    slots = []
    for r, block in enumerate(blocks):
        r1, r2 = r // half, r % half
        source = ((core + r1) % 2) * half + (place + half - r2) % half
        xs[r * SPAN : (r + 1) * SPAN, :] = block[:SPAN, :]
        ds[pl.ds(pl.multiple_of(source * slots_here, slots_here), slots_here), :] = block[SPAN:, :]
        slots.append(position[adapter[source * 2 + core]])
    for t in range(2):
        for g in range(groups):
            us[t, g * slots_here : (g + 1) * slots_here, :] = u_ref[2 * g + t]
    shrink = dot_last(xs[...], ds[...])
    which = lax.broadcasted_iota(jnp.int32, (SPAN, ranks), 1) // RANK
    masked = [
        jnp.where(which == slots[r], shrink[r * SPAN : (r + 1) * SPAN, :], 0.0) for r in range(rounds)
    ]
    shrink = (jnp.concatenate(masked, axis=0) * ADAPTER_SCALE).astype(jnp.bfloat16)
    for index, weights in ((core, own_ref), (1 - core, other_ref)):
        ps[index] = (dot(xs[...], weights[...]) + dot(shrink, us[index])).astype(jnp.bfloat16)
    for r in range(rounds):
        outs[2 * r][...] = ps[home_half, r * SPAN : (r + 1) * SPAN, :]
        outs[2 * r + 1][...] = ps[1 - home_half, r * SPAN : (r + 1) * SPAN, :]


def slice_products(blocks, own, other, ups, position, adapter, half):
    rounds = len(blocks)
    width, cols = own.shape
    ranks = rounds * (blocks[0].shape[0] - SPAN)
    vmem = pl.BlockSpec(memory_space=pltpu.VMEM)
    smem = pl.BlockSpec(memory_space=pltpu.SMEM)
    return pl.pallas_call(
        functools.partial(slice_kernel, half, rounds),
        in_specs=[smem, smem] + [vmem] * (3 + rounds),
        out_specs=[vmem] * (2 * rounds),
        out_shape=[jax.ShapeDtypeStruct((SPAN, cols), jnp.bfloat16)] * (2 * rounds),
        scratch_shapes=[
            pltpu.VMEM((rounds * SPAN, width), jnp.bfloat16),
            pltpu.VMEM((ranks, width), jnp.bfloat16),
            pltpu.VMEM((2, ranks, cols), jnp.bfloat16),
            pltpu.VMEM((2, rounds * SPAN, cols), jnp.bfloat16),
        ],
        compiler_params=pltpu.CompilerParams(vmem_limit_bytes=VMEM_LIMIT),
        name="slice_products",
    )(position, adapter, ups, own, other, *blocks)


def finish_kernel(half, rounds, mixed_ref, pf_ref, *refs):
    parts, (out_ref, values_ref, vals) = refs[: 2 * rounds], refs[2 * rounds :]
    group = lax.axis_index("group")
    span, kv = pl.program_id(0), pl.program_id(1)
    rows = pf_ref.shape[0]

    @pl.when((span == 0) & (kv == 0))
    def _():
        for r1 in range(2):
            total = None
            for part in parts[2 * r1 * half : 2 * (r1 + 1) * half]:
                part = part[...].astype(jnp.float32)
                total = part if total is None else total + part
            total = total.astype(jnp.bfloat16)
            home = (group // half + r1) % 2
            values_ref[pl.ds(pl.multiple_of(home * SPAN, SPAN), SPAN), :] = total
            for k in range(total.shape[1] // HD):
                vals[home, k] = total[:, k * HD : (k + 1) * HD]

    fresh = dot(pf_ref[...], vals[span, kv])
    for h in range(rows // SPAN):
        cols = slice(h * HD, (h + 1) * HD)
        out_ref[:, cols] = (mixed_ref[:, cols] + fresh[h * SPAN : (h + 1) * SPAN, :]).astype(jnp.bfloat16)


def finish(mixed, fresh_probs, parts, half):
    rounds = len(parts) // 2
    cols = parts[0].shape[1]
    kv_heads = cols // HD
    tokens, q_width = mixed.shape
    spans = tokens // SPAN
    rows = fresh_probs.shape[0] // (spans * kv_heads)
    head_width = q_width // kv_heads
    return pl.pallas_call(
        functools.partial(finish_kernel, half, rounds),
        grid=(spans, kv_heads),
        in_specs=[
            pl.BlockSpec((SPAN, head_width), lambda s, k: (s, k)),
            pl.BlockSpec((rows, SPAN), lambda s, k: (s * kv_heads + k, 0)),
        ]
        + [pl.BlockSpec((SPAN, cols), lambda s, k: (0, 0))] * (2 * rounds),
        out_specs=[
            pl.BlockSpec((SPAN, head_width), lambda s, k: (s, k)),
            pl.BlockSpec((tokens, cols), lambda s, k: (0, 0)),
        ],
        out_shape=[
            jax.ShapeDtypeStruct((tokens, q_width), jnp.bfloat16),
            jax.ShapeDtypeStruct((tokens, cols), jnp.bfloat16),
        ],
        scratch_shapes=[pltpu.VMEM((spans, kv_heads, SPAN, HD), jnp.bfloat16)],
        compiler_params=pltpu.CompilerParams(vmem_limit_bytes=VMEM_LIMIT),
        name="finish_attention",
    )(mixed, fresh_probs, *parts)


def on_device(
    normed_inputs,
    value_matrix,
    adapter_down_weight,
    adapter_up_weight,
    adapter_position,
    span_adapter_index,
    queries,
    incoming_keys,
    stored_keys,
    stored_values,
    cache_length,
):
    groups = lax.axis_size("group")
    half = groups // 2
    rounds = 2 * half
    width, cols = value_matrix.shape
    downs = adapter_down_weight.reshape(-1, adapter_down_weight.shape[2])
    ups = adapter_up_weight.reshape(-1, cols)

    def there(r, g, t):
        a, b = g // half, g % half
        return t * half + (b + r % half) % half, (a + r // half) % 2

    def pairs(r):
        return [((g, t), there(r, g, t)) for g in range(groups) for t in range(2)]

    def flat(place):
        return place[0] * 2 + place[1]

    sent = pack(normed_inputs, downs, width, half)
    blocks = [
        lax.ppermute(sent[r], BOTH, [(flat(s), flat(d)) for s, d in pairs(r)]) for r in range(rounds)
    ]
    other = lax.ppermute(value_matrix, "tensor", [(0, 1), (1, 0)])
    ups_all = lax.all_gather(ups, BOTH, axis=0)
    mixed, fresh_probs = cache_attention(queries, incoming_keys, stored_keys, stored_values, cache_length)
    products = slice_products(
        blocks, value_matrix, other, ups_all, adapter_position, span_adapter_index, half
    )
    parts = []
    for r in range(rounds):
        same = [(flat(d), flat((s[0], d[0] // half))) for s, d in pairs(r)]
        cross = [(flat(d), flat((s[0], 1 - d[0] // half))) for s, d in pairs(r)]
        parts.append(lax.ppermute(products[2 * r], BOTH, same))
        parts.append(lax.ppermute(products[2 * r + 1], BOTH, cross))
    attended, incoming_values = finish(mixed, fresh_probs, parts, half)
    return (attended, incoming_values)


def solution(mesh):
    in_specs = (
        P(("parts", "group"), "tensor"),
        P("group", "tensor"),
        P("group", None, None),
        P("group", None, "tensor"),
        P(),
        P("parts"),
        P(("parts", "group"), "tensor"),
        P(("parts", "group"), "tensor"),
        P(("parts", "group"), None, "tensor"),
        P(("parts", "group"), None, "tensor"),
        P(("parts", "group")),
    )
    out_specs = (P(("parts", "group"), "tensor"), P(("parts", "group"), "tensor"))
    return jax.shard_map(
        on_device, mesh=mesh, in_specs=in_specs, out_specs=out_specs, check_vma=False
    )
```

```python
import functools
import math

import jax
import jax.numpy as jnp
from jax import lax
from jax.experimental import pallas as pl
from jax.experimental.pallas import tpu as pltpu
from jax.sharding import PartitionSpec as P

HD = 128
RANK = 16
SPAN = 64
CHUNK = 512
ADAPTER_SCALE = 2.0
EXP2_SCALE = math.log2(math.e) / math.sqrt(HD)
DEAD = -1e30
BOTH = ("group", "tensor")
VMEM_LIMIT = 56 * 1024 * 1024


def dot_last(a, b):
    return lax.dot_general(a, b, (((1,), (1,)), ((), ())), preferred_element_type=jnp.float32)


def dot(a, b):
    return jnp.dot(a, b, preferred_element_type=jnp.float32)


def cache_kernel(kv_heads, group_size, lens, q_ref, fk_ref, k_ref, v_ref, out_ref, pf_ref, qs, m_s, l_s, acc):
    span, step = pl.program_id(0), pl.program_id(1)
    length = lens[span]
    rows = group_size * SPAN
    chunk = k_ref.shape[1]

    def fresh_scores(k):
        s = dot_last(fk_ref[:, k * HD : (k + 1) * HD], qs[k])
        key = lax.broadcasted_iota(jnp.int32, (SPAN, rows), 0)
        token = lax.broadcasted_iota(jnp.int32, (SPAN, rows), 1) % SPAN
        return jnp.where(key <= token, s, DEAD)

    @pl.when(step == 0)
    def _():
        for k in range(kv_heads):
            for h in range(group_size):
                col = (k * group_size + h) * HD
                qs[k, h * SPAN : (h + 1) * SPAN, :] = q_ref[:, col : col + HD]
            s = fresh_scores(k)
            top = jnp.max(s, axis=0, keepdims=True)
            m_s[k] = top
            l_s[k] = jnp.sum(jnp.exp2((s - top) * EXP2_SCALE), axis=0, keepdims=True)
            acc[k] = jnp.zeros((HD, rows), jnp.float32)

    def add_chunk(masked):
        for k in range(kv_heads):
            s = dot_last(k_ref[0, :, k * HD : (k + 1) * HD], qs[k])
            if masked:
                slot = step * chunk + lax.broadcasted_iota(jnp.int32, (chunk, rows), 0)
                s = jnp.where(slot < length, s, DEAD)
            before = m_s[k]
            top = jnp.maximum(before, jnp.max(s, axis=0, keepdims=True))
            alpha = jnp.exp2((before - top) * EXP2_SCALE)
            p = jnp.exp2((s - top) * EXP2_SCALE)
            m_s[k] = top
            l_s[k] = l_s[k] * alpha + jnp.sum(p, axis=0, keepdims=True)
            values = v_ref[0, :, k * HD : (k + 1) * HD].T
            acc[k] = acc[k] * alpha + dot(values, p.astype(jnp.bfloat16))

    @pl.when((step + 1) * chunk <= length)
    def _():
        add_chunk(False)

    @pl.when((step * chunk < length) & ((step + 1) * chunk > length))
    def _():
        add_chunk(True)

    @pl.when(step == pl.num_programs(1) - 1)
    def _():
        for k in range(kv_heads):
            inverse = 1.0 / l_s[k]
            p = jnp.exp2((fresh_scores(k) - m_s[k]) * EXP2_SCALE) * inverse
            pf_ref[k * rows : (k + 1) * rows, :] = p.T.astype(jnp.bfloat16)
            mixed = (acc[k] * inverse).T
            for h in range(group_size):
                col = (k * group_size + h) * HD
                out_ref[:, col : col + HD] = mixed[h * SPAN : (h + 1) * SPAN, :]


def cache_attention(queries, fresh_keys, keys, values, lengths):
    spans, slots, width = keys.shape
    kv_heads = width // HD
    q_width = queries.shape[1]
    group_size = q_width // width
    rows = group_size * SPAN
    chunk = min(CHUNK, slots)
    steps = slots // chunk

    def kv_index(s, i, lens):
        return (s, jnp.minimum(i, (lens[s] - 1) // chunk), 0)

    return pl.pallas_call(
        functools.partial(cache_kernel, kv_heads, group_size),
        grid_spec=pltpu.PrefetchScalarGridSpec(
            num_scalar_prefetch=1,
            grid=(spans, steps),
            in_specs=[
                pl.BlockSpec((SPAN, q_width), lambda s, i, lens: (s, 0)),
                pl.BlockSpec((SPAN, width), lambda s, i, lens: (s, 0)),
                pl.BlockSpec((1, chunk, width), kv_index),
                pl.BlockSpec((1, chunk, width), kv_index),
            ],
            out_specs=[
                pl.BlockSpec((SPAN, q_width), lambda s, i, lens: (s, 0)),
                pl.BlockSpec((kv_heads * rows, SPAN), lambda s, i, lens: (s, 0)),
            ],
            scratch_shapes=[
                pltpu.VMEM((kv_heads, rows, HD), jnp.bfloat16),
                pltpu.VMEM((kv_heads, 1, rows), jnp.float32),
                pltpu.VMEM((kv_heads, 1, rows), jnp.float32),
                pltpu.VMEM((kv_heads, HD, rows), jnp.float32),
            ],
        ),
        out_shape=[
            jax.ShapeDtypeStruct((spans * SPAN, q_width), jnp.float32),
            jax.ShapeDtypeStruct((spans * kv_heads * rows, SPAN), jnp.bfloat16),
        ],
        compiler_params=pltpu.CompilerParams(vmem_limit_bytes=VMEM_LIMIT),
        cost_estimate=pl.CostEstimate(
            flops=4 * spans * kv_heads * rows * slots * HD,
            bytes_accessed=2 * spans * slots * width * 2,
            transcendentals=spans * kv_heads * rows * slots,
        ),
        name="cache_attention",
    )(lengths, queries, fresh_keys, keys, values)


def pack_kernel(x_ref, x_other, d_ref, u_ref, u_other, out):
    core = lax.axis_index("tensor")
    groups, _, width = out.shape
    half = groups // 2
    cols = u_ref.shape[1]
    mine = pl.ds(pl.multiple_of(core * RANK, RANK), RANK)
    for piece in range(half):
        here = slice(piece * width, (piece + 1) * width)
        out[core * half + piece, :SPAN, :] = x_ref[pl.ds(pl.multiple_of(core * SPAN, SPAN), SPAN), here]
        out[(1 - core) * half + piece, :SPAN, :] = x_other[:, here]
    for g in range(groups):
        out[g, SPAN : SPAN + RANK, :] = d_ref[mine, g * width : (g + 1) * width]
        for side, ups in ((core, u_ref), (1 - core, u_other)):
            for begin in range(0, cols, min(cols, width)):
                place = side * cols + begin
                row = pl.multiple_of(SPAN + RANK + place // width * RANK, RANK)
                column = pl.multiple_of(place % width, min(cols, width))
                out[g, pl.ds(row, RANK), pl.ds(column, min(cols, width))] = ups[mine, begin : begin + min(cols, width)]


def pack(tokens, tokens_other, downs, ups, ups_other, width, groups):
    vmem = pl.BlockSpec(memory_space=pltpu.VMEM)
    pieces = 2 * ups.shape[1] // width
    return pl.pallas_call(
        pack_kernel,
        in_specs=[vmem] * 5,
        out_specs=vmem,
        out_shape=jax.ShapeDtypeStruct((groups, SPAN + (1 + pieces) * RANK, width), jnp.bfloat16),
        compiler_params=pltpu.CompilerParams(vmem_limit_bytes=VMEM_LIMIT),
        name="pack_tokens",
    )(tokens, tokens_other, downs, ups, ups_other)


def slice_kernel(position, adapter, got, maps_other, own_ref, other_ref, out, xs, ds, us):
    core = lax.axis_index("tensor")
    groups, _, width = got.shape
    cols = own_ref.shape[1]
    ranks = ds.shape[0]
    for g in range(groups):
        xs[g * SPAN : (g + 1) * SPAN, :] = got[g, :SPAN, :]
        mine = pl.ds(pl.multiple_of((2 * g + core) * RANK, RANK), RANK)
        theirs = pl.ds(pl.multiple_of((2 * g + 1 - core) * RANK, RANK), RANK)
        ds[mine, :] = got[g, SPAN : SPAN + RANK, :]
        ds[theirs, :] = maps_other[g, :RANK, :]
        for i in range(2 * cols // width):
            here = slice(i * width, (i + 1) * width)
            us[mine, here] = got[g, SPAN + (1 + i) * RANK : SPAN + (2 + i) * RANK, :]
            us[theirs, here] = maps_other[g, (1 + i) * RANK : (2 + i) * RANK, :]
    shrink = dot_last(xs[...], ds[...])
    which = lax.broadcasted_iota(jnp.int32, (SPAN, ranks), 1) // RANK
    masked = [
        jnp.where(which == position[adapter[2 * g + core]], shrink[g * SPAN : (g + 1) * SPAN, :], 0.0)
        for g in range(groups)
    ]
    shrink = (jnp.concatenate(masked, axis=0) * ADAPTER_SCALE).astype(jnp.bfloat16)
    for side, weights in ((core, own_ref), (1 - core, other_ref)):
        up = us[:, pl.ds(pl.multiple_of(side * cols, cols), cols)]
        product = (dot(xs[...], weights[...]) + dot(shrink, up)).astype(jnp.bfloat16)
        for g in range(groups):
            out[2 * g + side] = product[g * SPAN : (g + 1) * SPAN, :]


def slice_products(got, maps_other, own, other, position, adapter):
    groups, _, width = got.shape
    cols = own.shape[1]
    ranks = groups * 2 * RANK
    vmem = pl.BlockSpec(memory_space=pltpu.VMEM)
    smem = pl.BlockSpec(memory_space=pltpu.SMEM)
    return pl.pallas_call(
        slice_kernel,
        in_specs=[smem, smem] + [vmem] * 4,
        out_specs=vmem,
        out_shape=jax.ShapeDtypeStruct((2 * groups, SPAN, cols), jnp.bfloat16),
        scratch_shapes=[
            pltpu.VMEM((groups * SPAN, width), jnp.bfloat16),
            pltpu.VMEM((ranks, width), jnp.bfloat16),
            pltpu.VMEM((ranks, 2 * cols), jnp.bfloat16),
        ],
        compiler_params=pltpu.CompilerParams(vmem_limit_bytes=VMEM_LIMIT),
        name="slice_products",
    )(position, adapter, got, maps_other, own, other)


def finish_kernel(mixed_ref, pf_ref, parts, out_ref, values_ref, vals):
    span, kv = pl.program_id(0), pl.program_id(1)
    rows = pf_ref.shape[0]

    @pl.when((span == 0) & (kv == 0))
    def _():
        for u in range(2):
            total = parts[u].astype(jnp.float32)
            for g in range(1, parts.shape[0] // 2):
                total = total + parts[2 * g + u].astype(jnp.float32)
            total = total.astype(jnp.bfloat16)
            values_ref[u * SPAN : (u + 1) * SPAN, :] = total
            for k in range(total.shape[1] // HD):
                vals[u, k] = total[:, k * HD : (k + 1) * HD]

    fresh = dot(pf_ref[...], vals[span, kv])
    for h in range(rows // SPAN):
        cols = slice(h * HD, (h + 1) * HD)
        out_ref[:, cols] = (mixed_ref[:, cols] + fresh[h * SPAN : (h + 1) * SPAN, :]).astype(jnp.bfloat16)


def finish(mixed, fresh_probs, parts):
    cols = parts.shape[2]
    kv_heads = cols // HD
    tokens, q_width = mixed.shape
    spans = tokens // SPAN
    rows = fresh_probs.shape[0] // (spans * kv_heads)
    head_width = q_width // kv_heads
    return pl.pallas_call(
        finish_kernel,
        grid=(spans, kv_heads),
        in_specs=[
            pl.BlockSpec((SPAN, head_width), lambda s, k: (s, k)),
            pl.BlockSpec((rows, SPAN), lambda s, k: (s * kv_heads + k, 0)),
            pl.BlockSpec(parts.shape, lambda s, k: (0, 0, 0)),
        ],
        out_specs=[
            pl.BlockSpec((SPAN, head_width), lambda s, k: (s, k)),
            pl.BlockSpec((tokens, cols), lambda s, k: (0, 0)),
        ],
        out_shape=[
            jax.ShapeDtypeStruct((tokens, q_width), jnp.bfloat16),
            jax.ShapeDtypeStruct((tokens, cols), jnp.bfloat16),
        ],
        scratch_shapes=[pltpu.VMEM((spans, kv_heads, SPAN, HD), jnp.bfloat16)],
        compiler_params=pltpu.CompilerParams(vmem_limit_bytes=VMEM_LIMIT),
        name="finish_attention",
    )(mixed, fresh_probs, parts)


def on_device(
    normed_inputs,
    value_matrix,
    adapter_down_weight,
    adapter_up_weight,
    adapter_position,
    span_adapter_index,
    queries,
    incoming_keys,
    stored_keys,
    stored_values,
    cache_length,
):
    groups = lax.axis_size("group")
    core = lax.axis_index("tensor")
    width, cols = value_matrix.shape
    downs = adapter_down_weight.reshape(-1, adapter_down_weight.shape[2])
    ups = adapter_up_weight.reshape(-1, cols)
    swap = [(0, 1), (1, 0)]

    leaving = lax.dynamic_slice_in_dim(normed_inputs, (1 - core) * SPAN, SPAN, 0)
    tokens_other = lax.ppermute(leaving, "tensor", swap)
    ups_other = lax.ppermute(ups, "tensor", swap)
    other = lax.ppermute(value_matrix, "tensor", swap)
    sent = pack(normed_inputs, tokens_other, downs, ups, ups_other, width, groups)
    got = lax.all_to_all(sent, "group", 0, 0)
    maps_other = lax.ppermute(got[:, SPAN:], "tensor", swap)
    mixed, fresh_probs = cache_attention(queries, incoming_keys, stored_keys, stored_values, cache_length)
    products = slice_products(got, maps_other, value_matrix, other, adapter_position, span_adapter_index)
    parts = lax.all_to_all(products, BOTH, 0, 0)
    attended, incoming_values = finish(mixed, fresh_probs, parts)
    return (attended, incoming_values)


def solution(mesh):
    in_specs = (
        P(("parts", "group"), "tensor"),
        P("group", "tensor"),
        P("group", None, None),
        P("group", None, "tensor"),
        P(),
        P("parts"),
        P(("parts", "group"), "tensor"),
        P(("parts", "group"), "tensor"),
        P(("parts", "group"), None, "tensor"),
        P(("parts", "group"), None, "tensor"),
        P(("parts", "group")),
    )
    out_specs = (P(("parts", "group"), "tensor"), P(("parts", "group"), "tensor"))
    return jax.shard_map(
        on_device, mesh=mesh, in_specs=in_specs, out_specs=out_specs, check_vma=False
    )
```

```python
import functools
import math

import jax
import jax.numpy as jnp
from jax import lax
from jax.experimental import pallas as pl
from jax.experimental.pallas import tpu as pltpu
from jax.sharding import Mesh
from jax.sharding import PartitionSpec as P

HD = 128
RANK = 16
SPAN = 64
CHUNK = 512
CHUNKS = 2
ADAPTER_SCALE = 2.0
EXP2_SCALE = math.log2(math.e) / math.sqrt(HD)
DEAD = -1e30
MIB = 1024 * 1024
SWAP = [(0, 1), (1, 0)]


def dot_last(a, b):
    return lax.dot_general(a, b, (((1,), (1,)), ((), ())), preferred_element_type=jnp.float32)


def dot(a, b):
    return jnp.dot(a, b, preferred_element_type=jnp.float32)


def cache_kernel(span, kv_heads, group_size, lens, q_ref, fk_ref, k_ref, v_ref, out_ref, pf_ref, qs, m_s, l_s, acc):
    step = pl.program_id(0)
    length = lens[span]
    rows = group_size * SPAN
    chunk = k_ref.shape[1]

    def fresh_scores(k):
        s = dot_last(fk_ref[:, k * HD : (k + 1) * HD], qs[k])
        key = lax.broadcasted_iota(jnp.int32, (SPAN, rows), 0)
        token = lax.broadcasted_iota(jnp.int32, (SPAN, rows), 1) % SPAN
        return jnp.where(key <= token, s, DEAD)

    @pl.when(step == 0)
    def _():
        for k in range(kv_heads):
            for h in range(group_size):
                col = (k * group_size + h) * HD
                qs[k, h * SPAN : (h + 1) * SPAN, :] = q_ref[:, col : col + HD]
            s = fresh_scores(k)
            top = jnp.max(s, axis=0, keepdims=True)
            m_s[k] = top
            l_s[k] = jnp.sum(jnp.exp2((s - top) * EXP2_SCALE), axis=0, keepdims=True)
            acc[k] = jnp.zeros((HD, rows), jnp.float32)

    def add_chunk(masked):
        for k in range(kv_heads):
            s = dot_last(k_ref[0, :, k * HD : (k + 1) * HD], qs[k])
            if masked:
                slot = step * chunk + lax.broadcasted_iota(jnp.int32, (chunk, rows), 0)
                s = jnp.where(slot < length, s, DEAD)
            before = m_s[k]
            top = jnp.maximum(before, jnp.max(s, axis=0, keepdims=True))
            alpha = jnp.exp2((before - top) * EXP2_SCALE)
            p = jnp.exp2((s - top) * EXP2_SCALE)
            m_s[k] = top
            l_s[k] = l_s[k] * alpha + jnp.sum(p, axis=0, keepdims=True)
            values = v_ref[0, :, k * HD : (k + 1) * HD].T
            acc[k] = acc[k] * alpha + dot(values, p.astype(jnp.bfloat16))

    @pl.when((step + 1) * chunk <= length)
    def _():
        add_chunk(False)

    @pl.when((step * chunk < length) & ((step + 1) * chunk > length))
    def _():
        add_chunk(True)

    @pl.when(step == pl.num_programs(0) - 1)
    def _():
        for k in range(kv_heads):
            inverse = 1.0 / l_s[k]
            p = jnp.exp2((fresh_scores(k) - m_s[k]) * EXP2_SCALE) * inverse
            pf_ref[k * rows : (k + 1) * rows, :] = p.T.astype(jnp.bfloat16)
            mixed = (acc[k] * inverse).T
            for h in range(group_size):
                col = (k * group_size + h) * HD
                out_ref[:, col : col + HD] = mixed[h * SPAN : (h + 1) * SPAN, :]


def cache_attention(span, queries, fresh_keys, keys, values, lengths):
    _, slots, width = keys.shape
    kv_heads = width // HD
    q_width = queries.shape[1]
    group_size = q_width // width
    rows = group_size * SPAN
    chunk = min(CHUNK, slots)
    steps = slots // chunk

    def kv_index(i, lens):
        return (span, jnp.minimum(i, (lens[span] - 1) // chunk), 0)

    return pl.pallas_call(
        functools.partial(cache_kernel, span, kv_heads, group_size),
        grid_spec=pltpu.PrefetchScalarGridSpec(
            num_scalar_prefetch=1,
            grid=(steps,),
            in_specs=[
                pl.BlockSpec((SPAN, q_width), lambda i, lens: (span, 0)),
                pl.BlockSpec((SPAN, width), lambda i, lens: (span, 0)),
                pl.BlockSpec((1, chunk, width), kv_index),
                pl.BlockSpec((1, chunk, width), kv_index),
            ],
            out_specs=[
                pl.BlockSpec((SPAN, q_width), lambda i, lens: (0, 0)),
                pl.BlockSpec((kv_heads * rows, SPAN), lambda i, lens: (0, 0)),
            ],
            scratch_shapes=[
                pltpu.VMEM((kv_heads, rows, HD), jnp.bfloat16),
                pltpu.VMEM((kv_heads, 1, rows), jnp.float32),
                pltpu.VMEM((kv_heads, 1, rows), jnp.float32),
                pltpu.VMEM((kv_heads, HD, rows), jnp.float32),
            ],
        ),
        out_shape=[
            jax.ShapeDtypeStruct((SPAN, q_width), jnp.float32),
            jax.ShapeDtypeStruct((kv_heads * rows, SPAN), jnp.bfloat16),
        ],
        compiler_params=pltpu.CompilerParams(vmem_limit_bytes=32 * MIB),
        cost_estimate=pl.CostEstimate(
            flops=4 * kv_heads * rows * slots * HD,
            bytes_accessed=2 * slots * width * 2,
            transcendentals=kv_heads * rows * slots,
        ),
        name="cache_attention",
    )(lengths, queries, fresh_keys, keys, values)


def rows_kernel(w_ref, *refs):
    outs, sems = refs[:-1], refs[-1]
    chunk = outs[0].shape[0]
    first = lax.axis_index("parts") % 2 * (chunk * len(outs))
    copies = []
    for i, out in enumerate(outs):
        begin = pl.multiple_of(first + i * chunk, chunk)
        copies.append(pltpu.make_async_copy(w_ref.at[pl.ds(begin, chunk), :], out, sems.at[i]))
    for copy in copies:
        copy.start()
    for copy in copies:
        copy.wait()


def rows_to_send(weights, chunks):
    width, cols = weights.shape
    anywhere = pl.BlockSpec(memory_space=pl.ANY)
    return pl.pallas_call(
        rows_kernel,
        in_specs=[anywhere],
        out_specs=[anywhere] * chunks,
        out_shape=[jax.ShapeDtypeStruct((width // 2 // chunks, cols), weights.dtype)] * chunks,
        scratch_shapes=[pltpu.SemaphoreType.DMA((chunks,))],
        name="rows_to_send",
    )(weights)


def pack_kernel(x_ref, d_ref, u_ref, xs, du):
    part, core = lax.axis_index("parts") % 2, lax.axis_index("tensor")
    quads, _, width = xs.shape
    groups, _, sub = du.shape
    cols = u_ref.shape[1]
    mine = pl.ds(pl.multiple_of(part * RANK, RANK), RANK)
    downs = width // sub
    for j in range(quads):
        xs[j] = x_ref[:, j * width : (j + 1) * width]
        begin = core * (quads * width) + j * width
        for wing in range(2):
            g = wing * quads + j
            for i in range(downs):
                piece = pl.ds(pl.multiple_of(begin + i * sub, sub), sub)
                du[g, i * RANK : (i + 1) * RANK, :] = d_ref[mine, piece]
            for i in range(cols // sub):
                row = (downs + i) * RANK
                du[g, row : row + RANK, :] = u_ref[mine, i * sub : (i + 1) * sub]


def pack(tokens, downs, ups, width, quads):
    vmem = pl.BlockSpec(memory_space=pltpu.VMEM)
    cols = ups.shape[1]
    sub = min(width, cols)
    rows = RANK * (width // sub + cols // sub)
    return pl.pallas_call(
        pack_kernel,
        in_specs=[vmem] * 3,
        out_specs=[vmem] * 2,
        out_shape=[
            jax.ShapeDtypeStruct((quads, tokens.shape[0], width), tokens.dtype),
            jax.ShapeDtypeStruct((2 * quads, rows, sub), downs.dtype),
        ],
        compiler_params=pltpu.CompilerParams(vmem_limit_bytes=8 * MIB),
        name="pack_tokens",
    )(tokens, downs, ups)


def near_kernel(position, adapter, x_mine, x_theirs, own_ref, du_a, du_b, du_c, du_d, out, ds, us):
    part, core, wing = lax.axis_index("parts") % 2, lax.axis_index("tensor"), lax.axis_index("wing")
    quads, tokens, width = x_mine.shape
    groups, _, sub = du_a.shape
    cols = own_ref.shape[1]
    ranks = us.shape[0]
    downs = width // sub
    for g in range(groups):
        for parity, mine, theirs in ((part, du_a, du_c), (1 - part, du_b, du_d)):
            rows = pl.ds(pl.multiple_of((2 * g + parity) * RANK, RANK), RANK)
            for i in range(downs):
                here = slice(i * sub, (i + 1) * sub)
                ds[0, rows, here] = mine[g, i * RANK : (i + 1) * RANK, :]
                ds[1, rows, here] = theirs[g, i * RANK : (i + 1) * RANK, :]
            for i in range(cols // sub):
                row = (downs + i) * RANK
                us[rows, i * sub : (i + 1) * sub] = mine[g, row : row + RANK, :]
    flat = (quads * tokens, width)
    shrink = dot_last(x_mine[...].reshape(flat), ds[0]) + dot_last(x_theirs[...].reshape(flat), ds[1])
    which = lax.broadcasted_iota(jnp.int32, (SPAN, ranks), 1) // RANK
    spans = tokens // SPAN
    masked = []
    for i in range(quads * spans):
        slot = position[adapter[wing * (quads * spans) + i]]
        masked.append(jnp.where(which == slot, shrink[i * SPAN : (i + 1) * SPAN, :], 0.0))
    shrink = (jnp.concatenate(masked, axis=0) * ADAPTER_SCALE).astype(jnp.bfloat16)
    out[...] = dot(shrink, us[...])

    @pl.when(core == wing)
    def _():
        out[...] += dot(x_mine[...].reshape(flat), own_ref[...])

    @pl.when(core != wing)
    def _():
        out[...] += dot(x_theirs[...].reshape(flat), own_ref[...])


def near_products(x_mine, x_theirs, own, maps, position, adapter):
    quads, tokens, width = x_mine.shape
    cols = own.shape[1]
    ranks = 2 * maps[0].shape[0] * RANK
    vmem = pl.BlockSpec(memory_space=pltpu.VMEM)
    smem = pl.BlockSpec(memory_space=pltpu.SMEM)
    return pl.pallas_call(
        near_kernel,
        in_specs=[smem, smem] + [vmem] * 7,
        out_specs=vmem,
        out_shape=jax.ShapeDtypeStruct((quads * tokens, cols), jnp.float32),
        scratch_shapes=[
            pltpu.VMEM((2, ranks, width), jnp.bfloat16),
            pltpu.VMEM((ranks, cols), jnp.bfloat16),
        ],
        compiler_params=pltpu.CompilerParams(vmem_limit_bytes=48 * MIB if quads > 4 else 24 * MIB),
        cost_estimate=pl.CostEstimate(
            flops=2 * quads * tokens * width * (cols + 2 * ranks), bytes_accessed=6 * MIB, transcendentals=0
        ),
        name="near_products",
    )(position, adapter, x_mine, x_theirs, own, *maps)


def far_kernel(x_mine, x_theirs, near, *refs):
    weights, out, whole = refs[:-2], refs[-2], refs[-1]
    part, core, wing = lax.axis_index("parts") % 2, lax.axis_index("tensor"), lax.axis_index("wing")
    quads, tokens, width = x_mine.shape
    flat = (quads * tokens, width)
    chunk = weights[0].shape[0]
    chunks = len(weights) // 2
    for side in range(2):
        first = (part if side == 0 else 1 - part) * (chunks * chunk)
        for i in range(chunks):
            begin = pl.multiple_of(first + i * chunk, chunk)
            whole[pl.ds(begin, chunk), :] = weights[side * chunks + i][...]

    def store(x):
        out[...] = (near[...] + dot(x[...].reshape(flat), whole[...])).astype(jnp.bfloat16).reshape(out.shape)

    @pl.when(core == wing)
    def _():
        store(x_theirs)

    @pl.when(core != wing)
    def _():
        store(x_mine)


def far_products(x_mine, x_theirs, near, weights):
    quads, tokens, width = x_mine.shape
    cols = near.shape[1]
    vmem = pl.BlockSpec(memory_space=pltpu.VMEM)
    return pl.pallas_call(
        far_kernel,
        in_specs=[vmem] * (3 + len(weights)),
        out_specs=vmem,
        out_shape=jax.ShapeDtypeStruct((quads, tokens, cols), jnp.bfloat16),
        scratch_shapes=[pltpu.VMEM((width, cols), jnp.bfloat16)],
        compiler_params=pltpu.CompilerParams(vmem_limit_bytes=48 * MIB if quads > 4 else 16 * MIB),
        cost_estimate=pl.CostEstimate(
            flops=2 * quads * tokens * width * cols, bytes_accessed=5 * MIB, transcendentals=0
        ),
        name="far_products",
    )(x_mine, x_theirs, near, *weights)


def finish_kernel(spans, parts, *refs):
    mixed, probs, (out_ref, values_ref) = refs[:spans], refs[spans : 2 * spans], refs[2 * spans :]
    total = parts[0].astype(jnp.float32)
    for j in range(1, parts.shape[0]):
        total = total + parts[j].astype(jnp.float32)
    total = total.astype(jnp.bfloat16)
    values_ref[...] = total
    kv_heads = total.shape[1] // HD
    for span in range(spans):
        rows = slice(span * SPAN, (span + 1) * SPAN)
        count = probs[span].shape[0] // kv_heads
        for k in range(kv_heads):
            fresh = dot(probs[span][k * count : (k + 1) * count, :], total[rows, k * HD : (k + 1) * HD])
            for h in range(count // SPAN):
                col = (k * (count // SPAN) + h) * HD
                out_ref[rows, col : col + HD] = (
                    mixed[span][:, col : col + HD] + fresh[h * SPAN : (h + 1) * SPAN, :]
                ).astype(jnp.bfloat16)


def finish(mixed, fresh_probs, parts):
    _, tokens, cols = parts.shape
    vmem = pl.BlockSpec(memory_space=pltpu.VMEM)
    return pl.pallas_call(
        functools.partial(finish_kernel, len(mixed)),
        in_specs=[vmem] * (1 + 2 * len(mixed)),
        out_specs=[vmem] * 2,
        out_shape=[
            jax.ShapeDtypeStruct((tokens, mixed[0].shape[1]), jnp.bfloat16),
            jax.ShapeDtypeStruct((tokens, cols), jnp.bfloat16),
        ],
        compiler_params=pltpu.CompilerParams(vmem_limit_bytes=16 * MIB),
        name="finish_attention",
    )(parts, *mixed, *fresh_probs)


def on_device(
    normed_inputs,
    value_matrix,
    adapter_down_weight,
    adapter_up_weight,
    adapter_position,
    span_adapter_index,
    queries,
    incoming_keys,
    stored_keys,
    stored_values,
    cache_length,
):
    quads = lax.axis_size("quad")
    parts_swap = [(i, i ^ 1) for i in range(lax.axis_size("parts"))]
    width, cols = value_matrix.shape
    downs = adapter_down_weight.reshape(-1, adapter_down_weight.shape[2])
    ups = adapter_up_weight.reshape(-1, cols)

    def attention(span, lengths):
        return cache_attention(span, queries, incoming_keys, stored_keys, stored_values, lengths)

    leaving = rows_to_send(value_matrix, CHUNKS)
    far = [lax.ppermute(rows, "wing", SWAP) for rows in leaving]
    xs, du = pack(normed_inputs, downs, ups, width, quads)
    x_mine = lax.all_to_all(xs, "quad", 0, 0)
    maps_a = lax.all_to_all(du, ("wing", "quad"), 0, 0)

    lengths, _ = lax.optimization_barrier((cache_length, du))
    first = attention(0, lengths)
    x_mine, maps_a, far_0, _ = lax.optimization_barrier((x_mine, maps_a, far[0], first[1]))
    x_theirs = lax.ppermute(x_mine, "tensor", SWAP)
    maps_b = lax.ppermute(maps_a, "parts", parts_swap)
    maps_c = lax.ppermute(maps_a, "tensor", SWAP)
    far_0_other = lax.ppermute(far_0, "parts", parts_swap)

    lengths, _ = lax.optimization_barrier((cache_length, maps_a))
    second = attention(1, lengths)
    far_1, maps_b, _ = lax.optimization_barrier((far[1], maps_b, second[1]))
    far_1_other = lax.ppermute(far_1, "parts", parts_swap)
    maps_d = lax.ppermute(maps_b, "tensor", SWAP)

    near = near_products(
        x_mine, x_theirs, value_matrix, (maps_a, maps_b, maps_c, maps_d), adapter_position, span_adapter_index
    )
    products = far_products(x_mine, x_theirs, near, (far_0, far_1, far_0_other, far_1_other))
    parts = lax.all_to_all(products, "quad", 0, 0)
    mixed, fresh_probs = zip(first, second)
    attended, incoming_values = finish(mixed, fresh_probs, parts)
    return (attended, incoming_values)


def solution(mesh):
    sizes = mesh.devices.shape
    cut = Mesh(
        mesh.devices.reshape(sizes[0], 2, sizes[1] // 2, sizes[2]), ("parts", "wing", "quad", "tensor")
    )
    group = ("wing", "quad")
    home = ("parts", "wing", "quad")
    in_specs = (
        P(home, "tensor"),
        P(group, "tensor"),
        P(group, None, None),
        P(group, None, "tensor"),
        P(),
        P("parts"),
        P(home, "tensor"),
        P(home, "tensor"),
        P(home, None, "tensor"),
        P(home, None, "tensor"),
        P(home),
    )
    out_specs = (P(home, "tensor"), P(home, "tensor"))
    return jax.shard_map(
        on_device, mesh=cut, in_specs=in_specs, out_specs=out_specs, check_vma=False
    )
```

```python
import functools
import math

import jax
import jax.numpy as jnp
from jax import lax
from jax.experimental import pallas as pl
from jax.experimental.pallas import tpu as pltpu
from jax.sharding import Mesh
from jax.sharding import PartitionSpec as P

HD = 128
RANK = 16
SPAN = 64
CHUNK = 512
CHUNKS = 2
ADAPTER_SCALE = 2.0
EXP2_SCALE = math.log2(math.e) / math.sqrt(HD)
DEAD = -1e30
MIB = 1024 * 1024
SWAP = [(0, 1), (1, 0)]


def dot_last(a, b):
    return lax.dot_general(a, b, (((1,), (1,)), ((), ())), preferred_element_type=jnp.float32)


def dot(a, b):
    return jnp.dot(a, b, preferred_element_type=jnp.float32)


def cache_kernel(span, kv_heads, group_size, lens, q_ref, fk_ref, k_hbm, v_hbm, out_ref, pf_ref, qs, ks, vs, m_s, l_s, acc, sems):
    length = lens[span]
    rows = group_size * SPAN
    chunks, chunk, _ = ks.shape

    def copies(i):
        live = pl.ds(pl.multiple_of(i * chunk, chunk), chunk)
        return (
            pltpu.make_async_copy(k_hbm.at[span, live, :], ks.at[i], sems.at[0, i]),
            pltpu.make_async_copy(v_hbm.at[span, live, :], vs.at[i], sems.at[1, i]),
        )

    for i in range(chunks):

        @pl.when(i * chunk < length)
        def _():
            for copy in copies(i):
                copy.start()

    def fresh_scores(k):
        s = dot_last(fk_ref[span * SPAN : (span + 1) * SPAN, k * HD : (k + 1) * HD], qs[k])
        key = lax.broadcasted_iota(jnp.int32, (SPAN, rows), 0)
        token = lax.broadcasted_iota(jnp.int32, (SPAN, rows), 1) % SPAN
        return jnp.where(key <= token, s, DEAD)

    for k in range(kv_heads):
        for h in range(group_size):
            col = (k * group_size + h) * HD
            qs[k, h * SPAN : (h + 1) * SPAN, :] = q_ref[span * SPAN : (span + 1) * SPAN, col : col + HD]
        s = fresh_scores(k)
        top = jnp.max(s, axis=0, keepdims=True)
        m_s[k] = top
        l_s[k] = jnp.sum(jnp.exp2((s - top) * EXP2_SCALE), axis=0, keepdims=True)
        acc[k] = jnp.zeros((HD, rows), jnp.float32)

    def add_chunk(i, masked):
        for copy in copies(i):
            copy.wait()
        for k in range(kv_heads):
            s = dot_last(ks[i, :, k * HD : (k + 1) * HD], qs[k])
            if masked:
                slot = i * chunk + lax.broadcasted_iota(jnp.int32, (chunk, rows), 0)
                s = jnp.where(slot < length, s, DEAD)
            before = m_s[k]
            top = jnp.maximum(before, jnp.max(s, axis=0, keepdims=True))
            alpha = jnp.exp2((before - top) * EXP2_SCALE)
            p = jnp.exp2((s - top) * EXP2_SCALE)
            m_s[k] = top
            l_s[k] = l_s[k] * alpha + jnp.sum(p, axis=0, keepdims=True)
            values = vs[i, :, k * HD : (k + 1) * HD].T
            acc[k] = acc[k] * alpha + dot(values, p.astype(jnp.bfloat16))

    @pl.loop(0, length // chunk)
    def _(i):
        add_chunk(i, False)

    @pl.when(length % chunk != 0)
    def _():
        add_chunk(length // chunk, True)

    for k in range(kv_heads):
        inverse = 1.0 / l_s[k]
        p = jnp.exp2((fresh_scores(k) - m_s[k]) * EXP2_SCALE) * inverse
        pf_ref[k * rows : (k + 1) * rows, :] = p.T.astype(jnp.bfloat16)
        mixed = (acc[k] * inverse).T
        for h in range(group_size):
            col = (k * group_size + h) * HD
            out_ref[:, col : col + HD] = mixed[h * SPAN : (h + 1) * SPAN, :]


def cache_attention(span, queries, fresh_keys, keys, values, lengths):
    _, slots, width = keys.shape
    kv_heads = width // HD
    q_width = queries.shape[1]
    group_size = q_width // width
    rows = group_size * SPAN
    chunk = min(CHUNK, slots)
    chunks = slots // chunk
    vmem = pl.BlockSpec(memory_space=pltpu.VMEM)
    hbm = pl.BlockSpec(memory_space=pltpu.HBM)
    return pl.pallas_call(
        functools.partial(cache_kernel, span, kv_heads, group_size),
        in_specs=[pl.BlockSpec(memory_space=pltpu.SMEM), vmem, vmem, hbm, hbm],
        out_specs=[vmem, vmem],
        scratch_shapes=[
            pltpu.VMEM((kv_heads, rows, HD), jnp.bfloat16),
            pltpu.VMEM((chunks, chunk, width), jnp.bfloat16),
            pltpu.VMEM((chunks, chunk, width), jnp.bfloat16),
            pltpu.VMEM((kv_heads, 1, rows), jnp.float32),
            pltpu.VMEM((kv_heads, 1, rows), jnp.float32),
            pltpu.VMEM((kv_heads, HD, rows), jnp.float32),
            pltpu.SemaphoreType.DMA((2, chunks)),
        ],
        out_shape=[
            jax.ShapeDtypeStruct((SPAN, q_width), jnp.float32),
            jax.ShapeDtypeStruct((kv_heads * rows, SPAN), jnp.bfloat16),
        ],
        compiler_params=pltpu.CompilerParams(vmem_limit_bytes=57 * MIB),
        name="cache_attention",
    )(lengths, queries, fresh_keys, keys, values)


def cross_kernel(w_ref, d_ref, u_ref, maps, *outs):
    part, core = lax.axis_index("parts") % 2, lax.axis_index("tensor")
    chunk = outs[0].shape[0]
    cols = u_ref.shape[1]
    width = maps.shape[1] - cols
    first = part * (chunk * len(outs))
    maps[:, :width] = d_ref[:, pl.ds(pl.multiple_of(core * width, width), width)]
    maps[:, width:] = u_ref[...]
    for i, out in enumerate(outs):
        out[...] = w_ref[pl.ds(pl.multiple_of(first + i * chunk, chunk), chunk), :]


def cross_pack(weights, downs, ups, chunks):
    width, cols = weights.shape
    vmem = pl.BlockSpec(memory_space=pltpu.VMEM)
    rows = jax.ShapeDtypeStruct((width // 2 // chunks, cols), weights.dtype)
    maps = jax.ShapeDtypeStruct((downs.shape[0], downs.shape[1] // 2 + cols), downs.dtype)
    return pl.pallas_call(
        cross_kernel,
        in_specs=[vmem] * 3,
        out_specs=[vmem] * (1 + chunks),
        out_shape=[maps] + [rows] * chunks,
        compiler_params=pltpu.CompilerParams(vmem_limit_bytes=8 * MIB),
        name="cross_pack",
    )(weights, downs, ups)


def quad_kernel(x_ref, d_ref, u_ref, maps, out):
    core = lax.axis_index("tensor")
    quads, _, width = out.shape
    tokens, features = x_ref.shape
    ranks, cols = u_ref.shape
    sub = min(width, cols)
    for j in range(quads):
        here = slice(j * width, (j + 1) * width)
        out[j, :tokens, :] = x_ref[:, here]
        begin = pl.multiple_of(core * features + j * width, width)
        out[j, tokens : tokens + ranks, :] = d_ref[:, pl.ds(begin, width)]
        out[j, tokens + ranks : tokens + 2 * ranks, :] = maps[:, here]
        for side in range(2):
            for first in range(0, cols, sub):
                row = tokens + (2 + (side * cols + first) // width) * ranks
                col = (side * cols + first) % width
                up = u_ref[:, first : first + sub] if side == 0 else maps[:, features + first : features + first + sub]
                out[j, row : row + ranks, col : col + sub] = up


def quad_pack(tokens, downs, ups, maps, width, quads):
    vmem = pl.BlockSpec(memory_space=pltpu.VMEM)
    ranks, cols = ups.shape
    rows = tokens.shape[0] + ranks * (2 + 2 * cols // width)
    return pl.pallas_call(
        quad_kernel,
        in_specs=[vmem] * 4,
        out_specs=vmem,
        out_shape=jax.ShapeDtypeStruct((quads, rows, width), tokens.dtype),
        compiler_params=pltpu.CompilerParams(vmem_limit_bytes=8 * MIB),
        name="quad_pack",
    )(tokens, downs, ups, maps)


def near_kernel(tokens, position, adapter, mine, theirs, own_ref, out, ds, us):
    core, wing = lax.axis_index("tensor"), lax.axis_index("wing")
    quads, _, width = mine.shape
    cols = own_ref.shape[1]
    ranks = us.shape[0] // (2 * quads)
    for side in range(2):
        for j in range(quads):
            rows = slice((side * quads + j) * ranks, (side * quads + j + 1) * ranks)
            row = tokens + side * ranks
            ds[0, rows, :] = mine[j, row : row + ranks, :]
            ds[1, rows, :] = theirs[j, row : row + ranks, :]
            sub = min(width, cols)
            for first in range(0, cols, sub):
                row = tokens + (2 + (side * cols + first) // width) * ranks
                col = (side * cols + first) % width
                us[rows, first : first + sub] = mine[j, row : row + ranks, col : col + sub]

    def product(x, weights):
        return dot(x[:, :tokens, :].reshape(quads * tokens, width), weights)

    shrink = dot_last(mine[:, :tokens, :].reshape(quads * tokens, width), ds[0])
    shrink += dot_last(theirs[:, :tokens, :].reshape(quads * tokens, width), ds[1])
    slots = us.shape[0] // RANK
    which = lax.broadcasted_iota(jnp.int32, (SPAN, slots * RANK), 1) // RANK + wing * (slots // 2)
    which = jnp.where(which >= slots, which - slots, which)
    spans = quads * tokens // SPAN
    masked = []
    for i in range(spans):
        slot = position[adapter[wing * spans + i]]
        masked.append(jnp.where(which == slot, shrink[i * SPAN : (i + 1) * SPAN, :], 0.0))
    shrink = (jnp.concatenate(masked, axis=0) * ADAPTER_SCALE).astype(jnp.bfloat16)
    out[...] = dot(shrink, us[...])

    @pl.when(core == wing)
    def _():
        out[...] += product(mine, own_ref[...])

    @pl.when(core != wing)
    def _():
        out[...] += product(theirs, own_ref[...])


def near_products(mine, theirs, own, position, adapter, tokens, ranks):
    quads, _, width = mine.shape
    cols = own.shape[1]
    vmem = pl.BlockSpec(memory_space=pltpu.VMEM)
    smem = pl.BlockSpec(memory_space=pltpu.SMEM)
    return pl.pallas_call(
        functools.partial(near_kernel, tokens),
        in_specs=[smem, smem] + [vmem] * 3,
        out_specs=vmem,
        out_shape=jax.ShapeDtypeStruct((quads * tokens, cols), jnp.float32),
        scratch_shapes=[
            pltpu.VMEM((2, 2 * quads * ranks, width), jnp.bfloat16),
            pltpu.VMEM((2 * quads * ranks, cols), jnp.bfloat16),
        ],
        compiler_params=pltpu.CompilerParams(vmem_limit_bytes=48 * MIB if quads > 4 else 24 * MIB),
        name="near_products",
    )(position, adapter, mine, theirs, own)


def far_kernel(tokens, mine, theirs, near, *refs):
    weights, out, whole = refs[:-2], refs[-2], refs[-1]
    part, core, wing = lax.axis_index("parts") % 2, lax.axis_index("tensor"), lax.axis_index("wing")
    quads, _, width = mine.shape
    chunk = weights[0].shape[0]
    chunks = len(weights) // 2
    for side in range(2):
        first = (part if side == 0 else 1 - part) * (chunks * chunk)
        for i in range(chunks):
            begin = pl.multiple_of(first + i * chunk, chunk)
            whole[pl.ds(begin, chunk), :] = weights[side * chunks + i][...]

    def store(x):
        product = dot(x[:, :tokens, :].reshape(quads * tokens, width), whole[...])
        out[...] = (near[...] + product).astype(jnp.bfloat16).reshape(out.shape)

    @pl.when(core == wing)
    def _():
        store(theirs)

    @pl.when(core != wing)
    def _():
        store(mine)


def far_products(mine, theirs, near, weights, tokens):
    quads, _, width = mine.shape
    cols = near.shape[1]
    vmem = pl.BlockSpec(memory_space=pltpu.VMEM)
    return pl.pallas_call(
        functools.partial(far_kernel, tokens),
        in_specs=[vmem] * (3 + len(weights)),
        out_specs=vmem,
        out_shape=jax.ShapeDtypeStruct((quads, tokens, cols), jnp.bfloat16),
        scratch_shapes=[pltpu.VMEM((width, cols), jnp.bfloat16)],
        compiler_params=pltpu.CompilerParams(vmem_limit_bytes=48 * MIB if quads > 4 else 16 * MIB),
        name="far_products",
    )(mine, theirs, near, *weights)


def finish_kernel(spans, parts, *refs):
    mixed, probs, (out_ref, values_ref) = refs[:spans], refs[spans : 2 * spans], refs[2 * spans :]
    total = parts[0].astype(jnp.float32)
    for j in range(1, parts.shape[0]):
        total = total + parts[j].astype(jnp.float32)
    total = total.astype(jnp.bfloat16)
    values_ref[...] = total
    kv_heads = total.shape[1] // HD
    for span in range(spans):
        rows = slice(span * SPAN, (span + 1) * SPAN)
        count = probs[span].shape[0] // kv_heads
        for k in range(kv_heads):
            fresh = dot(probs[span][k * count : (k + 1) * count, :], total[rows, k * HD : (k + 1) * HD])
            for h in range(count // SPAN):
                col = (k * (count // SPAN) + h) * HD
                out_ref[rows, col : col + HD] = (
                    mixed[span][:, col : col + HD] + fresh[h * SPAN : (h + 1) * SPAN, :]
                ).astype(jnp.bfloat16)


def finish(mixed, fresh_probs, parts):
    _, tokens, cols = parts.shape
    vmem = pl.BlockSpec(memory_space=pltpu.VMEM)
    return pl.pallas_call(
        functools.partial(finish_kernel, len(mixed)),
        in_specs=[vmem] * (1 + 2 * len(mixed)),
        out_specs=[vmem] * 2,
        out_shape=[
            jax.ShapeDtypeStruct((tokens, mixed[0].shape[1]), jnp.bfloat16),
            jax.ShapeDtypeStruct((tokens, cols), jnp.bfloat16),
        ],
        compiler_params=pltpu.CompilerParams(vmem_limit_bytes=16 * MIB),
        name="finish_attention",
    )(parts, *mixed, *fresh_probs)


def on_device(
    normed_inputs,
    value_matrix,
    adapter_down_weight,
    adapter_up_weight,
    adapter_position,
    span_adapter_index,
    queries,
    incoming_keys,
    stored_keys,
    stored_values,
    cache_length,
):
    quads = lax.axis_size("quad")
    parts_swap = [(i, i ^ 1) for i in range(lax.axis_size("parts"))]
    width, cols = value_matrix.shape
    downs = adapter_down_weight.reshape(-1, adapter_down_weight.shape[2])
    ups = adapter_up_weight.reshape(-1, cols)

    def attention(span, lengths):
        return cache_attention(span, queries, incoming_keys, stored_keys, stored_values, lengths)

    maps, *leaving = cross_pack(value_matrix, downs, ups, CHUNKS)
    maps = lax.ppermute(maps, "wing", SWAP)
    far = [lax.ppermute(rows, "wing", SWAP) for rows in leaving]
    message = quad_pack(normed_inputs, downs, ups, maps, width, quads)
    mine = lax.all_to_all(message, "quad", 0, 0)

    lengths, _ = lax.optimization_barrier((cache_length, message))
    first = attention(0, lengths)
    far_0, _ = lax.optimization_barrier((far[0], first[1]))
    far_0_other = lax.ppermute(far_0, "parts", parts_swap)

    lengths, _ = lax.optimization_barrier((cache_length, far_0))
    second = attention(1, lengths)
    mine, far_1, _ = lax.optimization_barrier((mine, far[1], second[1]))
    theirs = lax.ppermute(mine, "tensor", SWAP)
    far_1_other = lax.ppermute(far_1, "parts", parts_swap)

    tokens = normed_inputs.shape[0]
    near = near_products(
        mine, theirs, value_matrix, adapter_position, span_adapter_index, tokens, downs.shape[0]
    )
    products = far_products(mine, theirs, near, (far_0, far_1, far_0_other, far_1_other), tokens)
    parts = lax.all_to_all(products, "quad", 0, 0)
    mixed, fresh_probs = zip(first, second)
    attended, incoming_values = finish(mixed, fresh_probs, parts)
    return (attended, incoming_values)


def solution(mesh):
    sizes = mesh.devices.shape
    cut = Mesh(
        mesh.devices.reshape(sizes[0], 2, sizes[1] // 2, sizes[2]), ("parts", "wing", "quad", "tensor")
    )
    group = ("wing", "quad")
    home = ("parts", "wing", "quad")
    in_specs = (
        P(home, "tensor"),
        P(group, "tensor"),
        P(group, None, None),
        P(group, None, "tensor"),
        P(),
        P("parts"),
        P(home, "tensor"),
        P(home, "tensor"),
        P(home, None, "tensor"),
        P(home, None, "tensor"),
        P(home),
    )
    out_specs = (P(home, "tensor"), P(home, "tensor"))
    return jax.shard_map(
        on_device, mesh=cut, in_specs=in_specs, out_specs=out_specs, check_vma=False
    )
```

```python
import functools
import math

import jax
import jax.numpy as jnp
from jax import lax
from jax.experimental import pallas as pl
from jax.experimental.pallas import tpu as pltpu
from jax.sharding import Mesh
from jax.sharding import PartitionSpec as P

HD = 128
RANK = 16
SPAN = 64
CHUNK = 512
EARLY = 2
ONES = 16
ADAPTER_SCALE = 2.0
EXP2_SCALE = math.log2(math.e) / math.sqrt(HD)
DEAD = -1e30
MIB = 1024 * 1024
SWAP = [(0, 1), (1, 0)]
FREE = pl.CostEstimate(flops=1, bytes_accessed=1, transcendentals=0)


def dot_last(a, b):
    return lax.dot_general(a, b, (((1,), (1,)), ((), ())), preferred_element_type=jnp.float32)


def dot(a, b):
    return jnp.dot(a, b, preferred_element_type=jnp.float32)


def cache_kernel(span, first_head, kv_heads, group_size, lens, q_ref, fk_ref, k_hbm, v_hbm, out_ref, pf_ref, qs, ks, vs, m_s, acc, sems):
    length = lens[span]
    rows = group_size * SPAN
    chunks, chunk, width = ks.shape
    heads = slice(first_head * HD, first_head * HD + width)

    def copies(i):
        live = pl.ds(pl.multiple_of(i * chunk, chunk), chunk)
        return (
            pltpu.make_async_copy(k_hbm.at[span, live, heads], ks.at[i], sems.at[0, i]),
            pltpu.make_async_copy(v_hbm.at[span, live, heads], vs.at[i], sems.at[1, i]),
        )

    for i in range(chunks):

        @pl.when(i * chunk < length)
        def _():
            for copy in copies(i):
                copy.start()

    def fresh_scores(k):
        s = dot_last(fk_ref[span * SPAN : (span + 1) * SPAN, (first_head + k) * HD : (first_head + k + 1) * HD], qs[k])
        key = lax.broadcasted_iota(jnp.int32, (SPAN, rows), 0)
        token = lax.broadcasted_iota(jnp.int32, (SPAN, rows), 1) % SPAN
        return jnp.where(key <= token, s, DEAD)

    for k in range(kv_heads):
        for h in range(group_size):
            col = ((first_head + k) * group_size + h) * HD
            qs[k, h * SPAN : (h + 1) * SPAN, :] = q_ref[span * SPAN : (span + 1) * SPAN, col : col + HD]
        m_s[k] = jnp.max(fresh_scores(k), axis=0, keepdims=True)
        acc[k] = jnp.zeros((HD + ONES, rows), jnp.float32)

    ones = jnp.ones((ONES, chunk), jnp.bfloat16)

    def add_chunk(i, masked):
        for copy in copies(i):
            copy.wait()

        def scores(k):
            s = dot_last(ks[i, :, k * HD : (k + 1) * HD], qs[k])
            if masked:
                slot = i * chunk + lax.broadcasted_iota(jnp.int32, (chunk, rows), 0)
                s = jnp.where(slot < length, s, DEAD)
            return s

        s = scores(0)
        for k in range(kv_heads):
            later = scores(k + 1) if k + 1 < kv_heads else None
            before = m_s[k]
            top = jnp.maximum(before, jnp.max(s, axis=0, keepdims=True))
            m_s[k] = top
            p = jnp.exp2((s - top) * EXP2_SCALE).astype(jnp.bfloat16)
            alpha = jnp.exp2((before - top) * EXP2_SCALE)
            values = jnp.concatenate([vs[i, :, k * HD : (k + 1) * HD].T, ones], axis=0)
            acc[k] = acc[k] * alpha + dot(values, p)
            s = later

    @pl.loop(0, length // chunk)
    def _(i):
        add_chunk(i, False)

    @pl.when(length % chunk != 0)
    def _():
        add_chunk(length // chunk, True)

    for k in range(kv_heads):
        p = jnp.exp2((fresh_scores(k) - m_s[k]) * EXP2_SCALE)
        inverse = 1.0 / (acc[k, HD : HD + 1, :] + jnp.sum(p, axis=0, keepdims=True))
        pf_ref[k * rows : (k + 1) * rows, :] = (p * inverse).T.astype(jnp.bfloat16)
        mixed = (acc[k, :HD, :] * inverse).T
        for h in range(group_size):
            col = (k * group_size + h) * HD
            out_ref[:, col : col + HD] = mixed[h * SPAN : (h + 1) * SPAN, :]


def cache_attention(span, first_head, kv_heads, hides, queries, fresh_keys, keys, values, lengths):
    slots = keys.shape[1]
    group_size = queries.shape[1] // keys.shape[2]
    width = kv_heads * HD
    rows = group_size * SPAN
    chunk = min(CHUNK, slots)
    chunks = slots // chunk
    vmem = pl.BlockSpec(memory_space=pltpu.VMEM)
    hbm = pl.BlockSpec(memory_space=pltpu.HBM)
    return pl.pallas_call(
        functools.partial(cache_kernel, span, first_head, kv_heads, group_size),
        in_specs=[pl.BlockSpec(memory_space=pltpu.SMEM), vmem, vmem, hbm, hbm],
        out_specs=[vmem, vmem],
        scratch_shapes=[
            pltpu.VMEM((kv_heads, rows, HD), jnp.bfloat16),
            pltpu.VMEM((chunks, chunk, width), jnp.bfloat16),
            pltpu.VMEM((chunks, chunk, width), jnp.bfloat16),
            pltpu.VMEM((kv_heads, 1, rows), jnp.float32),
            pltpu.VMEM((kv_heads, HD + ONES, rows), jnp.float32),
            pltpu.SemaphoreType.DMA((2, chunks)),
        ],
        out_shape=[
            jax.ShapeDtypeStruct((SPAN, group_size * width), jnp.float32),
            jax.ShapeDtypeStruct((kv_heads * rows, SPAN), jnp.bfloat16),
        ],
        compiler_params=pltpu.CompilerParams(vmem_limit_bytes=57 * MIB),
        cost_estimate=pl.CostEstimate(
            flops=4 * rows * slots * width, bytes_accessed=4 * slots * width, transcendentals=0
        )
        if hides
        else FREE,
        name="cache_attention",
    )(lengths, queries, fresh_keys, keys, values)


def run_copies(copies, sems):
    copies = [pltpu.make_async_copy(src, dst, sems.at[i]) for i, (src, dst) in enumerate(copies)]
    for copy in copies:
        copy.start()
    for copy in copies:
        copy.wait()


def cross_kernel(w_hbm, d_hbm, u_hbm, early, late, sems):
    part, core = lax.axis_index("parts") % 2, lax.axis_index("tensor")
    cols = u_hbm.shape[1]
    features = d_hbm.shape[1] // 2
    pieces = features // cols
    ranks = d_hbm.shape[0]
    head = early.shape[0] - (pieces + 1) * ranks
    begin = part * (head + late.shape[0])
    copies = []
    for i in range(pieces):
        here = pl.ds(pl.multiple_of(core * features + i * cols, cols), cols)
        copies.append((d_hbm.at[:, here], early.at[head + i * ranks : head + (i + 1) * ranks, :]))
    copies.append((u_hbm, early.at[head + pieces * ranks :, :]))
    copies.append((w_hbm.at[pl.ds(pl.multiple_of(begin, head), head), :], early.at[:head, :]))
    rest = pl.ds(pl.multiple_of(begin + head, head), late.shape[0])
    copies.append((w_hbm.at[rest, :], late))
    run_copies(copies, sems)


def cross_pack(weights, downs, ups):
    width, cols = weights.shape
    head = width // 2 // EARLY
    pieces = downs.shape[1] // 2 // cols
    vmem = pl.BlockSpec(memory_space=pltpu.VMEM)
    hbm = pl.BlockSpec(memory_space=pltpu.HBM)
    return pl.pallas_call(
        cross_kernel,
        in_specs=[hbm] * 3,
        out_specs=[vmem] * 2,
        out_shape=[
            jax.ShapeDtypeStruct((head + (pieces + 1) * downs.shape[0], cols), weights.dtype),
            jax.ShapeDtypeStruct((width // 2 - head, cols), weights.dtype),
        ],
        scratch_shapes=[pltpu.SemaphoreType.DMA((pieces + 3,))],
        compiler_params=pltpu.CompilerParams(vmem_limit_bytes=57 * MIB),
        cost_estimate=FREE,
        name="cross_pack",
    )(weights, downs, ups)


def up_places(cols, width):
    step = min(cols, width)
    return [
        (slot, first, (slot * cols + first) // width * RANK, (slot * cols + first) % width)
        for slot in range(2)
        for first in range(0, cols, step)
    ]


def quad_kernel(x_hbm, d_hbm, u_hbm, out, sems):
    core = lax.axis_index("tensor")
    quads, _, width = out.shape
    tokens, features = x_hbm.shape
    ranks, cols = u_hbm.shape
    step = min(cols, width)
    copies = []
    for j in range(quads):
        begin = pl.multiple_of(core * features + j * width, width)
        copies.append((x_hbm.at[:, j * width : (j + 1) * width], out.at[j, :tokens, :]))
        copies.append((d_hbm.at[:, pl.ds(begin, width)], out.at[j, tokens : tokens + ranks, :]))
        for slot, first, row, col in up_places(cols, width):
            row += tokens + ranks
            copies.append(
                (
                    u_hbm.at[slot * RANK : (slot + 1) * RANK, first : first + step],
                    out.at[j, row : row + RANK, col : col + step],
                )
            )
    run_copies(copies, sems)


def quad_pack(tokens, downs, ups, width, quads):
    vmem = pl.BlockSpec(memory_space=pltpu.VMEM)
    hbm = pl.BlockSpec(memory_space=pltpu.HBM)
    ranks, cols = ups.shape
    rows = tokens.shape[0] + ranks + RANK * (2 * cols // width)
    count = quads * (2 + len(up_places(cols, width)))
    return pl.pallas_call(
        quad_kernel,
        in_specs=[hbm] * 3,
        out_specs=vmem,
        out_shape=jax.ShapeDtypeStruct((quads, rows, width), tokens.dtype),
        scratch_shapes=[pltpu.SemaphoreType.DMA((count,))],
        compiler_params=pltpu.CompilerParams(vmem_limit_bytes=57 * MIB),
        cost_estimate=FREE,
        name="quad_pack",
    )(tokens, downs, ups)


def maps_kernel(here, rows_out, *outs):
    quad = lax.axis_index("quad")
    width = outs[0].shape[1]
    cols = here.shape[1]
    ranks = 2 * RANK
    step = min(cols, width)
    head = rows_out.shape[0]
    last = here.shape[0] - ranks
    rows_out[...] = here[:head, :]
    for q, out in enumerate(outs):
        for first in range(0, width, step):
            place = (quad ^ q) * width + first
            row = pl.multiple_of(head + place // cols * ranks, RANK)
            col = pl.multiple_of(place % cols, step)
            out[:ranks, first : first + step] = here[pl.ds(row, ranks), pl.ds(col, step)]
        for slot, first, row, col in up_places(cols, width):
            up = here[last + slot * RANK : last + (slot + 1) * RANK, first : first + step]
            out[ranks + row : ranks + row + RANK, col : col + step] = up


def maps_pack(here, width, quads):
    vmem = pl.BlockSpec(memory_space=pltpu.VMEM)
    rows, cols = here.shape
    head = rows - (quads * width // cols + 1) * 2 * RANK
    maps = jax.ShapeDtypeStruct((RANK * (2 + 2 * cols // width), width), here.dtype)
    return pl.pallas_call(
        maps_kernel,
        in_specs=[vmem],
        out_specs=[vmem] * (1 + quads),
        out_shape=[jax.ShapeDtypeStruct((head, cols), here.dtype)] + [maps] * quads,
        compiler_params=pltpu.CompilerParams(vmem_limit_bytes=4 * MIB),
        cost_estimate=FREE,
        name="maps_pack",
    )(here)


def near_kernel(tokens, position, adapter, mine, theirs, maps_mine, maps_theirs, own_ref, out, ds, us):
    core, wing, quad = lax.axis_index("tensor"), lax.axis_index("wing"), lax.axis_index("quad")
    quads, _, width = mine.shape
    cols = own_ref.shape[1]
    ranks = 2 * RANK
    step = min(cols, width)
    for j in range(quads):
        for side, here, there, base, index in (
            (0, mine.at[j], theirs.at[j], tokens, j),
            (1, maps_mine.at[j], maps_theirs.at[j], 0, quad ^ j),
        ):
            first_row = (side * quads + index) * ranks
            rows = pl.ds(pl.multiple_of(first_row, ranks), ranks)
            ds[0, rows, :] = here[base : base + ranks, :]
            ds[1, rows, :] = there[base : base + ranks, :]
            for slot, first, row, col in up_places(cols, width):
                row += base + ranks
                place = pl.ds(pl.multiple_of(first_row + slot * RANK, RANK), RANK)
                us[place, first : first + step] = here[row : row + RANK, col : col + step]

    x_mine = mine[:, :tokens, :].reshape(quads * tokens, width)
    x_theirs = theirs[:, :tokens, :].reshape(quads * tokens, width)
    shrink = dot_last(x_mine, ds[0]) + dot_last(x_theirs, ds[1])
    slots = us.shape[0] // RANK
    which = lax.broadcasted_iota(jnp.int32, (SPAN, slots * RANK), 1) // RANK + wing * (slots // 2)
    which = jnp.where(which >= slots, which - slots, which)
    spans = quads * tokens // SPAN
    masked = []
    for i in range(spans):
        slot = position[adapter[wing * spans + i]]
        masked.append(jnp.where(which == slot, shrink[i * SPAN : (i + 1) * SPAN, :], 0.0))
    shrink = (jnp.concatenate(masked, axis=0) * ADAPTER_SCALE).astype(jnp.bfloat16)
    out[...] = dot(shrink, us[...])

    @pl.when(core == wing)
    def _():
        out[...] += dot(x_mine, own_ref[...])

    @pl.when(core != wing)
    def _():
        out[...] += dot(x_theirs, own_ref[...])


def near_products(mine, theirs, maps_mine, maps_theirs, own, position, adapter, tokens):
    quads, _, width = mine.shape
    cols = own.shape[1]
    ranks = 4 * quads * RANK
    vmem = pl.BlockSpec(memory_space=pltpu.VMEM)
    smem = pl.BlockSpec(memory_space=pltpu.SMEM)
    return pl.pallas_call(
        functools.partial(near_kernel, tokens),
        in_specs=[smem, smem] + [vmem] * 5,
        out_specs=vmem,
        out_shape=jax.ShapeDtypeStruct((quads * tokens, cols), jnp.float32),
        scratch_shapes=[
            pltpu.VMEM((2, ranks, width), jnp.bfloat16),
            pltpu.VMEM((ranks, cols), jnp.bfloat16),
        ],
        compiler_params=pltpu.CompilerParams(vmem_limit_bytes=48 * MIB if quads > 4 else 24 * MIB),
        cost_estimate=FREE,
        name="near_products",
    )(position, adapter, mine, theirs, maps_mine, maps_theirs, own)


def far_kernel(tokens, mine, theirs, near, *refs):
    quads, _, width = mine.shape
    outs, (whole, total) = refs[-2 - quads : -2], refs[-2:]
    weights = refs[:4]
    part, core, wing = lax.axis_index("parts") % 2, lax.axis_index("tensor"), lax.axis_index("wing")
    quad = lax.axis_index("quad")
    late = weights[1].shape[0]
    head = width // 2 - late
    for side in range(2):
        begin = (part if side == 0 else 1 - part) * (width // 2)
        whole[pl.ds(pl.multiple_of(begin, head), head), :] = weights[2 * side][...]
        whole[pl.ds(pl.multiple_of(begin + head, head), late), :] = weights[2 * side + 1][...]

    def store(x):
        product = dot(x[:, :tokens, :].reshape(quads * tokens, width), whole[...])
        total[...] = (near[...] + product).astype(jnp.bfloat16).reshape(total.shape)

    @pl.when(core == wing)
    def _():
        store(theirs)

    @pl.when(core != wing)
    def _():
        store(mine)

    for q in range(quads):
        outs[q][...] = total[quad ^ q]


def far_products(mine, theirs, near, weights, tokens):
    quads, _, width = mine.shape
    cols = near.shape[1]
    vmem = pl.BlockSpec(memory_space=pltpu.VMEM)
    return pl.pallas_call(
        functools.partial(far_kernel, tokens),
        in_specs=[vmem] * (3 + len(weights)),
        out_specs=[vmem] * quads,
        out_shape=[jax.ShapeDtypeStruct((tokens, cols), jnp.bfloat16)] * quads,
        scratch_shapes=[
            pltpu.VMEM((width, cols), jnp.bfloat16),
            pltpu.VMEM((quads, tokens, cols), jnp.bfloat16),
        ],
        compiler_params=pltpu.CompilerParams(vmem_limit_bytes=48 * MIB if quads > 4 else 16 * MIB),
        cost_estimate=FREE,
        name="far_products",
    )(mine, theirs, near, *weights)


def finish_kernel(places, *refs):
    count = len(places)
    out_ref, values_ref = refs[-2:]
    mixed, probs, parts = refs[:count], refs[count : 2 * count], refs[2 * count : -2]
    total = parts[0][...].astype(jnp.float32)
    for part in parts[1:]:
        total = total + part[...].astype(jnp.float32)
    total = total.astype(jnp.bfloat16)
    values_ref[...] = total
    for (span, head), mix, prob in zip(places, mixed, probs):
        rows = slice(span * SPAN, (span + 1) * SPAN)
        group_size = out_ref.shape[1] // total.shape[1]
        queries = group_size * SPAN
        for k in range(prob.shape[0] // queries):
            values = total[rows, (head + k) * HD : (head + k + 1) * HD]
            fresh = dot(prob[k * queries : (k + 1) * queries, :], values)
            for h in range(group_size):
                here = slice((k * group_size + h) * HD, (k * group_size + h + 1) * HD)
                col = ((head + k) * group_size + h) * HD
                out_ref[rows, col : col + HD] = (
                    mix[:, here] + fresh[h * SPAN : (h + 1) * SPAN, :]
                ).astype(jnp.bfloat16)


def finish(places, mixed, fresh_probs, parts, q_width):
    tokens, cols = parts[0].shape
    vmem = pl.BlockSpec(memory_space=pltpu.VMEM)
    return pl.pallas_call(
        functools.partial(finish_kernel, places),
        in_specs=[vmem] * (len(parts) + 2 * len(mixed)),
        out_specs=[vmem] * 2,
        out_shape=[
            jax.ShapeDtypeStruct((tokens, q_width), jnp.bfloat16),
            jax.ShapeDtypeStruct((tokens, cols), jnp.bfloat16),
        ],
        compiler_params=pltpu.CompilerParams(vmem_limit_bytes=16 * MIB),
        cost_estimate=FREE,
        name="finish_attention",
    )(*mixed, *fresh_probs, *parts)


def on_device(
    normed_inputs,
    value_matrix,
    adapter_down_weight,
    adapter_up_weight,
    adapter_position,
    span_adapter_index,
    queries,
    incoming_keys,
    stored_keys,
    stored_values,
    cache_length,
):
    quads = lax.axis_size("quad")
    parts_swap = [(i, i ^ 1) for i in range(lax.axis_size("parts"))]
    width, cols = value_matrix.shape
    downs = adapter_down_weight.reshape(-1, adapter_down_weight.shape[2])
    ups = adapter_up_weight.reshape(-1, cols)

    kv_heads = cols // HD
    places = [(span, head) for span in range(2) for head in range(0, kv_heads, kv_heads // 2)]

    def attention(place, lengths):
        span, head = places[place]
        return cache_attention(
            span, head, kv_heads // 2, place > 1, queries, incoming_keys, stored_keys, stored_values, lengths
        )

    def after(value, *others):
        return lax.optimization_barrier((value, *others))[0]

    def to_quad(value, q):
        return lax.ppermute(value, "quad", [(j, j ^ q) for j in range(quads)])

    early, late = cross_pack(value_matrix, downs, ups)
    message = quad_pack(after(normed_inputs, early), downs, ups, width, quads)
    early = lax.ppermute(early, "wing", SWAP)
    mine = lax.all_to_all(message, "quad", 0, 0)

    attn = [attention(0, after(cache_length, message))]
    attn.append(attention(1, after(cache_length, attn[0][1])))
    early = after(early, attn[1][1])
    late = lax.ppermute(after(late, early), "wing", SWAP)
    early, *passed = maps_pack(early, width, quads)
    early_other = lax.ppermute(early, "parts", parts_swap)
    passed_on = [to_quad(passed[q], q) for q in range(1, quads)]

    attn.append(attention(2, after(cache_length, early)))
    maps_mine = jnp.stack([passed[0]] + [after(maps, attn[2][1]) for maps in passed_on])
    theirs = lax.ppermute(after(mine, early), "tensor", SWAP)
    maps_theirs = lax.ppermute(maps_mine, "tensor", SWAP)
    late_other = lax.ppermute(after(late, attn[2][1]), "parts", parts_swap)

    tokens, q_width = queries.shape
    near = near_products(
        mine, theirs, maps_mine, maps_theirs, value_matrix, adapter_position, span_adapter_index, tokens
    )
    products = far_products(mine, theirs, near, (early, late, early_other, late_other), tokens)
    parts = [to_quad(products[q], q) for q in range(1, quads)]
    attn.append(attention(3, after(cache_length, products[0])))
    parts = [products[0]] + [after(part, attn[3][1]) for part in parts]
    mixed, fresh_probs = zip(*attn)
    attended, incoming_values = finish(places, mixed, fresh_probs, parts, q_width)
    return (attended, incoming_values)


def solution(mesh):
    sizes = mesh.devices.shape
    cut = Mesh(
        mesh.devices.reshape(sizes[0], 2, sizes[1] // 2, sizes[2]), ("parts", "wing", "quad", "tensor")
    )
    group = ("wing", "quad")
    home = ("parts", "wing", "quad")
    in_specs = (
        P(home, "tensor"),
        P(group, "tensor"),
        P(group, None, None),
        P(group, None, "tensor"),
        P(),
        P("parts"),
        P(home, "tensor"),
        P(home, "tensor"),
        P(home, None, "tensor"),
        P(home, None, "tensor"),
        P(home),
    )
    out_specs = (P(home, "tensor"), P(home, "tensor"))
    return jax.shard_map(
        on_device, mesh=cut, in_specs=in_specs, out_specs=out_specs, check_vma=False
    )
```

```python
import functools
import math

import jax
import jax.numpy as jnp
from jax import lax
from jax.experimental import pallas as pl
from jax.experimental.pallas import tpu as pltpu
from jax.sharding import Mesh
from jax.sharding import PartitionSpec as P

HD = 128
RANK = 16
SPAN = 64
CHUNK = 512
EARLY = 2
ONES = 16
ADAPTER_SCALE = 2.0
EXP2_SCALE = math.log2(math.e) / math.sqrt(HD)
DEAD = -1e30
MIB = 1024 * 1024
SWAP = [(0, 1), (1, 0)]
FREE = pl.CostEstimate(flops=1, bytes_accessed=1, transcendentals=0)


def dot_last(a, b):
    return lax.dot_general(a, b, (((1,), (1,)), ((), ())), preferred_element_type=jnp.float32)


def dot(a, b):
    return jnp.dot(a, b, preferred_element_type=jnp.float32)


def cache_kernel(span, first_head, kv_heads, group_size, lens, q_ref, fk_ref, k_hbm, v_hbm, out_ref, pf_ref, qs, ks, vs, m_s, acc, sems):
    length = lens[span]
    rows = group_size * SPAN
    chunks, chunk, width = ks.shape
    heads = slice(first_head * HD, first_head * HD + width)

    def copies(i):
        live = pl.ds(pl.multiple_of(i * chunk, chunk), chunk)
        return (
            pltpu.make_async_copy(k_hbm.at[span, live, heads], ks.at[i], sems.at[0, i]),
            pltpu.make_async_copy(v_hbm.at[span, live, heads], vs.at[i], sems.at[1, i]),
        )

    for i in range(chunks):

        @pl.when(i * chunk < length)
        def _():
            for copy in copies(i):
                copy.start()

    def fresh_scores(k):
        s = dot_last(fk_ref[span * SPAN : (span + 1) * SPAN, (first_head + k) * HD : (first_head + k + 1) * HD], qs[k])
        key = lax.broadcasted_iota(jnp.int32, (SPAN, rows), 0)
        token = lax.broadcasted_iota(jnp.int32, (SPAN, rows), 1) % SPAN
        return jnp.where(key <= token, s, DEAD)

    for k in range(kv_heads):
        for h in range(group_size):
            col = ((first_head + k) * group_size + h) * HD
            qs[k, h * SPAN : (h + 1) * SPAN, :] = q_ref[span * SPAN : (span + 1) * SPAN, col : col + HD]
        m_s[k] = jnp.max(fresh_scores(k), axis=0, keepdims=True)
        acc[k] = jnp.zeros((HD + ONES, rows), jnp.float32)

    ones = jnp.ones((ONES, chunk), jnp.bfloat16)

    def add_chunk(i, masked):
        for copy in copies(i):
            copy.wait()

        def scores(k):
            s = dot_last(ks[i, :, k * HD : (k + 1) * HD], qs[k])
            if masked:
                slot = i * chunk + lax.broadcasted_iota(jnp.int32, (chunk, rows), 0)
                s = jnp.where(slot < length, s, DEAD)
            return s

        s = scores(0)
        for k in range(kv_heads):
            later = scores(k + 1) if k + 1 < kv_heads else None
            before = m_s[k]
            top = jnp.maximum(before, jnp.max(s, axis=0, keepdims=True))
            m_s[k] = top
            p = jnp.exp2((s - top) * EXP2_SCALE).astype(jnp.bfloat16)
            alpha = jnp.exp2((before - top) * EXP2_SCALE)
            values = jnp.concatenate([vs[i, :, k * HD : (k + 1) * HD].T, ones], axis=0)
            acc[k] = acc[k] * alpha + dot(values, p)
            s = later

    @pl.loop(0, length // chunk)
    def _(i):
        add_chunk(i, False)

    @pl.when(length % chunk != 0)
    def _():
        add_chunk(length // chunk, True)

    for k in range(kv_heads):
        p = jnp.exp2((fresh_scores(k) - m_s[k]) * EXP2_SCALE)
        inverse = 1.0 / (acc[k, HD : HD + 1, :] + jnp.sum(p, axis=0, keepdims=True))
        pf_ref[k * rows : (k + 1) * rows, :] = (p * inverse).T.astype(jnp.bfloat16)
        mixed = (acc[k, :HD, :] * inverse).T
        for h in range(group_size):
            col = (k * group_size + h) * HD
            out_ref[:, col : col + HD] = mixed[h * SPAN : (h + 1) * SPAN, :]


def cache_attention(span, first_head, kv_heads, hides, queries, fresh_keys, keys, values, lengths):
    slots = keys.shape[1]
    group_size = queries.shape[1] // keys.shape[2]
    width = kv_heads * HD
    rows = group_size * SPAN
    chunk = min(CHUNK, slots)
    chunks = slots // chunk
    vmem = pl.BlockSpec(memory_space=pltpu.VMEM)
    hbm = pl.BlockSpec(memory_space=pltpu.HBM)
    return pl.pallas_call(
        functools.partial(cache_kernel, span, first_head, kv_heads, group_size),
        in_specs=[pl.BlockSpec(memory_space=pltpu.SMEM), vmem, vmem, hbm, hbm],
        out_specs=[vmem, vmem],
        scratch_shapes=[
            pltpu.VMEM((kv_heads, rows, HD), jnp.bfloat16),
            pltpu.VMEM((chunks, chunk, width), jnp.bfloat16),
            pltpu.VMEM((chunks, chunk, width), jnp.bfloat16),
            pltpu.VMEM((kv_heads, 1, rows), jnp.float32),
            pltpu.VMEM((kv_heads, HD + ONES, rows), jnp.float32),
            pltpu.SemaphoreType.DMA((2, chunks)),
        ],
        out_shape=[
            jax.ShapeDtypeStruct((SPAN, group_size * width), jnp.float32),
            jax.ShapeDtypeStruct((kv_heads * rows, SPAN), jnp.bfloat16),
        ],
        compiler_params=pltpu.CompilerParams(vmem_limit_bytes=57 * MIB),
        cost_estimate=pl.CostEstimate(
            flops=4 * rows * slots * width, bytes_accessed=4 * slots * width, transcendentals=0
        )
        if hides
        else FREE,
        name="cache_attention",
    )(lengths, queries, fresh_keys, keys, values)


def run_copies(copies, sems):
    copies = [pltpu.make_async_copy(src, dst, sems.at[i]) for i, (src, dst) in enumerate(copies)]
    for copy in copies:
        copy.start()
    for copy in copies:
        copy.wait()


def cross_kernel(w_hbm, d_hbm, u_hbm, early, late, sems):
    part, core = lax.axis_index("parts") % 2, lax.axis_index("tensor")
    cols = u_hbm.shape[1]
    features = d_hbm.shape[1] // 2
    pieces = features // cols
    ranks = d_hbm.shape[0]
    head = early.shape[0] - (pieces + 1) * ranks
    begin = part * (head + late.shape[0])
    copies = []
    for i in range(pieces):
        here = pl.ds(pl.multiple_of(core * features + i * cols, cols), cols)
        copies.append((d_hbm.at[:, here], early.at[head + i * ranks : head + (i + 1) * ranks, :]))
    copies.append((u_hbm, early.at[head + pieces * ranks :, :]))
    copies.append((w_hbm.at[pl.ds(pl.multiple_of(begin, head), head), :], early.at[:head, :]))
    rest = pl.ds(pl.multiple_of(begin + head, head), late.shape[0])
    copies.append((w_hbm.at[rest, :], late))
    run_copies(copies, sems)


def cross_pack(weights, downs, ups):
    width, cols = weights.shape
    head = width // 2 // EARLY
    pieces = downs.shape[1] // 2 // cols
    vmem = pl.BlockSpec(memory_space=pltpu.VMEM)
    hbm = pl.BlockSpec(memory_space=pltpu.HBM)
    return pl.pallas_call(
        cross_kernel,
        in_specs=[hbm] * 3,
        out_specs=[vmem] * 2,
        out_shape=[
            jax.ShapeDtypeStruct((head + (pieces + 1) * downs.shape[0], cols), weights.dtype),
            jax.ShapeDtypeStruct((width // 2 - head, cols), weights.dtype),
        ],
        scratch_shapes=[pltpu.SemaphoreType.DMA((pieces + 3,))],
        compiler_params=pltpu.CompilerParams(vmem_limit_bytes=57 * MIB),
        cost_estimate=FREE,
        name="cross_pack",
    )(weights, downs, ups)


def up_places(cols, width):
    step = min(cols, width)
    return [
        (slot, first, (slot * cols + first) // width * RANK, (slot * cols + first) % width)
        for slot in range(2)
        for first in range(0, cols, step)
    ]


def quad_kernel(x_hbm, d_hbm, u_hbm, out, sems):
    core = lax.axis_index("tensor")
    quads, _, width = out.shape
    tokens, features = x_hbm.shape
    ranks, cols = u_hbm.shape
    step = min(cols, width)
    copies = []
    for j in range(quads):
        begin = pl.multiple_of(core * features + j * width, width)
        copies.append((x_hbm.at[:, j * width : (j + 1) * width], out.at[j, :tokens, :]))
        copies.append((d_hbm.at[:, pl.ds(begin, width)], out.at[j, tokens : tokens + ranks, :]))
        for slot, first, row, col in up_places(cols, width):
            row += tokens + ranks
            copies.append(
                (
                    u_hbm.at[slot * RANK : (slot + 1) * RANK, first : first + step],
                    out.at[j, row : row + RANK, col : col + step],
                )
            )
    run_copies(copies, sems)


def quad_pack(tokens, downs, ups, width, quads):
    vmem = pl.BlockSpec(memory_space=pltpu.VMEM)
    hbm = pl.BlockSpec(memory_space=pltpu.HBM)
    ranks, cols = ups.shape
    rows = tokens.shape[0] + ranks + RANK * (2 * cols // width)
    count = quads * (2 + len(up_places(cols, width)))
    return pl.pallas_call(
        quad_kernel,
        in_specs=[hbm] * 3,
        out_specs=vmem,
        out_shape=jax.ShapeDtypeStruct((quads, rows, width), tokens.dtype),
        scratch_shapes=[pltpu.SemaphoreType.DMA((count,))],
        compiler_params=pltpu.CompilerParams(vmem_limit_bytes=57 * MIB),
        cost_estimate=FREE,
        name="quad_pack",
    )(tokens, downs, ups)


def maps_kernel(here, rows_out, *outs):
    quad = lax.axis_index("quad")
    width = outs[0].shape[1]
    cols = here.shape[1]
    ranks = 2 * RANK
    step = min(cols, width)
    head = rows_out.shape[0]
    last = here.shape[0] - ranks
    rows_out[...] = here[:head, :]
    for q, out in enumerate(outs):
        for first in range(0, width, step):
            place = (quad ^ q) * width + first
            row = pl.multiple_of(head + place // cols * ranks, RANK)
            col = pl.multiple_of(place % cols, step)
            out[:ranks, first : first + step] = here[pl.ds(row, ranks), pl.ds(col, step)]
        for slot, first, row, col in up_places(cols, width):
            up = here[last + slot * RANK : last + (slot + 1) * RANK, first : first + step]
            out[ranks + row : ranks + row + RANK, col : col + step] = up


def maps_pack(here, width, quads):
    vmem = pl.BlockSpec(memory_space=pltpu.VMEM)
    rows, cols = here.shape
    head = rows - (quads * width // cols + 1) * 2 * RANK
    maps = jax.ShapeDtypeStruct((RANK * (2 + 2 * cols // width), width), here.dtype)
    return pl.pallas_call(
        maps_kernel,
        in_specs=[vmem],
        out_specs=[vmem] * (1 + quads),
        out_shape=[jax.ShapeDtypeStruct((head, cols), here.dtype)] + [maps] * quads,
        compiler_params=pltpu.CompilerParams(vmem_limit_bytes=4 * MIB),
        cost_estimate=FREE,
        name="maps_pack",
    )(here)


def near_kernel(tokens, position, adapter, mine, theirs, maps_mine, maps_theirs, own_ref, out, ds, us):
    core, wing, quad = lax.axis_index("tensor"), lax.axis_index("wing"), lax.axis_index("quad")
    quads, _, width = mine.shape
    cols = own_ref.shape[1]
    ranks = 2 * RANK
    step = min(cols, width)
    for j in range(quads):
        for side, here, there, base, index in (
            (0, mine.at[j], theirs.at[j], tokens, j),
            (1, maps_mine.at[j], maps_theirs.at[j], 0, quad ^ j),
        ):
            first_row = (side * quads + index) * ranks
            rows = pl.ds(pl.multiple_of(first_row, ranks), ranks)
            ds[0, rows, :] = here[base : base + ranks, :]
            ds[1, rows, :] = there[base : base + ranks, :]
            for slot, first, row, col in up_places(cols, width):
                row += base + ranks
                place = pl.ds(pl.multiple_of(first_row + slot * RANK, RANK), RANK)
                us[place, first : first + step] = here[row : row + RANK, col : col + step]

    x_mine = mine[:, :tokens, :].reshape(quads * tokens, width)
    x_theirs = theirs[:, :tokens, :].reshape(quads * tokens, width)
    shrink = dot_last(x_mine, ds[0]) + dot_last(x_theirs, ds[1])
    slots = us.shape[0] // RANK
    which = lax.broadcasted_iota(jnp.int32, (SPAN, slots * RANK), 1) // RANK + wing * (slots // 2)
    which = jnp.where(which >= slots, which - slots, which)
    spans = quads * tokens // SPAN
    masked = []
    for i in range(spans):
        slot = position[adapter[wing * spans + i]]
        masked.append(jnp.where(which == slot, shrink[i * SPAN : (i + 1) * SPAN, :], 0.0))
    shrink = (jnp.concatenate(masked, axis=0) * ADAPTER_SCALE).astype(jnp.bfloat16)
    out[...] = dot(shrink, us[...])

    @pl.when(core == wing)
    def _():
        out[...] += dot(x_mine, own_ref[...])

    @pl.when(core != wing)
    def _():
        out[...] += dot(x_theirs, own_ref[...])


def near_products(mine, theirs, maps_mine, maps_theirs, own, position, adapter, tokens):
    quads, _, width = mine.shape
    cols = own.shape[1]
    ranks = 4 * quads * RANK
    vmem = pl.BlockSpec(memory_space=pltpu.VMEM)
    smem = pl.BlockSpec(memory_space=pltpu.SMEM)
    return pl.pallas_call(
        functools.partial(near_kernel, tokens),
        in_specs=[smem, smem] + [vmem] * 5,
        out_specs=vmem,
        out_shape=jax.ShapeDtypeStruct((quads * tokens, cols), jnp.float32),
        scratch_shapes=[
            pltpu.VMEM((2, ranks, width), jnp.bfloat16),
            pltpu.VMEM((ranks, cols), jnp.bfloat16),
        ],
        compiler_params=pltpu.CompilerParams(vmem_limit_bytes=48 * MIB if quads > 4 else 24 * MIB),
        cost_estimate=FREE,
        name="near_products",
    )(position, adapter, mine, theirs, maps_mine, maps_theirs, own)


def far_kernel(tokens, mine, theirs, near, *refs):
    quads, _, width = mine.shape
    outs, (whole, total) = refs[-2 - quads : -2], refs[-2:]
    weights = refs[:4]
    part, core, wing = lax.axis_index("parts") % 2, lax.axis_index("tensor"), lax.axis_index("wing")
    quad = lax.axis_index("quad")
    late = weights[1].shape[0]
    head = width // 2 - late
    for side in range(2):
        begin = (part if side == 0 else 1 - part) * (width // 2)
        whole[pl.ds(pl.multiple_of(begin, head), head), :] = weights[2 * side][...]
        whole[pl.ds(pl.multiple_of(begin + head, head), late), :] = weights[2 * side + 1][...]

    def store(x):
        product = dot(x[:, :tokens, :].reshape(quads * tokens, width), whole[...])
        total[...] = (near[...] + product).astype(jnp.bfloat16).reshape(total.shape)

    @pl.when(core == wing)
    def _():
        store(theirs)

    @pl.when(core != wing)
    def _():
        store(mine)

    for q in range(quads):
        outs[q][...] = total[quad ^ q]


def far_products(mine, theirs, near, weights, tokens):
    quads, _, width = mine.shape
    cols = near.shape[1]
    vmem = pl.BlockSpec(memory_space=pltpu.VMEM)
    return pl.pallas_call(
        functools.partial(far_kernel, tokens),
        in_specs=[vmem] * (3 + len(weights)),
        out_specs=[vmem] * quads,
        out_shape=[jax.ShapeDtypeStruct((tokens, cols), jnp.bfloat16)] * quads,
        scratch_shapes=[
            pltpu.VMEM((width, cols), jnp.bfloat16),
            pltpu.VMEM((quads, tokens, cols), jnp.bfloat16),
        ],
        compiler_params=pltpu.CompilerParams(vmem_limit_bytes=48 * MIB if quads > 4 else 16 * MIB),
        cost_estimate=FREE,
        name="far_products",
    )(mine, theirs, near, *weights)


def finish_kernel(places, *refs):
    count = len(places)
    out_ref, values_ref = refs[-2:]
    mixed, probs, parts = refs[:count], refs[count : 2 * count], refs[2 * count : -2]
    total = parts[0][...].astype(jnp.float32)
    for part in parts[1:]:
        total = total + part[...].astype(jnp.float32)
    total = total.astype(jnp.bfloat16)
    values_ref[...] = total
    for (span, head), mix, prob in zip(places, mixed, probs):
        rows = slice(span * SPAN, (span + 1) * SPAN)
        group_size = out_ref.shape[1] // total.shape[1]
        queries = group_size * SPAN
        for k in range(prob.shape[0] // queries):
            values = total[rows, (head + k) * HD : (head + k + 1) * HD]
            fresh = dot(prob[k * queries : (k + 1) * queries, :], values)
            for h in range(group_size):
                here = slice((k * group_size + h) * HD, (k * group_size + h + 1) * HD)
                col = ((head + k) * group_size + h) * HD
                out_ref[rows, col : col + HD] = (
                    mix[:, here] + fresh[h * SPAN : (h + 1) * SPAN, :]
                ).astype(jnp.bfloat16)


def finish(places, mixed, fresh_probs, parts, q_width):
    tokens, cols = parts[0].shape
    vmem = pl.BlockSpec(memory_space=pltpu.VMEM)
    return pl.pallas_call(
        functools.partial(finish_kernel, places),
        in_specs=[vmem] * (len(parts) + 2 * len(mixed)),
        out_specs=[vmem] * 2,
        out_shape=[
            jax.ShapeDtypeStruct((tokens, q_width), jnp.bfloat16),
            jax.ShapeDtypeStruct((tokens, cols), jnp.bfloat16),
        ],
        compiler_params=pltpu.CompilerParams(vmem_limit_bytes=16 * MIB),
        cost_estimate=FREE,
        name="finish_attention",
    )(*mixed, *fresh_probs, *parts)


def on_device(
    normed_inputs,
    value_matrix,
    adapter_down_weight,
    adapter_up_weight,
    adapter_position,
    span_adapter_index,
    queries,
    incoming_keys,
    stored_keys,
    stored_values,
    cache_length,
):
    quads = lax.axis_size("quad")
    parts_swap = [(i, i ^ 1) for i in range(lax.axis_size("parts"))]
    width, cols = value_matrix.shape
    downs = adapter_down_weight.reshape(-1, adapter_down_weight.shape[2])
    ups = adapter_up_weight.reshape(-1, cols)

    kv_heads = cols // HD
    def attention(span, lengths):
        return cache_attention(
            span, 0, cols // HD, False, queries, incoming_keys, stored_keys, stored_values, lengths
        )

    def after(value, *others):
        return lax.optimization_barrier((value, *others))[0]

    def to_quad(value, q):
        return lax.ppermute(value, "quad", [(j, j ^ q) for j in range(quads)])

    early, late = cross_pack(value_matrix, downs, ups)
    message = quad_pack(after(normed_inputs, early), downs, ups, width, quads)
    early = lax.ppermute(early, "wing", SWAP)
    mine = lax.all_to_all(message, "quad", 0, 0)

    attn = [attention(0, after(cache_length, message))]
    attn.append(attention(1, after(cache_length, attn[0][1])))
    early = after(early, attn[1][1])
    late = lax.ppermute(after(late, early), "wing", SWAP)
    early, *passed = maps_pack(early, width, quads)
    early_other = lax.ppermute(early, "parts", parts_swap)
    passed_on = [to_quad(passed[q], q) for q in range(1, quads)]

    maps_mine = jnp.stack([passed[0]] + passed_on)
    theirs = lax.ppermute(after(mine, early), "tensor", SWAP)
    maps_theirs = lax.ppermute(after(maps_mine, early_other, late), "tensor", SWAP)
    late_other = lax.ppermute(late, "parts", parts_swap)

    tokens, q_width = queries.shape
    near = near_products(
        mine, theirs, maps_mine, maps_theirs, value_matrix, adapter_position, span_adapter_index, tokens
    )
    products = far_products(mine, theirs, near, (early, late, early_other, late_other), tokens)
    parts = [products[0]] + [to_quad(products[q], q) for q in range(1, quads)]
    mixed, fresh_probs = zip(*attn)
    attended, incoming_values = finish([(0, 0), (1, 0)], mixed, fresh_probs, parts, q_width)
    return (attended, incoming_values)


def solution(mesh):
    sizes = mesh.devices.shape
    cut = Mesh(
        mesh.devices.reshape(sizes[0], 2, sizes[1] // 2, sizes[2]), ("parts", "wing", "quad", "tensor")
    )
    group = ("wing", "quad")
    home = ("parts", "wing", "quad")
    in_specs = (
        P(home, "tensor"),
        P(group, "tensor"),
        P(group, None, None),
        P(group, None, "tensor"),
        P(),
        P("parts"),
        P(home, "tensor"),
        P(home, "tensor"),
        P(home, None, "tensor"),
        P(home, None, "tensor"),
        P(home),
    )
    out_specs = (P(home, "tensor"), P(home, "tensor"))
    return jax.shard_map(
        on_device, mesh=cut, in_specs=in_specs, out_specs=out_specs, check_vma=False
    )
```

```python
import functools
import math

import jax
import jax.numpy as jnp
from jax import lax
from jax.experimental import pallas as pl
from jax.experimental.pallas import tpu as pltpu
from jax.sharding import Mesh
from jax.sharding import PartitionSpec as P

HD = 128
RANK = 16
SPAN = 64
CHUNK = 512
CHUNKS = 1
ONES = 16
ADAPTER_SCALE = 2.0
EXP2_SCALE = math.log2(math.e) / math.sqrt(HD)
DEAD = -1e30
MIB = 1024 * 1024
SWAP = [(0, 1), (1, 0)]
FREE = pl.CostEstimate(flops=1, bytes_accessed=1, transcendentals=0)


def dot_last(a, b):
    return lax.dot_general(a, b, (((1,), (1,)), ((), ())), preferred_element_type=jnp.float32)


def dot(a, b):
    return jnp.dot(a, b, preferred_element_type=jnp.float32)


def cache_kernel(span, first_head, kv_heads, group_size, lens, q_ref, fk_ref, k_hbm, v_hbm, out_ref, pf_ref, qs, ks, vs, m_s, acc, sems):
    length = lens[span]
    rows = group_size * SPAN
    chunks, chunk, width = ks.shape
    heads = slice(first_head * HD, first_head * HD + width)

    def copies(i):
        live = pl.ds(pl.multiple_of(i * chunk, chunk), chunk)
        return (
            pltpu.make_async_copy(k_hbm.at[span, live, heads], ks.at[i], sems.at[0, i]),
            pltpu.make_async_copy(v_hbm.at[span, live, heads], vs.at[i], sems.at[1, i]),
        )

    for i in range(chunks):

        @pl.when(i * chunk < length)
        def _():
            for copy in copies(i):
                copy.start()

    def fresh_scores(k):
        s = dot_last(fk_ref[span * SPAN : (span + 1) * SPAN, (first_head + k) * HD : (first_head + k + 1) * HD], qs[k])
        key = lax.broadcasted_iota(jnp.int32, (SPAN, rows), 0)
        token = lax.broadcasted_iota(jnp.int32, (SPAN, rows), 1) % SPAN
        return jnp.where(key <= token, s, DEAD)

    for k in range(kv_heads):
        for h in range(group_size):
            col = ((first_head + k) * group_size + h) * HD
            qs[k, h * SPAN : (h + 1) * SPAN, :] = q_ref[span * SPAN : (span + 1) * SPAN, col : col + HD]
        m_s[k] = jnp.max(fresh_scores(k), axis=0, keepdims=True)
        acc[k] = jnp.zeros((HD + ONES, rows), jnp.float32)

    ones = jnp.ones((ONES, chunk), jnp.bfloat16)

    def add_chunk(i, masked):
        for copy in copies(i):
            copy.wait()

        def scores(k):
            s = dot_last(ks[i, :, k * HD : (k + 1) * HD], qs[k])
            if masked:
                slot = i * chunk + lax.broadcasted_iota(jnp.int32, (chunk, rows), 0)
                s = jnp.where(slot < length, s, DEAD)
            return s

        s = scores(0)
        for k in range(kv_heads):
            later = scores(k + 1) if k + 1 < kv_heads else None
            before = m_s[k]
            top = jnp.maximum(before, jnp.max(s, axis=0, keepdims=True))
            m_s[k] = top
            p = jnp.exp2((s - top) * EXP2_SCALE).astype(jnp.bfloat16)
            alpha = jnp.exp2((before - top) * EXP2_SCALE)
            values = jnp.concatenate([vs[i, :, k * HD : (k + 1) * HD].T, ones], axis=0)
            acc[k] = acc[k] * alpha + dot(values, p)
            s = later

    @pl.loop(0, length // chunk)
    def _(i):
        add_chunk(i, False)

    @pl.when(length % chunk != 0)
    def _():
        add_chunk(length // chunk, True)

    for k in range(kv_heads):
        p = jnp.exp2((fresh_scores(k) - m_s[k]) * EXP2_SCALE)
        inverse = 1.0 / (acc[k, HD : HD + 1, :] + jnp.sum(p, axis=0, keepdims=True))
        pf_ref[k * rows : (k + 1) * rows, :] = (p * inverse).T.astype(jnp.bfloat16)
        mixed = (acc[k, :HD, :] * inverse).T
        for h in range(group_size):
            col = (k * group_size + h) * HD
            out_ref[:, col : col + HD] = mixed[h * SPAN : (h + 1) * SPAN, :]


def cache_attention(span, first_head, kv_heads, hides, queries, fresh_keys, keys, values, lengths):
    slots = keys.shape[1]
    group_size = queries.shape[1] // keys.shape[2]
    width = kv_heads * HD
    rows = group_size * SPAN
    chunk = min(CHUNK, slots)
    chunks = slots // chunk
    vmem = pl.BlockSpec(memory_space=pltpu.VMEM)
    hbm = pl.BlockSpec(memory_space=pltpu.HBM)
    return pl.pallas_call(
        functools.partial(cache_kernel, span, first_head, kv_heads, group_size),
        in_specs=[pl.BlockSpec(memory_space=pltpu.SMEM), vmem, vmem, hbm, hbm],
        out_specs=[vmem, vmem],
        scratch_shapes=[
            pltpu.VMEM((kv_heads, rows, HD), jnp.bfloat16),
            pltpu.VMEM((chunks, chunk, width), jnp.bfloat16),
            pltpu.VMEM((chunks, chunk, width), jnp.bfloat16),
            pltpu.VMEM((kv_heads, 1, rows), jnp.float32),
            pltpu.VMEM((kv_heads, HD + ONES, rows), jnp.float32),
            pltpu.SemaphoreType.DMA((2, chunks)),
        ],
        out_shape=[
            jax.ShapeDtypeStruct((SPAN, group_size * width), jnp.float32),
            jax.ShapeDtypeStruct((kv_heads * rows, SPAN), jnp.bfloat16),
        ],
        compiler_params=pltpu.CompilerParams(vmem_limit_bytes=57 * MIB),
        cost_estimate=pl.CostEstimate(
            flops=4 * rows * slots * width, bytes_accessed=4 * slots * width, transcendentals=0
        )
        if hides
        else FREE,
        name="cache_attention",
    )(lengths, queries, fresh_keys, keys, values)


def run_copies(copies, sems):
    copies = [pltpu.make_async_copy(src, dst, sems.at[i]) for i, (src, dst) in enumerate(copies)]
    for copy in copies:
        copy.start()
    for copy in copies:
        copy.wait()


def up_places(cols, width):
    step = min(cols, width)
    return [
        (slot, first, (slot * cols + first) // width * RANK, (slot * cols + first) % width)
        for slot in range(2)
        for first in range(0, cols, step)
    ]


def pack_kernel(x_hbm, d_hbm, u_hbm, w_hbm, out, maps, *refs):
    rows, sems = refs[:-1], refs[-1]
    part, core = lax.axis_index("parts") % 2, lax.axis_index("tensor")
    quads, _, width = out.shape
    tokens, features = x_hbm.shape
    ranks, cols = u_hbm.shape
    step = min(cols, width)
    begin = part * (w_hbm.shape[0] // 2)
    copies = []
    for piece in rows:
        size = piece.shape[0]
        copies.append((w_hbm.at[pl.ds(pl.multiple_of(begin, size), size), :], piece))
        begin = begin + size
    copies.append((d_hbm.at[:, pl.ds(pl.multiple_of(core * features, features), features)], maps.at[:, :features]))
    copies.append((u_hbm, maps.at[:, features:]))
    for j in range(quads):
        first = pl.multiple_of(core * features + j * width, width)
        copies.append((x_hbm.at[:, j * width : (j + 1) * width], out.at[j, :tokens, :]))
        copies.append((d_hbm.at[:, pl.ds(first, width)], out.at[j, tokens : tokens + ranks, :]))
        for slot, first, row, col in up_places(cols, width):
            row += tokens + ranks
            copies.append(
                (
                    u_hbm.at[slot * RANK : (slot + 1) * RANK, first : first + step],
                    out.at[j, row : row + RANK, col : col + step],
                )
            )
    run_copies(copies, sems)


def pack(tokens, downs, ups, weights, quads):
    vmem = pl.BlockSpec(memory_space=pltpu.VMEM)
    hbm = pl.BlockSpec(memory_space=pltpu.HBM)
    ranks, cols = ups.shape
    width = weights.shape[0]
    rows = tokens.shape[0] + ranks + RANK * (2 * cols // width)
    count = CHUNKS + 2 + quads * (2 + len(up_places(cols, width)))
    piece = jax.ShapeDtypeStruct((width // 2 // CHUNKS, cols), weights.dtype)
    return pl.pallas_call(
        pack_kernel,
        in_specs=[hbm] * 4,
        out_specs=[vmem] * (2 + CHUNKS),
        out_shape=[
            jax.ShapeDtypeStruct((quads, rows, width), tokens.dtype),
            jax.ShapeDtypeStruct((ranks, tokens.shape[1] + cols), downs.dtype),
        ]
        + [piece] * CHUNKS,
        scratch_shapes=[pltpu.SemaphoreType.DMA((count,))],
        compiler_params=pltpu.CompilerParams(vmem_limit_bytes=57 * MIB),
        cost_estimate=FREE,
        name="pack",
    )(tokens, downs, ups, weights)


def maps_kernel(here, *outs):
    quad = lax.axis_index("quad")
    width = outs[0].shape[1]
    ranks = here.shape[0]
    features = len(outs) * width
    cols = here.shape[1] - features
    step = min(cols, width)
    for q, out in enumerate(outs):
        out[:ranks, :] = here[:, pl.ds(pl.multiple_of((quad ^ q) * width, width), width)]
        for slot, first, row, col in up_places(cols, width):
            up = here[slot * RANK : (slot + 1) * RANK, features + first : features + first + step]
            out[ranks + row : ranks + row + RANK, col : col + step] = up


def maps_pack(here, width, quads):
    vmem = pl.BlockSpec(memory_space=pltpu.VMEM)
    cols = here.shape[1] - quads * width
    maps = jax.ShapeDtypeStruct((RANK * (2 + 2 * cols // width), width), here.dtype)
    return pl.pallas_call(
        maps_kernel,
        in_specs=[vmem],
        out_specs=[vmem] * quads,
        out_shape=[maps] * quads,
        compiler_params=pltpu.CompilerParams(vmem_limit_bytes=4 * MIB),
        cost_estimate=FREE,
        name="maps_pack",
    )(here)


def near_kernel(tokens, position, adapter, mine, theirs, maps_mine, maps_theirs, own_ref, out, ds, us):
    core, wing, quad = lax.axis_index("tensor"), lax.axis_index("wing"), lax.axis_index("quad")
    quads, _, width = mine.shape
    cols = own_ref.shape[1]
    ranks = 2 * RANK
    step = min(cols, width)
    for j in range(quads):
        for side, here, there, base, index in (
            (0, mine.at[j], theirs.at[j], tokens, j),
            (1, maps_mine.at[j], maps_theirs.at[j], 0, quad ^ j),
        ):
            first_row = (side * quads + index) * ranks
            rows = pl.ds(pl.multiple_of(first_row, ranks), ranks)
            ds[0, rows, :] = here[base : base + ranks, :]
            ds[1, rows, :] = there[base : base + ranks, :]
            for slot, first, row, col in up_places(cols, width):
                row += base + ranks
                place = pl.ds(pl.multiple_of(first_row + slot * RANK, RANK), RANK)
                us[place, first : first + step] = here[row : row + RANK, col : col + step]

    x_mine = mine[:, :tokens, :].reshape(quads * tokens, width)
    x_theirs = theirs[:, :tokens, :].reshape(quads * tokens, width)
    shrink = dot_last(x_mine, ds[0]) + dot_last(x_theirs, ds[1])
    slots = us.shape[0] // RANK
    which = lax.broadcasted_iota(jnp.int32, (SPAN, slots * RANK), 1) // RANK + wing * (slots // 2)
    which = jnp.where(which >= slots, which - slots, which)
    spans = quads * tokens // SPAN
    masked = []
    for i in range(spans):
        slot = position[adapter[wing * spans + i]]
        masked.append(jnp.where(which == slot, shrink[i * SPAN : (i + 1) * SPAN, :], 0.0))
    shrink = (jnp.concatenate(masked, axis=0) * ADAPTER_SCALE).astype(jnp.bfloat16)
    out[...] = dot(shrink, us[...])

    @pl.when(core == wing)
    def _():
        out[...] += dot(x_mine, own_ref[...])

    @pl.when(core != wing)
    def _():
        out[...] += dot(x_theirs, own_ref[...])


def near_products(mine, theirs, maps_mine, maps_theirs, own, position, adapter, tokens):
    quads, _, width = mine.shape
    cols = own.shape[1]
    ranks = 4 * quads * RANK
    vmem = pl.BlockSpec(memory_space=pltpu.VMEM)
    smem = pl.BlockSpec(memory_space=pltpu.SMEM)
    return pl.pallas_call(
        functools.partial(near_kernel, tokens),
        in_specs=[smem, smem] + [vmem] * 5,
        out_specs=vmem,
        out_shape=jax.ShapeDtypeStruct((quads * tokens, cols), jnp.float32),
        scratch_shapes=[
            pltpu.VMEM((2, ranks, width), jnp.bfloat16),
            pltpu.VMEM((ranks, cols), jnp.bfloat16),
        ],
        compiler_params=pltpu.CompilerParams(vmem_limit_bytes=48 * MIB if quads > 4 else 24 * MIB),
        cost_estimate=FREE,
        name="near_products",
    )(position, adapter, mine, theirs, maps_mine, maps_theirs, own)


def far_kernel(tokens, mine, theirs, near, *refs):
    quads, _, width = mine.shape
    outs, (whole, total) = refs[-2 - quads : -2], refs[-2:]
    weights = refs[: -2 - quads]
    part, core, wing = lax.axis_index("parts") % 2, lax.axis_index("tensor"), lax.axis_index("wing")
    quad = lax.axis_index("quad")
    chunk = weights[0].shape[0]
    chunks = len(weights) // 2
    for side in range(2):
        begin = (part if side == 0 else 1 - part) * (width // 2)
        for i in range(chunks):
            row = pl.multiple_of(begin + i * chunk, chunk)
            whole[pl.ds(row, chunk), :] = weights[side * chunks + i][...]

    def store(x):
        product = dot(x[:, :tokens, :].reshape(quads * tokens, width), whole[...])
        total[...] = (near[...] + product).astype(jnp.bfloat16).reshape(total.shape)

    @pl.when(core == wing)
    def _():
        store(theirs)

    @pl.when(core != wing)
    def _():
        store(mine)

    for q in range(quads):
        outs[q][...] = total[quad ^ q]


def far_products(mine, theirs, near, weights, tokens):
    quads, _, width = mine.shape
    cols = near.shape[1]
    vmem = pl.BlockSpec(memory_space=pltpu.VMEM)
    return pl.pallas_call(
        functools.partial(far_kernel, tokens),
        in_specs=[vmem] * (3 + len(weights)),
        out_specs=[vmem] * quads,
        out_shape=[jax.ShapeDtypeStruct((tokens, cols), jnp.bfloat16)] * quads,
        scratch_shapes=[
            pltpu.VMEM((width, cols), jnp.bfloat16),
            pltpu.VMEM((quads, tokens, cols), jnp.bfloat16),
        ],
        compiler_params=pltpu.CompilerParams(vmem_limit_bytes=48 * MIB if quads > 4 else 16 * MIB),
        cost_estimate=FREE,
        name="far_products",
    )(mine, theirs, near, *weights)


def finish_kernel(places, *refs):
    count = len(places)
    out_ref, values_ref = refs[-2:]
    mixed, probs, parts = refs[:count], refs[count : 2 * count], refs[2 * count : -2]
    total = parts[0][...].astype(jnp.float32)
    for part in parts[1:]:
        total = total + part[...].astype(jnp.float32)
    total = total.astype(jnp.bfloat16)
    values_ref[...] = total
    for (span, head), mix, prob in zip(places, mixed, probs):
        rows = slice(span * SPAN, (span + 1) * SPAN)
        group_size = out_ref.shape[1] // total.shape[1]
        queries = group_size * SPAN
        for k in range(prob.shape[0] // queries):
            values = total[rows, (head + k) * HD : (head + k + 1) * HD]
            fresh = dot(prob[k * queries : (k + 1) * queries, :], values)
            for h in range(group_size):
                here = slice((k * group_size + h) * HD, (k * group_size + h + 1) * HD)
                col = ((head + k) * group_size + h) * HD
                out_ref[rows, col : col + HD] = (
                    mix[:, here] + fresh[h * SPAN : (h + 1) * SPAN, :]
                ).astype(jnp.bfloat16)


def finish(places, mixed, fresh_probs, parts, q_width):
    tokens, cols = parts[0].shape
    vmem = pl.BlockSpec(memory_space=pltpu.VMEM)
    return pl.pallas_call(
        functools.partial(finish_kernel, places),
        in_specs=[vmem] * (len(parts) + 2 * len(mixed)),
        out_specs=[vmem] * 2,
        out_shape=[
            jax.ShapeDtypeStruct((tokens, q_width), jnp.bfloat16),
            jax.ShapeDtypeStruct((tokens, cols), jnp.bfloat16),
        ],
        compiler_params=pltpu.CompilerParams(vmem_limit_bytes=16 * MIB),
        cost_estimate=FREE,
        name="finish_attention",
    )(*mixed, *fresh_probs, *parts)


def on_device(
    normed_inputs,
    value_matrix,
    adapter_down_weight,
    adapter_up_weight,
    adapter_position,
    span_adapter_index,
    queries,
    incoming_keys,
    stored_keys,
    stored_values,
    cache_length,
):
    quads = lax.axis_size("quad")
    parts_swap = [(i, i ^ 1) for i in range(lax.axis_size("parts"))]
    width, cols = value_matrix.shape
    downs = adapter_down_weight.reshape(-1, adapter_down_weight.shape[2])
    ups = adapter_up_weight.reshape(-1, cols)

    kv_heads = cols // HD
    def attention(span, lengths):
        return cache_attention(
            span, 0, cols // HD, False, queries, incoming_keys, stored_keys, stored_values, lengths
        )

    def after(value, *others):
        return lax.optimization_barrier((value, *others))[0]

    def to_quad(value, q):
        return lax.ppermute(value, "quad", [(j, j ^ q) for j in range(quads)])

    message, maps, *rows = pack(normed_inputs, downs, ups, value_matrix, quads)
    mine = lax.all_to_all(message, "quad", 0, 0)
    maps = lax.ppermute(maps, "wing", SWAP)
    rows = [lax.ppermute(piece, "wing", SWAP) for piece in rows]

    attn = [attention(0, after(cache_length, message))]
    attn.append(attention(1, after(cache_length, attn[0][1])))
    maps, *rows = lax.optimization_barrier((maps, *rows, attn[1][1]))[:-1]
    passed = maps_pack(maps, width, quads)
    passed_on = [to_quad(passed[q], q) for q in range(1, quads)]
    rows_other = [lax.ppermute(piece, "parts", parts_swap) for piece in rows]

    maps_mine = jnp.stack([passed[0]] + passed_on)
    theirs = lax.ppermute(after(mine, rows[0]), "tensor", SWAP)
    maps_theirs = lax.ppermute(maps_mine, "tensor", SWAP)

    tokens, q_width = queries.shape
    near = near_products(
        mine, theirs, maps_mine, maps_theirs, value_matrix, adapter_position, span_adapter_index, tokens
    )
    products = far_products(mine, theirs, near, (*rows, *rows_other), tokens)
    parts = [products[0]] + [to_quad(products[q], q) for q in range(1, quads)]
    mixed, fresh_probs = zip(*attn)
    attended, incoming_values = finish([(0, 0), (1, 0)], mixed, fresh_probs, parts, q_width)
    return (attended, incoming_values)


def solution(mesh):
    sizes = mesh.devices.shape
    cut = Mesh(
        mesh.devices.reshape(sizes[0], 2, sizes[1] // 2, sizes[2]), ("parts", "wing", "quad", "tensor")
    )
    group = ("wing", "quad")
    home = ("parts", "wing", "quad")
    in_specs = (
        P(home, "tensor"),
        P(group, "tensor"),
        P(group, None, None),
        P(group, None, "tensor"),
        P(),
        P("parts"),
        P(home, "tensor"),
        P(home, "tensor"),
        P(home, None, "tensor"),
        P(home, None, "tensor"),
        P(home),
    )
    out_specs = (P(home, "tensor"), P(home, "tensor"))
    return jax.shard_map(
        on_device, mesh=cut, in_specs=in_specs, out_specs=out_specs, check_vma=False
    )
```

```python
import functools
import math

import jax
import jax.numpy as jnp
from jax import lax
from jax.experimental import pallas as pl
from jax.experimental.pallas import tpu as pltpu
from jax.sharding import Mesh
from jax.sharding import PartitionSpec as P

HD = 128
RANK = 16
SPAN = 64
CHUNK = 512
ONES = 16
ADAPTER_SCALE = 2.0
EXP2_SCALE = math.log2(math.e) / math.sqrt(HD)
DEAD = -1e30
MIB = 1024 * 1024
SWAP = [(0, 1), (1, 0)]
FREE = pl.CostEstimate(flops=1, bytes_accessed=1, transcendentals=0)


def dot_last(a, b):
    return lax.dot_general(a, b, (((1,), (1,)), ((), ())), preferred_element_type=jnp.float32)


def dot(a, b):
    return jnp.dot(a, b, preferred_element_type=jnp.float32)


def cache_kernel(span, first_head, kv_heads, group_size, lens, q_ref, fk_ref, k_hbm, v_hbm, out_ref, pf_ref, qs, ks, vs, m_s, acc, sems):
    length = lens[span]
    rows = group_size * SPAN
    chunks, chunk, width = ks.shape
    heads = slice(first_head * HD, first_head * HD + width)

    def copies(i):
        live = pl.ds(pl.multiple_of(i * chunk, chunk), chunk)
        return (
            pltpu.make_async_copy(k_hbm.at[span, live, heads], ks.at[i], sems.at[0, i]),
            pltpu.make_async_copy(v_hbm.at[span, live, heads], vs.at[i], sems.at[1, i]),
        )

    for i in range(chunks):

        @pl.when(i * chunk < length)
        def _():
            for copy in copies(i):
                copy.start()

    def fresh_scores(k):
        s = dot_last(fk_ref[span * SPAN : (span + 1) * SPAN, (first_head + k) * HD : (first_head + k + 1) * HD], qs[k])
        key = lax.broadcasted_iota(jnp.int32, (SPAN, rows), 0)
        token = lax.broadcasted_iota(jnp.int32, (SPAN, rows), 1) % SPAN
        return jnp.where(key <= token, s, DEAD)

    for k in range(kv_heads):
        for h in range(group_size):
            col = ((first_head + k) * group_size + h) * HD
            qs[k, h * SPAN : (h + 1) * SPAN, :] = q_ref[span * SPAN : (span + 1) * SPAN, col : col + HD]
        m_s[k] = jnp.max(fresh_scores(k), axis=0, keepdims=True)
        acc[k] = jnp.zeros((HD + ONES, rows), jnp.float32)

    ones = jnp.ones((ONES, chunk), jnp.bfloat16)

    def add_chunk(i, masked):
        for copy in copies(i):
            copy.wait()

        def scores(k):
            s = dot_last(ks[i, :, k * HD : (k + 1) * HD], qs[k])
            if masked:
                slot = i * chunk + lax.broadcasted_iota(jnp.int32, (chunk, rows), 0)
                s = jnp.where(slot < length, s, DEAD)
            return s

        s = scores(0)
        for k in range(kv_heads):
            later = scores(k + 1) if k + 1 < kv_heads else None
            before = m_s[k]
            top = jnp.maximum(before, jnp.max(s, axis=0, keepdims=True))
            m_s[k] = top
            p = jnp.exp2((s - top) * EXP2_SCALE).astype(jnp.bfloat16)
            alpha = jnp.exp2((before - top) * EXP2_SCALE)
            values = jnp.concatenate([vs[i, :, k * HD : (k + 1) * HD].T, ones], axis=0)
            acc[k] = acc[k] * alpha + dot(values, p)
            s = later

    @pl.loop(0, length // chunk)
    def _(i):
        add_chunk(i, False)

    @pl.when(length % chunk != 0)
    def _():
        add_chunk(length // chunk, True)

    for k in range(kv_heads):
        p = jnp.exp2((fresh_scores(k) - m_s[k]) * EXP2_SCALE)
        inverse = 1.0 / (acc[k, HD : HD + 1, :] + jnp.sum(p, axis=0, keepdims=True))
        pf_ref[k * rows : (k + 1) * rows, :] = (p * inverse).T.astype(jnp.bfloat16)
        mixed = (acc[k, :HD, :] * inverse).T
        for h in range(group_size):
            col = (k * group_size + h) * HD
            out_ref[:, col : col + HD] = mixed[h * SPAN : (h + 1) * SPAN, :]


def cache_attention(span, first_head, kv_heads, hides, queries, fresh_keys, keys, values, lengths):
    slots = keys.shape[1]
    group_size = queries.shape[1] // keys.shape[2]
    width = kv_heads * HD
    rows = group_size * SPAN
    chunk = min(CHUNK, slots)
    chunks = slots // chunk
    vmem = pl.BlockSpec(memory_space=pltpu.VMEM)
    hbm = pl.BlockSpec(memory_space=pltpu.HBM)
    return pl.pallas_call(
        functools.partial(cache_kernel, span, first_head, kv_heads, group_size),
        in_specs=[pl.BlockSpec(memory_space=pltpu.SMEM), vmem, vmem, hbm, hbm],
        out_specs=[vmem, vmem],
        scratch_shapes=[
            pltpu.VMEM((kv_heads, rows, HD), jnp.bfloat16),
            pltpu.VMEM((chunks, chunk, width), jnp.bfloat16),
            pltpu.VMEM((chunks, chunk, width), jnp.bfloat16),
            pltpu.VMEM((kv_heads, 1, rows), jnp.float32),
            pltpu.VMEM((kv_heads, HD + ONES, rows), jnp.float32),
            pltpu.SemaphoreType.DMA((2, chunks)),
        ],
        out_shape=[
            jax.ShapeDtypeStruct((SPAN, group_size * width), jnp.float32),
            jax.ShapeDtypeStruct((kv_heads * rows, SPAN), jnp.bfloat16),
        ],
        compiler_params=pltpu.CompilerParams(vmem_limit_bytes=57 * MIB),
        cost_estimate=pl.CostEstimate(
            flops=4 * rows * slots * width, bytes_accessed=4 * slots * width, transcendentals=0
        )
        if hides
        else FREE,
        name="cache_attention",
    )(lengths, queries, fresh_keys, keys, values)


def run_copies(copies, sems):
    copies = [pltpu.make_async_copy(src, dst, sems.at[i]) for i, (src, dst) in enumerate(copies)]
    for copy in copies:
        copy.start()
    for copy in copies:
        copy.wait()


def up_places(cols, width):
    step = min(cols, width)
    return [
        (slot, first, (slot * cols + first) // width * RANK, (slot * cols + first) % width)
        for slot in range(2)
        for first in range(0, cols, step)
    ]


def cross_kernel(w_hbm, d_hbm, u_hbm, maps, *refs):
    rows, sems = refs[:-1], refs[-1]
    part, core = lax.axis_index("parts") % 2, lax.axis_index("tensor")
    cols = u_hbm.shape[1]
    features = maps.shape[1] - cols
    mine = pl.ds(pl.multiple_of(part * RANK, RANK), RANK)
    here = pl.ds(pl.multiple_of(core * features, features), features)
    copies = [(d_hbm.at[mine, here], maps.at[:, :features]), (u_hbm.at[mine, :], maps.at[:, features:])]
    begin = part * (w_hbm.shape[0] // 2)
    for piece in rows:
        size = piece.shape[0]
        copies.append((w_hbm.at[pl.ds(pl.multiple_of(begin, RANK), size), :], piece))
        begin = begin + size
    run_copies(copies, sems)


def cross_pack(weights, downs, ups):
    width, cols = weights.shape
    vmem = pl.BlockSpec(memory_space=pltpu.VMEM)
    hbm = pl.BlockSpec(memory_space=pltpu.HBM)
    maps = jax.ShapeDtypeStruct((RANK, downs.shape[1] // 2 + cols), downs.dtype)
    first = width // 2 * 3 // 8
    rows = [jax.ShapeDtypeStruct((size, cols), weights.dtype) for size in (first, width // 2 - first)]
    return pl.pallas_call(
        cross_kernel,
        in_specs=[hbm] * 3,
        out_specs=[vmem] * 3,
        out_shape=[maps] + rows,
        scratch_shapes=[pltpu.SemaphoreType.DMA((4,))],
        compiler_params=pltpu.CompilerParams(vmem_limit_bytes=57 * MIB),
        cost_estimate=FREE,
        name="cross_pack",
    )(weights, downs, ups)


def quad_kernel(x_hbm, d_hbm, u_hbm, out, sems):
    core = lax.axis_index("tensor")
    quads, _, width = out.shape
    tokens, features = x_hbm.shape
    ranks, cols = u_hbm.shape
    step = min(cols, width)
    copies = []
    for j in range(quads):
        begin = pl.multiple_of(core * features + j * width, width)
        copies.append((x_hbm.at[:, j * width : (j + 1) * width], out.at[j, :tokens, :]))
        copies.append((d_hbm.at[:, pl.ds(begin, width)], out.at[j, tokens : tokens + ranks, :]))
        for slot, first, row, col in up_places(cols, width):
            row += tokens + ranks
            copies.append(
                (
                    u_hbm.at[slot * RANK : (slot + 1) * RANK, first : first + step],
                    out.at[j, row : row + RANK, col : col + step],
                )
            )
    run_copies(copies, sems)


def quad_pack(tokens, downs, ups, width, quads):
    vmem = pl.BlockSpec(memory_space=pltpu.VMEM)
    hbm = pl.BlockSpec(memory_space=pltpu.HBM)
    ranks, cols = ups.shape
    rows = tokens.shape[0] + ranks + RANK * (2 * cols // width)
    count = quads * (2 + len(up_places(cols, width)))
    return pl.pallas_call(
        quad_kernel,
        in_specs=[hbm] * 3,
        out_specs=vmem,
        out_shape=jax.ShapeDtypeStruct((quads, rows, width), tokens.dtype),
        scratch_shapes=[pltpu.SemaphoreType.DMA((count,))],
        compiler_params=pltpu.CompilerParams(vmem_limit_bytes=57 * MIB),
        cost_estimate=FREE,
        name="quad_pack",
    )(tokens, downs, ups)


def maps_kernel(here, there, *outs):
    part, quad = lax.axis_index("parts") % 2, lax.axis_index("quad")
    width = outs[0].shape[1]
    features = len(outs) * width
    cols = here.shape[1] - features
    step = min(cols, width)
    for q, out in enumerate(outs):
        column = pl.ds(pl.multiple_of((quad ^ q) * width, width), width)
        for slot, maps in ((part, here), (1 - part, there)):
            out[pl.ds(pl.multiple_of(slot * RANK, RANK), RANK), :] = maps[:, column]
            for first in range(0, cols, step):
                place = slot * cols + first
                row = pl.multiple_of((2 + place // width) * RANK, RANK)
                col = pl.multiple_of(place % width, step)
                out[pl.ds(row, RANK), pl.ds(col, step)] = maps[:, features + first : features + first + step]


def maps_pack(here, there, width, quads):
    vmem = pl.BlockSpec(memory_space=pltpu.VMEM)
    cols = here.shape[1] - quads * width
    maps = jax.ShapeDtypeStruct((RANK * (2 + 2 * cols // width), width), here.dtype)
    return pl.pallas_call(
        maps_kernel,
        in_specs=[vmem] * 2,
        out_specs=[vmem] * quads,
        out_shape=[maps] * quads,
        compiler_params=pltpu.CompilerParams(vmem_limit_bytes=4 * MIB),
        cost_estimate=FREE,
        name="maps_pack",
    )(here, there)


def near_kernel(tokens, position, adapter, mine, theirs, maps_mine, maps_theirs, own_ref, out, ds, us):
    core, wing, quad = lax.axis_index("tensor"), lax.axis_index("wing"), lax.axis_index("quad")
    quads, _, width = mine.shape
    cols = own_ref.shape[1]
    ranks = 2 * RANK
    step = min(cols, width)
    for j in range(quads):
        for side, here, there, base, index in (
            (0, mine.at[j], theirs.at[j], tokens, j),
            (1, maps_mine.at[j], maps_theirs.at[j], 0, quad ^ j),
        ):
            first_row = (side * quads + index) * ranks
            rows = pl.ds(pl.multiple_of(first_row, ranks), ranks)
            ds[0, rows, :] = here[base : base + ranks, :]
            ds[1, rows, :] = there[base : base + ranks, :]
            for slot, first, row, col in up_places(cols, width):
                row += base + ranks
                place = pl.ds(pl.multiple_of(first_row + slot * RANK, RANK), RANK)
                us[place, first : first + step] = here[row : row + RANK, col : col + step]

    x_mine = mine[:, :tokens, :].reshape(quads * tokens, width)
    x_theirs = theirs[:, :tokens, :].reshape(quads * tokens, width)
    shrink = dot_last(x_mine, ds[0]) + dot_last(x_theirs, ds[1])
    slots = us.shape[0] // RANK
    which = lax.broadcasted_iota(jnp.int32, (SPAN, slots * RANK), 1) // RANK + wing * (slots // 2)
    which = jnp.where(which >= slots, which - slots, which)
    spans = quads * tokens // SPAN
    masked = []
    for i in range(spans):
        slot = position[adapter[wing * spans + i]]
        masked.append(jnp.where(which == slot, shrink[i * SPAN : (i + 1) * SPAN, :], 0.0))
    shrink = (jnp.concatenate(masked, axis=0) * ADAPTER_SCALE).astype(jnp.bfloat16)
    out[...] = dot(shrink, us[...])

    @pl.when(core == wing)
    def _():
        out[...] += dot(x_mine, own_ref[...])

    @pl.when(core != wing)
    def _():
        out[...] += dot(x_theirs, own_ref[...])


def near_products(mine, theirs, maps_mine, maps_theirs, own, position, adapter, tokens):
    quads, _, width = mine.shape
    cols = own.shape[1]
    ranks = 4 * quads * RANK
    vmem = pl.BlockSpec(memory_space=pltpu.VMEM)
    smem = pl.BlockSpec(memory_space=pltpu.SMEM)
    return pl.pallas_call(
        functools.partial(near_kernel, tokens),
        in_specs=[smem, smem] + [vmem] * 5,
        out_specs=vmem,
        out_shape=jax.ShapeDtypeStruct((quads * tokens, cols), jnp.float32),
        scratch_shapes=[
            pltpu.VMEM((2, ranks, width), jnp.bfloat16),
            pltpu.VMEM((ranks, cols), jnp.bfloat16),
        ],
        compiler_params=pltpu.CompilerParams(vmem_limit_bytes=48 * MIB if quads > 4 else 24 * MIB),
        cost_estimate=FREE,
        name="near_products",
    )(position, adapter, mine, theirs, maps_mine, maps_theirs, own)


def far_kernel(tokens, mine, theirs, near, *refs):
    quads, _, width = mine.shape
    outs, (whole, total) = refs[-2 - quads : -2], refs[-2:]
    weights = refs[: -2 - quads]
    part, core, wing = lax.axis_index("parts") % 2, lax.axis_index("tensor"), lax.axis_index("wing")
    quad = lax.axis_index("quad")
    for side in range(2):
        begin = (part if side == 0 else 1 - part) * (width // 2)
        for piece in weights[2 * side : 2 * side + 2]:
            whole[pl.ds(pl.multiple_of(begin, RANK), piece.shape[0]), :] = piece[...]
            begin = begin + piece.shape[0]

    def store(x):
        product = dot(x[:, :tokens, :].reshape(quads * tokens, width), whole[...])
        total[...] = (near[...] + product).astype(jnp.bfloat16).reshape(total.shape)

    @pl.when(core == wing)
    def _():
        store(theirs)

    @pl.when(core != wing)
    def _():
        store(mine)

    for q in range(quads):
        outs[q][...] = total[quad ^ q]


def far_products(mine, theirs, near, weights, tokens):
    quads, _, width = mine.shape
    cols = near.shape[1]
    vmem = pl.BlockSpec(memory_space=pltpu.VMEM)
    return pl.pallas_call(
        functools.partial(far_kernel, tokens),
        in_specs=[vmem] * (3 + len(weights)),
        out_specs=[vmem] * quads,
        out_shape=[jax.ShapeDtypeStruct((tokens, cols), jnp.bfloat16)] * quads,
        scratch_shapes=[
            pltpu.VMEM((width, cols), jnp.bfloat16),
            pltpu.VMEM((quads, tokens, cols), jnp.bfloat16),
        ],
        compiler_params=pltpu.CompilerParams(vmem_limit_bytes=48 * MIB if quads > 4 else 16 * MIB),
        cost_estimate=FREE,
        name="far_products",
    )(mine, theirs, near, *weights)


def finish_kernel(places, *refs):
    count = len(places)
    out_ref, values_ref = refs[-2:]
    mixed, probs, parts = refs[:count], refs[count : 2 * count], refs[2 * count : -2]
    total = parts[0][...].astype(jnp.float32)
    for part in parts[1:]:
        total = total + part[...].astype(jnp.float32)
    total = total.astype(jnp.bfloat16)
    values_ref[...] = total
    for (span, head), mix, prob in zip(places, mixed, probs):
        rows = slice(span * SPAN, (span + 1) * SPAN)
        group_size = out_ref.shape[1] // total.shape[1]
        queries = group_size * SPAN
        for k in range(prob.shape[0] // queries):
            values = total[rows, (head + k) * HD : (head + k + 1) * HD]
            fresh = dot(prob[k * queries : (k + 1) * queries, :], values)
            for h in range(group_size):
                here = slice((k * group_size + h) * HD, (k * group_size + h + 1) * HD)
                col = ((head + k) * group_size + h) * HD
                out_ref[rows, col : col + HD] = (
                    mix[:, here] + fresh[h * SPAN : (h + 1) * SPAN, :]
                ).astype(jnp.bfloat16)


def finish(places, mixed, fresh_probs, parts, q_width):
    tokens, cols = parts[0].shape
    vmem = pl.BlockSpec(memory_space=pltpu.VMEM)
    return pl.pallas_call(
        functools.partial(finish_kernel, places),
        in_specs=[vmem] * (len(parts) + 2 * len(mixed)),
        out_specs=[vmem] * 2,
        out_shape=[
            jax.ShapeDtypeStruct((tokens, q_width), jnp.bfloat16),
            jax.ShapeDtypeStruct((tokens, cols), jnp.bfloat16),
        ],
        compiler_params=pltpu.CompilerParams(vmem_limit_bytes=16 * MIB),
        cost_estimate=FREE,
        name="finish_attention",
    )(*mixed, *fresh_probs, *parts)


def on_device(
    normed_inputs,
    value_matrix,
    adapter_down_weight,
    adapter_up_weight,
    adapter_position,
    span_adapter_index,
    queries,
    incoming_keys,
    stored_keys,
    stored_values,
    cache_length,
):
    quads = lax.axis_size("quad")
    parts_swap = [(i, i ^ 1) for i in range(lax.axis_size("parts"))]
    width, cols = value_matrix.shape
    downs = adapter_down_weight.reshape(-1, adapter_down_weight.shape[2])
    ups = adapter_up_weight.reshape(-1, cols)

    kv_heads = cols // HD
    kv_heads = cols // HD
    pieces = [(0, 0, 1), (0, 1, 1), (0, 2, kv_heads - 2), (1, 0, kv_heads // 2), (1, kv_heads // 2, kv_heads // 2)]

    def attention(piece, lengths):
        return cache_attention(
            *pieces[piece], False, queries, incoming_keys, stored_keys, stored_values, lengths
        )

    def after(value, *others):
        return lax.optimization_barrier((value, *others))[0]

    def to_quad(value, q):
        return lax.ppermute(value, "quad", [(j, j ^ q) for j in range(quads)])

    leaving, *rows = cross_pack(value_matrix, downs, ups)
    maps = lax.ppermute(leaving, "wing", SWAP)
    rows = [lax.ppermute(piece, "wing", SWAP) for piece in rows]

    attn = [attention(0, after(cache_length, leaving))]
    message = quad_pack(after(normed_inputs, attn[0][1]), downs, ups, width, quads)
    mine = lax.all_to_all(message, "quad", 0, 0)
    maps = after(maps, message)
    maps_other = lax.ppermute(maps, "parts", parts_swap)

    attn.append(attention(1, after(cache_length, maps)))
    maps_other, rows[0] = lax.optimization_barrier((maps_other, rows[0], attn[1][1]))[:-1]
    rows_other = [lax.ppermute(rows[0], "parts", parts_swap)]
    passed = maps_pack(maps, maps_other, width, quads)
    passed_on = [to_quad(passed[q], q) for q in range(1, quads)]

    attn.append(attention(2, after(cache_length, passed[0])))
    attn.append(attention(3, after(cache_length, attn[2][1])))
    rows[1], rows_other[0], mine, *passed_on = lax.optimization_barrier(
        (rows[1], rows_other[0], mine, *passed_on, attn[3][1])
    )[:-1]
    rows_other.append(lax.ppermute(rows[1], "parts", parts_swap))
    theirs = lax.ppermute(mine, "tensor", SWAP)
    maps_mine = jnp.stack([passed[0]] + passed_on)
    maps_theirs = lax.ppermute(maps_mine, "tensor", SWAP)

    attn.append(attention(4, after(cache_length, rows[1], mine, maps_mine)))
    theirs, maps_theirs, rows_other[1] = lax.optimization_barrier(
        (theirs, maps_theirs, rows_other[1], attn[4][1])
    )[:-1]

    tokens, q_width = queries.shape
    near = near_products(
        mine, theirs, maps_mine, maps_theirs, value_matrix, adapter_position, span_adapter_index, tokens
    )
    products = far_products(mine, theirs, near, (*rows, *rows_other), tokens)
    parts = [products[0]] + [to_quad(products[q], q) for q in range(1, quads)]
    mixed, fresh_probs = zip(*attn)
    attended, incoming_values = finish([piece[:2] for piece in pieces], mixed, fresh_probs, parts, q_width)
    return (attended, incoming_values)


def solution(mesh):
    sizes = mesh.devices.shape
    cut = Mesh(
        mesh.devices.reshape(sizes[0], 2, sizes[1] // 2, sizes[2]), ("parts", "wing", "quad", "tensor")
    )
    group = ("wing", "quad")
    home = ("parts", "wing", "quad")
    in_specs = (
        P(home, "tensor"),
        P(group, "tensor"),
        P(group, None, None),
        P(group, None, "tensor"),
        P(),
        P("parts"),
        P(home, "tensor"),
        P(home, "tensor"),
        P(home, None, "tensor"),
        P(home, None, "tensor"),
        P(home),
    )
    out_specs = (P(home, "tensor"), P(home, "tensor"))
    return jax.shard_map(
        on_device, mesh=cut, in_specs=in_specs, out_specs=out_specs, check_vma=False
    )
```

```python
import functools
import math

import jax
import jax.numpy as jnp
from jax import lax
from jax.experimental import pallas as pl
from jax.experimental.pallas import tpu as pltpu
from jax.sharding import Mesh
from jax.sharding import PartitionSpec as P

HD = 128
RANK = 16
SPAN = 64
CHUNK = 512
ONES = 16
ADAPTER_SCALE = 2.0
EXP2_SCALE = math.log2(math.e) / math.sqrt(HD)
DEAD = -1e30
MIB = 1024 * 1024
SWAP = [(0, 1), (1, 0)]
FREE = pl.CostEstimate(flops=1, bytes_accessed=1, transcendentals=0)


def dot_last(a, b):
    return lax.dot_general(a, b, (((1,), (1,)), ((), ())), preferred_element_type=jnp.float32)


def dot(a, b):
    return jnp.dot(a, b, preferred_element_type=jnp.float32)


def cache_kernel(span, first_head, kv_heads, group_size, lens, q_ref, fk_ref, k_hbm, v_hbm, out_ref, pf_ref, qs, ks, vs, m_s, acc, sems):
    length = lens[span]
    rows = group_size * SPAN
    chunks, chunk, width = ks.shape
    heads = slice(first_head * HD, first_head * HD + width)

    def copies(i):
        live = pl.ds(pl.multiple_of(i * chunk, chunk), chunk)
        return (
            pltpu.make_async_copy(k_hbm.at[span, live, heads], ks.at[i], sems.at[0, i]),
            pltpu.make_async_copy(v_hbm.at[span, live, heads], vs.at[i], sems.at[1, i]),
        )

    for i in range(chunks):

        @pl.when(i * chunk < length)
        def _():
            for copy in copies(i):
                copy.start()

    def fresh_scores(k):
        s = dot_last(fk_ref[span * SPAN : (span + 1) * SPAN, (first_head + k) * HD : (first_head + k + 1) * HD], qs[k])
        key = lax.broadcasted_iota(jnp.int32, (SPAN, rows), 0)
        token = lax.broadcasted_iota(jnp.int32, (SPAN, rows), 1) % SPAN
        return jnp.where(key <= token, s, DEAD)

    for k in range(kv_heads):
        for h in range(group_size):
            col = ((first_head + k) * group_size + h) * HD
            qs[k, h * SPAN : (h + 1) * SPAN, :] = q_ref[span * SPAN : (span + 1) * SPAN, col : col + HD]
        m_s[k] = jnp.max(fresh_scores(k), axis=0, keepdims=True)
        acc[k] = jnp.zeros((HD + ONES, rows), jnp.float32)

    ones = jnp.ones((ONES, chunk), jnp.bfloat16)

    def add_chunk(i, masked):
        for copy in copies(i):
            copy.wait()

        def scores(k):
            s = dot_last(ks[i, :, k * HD : (k + 1) * HD], qs[k])
            if masked:
                slot = i * chunk + lax.broadcasted_iota(jnp.int32, (chunk, rows), 0)
                s = jnp.where(slot < length, s, DEAD)
            return s

        s = scores(0)
        for k in range(kv_heads):
            later = scores(k + 1) if k + 1 < kv_heads else None
            before = m_s[k]
            top = jnp.maximum(before, jnp.max(s, axis=0, keepdims=True))
            m_s[k] = top
            p = jnp.exp2((s - top) * EXP2_SCALE).astype(jnp.bfloat16)
            alpha = jnp.exp2((before - top) * EXP2_SCALE)
            values = jnp.concatenate([vs[i, :, k * HD : (k + 1) * HD].T, ones], axis=0)
            acc[k] = acc[k] * alpha + dot(values, p)
            s = later

    @pl.loop(0, length // chunk)
    def _(i):
        add_chunk(i, False)

    @pl.when(length % chunk != 0)
    def _():
        add_chunk(length // chunk, True)

    for k in range(kv_heads):
        p = jnp.exp2((fresh_scores(k) - m_s[k]) * EXP2_SCALE)
        inverse = 1.0 / (acc[k, HD : HD + 1, :] + jnp.sum(p, axis=0, keepdims=True))
        pf_ref[k * rows : (k + 1) * rows, :] = (p * inverse).T.astype(jnp.bfloat16)
        mixed = (acc[k, :HD, :] * inverse).T
        for h in range(group_size):
            col = (k * group_size + h) * HD
            out_ref[:, col : col + HD] = mixed[h * SPAN : (h + 1) * SPAN, :]


def cache_attention(span, first_head, kv_heads, hides, queries, fresh_keys, keys, values, lengths):
    slots = keys.shape[1]
    group_size = queries.shape[1] // keys.shape[2]
    width = kv_heads * HD
    rows = group_size * SPAN
    chunk = min(CHUNK, slots)
    chunks = slots // chunk
    vmem = pl.BlockSpec(memory_space=pltpu.VMEM)
    hbm = pl.BlockSpec(memory_space=pltpu.HBM)
    return pl.pallas_call(
        functools.partial(cache_kernel, span, first_head, kv_heads, group_size),
        in_specs=[pl.BlockSpec(memory_space=pltpu.SMEM), vmem, vmem, hbm, hbm],
        out_specs=[vmem, vmem],
        scratch_shapes=[
            pltpu.VMEM((kv_heads, rows, HD), jnp.bfloat16),
            pltpu.VMEM((chunks, chunk, width), jnp.bfloat16),
            pltpu.VMEM((chunks, chunk, width), jnp.bfloat16),
            pltpu.VMEM((kv_heads, 1, rows), jnp.float32),
            pltpu.VMEM((kv_heads, HD + ONES, rows), jnp.float32),
            pltpu.SemaphoreType.DMA((2, chunks)),
        ],
        out_shape=[
            jax.ShapeDtypeStruct((SPAN, group_size * width), jnp.float32),
            jax.ShapeDtypeStruct((kv_heads * rows, SPAN), jnp.bfloat16),
        ],
        compiler_params=pltpu.CompilerParams(vmem_limit_bytes=57 * MIB),
        cost_estimate=pl.CostEstimate(
            flops=4 * rows * slots * width, bytes_accessed=4 * slots * width, transcendentals=0
        )
        if hides
        else FREE,
        name="cache_attention",
    )(lengths, queries, fresh_keys, keys, values)


def run_copies(copies, sems):
    copies = [pltpu.make_async_copy(src, dst, sems.at[i]) for i, (src, dst) in enumerate(copies)]
    for copy in copies:
        copy.start()
    for copy in copies:
        copy.wait()


def up_places(cols, width):
    step = min(cols, width)
    return [
        (slot, first, (slot * cols + first) // width * RANK, (slot * cols + first) % width)
        for slot in range(2)
        for first in range(0, cols, step)
    ]


def pack_kernel(x_hbm, d_hbm, u_hbm, w_hbm, out, maps, *refs):
    rows, sems = refs[:-1], refs[-1]
    part, core = lax.axis_index("parts") % 2, lax.axis_index("tensor")
    quads, _, width = out.shape
    tokens, features = x_hbm.shape
    ranks, cols = u_hbm.shape
    step = min(cols, width)
    begin = part * (w_hbm.shape[0] // 2)
    copies = []
    for piece in rows:
        size = piece.shape[0]
        copies.append((w_hbm.at[pl.ds(pl.multiple_of(begin, RANK), size), :], piece))
        begin = begin + size
    copies.append((d_hbm.at[:, pl.ds(pl.multiple_of(core * features, features), features)], maps.at[:, :features]))
    copies.append((u_hbm, maps.at[:, features:]))
    for j in range(quads):
        first = pl.multiple_of(core * features + j * width, width)
        copies.append((x_hbm.at[:, j * width : (j + 1) * width], out.at[j, :tokens, :]))
        copies.append((d_hbm.at[:, pl.ds(first, width)], out.at[j, tokens : tokens + ranks, :]))
        for slot, first, row, col in up_places(cols, width):
            row += tokens + ranks
            copies.append(
                (
                    u_hbm.at[slot * RANK : (slot + 1) * RANK, first : first + step],
                    out.at[j, row : row + RANK, col : col + step],
                )
            )
    run_copies(copies, sems)


def pack(tokens, downs, ups, weights, quads):
    vmem = pl.BlockSpec(memory_space=pltpu.VMEM)
    hbm = pl.BlockSpec(memory_space=pltpu.HBM)
    ranks, cols = ups.shape
    width = weights.shape[0]
    rows = tokens.shape[0] + ranks + RANK * (2 * cols // width)
    count = 4 + quads * (2 + len(up_places(cols, width)))
    first = width // 2 * 3 // 8
    pieces = [jax.ShapeDtypeStruct((size, cols), weights.dtype) for size in (first, width // 2 - first)]
    return pl.pallas_call(
        pack_kernel,
        in_specs=[hbm] * 4,
        out_specs=[vmem] * 4,
        out_shape=[
            jax.ShapeDtypeStruct((quads, rows, width), tokens.dtype),
            jax.ShapeDtypeStruct((ranks, tokens.shape[1] + cols), downs.dtype),
        ]
        + pieces,
        scratch_shapes=[pltpu.SemaphoreType.DMA((count,))],
        compiler_params=pltpu.CompilerParams(vmem_limit_bytes=57 * MIB),
        cost_estimate=FREE,
        name="pack",
    )(tokens, downs, ups, weights)


def maps_kernel(here, *outs):
    quad = lax.axis_index("quad")
    width = outs[0].shape[1]
    ranks = here.shape[0]
    features = len(outs) * width
    cols = here.shape[1] - features
    step = min(cols, width)
    for q, out in enumerate(outs):
        out[:ranks, :] = here[:, pl.ds(pl.multiple_of((quad ^ q) * width, width), width)]
        for slot, first, row, col in up_places(cols, width):
            up = here[slot * RANK : (slot + 1) * RANK, features + first : features + first + step]
            out[ranks + row : ranks + row + RANK, col : col + step] = up


def maps_pack(here, width, quads):
    vmem = pl.BlockSpec(memory_space=pltpu.VMEM)
    cols = here.shape[1] - quads * width
    maps = jax.ShapeDtypeStruct((RANK * (2 + 2 * cols // width), width), here.dtype)
    return pl.pallas_call(
        maps_kernel,
        in_specs=[vmem],
        out_specs=[vmem] * quads,
        out_shape=[maps] * quads,
        compiler_params=pltpu.CompilerParams(vmem_limit_bytes=4 * MIB),
        cost_estimate=FREE,
        name="maps_pack",
    )(here)


def near_kernel(tokens, position, adapter, mine, theirs, maps_mine, maps_theirs, own_ref, out, ds, us):
    core, wing, quad = lax.axis_index("tensor"), lax.axis_index("wing"), lax.axis_index("quad")
    quads, _, width = mine.shape
    cols = own_ref.shape[1]
    ranks = 2 * RANK
    step = min(cols, width)
    for j in range(quads):
        for side, here, there, base, index in (
            (0, mine.at[j], theirs.at[j], tokens, j),
            (1, maps_mine.at[j], maps_theirs.at[j], 0, quad ^ j),
        ):
            first_row = (side * quads + index) * ranks
            rows = pl.ds(pl.multiple_of(first_row, ranks), ranks)
            ds[0, rows, :] = here[base : base + ranks, :]
            ds[1, rows, :] = there[base : base + ranks, :]
            for slot, first, row, col in up_places(cols, width):
                row += base + ranks
                place = pl.ds(pl.multiple_of(first_row + slot * RANK, RANK), RANK)
                us[place, first : first + step] = here[row : row + RANK, col : col + step]

    x_mine = mine[:, :tokens, :].reshape(quads * tokens, width)
    x_theirs = theirs[:, :tokens, :].reshape(quads * tokens, width)
    shrink = dot_last(x_mine, ds[0]) + dot_last(x_theirs, ds[1])
    slots = us.shape[0] // RANK
    which = lax.broadcasted_iota(jnp.int32, (SPAN, slots * RANK), 1) // RANK + wing * (slots // 2)
    which = jnp.where(which >= slots, which - slots, which)
    spans = quads * tokens // SPAN
    masked = []
    for i in range(spans):
        slot = position[adapter[wing * spans + i]]
        masked.append(jnp.where(which == slot, shrink[i * SPAN : (i + 1) * SPAN, :], 0.0))
    shrink = (jnp.concatenate(masked, axis=0) * ADAPTER_SCALE).astype(jnp.bfloat16)
    out[...] = dot(shrink, us[...])

    @pl.when(core == wing)
    def _():
        out[...] += dot(x_mine, own_ref[...])

    @pl.when(core != wing)
    def _():
        out[...] += dot(x_theirs, own_ref[...])


def near_products(mine, theirs, maps_mine, maps_theirs, own, position, adapter, tokens):
    quads, _, width = mine.shape
    cols = own.shape[1]
    ranks = 4 * quads * RANK
    vmem = pl.BlockSpec(memory_space=pltpu.VMEM)
    smem = pl.BlockSpec(memory_space=pltpu.SMEM)
    return pl.pallas_call(
        functools.partial(near_kernel, tokens),
        in_specs=[smem, smem] + [vmem] * 5,
        out_specs=vmem,
        out_shape=jax.ShapeDtypeStruct((quads * tokens, cols), jnp.float32),
        scratch_shapes=[
            pltpu.VMEM((2, ranks, width), jnp.bfloat16),
            pltpu.VMEM((ranks, cols), jnp.bfloat16),
        ],
        compiler_params=pltpu.CompilerParams(vmem_limit_bytes=48 * MIB if quads > 4 else 24 * MIB),
        cost_estimate=FREE,
        name="near_products",
    )(position, adapter, mine, theirs, maps_mine, maps_theirs, own)


def far_kernel(tokens, mine, theirs, near, *refs):
    quads, _, width = mine.shape
    outs, (whole, total) = refs[-2 - quads : -2], refs[-2:]
    weights = refs[: -2 - quads]
    part, core, wing = lax.axis_index("parts") % 2, lax.axis_index("tensor"), lax.axis_index("wing")
    quad = lax.axis_index("quad")
    for side in range(2):
        begin = (part if side == 0 else 1 - part) * (width // 2)
        for piece in weights[2 * side : 2 * side + 2]:
            whole[pl.ds(pl.multiple_of(begin, RANK), piece.shape[0]), :] = piece[...]
            begin = begin + piece.shape[0]

    def store(x):
        product = dot(x[:, :tokens, :].reshape(quads * tokens, width), whole[...])
        total[...] = (near[...] + product).astype(jnp.bfloat16).reshape(total.shape)

    @pl.when(core == wing)
    def _():
        store(theirs)

    @pl.when(core != wing)
    def _():
        store(mine)

    for q in range(quads):
        outs[q][...] = total[quad ^ q]


def far_products(mine, theirs, near, weights, tokens):
    quads, _, width = mine.shape
    cols = near.shape[1]
    vmem = pl.BlockSpec(memory_space=pltpu.VMEM)
    return pl.pallas_call(
        functools.partial(far_kernel, tokens),
        in_specs=[vmem] * (3 + len(weights)),
        out_specs=[vmem] * quads,
        out_shape=[jax.ShapeDtypeStruct((tokens, cols), jnp.bfloat16)] * quads,
        scratch_shapes=[
            pltpu.VMEM((width, cols), jnp.bfloat16),
            pltpu.VMEM((quads, tokens, cols), jnp.bfloat16),
        ],
        compiler_params=pltpu.CompilerParams(vmem_limit_bytes=48 * MIB if quads > 4 else 16 * MIB),
        cost_estimate=FREE,
        name="far_products",
    )(mine, theirs, near, *weights)


def finish_kernel(places, *refs):
    count = len(places)
    out_ref, values_ref = refs[-2:]
    mixed, probs, parts = refs[:count], refs[count : 2 * count], refs[2 * count : -2]
    total = parts[0][...].astype(jnp.float32)
    for part in parts[1:]:
        total = total + part[...].astype(jnp.float32)
    total = total.astype(jnp.bfloat16)
    values_ref[...] = total
    for (span, head), mix, prob in zip(places, mixed, probs):
        rows = slice(span * SPAN, (span + 1) * SPAN)
        group_size = out_ref.shape[1] // total.shape[1]
        queries = group_size * SPAN
        for k in range(prob.shape[0] // queries):
            values = total[rows, (head + k) * HD : (head + k + 1) * HD]
            fresh = dot(prob[k * queries : (k + 1) * queries, :], values)
            for h in range(group_size):
                here = slice((k * group_size + h) * HD, (k * group_size + h + 1) * HD)
                col = ((head + k) * group_size + h) * HD
                out_ref[rows, col : col + HD] = (
                    mix[:, here] + fresh[h * SPAN : (h + 1) * SPAN, :]
                ).astype(jnp.bfloat16)


def finish(places, mixed, fresh_probs, parts, q_width):
    tokens, cols = parts[0].shape
    vmem = pl.BlockSpec(memory_space=pltpu.VMEM)
    return pl.pallas_call(
        functools.partial(finish_kernel, places),
        in_specs=[vmem] * (len(parts) + 2 * len(mixed)),
        out_specs=[vmem] * 2,
        out_shape=[
            jax.ShapeDtypeStruct((tokens, q_width), jnp.bfloat16),
            jax.ShapeDtypeStruct((tokens, cols), jnp.bfloat16),
        ],
        compiler_params=pltpu.CompilerParams(vmem_limit_bytes=16 * MIB),
        cost_estimate=FREE,
        name="finish_attention",
    )(*mixed, *fresh_probs, *parts)


def on_device(
    normed_inputs,
    value_matrix,
    adapter_down_weight,
    adapter_up_weight,
    adapter_position,
    span_adapter_index,
    queries,
    incoming_keys,
    stored_keys,
    stored_values,
    cache_length,
):
    quads = lax.axis_size("quad")
    parts_swap = [(i, i ^ 1) for i in range(lax.axis_size("parts"))]
    width, cols = value_matrix.shape
    downs = adapter_down_weight.reshape(-1, adapter_down_weight.shape[2])
    ups = adapter_up_weight.reshape(-1, cols)

    kv_heads = cols // HD
    kv_heads = cols // HD
    pieces = [(0, 0, kv_heads), (1, 0, kv_heads // 2), (1, kv_heads // 2, kv_heads - kv_heads // 2)]

    def attention(piece, lengths):
        return cache_attention(
            *pieces[piece], False, queries, incoming_keys, stored_keys, stored_values, lengths
        )

    def after(value, *others):
        return lax.optimization_barrier((value, *others))[0]

    def to_quad(value, q):
        return lax.ppermute(value, "quad", [(j, j ^ q) for j in range(quads)])

    message, maps, *rows = pack(normed_inputs, downs, ups, value_matrix, quads)
    mine = lax.all_to_all(message, "quad", 0, 0)
    maps = lax.ppermute(maps, "wing", SWAP)
    rows = [lax.ppermute(piece, "wing", SWAP) for piece in rows]

    attn = [attention(0, after(cache_length, message))]
    passed = maps_pack(after(maps, attn[0][1]), width, quads)
    passed_on = [to_quad(passed[q], q) for q in range(1, quads)]

    attn.append(attention(1, after(cache_length, passed[0])))
    rows[0], *passed_on = lax.optimization_barrier((rows[0], *passed_on, attn[1][1]))[:-1]
    rows_other = [lax.ppermute(rows[0], "parts", parts_swap)]
    maps_mine = jnp.stack([passed[0]] + passed_on)

    attn.append(attention(2, after(cache_length, rows[0], maps_mine)))
    rows[1], rows_other[0], mine, maps_mine = lax.optimization_barrier(
        (rows[1], rows_other[0], mine, maps_mine, attn[2][1])
    )[:-1]
    rows_other.append(lax.ppermute(rows[1], "parts", parts_swap))
    theirs = lax.ppermute(mine, "tensor", SWAP)
    maps_theirs = lax.ppermute(maps_mine, "tensor", SWAP)

    tokens, q_width = queries.shape
    near = near_products(
        mine, theirs, maps_mine, maps_theirs, value_matrix, adapter_position, span_adapter_index, tokens
    )
    products = far_products(mine, theirs, near, (*rows, *rows_other), tokens)
    parts = [products[0]] + [to_quad(products[q], q) for q in range(1, quads)]
    mixed, fresh_probs = zip(*attn)
    attended, incoming_values = finish([piece[:2] for piece in pieces], mixed, fresh_probs, parts, q_width)
    return (attended, incoming_values)


def solution(mesh):
    sizes = mesh.devices.shape
    cut = Mesh(
        mesh.devices.reshape(sizes[0], 2, sizes[1] // 2, sizes[2]), ("parts", "wing", "quad", "tensor")
    )
    group = ("wing", "quad")
    home = ("parts", "wing", "quad")
    in_specs = (
        P(home, "tensor"),
        P(group, "tensor"),
        P(group, None, None),
        P(group, None, "tensor"),
        P(),
        P("parts"),
        P(home, "tensor"),
        P(home, "tensor"),
        P(home, None, "tensor"),
        P(home, None, "tensor"),
        P(home),
    )
    out_specs = (P(home, "tensor"), P(home, "tensor"))
    return jax.shard_map(
        on_device, mesh=cut, in_specs=in_specs, out_specs=out_specs, check_vma=False
    )
```

```python
import functools
import math

import jax
import jax.numpy as jnp
from jax import lax
from jax.experimental import pallas as pl
from jax.experimental.pallas import tpu as pltpu
from jax.sharding import Mesh
from jax.sharding import PartitionSpec as P

HD = 128
RANK = 16
SPAN = 64
CHUNK = 512
ONES = 16
ADAPTER_SCALE = 2.0
EXP2_SCALE = math.log2(math.e) / math.sqrt(HD)
DEAD = -1e30
MIB = 1024 * 1024
SWAP = [(0, 1), (1, 0)]
FREE = pl.CostEstimate(flops=1, bytes_accessed=1, transcendentals=0)


def dot_last(a, b):
    return lax.dot_general(a, b, (((1,), (1,)), ((), ())), preferred_element_type=jnp.float32)


def dot(a, b):
    return jnp.dot(a, b, preferred_element_type=jnp.float32)


def cache_kernel(span, first_head, kv_heads, group_size, lens, q_ref, fk_ref, k_hbm, v_hbm, out_ref, pf_ref, qs, ks, vs, m_s, acc, sems):
    length = lens[span]
    rows = group_size * SPAN
    chunks, chunk, width = ks.shape
    heads = slice(first_head * HD, first_head * HD + width)

    def copies(i):
        live = pl.ds(pl.multiple_of(i * chunk, chunk), chunk)
        return (
            pltpu.make_async_copy(k_hbm.at[span, live, heads], ks.at[i], sems.at[0, i]),
            pltpu.make_async_copy(v_hbm.at[span, live, heads], vs.at[i], sems.at[1, i]),
        )

    for i in range(chunks):

        @pl.when(i * chunk < length)
        def _():
            for copy in copies(i):
                copy.start()

    def fresh_scores(k):
        s = dot_last(fk_ref[span * SPAN : (span + 1) * SPAN, (first_head + k) * HD : (first_head + k + 1) * HD], qs[k])
        key = lax.broadcasted_iota(jnp.int32, (SPAN, rows), 0)
        token = lax.broadcasted_iota(jnp.int32, (SPAN, rows), 1) % SPAN
        return jnp.where(key <= token, s, DEAD)

    for k in range(kv_heads):
        for h in range(group_size):
            col = ((first_head + k) * group_size + h) * HD
            qs[k, h * SPAN : (h + 1) * SPAN, :] = q_ref[span * SPAN : (span + 1) * SPAN, col : col + HD]
        m_s[k] = jnp.max(fresh_scores(k), axis=0, keepdims=True)
        acc[k] = jnp.zeros((HD + ONES, rows), jnp.float32)

    ones = jnp.ones((ONES, chunk), jnp.bfloat16)

    def add_chunk(i, masked):
        for copy in copies(i):
            copy.wait()

        def scores(k):
            s = dot_last(ks[i, :, k * HD : (k + 1) * HD], qs[k])
            if masked:
                slot = i * chunk + lax.broadcasted_iota(jnp.int32, (chunk, rows), 0)
                s = jnp.where(slot < length, s, DEAD)
            return s

        s = scores(0)
        for k in range(kv_heads):
            later = scores(k + 1) if k + 1 < kv_heads else None
            before = m_s[k]
            top = jnp.maximum(before, jnp.max(s, axis=0, keepdims=True))
            m_s[k] = top
            p = jnp.exp2((s - top) * EXP2_SCALE).astype(jnp.bfloat16)
            alpha = jnp.exp2((before - top) * EXP2_SCALE)
            values = jnp.concatenate([vs[i, :, k * HD : (k + 1) * HD].T, ones], axis=0)
            acc[k] = acc[k] * alpha + dot(values, p)
            s = later

    @pl.loop(0, length // chunk)
    def _(i):
        add_chunk(i, False)

    @pl.when(length % chunk != 0)
    def _():
        add_chunk(length // chunk, True)

    for k in range(kv_heads):
        p = jnp.exp2((fresh_scores(k) - m_s[k]) * EXP2_SCALE)
        inverse = 1.0 / (acc[k, HD : HD + 1, :] + jnp.sum(p, axis=0, keepdims=True))
        pf_ref[k * rows : (k + 1) * rows, :] = (p * inverse).T.astype(jnp.bfloat16)
        mixed = (acc[k, :HD, :] * inverse).T
        for h in range(group_size):
            col = (k * group_size + h) * HD
            out_ref[:, col : col + HD] = mixed[h * SPAN : (h + 1) * SPAN, :]


def cache_attention(span, first_head, kv_heads, hides, queries, fresh_keys, keys, values, lengths):
    slots = keys.shape[1]
    group_size = queries.shape[1] // keys.shape[2]
    width = kv_heads * HD
    rows = group_size * SPAN
    chunk = min(CHUNK, slots)
    chunks = slots // chunk
    vmem = pl.BlockSpec(memory_space=pltpu.VMEM)
    hbm = pl.BlockSpec(memory_space=pltpu.HBM)
    return pl.pallas_call(
        functools.partial(cache_kernel, span, first_head, kv_heads, group_size),
        in_specs=[pl.BlockSpec(memory_space=pltpu.SMEM), vmem, vmem, hbm, hbm],
        out_specs=[vmem, vmem],
        scratch_shapes=[
            pltpu.VMEM((kv_heads, rows, HD), jnp.bfloat16),
            pltpu.VMEM((chunks, chunk, width), jnp.bfloat16),
            pltpu.VMEM((chunks, chunk, width), jnp.bfloat16),
            pltpu.VMEM((kv_heads, 1, rows), jnp.float32),
            pltpu.VMEM((kv_heads, HD + ONES, rows), jnp.float32),
            pltpu.SemaphoreType.DMA((2, chunks)),
        ],
        out_shape=[
            jax.ShapeDtypeStruct((SPAN, group_size * width), jnp.float32),
            jax.ShapeDtypeStruct((kv_heads * rows, SPAN), jnp.bfloat16),
        ],
        compiler_params=pltpu.CompilerParams(vmem_limit_bytes=57 * MIB),
        cost_estimate=pl.CostEstimate(
            flops=4 * rows * slots * width, bytes_accessed=4 * slots * width, transcendentals=0
        )
        if hides
        else FREE,
        name="cache_attention",
    )(lengths, queries, fresh_keys, keys, values)


def pack_kernel(x_hbm, d_hbm, u_hbm, w_hbm, tokens_out, *refs):
    quads = tokens_out.shape[0]
    maps_out, rows, sems = refs[:quads], refs[quads:-1], refs[-1]
    part, core, quad = lax.axis_index("parts") % 2, lax.axis_index("tensor"), lax.axis_index("quad")
    tokens, features = x_hbm.shape
    width, cols = w_hbm.shape
    ranks = d_hbm.shape[0]
    step = maps_out[0].shape[1]
    mine = pl.ds(pl.multiple_of(part * RANK, RANK), RANK)
    copies = []
    for q, out in enumerate(maps_out):
        begin = core * features + (quad ^ q) * width
        for i, first in enumerate(range(0, width, step)):
            here = pl.ds(pl.multiple_of(begin + first, step), step)
            copies.append((d_hbm.at[mine, here], out.at[i * RANK : (i + 1) * RANK, :]))
        for i, first in enumerate(range(0, cols, step)):
            row = width // step * RANK + i * RANK
            copies.append((u_hbm.at[mine, first : first + step], out.at[row : row + RANK, :]))
    begin = part * (width // 2)
    for piece in rows:
        size = piece.shape[0]
        copies.append((w_hbm.at[pl.ds(pl.multiple_of(begin, RANK), size), :], piece))
        begin = begin + size
    for j in range(quads):
        out = tokens_out.at[j]
        copies.append((x_hbm.at[:, j * width : (j + 1) * width], out.at[:tokens, :]))
        here = pl.ds(pl.multiple_of(core * features + j * width, width), width)
        copies.append((d_hbm.at[:, here], out.at[tokens : tokens + ranks, :]))
        for slot, first, row, col in up_places(cols, width):
            row += tokens + ranks
            up = u_hbm.at[slot * RANK : (slot + 1) * RANK, first : first + step]
            copies.append((up, out.at[row : row + RANK, col : col + step]))
    copies = [pltpu.make_async_copy(src, dst, sems.at[i]) for i, (src, dst) in enumerate(copies)]
    for copy in copies:
        copy.start()
    for copy in copies:
        copy.wait()


def up_places(cols, width):
    step = min(cols, width)
    return [
        (slot, first, (slot * cols + first) // width * RANK, (slot * cols + first) % width)
        for slot in range(2)
        for first in range(0, cols, step)
    ]


def pack(tokens, downs, ups, weights, quads):
    vmem = pl.BlockSpec(memory_space=pltpu.VMEM)
    hbm = pl.BlockSpec(memory_space=pltpu.HBM)
    ranks, cols = ups.shape
    width = weights.shape[0]
    step = min(cols, width)
    kind = tokens.dtype
    pieces = (width + cols) // step
    first = width // 4
    sizes = [(quads, tokens.shape[0] + ranks + RANK * (2 * cols // width), width)]
    sizes += [(RANK * pieces, step)] * quads + [(first, cols), (width // 2 - first, cols)]
    count = quads * (pieces + 2 + len(up_places(cols, width))) + 2
    return pl.pallas_call(
        pack_kernel,
        in_specs=[hbm] * 4,
        out_specs=[vmem] * len(sizes),
        out_shape=[jax.ShapeDtypeStruct(size, kind) for size in sizes],
        scratch_shapes=[pltpu.SemaphoreType.DMA((count,))],
        compiler_params=pltpu.CompilerParams(vmem_limit_bytes=57 * MIB),
        cost_estimate=FREE,
        name="pack",
    )(tokens, downs, ups, weights)


def near_kernel(tokens, quads, position, adapter, own_ref, *refs):
    maps_mine, maps_theirs, refs = refs[:2], refs[2:4], refs[4:]
    mine, theirs, out, ds, us = refs
    part, core = lax.axis_index("parts") % 2, lax.axis_index("tensor")
    wing, quad = lax.axis_index("wing"), lax.axis_index("quad")
    width = mine.shape[2]
    cols = own_ref.shape[1]
    ranks = 2 * RANK
    step = min(cols, width)
    for q in range(quads):
        rows = slice(q * ranks, (q + 1) * ranks)
        ds[0, rows, :] = mine[q, tokens : tokens + ranks, :]
        ds[1, rows, :] = theirs[q, tokens : tokens + ranks, :]
        for slot, first, row, col in up_places(cols, width):
            row += tokens + ranks
            place = q * ranks + slot * RANK
            us[place : place + RANK, first : first + step] = mine[q, row : row + RANK, col : col + step]
        for side in range(2):
            place = (quads + q) * ranks + side * RANK
            for i, first in enumerate(range(0, width, step)):
                row = i * RANK
                ds[0, place : place + RANK, first : first + step] = maps_mine[side][q, row : row + RANK, :]
                ds[1, place : place + RANK, first : first + step] = maps_theirs[side][q, row : row + RANK, :]
            for i, first in enumerate(range(0, cols, step)):
                row = (width // step + i) * RANK
                us[place : place + RANK, first : first + step] = maps_mine[side][q, row : row + RANK, :]

    x_mine = mine[:, :tokens, :].reshape(quads * tokens, width)
    x_theirs = theirs[:, :tokens, :].reshape(quads * tokens, width)
    shrink = dot_last(x_mine, ds[0]) + dot_last(x_theirs, ds[1])
    place = lax.broadcasted_iota(jnp.int32, (SPAN, us.shape[0]), 1)
    far = (place >= quads * ranks).astype(jnp.int32)
    index = place - far * (quads * ranks)
    group = (wing ^ far) * quads + ((far * quad) ^ (index >> 5))
    which = 2 * group + (((index >> 4) & 1) ^ (far * part))
    spans = tokens // SPAN
    masked = []
    for q in range(quads):
        for i in range(spans):
            slot = position[adapter[(wing * quads + q) * spans + i]]
            row = (q * spans + i) * SPAN
            masked.append(jnp.where(which == slot, shrink[row : row + SPAN, :], 0.0))
    shrink = (jnp.concatenate(masked, axis=0) * ADAPTER_SCALE).astype(jnp.bfloat16)
    out[...] = dot(shrink, us[...])

    @pl.when(core == wing)
    def _():
        out[...] += dot(x_mine, own_ref[...])

    @pl.when(core != wing)
    def _():
        out[...] += dot(x_theirs, own_ref[...])


def near_products(mine, theirs, maps_mine, maps_theirs, own, position, adapter, tokens):
    quads, _, width = mine.shape
    cols = own.shape[1]
    ranks = 4 * quads * RANK
    vmem = pl.BlockSpec(memory_space=pltpu.VMEM)
    smem = pl.BlockSpec(memory_space=pltpu.SMEM)
    return pl.pallas_call(
        functools.partial(near_kernel, tokens, quads),
        in_specs=[smem, smem] + [vmem] * 7,
        out_specs=vmem,
        out_shape=jax.ShapeDtypeStruct((quads * tokens, cols), jnp.float32),
        scratch_shapes=[
            pltpu.VMEM((2, ranks, width), jnp.bfloat16),
            pltpu.VMEM((ranks, cols), jnp.bfloat16),
        ],
        compiler_params=pltpu.CompilerParams(vmem_limit_bytes=48 * MIB if quads > 4 else 24 * MIB),
        cost_estimate=FREE,
        name="near_products",
    )(position, adapter, own, *maps_mine, *maps_theirs, mine, theirs)


def far_kernel(tokens, quads, near, *refs):
    weights, (mine, theirs) = refs[:4], refs[4:6]
    outs, (whole, total) = refs[6:-2], refs[-2:]
    quad = lax.axis_index("quad")
    part, core, wing = lax.axis_index("parts") % 2, lax.axis_index("tensor"), lax.axis_index("wing")
    for side in range(2):
        begin = (part if side == 0 else 1 - part) * (whole.shape[0] // 2)
        for piece in weights[2 * side : 2 * side + 2]:
            whole[pl.ds(pl.multiple_of(begin, RANK), piece.shape[0]), :] = piece[...]
            begin = begin + piece.shape[0]

    def store(blocks):
        x = blocks[:, :tokens, :].reshape(near.shape[0], -1)
        product = (near[...] + dot(x, whole[...])).astype(jnp.bfloat16)
        total[...] = product.reshape(total.shape)

    @pl.when(core == wing)
    def _():
        store(theirs)

    @pl.when(core != wing)
    def _():
        store(mine)

    for q, out in enumerate(outs):
        out[...] = total[quad ^ q]


def far_products(mine, theirs, near, weights, tokens):
    quads, _, width = mine.shape
    cols = near.shape[1]
    vmem = pl.BlockSpec(memory_space=pltpu.VMEM)
    return pl.pallas_call(
        functools.partial(far_kernel, tokens, quads),
        in_specs=[vmem] * (3 + len(weights)),
        out_specs=[vmem] * quads,
        out_shape=[jax.ShapeDtypeStruct((tokens, cols), jnp.bfloat16)] * quads,
        scratch_shapes=[
            pltpu.VMEM((width, cols), jnp.bfloat16),
            pltpu.VMEM((quads, tokens, cols), jnp.bfloat16),
        ],
        compiler_params=pltpu.CompilerParams(vmem_limit_bytes=48 * MIB if quads > 4 else 16 * MIB),
        cost_estimate=FREE,
        name="far_products",
    )(near, *weights, mine, theirs)


def finish_kernel(places, *refs):
    count = len(places)
    out_ref, values_ref = refs[-2:]
    mixed, probs, parts = refs[:count], refs[count : 2 * count], refs[2 * count : -2]
    total = parts[0][...].astype(jnp.float32)
    for part in parts[1:]:
        total = total + part[...].astype(jnp.float32)
    total = total.astype(jnp.bfloat16)
    values_ref[...] = total
    for (span, head), mix, prob in zip(places, mixed, probs):
        rows = slice(span * SPAN, (span + 1) * SPAN)
        group_size = out_ref.shape[1] // total.shape[1]
        queries = group_size * SPAN
        for k in range(prob.shape[0] // queries):
            values = total[rows, (head + k) * HD : (head + k + 1) * HD]
            fresh = dot(prob[k * queries : (k + 1) * queries, :], values)
            for h in range(group_size):
                here = slice((k * group_size + h) * HD, (k * group_size + h + 1) * HD)
                col = ((head + k) * group_size + h) * HD
                out_ref[rows, col : col + HD] = (
                    mix[:, here] + fresh[h * SPAN : (h + 1) * SPAN, :]
                ).astype(jnp.bfloat16)


def finish(places, mixed, fresh_probs, parts, q_width):
    tokens, cols = parts[0].shape
    vmem = pl.BlockSpec(memory_space=pltpu.VMEM)
    return pl.pallas_call(
        functools.partial(finish_kernel, places),
        in_specs=[vmem] * (len(parts) + 2 * len(mixed)),
        out_specs=[vmem] * 2,
        out_shape=[
            jax.ShapeDtypeStruct((tokens, q_width), jnp.bfloat16),
            jax.ShapeDtypeStruct((tokens, cols), jnp.bfloat16),
        ],
        compiler_params=pltpu.CompilerParams(vmem_limit_bytes=16 * MIB),
        cost_estimate=FREE,
        name="finish_attention",
    )(*mixed, *fresh_probs, *parts)


def on_device(
    normed_inputs,
    value_matrix,
    adapter_down_weight,
    adapter_up_weight,
    adapter_position,
    span_adapter_index,
    queries,
    incoming_keys,
    stored_keys,
    stored_values,
    cache_length,
):
    quads = lax.axis_size("quad")
    parts_swap = [(i, i ^ 1) for i in range(lax.axis_size("parts"))]
    width, cols = value_matrix.shape
    downs = adapter_down_weight.reshape(-1, adapter_down_weight.shape[2])
    ups = adapter_up_weight.reshape(-1, cols)

    kv_heads = cols // HD
    kv_heads = cols // HD
    pieces = [(0, 0, kv_heads), (1, 0, kv_heads)]

    def attention(piece, lengths):
        return cache_attention(
            *pieces[piece], False, queries, incoming_keys, stored_keys, stored_values, lengths
        )

    def after(value, *others):
        return lax.optimization_barrier((value, *others))[0]

    def to_quad(value, q):
        return lax.ppermute(value, "quad", [(j, j ^ q) for j in range(quads)])

    def to_other_wing(value, q):
        pairs = [(w * quads + j, (1 - w) * quads + (j ^ q)) for w in range(2) for j in range(quads)]
        return lax.ppermute(value, ("wing", "quad"), pairs)

    message, *maps, early, late = pack(normed_inputs, downs, ups, value_matrix, quads)
    mine = lax.all_to_all(message, "quad", 0, 0)
    maps = [to_other_wing(each, q) for q, each in enumerate(maps)]
    early = lax.ppermute(early, "wing", SWAP)

    attn = [attention(0, after(cache_length, message))]
    attn.append(attention(1, after(cache_length, attn[0][1])))
    early, *maps = lax.optimization_barrier((early, *maps, attn[1][1]))[:-1]
    maps = jnp.stack(maps)
    mine = after(mine, early)

    late = lax.ppermute(after(late, early), "wing", SWAP)
    early_other = lax.ppermute(early, "parts", parts_swap)
    late_other = lax.ppermute(late, "parts", parts_swap)
    maps_other = lax.ppermute(maps, "parts", parts_swap)
    maps_mine = (maps, maps_other)
    maps_theirs = [lax.ppermute(each, "tensor", SWAP) for each in maps_mine]
    theirs = lax.ppermute(mine, "tensor", SWAP)

    tokens, q_width = queries.shape
    near = near_products(
        mine, theirs, maps_mine, maps_theirs, value_matrix, adapter_position, span_adapter_index, tokens
    )
    products = far_products(mine, theirs, near, (early, late, early_other, late_other), tokens)
    parts = [products[0]] + [to_quad(products[q], q) for q in range(1, quads)]
    mixed, fresh_probs = zip(*attn)
    attended, incoming_values = finish([piece[:2] for piece in pieces], mixed, fresh_probs, parts, q_width)
    return (attended, incoming_values)


def solution(mesh):
    sizes = mesh.devices.shape
    cut = Mesh(
        mesh.devices.reshape(sizes[0], 2, sizes[1] // 2, sizes[2]), ("parts", "wing", "quad", "tensor")
    )
    group = ("wing", "quad")
    home = ("parts", "wing", "quad")
    in_specs = (
        P(home, "tensor"),
        P(group, "tensor"),
        P(group, None, None),
        P(group, None, "tensor"),
        P(),
        P("parts"),
        P(home, "tensor"),
        P(home, "tensor"),
        P(home, None, "tensor"),
        P(home, None, "tensor"),
        P(home),
    )
    out_specs = (P(home, "tensor"), P(home, "tensor"))
    return jax.shard_map(
        on_device, mesh=cut, in_specs=in_specs, out_specs=out_specs, check_vma=False
    )
```

```python
import functools
import math

import jax
import jax.numpy as jnp
from jax import lax
from jax.experimental import pallas as pl
from jax.experimental.pallas import tpu as pltpu
from jax.sharding import Mesh
from jax.sharding import PartitionSpec as P

HD = 128
RANK = 16
SPAN = 64
CHUNK = 512
ONES = 16
ADAPTER_SCALE = 2.0
EXP2_SCALE = math.log2(math.e) / math.sqrt(HD)
DEAD = -1e30
MIB = 1024 * 1024
SWAP = [(0, 1), (1, 0)]
FREE = pl.CostEstimate(flops=1, bytes_accessed=1, transcendentals=0)


def dot_last(a, b):
    return lax.dot_general(a, b, (((1,), (1,)), ((), ())), preferred_element_type=jnp.float32)


def dot(a, b):
    return jnp.dot(a, b, preferred_element_type=jnp.float32)


def cache_kernel(span, first_head, kv_heads, group_size, lens, q_ref, fk_ref, k_hbm, v_hbm, out_ref, pf_ref, qs, ks, vs, m_s, acc, sems):
    length = lens[span]
    rows = group_size * SPAN
    chunks, chunk, width = ks.shape
    heads = slice(first_head * HD, first_head * HD + width)

    def copies(i):
        live = pl.ds(pl.multiple_of(i * chunk, chunk), chunk)
        return (
            pltpu.make_async_copy(k_hbm.at[span, live, heads], ks.at[i], sems.at[0, i]),
            pltpu.make_async_copy(v_hbm.at[span, live, heads], vs.at[i], sems.at[1, i]),
        )

    for i in range(chunks):

        @pl.when(i * chunk < length)
        def _():
            for copy in copies(i):
                copy.start()

    def fresh_scores(k):
        s = dot_last(fk_ref[span * SPAN : (span + 1) * SPAN, (first_head + k) * HD : (first_head + k + 1) * HD], qs[k])
        key = lax.broadcasted_iota(jnp.int32, (SPAN, rows), 0)
        token = lax.broadcasted_iota(jnp.int32, (SPAN, rows), 1) % SPAN
        return jnp.where(key <= token, s, DEAD)

    for k in range(kv_heads):
        for h in range(group_size):
            col = ((first_head + k) * group_size + h) * HD
            qs[k, h * SPAN : (h + 1) * SPAN, :] = q_ref[span * SPAN : (span + 1) * SPAN, col : col + HD]
        m_s[k] = jnp.max(fresh_scores(k), axis=0, keepdims=True)
        acc[k] = jnp.zeros((HD + ONES, rows), jnp.float32)

    ones = jnp.ones((ONES, chunk), jnp.bfloat16)

    def add_chunk(i, masked):
        for copy in copies(i):
            copy.wait()

        def scores(k):
            s = dot_last(ks[i, :, k * HD : (k + 1) * HD], qs[k])
            if masked:
                slot = i * chunk + lax.broadcasted_iota(jnp.int32, (chunk, rows), 0)
                s = jnp.where(slot < length, s, DEAD)
            return s

        s = scores(0)
        for k in range(kv_heads):
            later = scores(k + 1) if k + 1 < kv_heads else None
            before = m_s[k]
            top = jnp.maximum(before, jnp.max(s, axis=0, keepdims=True))
            m_s[k] = top
            p = jnp.exp2((s - top) * EXP2_SCALE).astype(jnp.bfloat16)
            alpha = jnp.exp2((before - top) * EXP2_SCALE)
            values = jnp.concatenate([vs[i, :, k * HD : (k + 1) * HD].T, ones], axis=0)
            acc[k] = acc[k] * alpha + dot(values, p)
            s = later

    @pl.loop(0, length // chunk)
    def _(i):
        add_chunk(i, False)

    @pl.when(length % chunk != 0)
    def _():
        add_chunk(length // chunk, True)

    for k in range(kv_heads):
        p = jnp.exp2((fresh_scores(k) - m_s[k]) * EXP2_SCALE)
        inverse = 1.0 / (acc[k, HD : HD + 1, :] + jnp.sum(p, axis=0, keepdims=True))
        pf_ref[k * rows : (k + 1) * rows, :] = (p * inverse).T.astype(jnp.bfloat16)
        mixed = (acc[k, :HD, :] * inverse).T
        for h in range(group_size):
            col = (k * group_size + h) * HD
            out_ref[:, col : col + HD] = mixed[h * SPAN : (h + 1) * SPAN, :]


def cache_attention(span, first_head, kv_heads, hides, queries, fresh_keys, keys, values, lengths):
    slots = keys.shape[1]
    group_size = queries.shape[1] // keys.shape[2]
    width = kv_heads * HD
    rows = group_size * SPAN
    chunk = min(CHUNK, slots)
    chunks = slots // chunk
    vmem = pl.BlockSpec(memory_space=pltpu.VMEM)
    hbm = pl.BlockSpec(memory_space=pltpu.HBM)
    return pl.pallas_call(
        functools.partial(cache_kernel, span, first_head, kv_heads, group_size),
        in_specs=[pl.BlockSpec(memory_space=pltpu.SMEM), vmem, vmem, hbm, hbm],
        out_specs=[vmem, vmem],
        scratch_shapes=[
            pltpu.VMEM((kv_heads, rows, HD), jnp.bfloat16),
            pltpu.VMEM((chunks, chunk, width), jnp.bfloat16),
            pltpu.VMEM((chunks, chunk, width), jnp.bfloat16),
            pltpu.VMEM((kv_heads, 1, rows), jnp.float32),
            pltpu.VMEM((kv_heads, HD + ONES, rows), jnp.float32),
            pltpu.SemaphoreType.DMA((2, chunks)),
        ],
        out_shape=[
            jax.ShapeDtypeStruct((SPAN, group_size * width), jnp.float32),
            jax.ShapeDtypeStruct((kv_heads * rows, SPAN), jnp.bfloat16),
        ],
        compiler_params=pltpu.CompilerParams(vmem_limit_bytes=57 * MIB),
        cost_estimate=pl.CostEstimate(
            flops=4 * rows * slots * width, bytes_accessed=4 * slots * width, transcendentals=0
        )
        if hides
        else FREE,
        name="cache_attention",
    )(lengths, queries, fresh_keys, keys, values)


def pack_kernel(x_hbm, d_hbm, u_hbm, w_hbm, tokens_out, *refs):
    quads = tokens_out.shape[0]
    maps_out, rows, sems = refs[:quads], refs[quads:-1], refs[-1]
    part, core, quad = lax.axis_index("parts") % 2, lax.axis_index("tensor"), lax.axis_index("quad")
    tokens, features = x_hbm.shape
    width, cols = w_hbm.shape
    ranks = d_hbm.shape[0]
    step = maps_out[0].shape[1]
    mine = pl.ds(pl.multiple_of(part * RANK, RANK), RANK)
    copies = []
    for q, out in enumerate(maps_out):
        begin = core * features + (quad ^ q) * width
        for i, first in enumerate(range(0, width, step)):
            here = pl.ds(pl.multiple_of(begin + first, step), step)
            copies.append((d_hbm.at[mine, here], out.at[i * RANK : (i + 1) * RANK, :]))
        for i, first in enumerate(range(0, cols, step)):
            row = width // step * RANK + i * RANK
            copies.append((u_hbm.at[mine, first : first + step], out.at[row : row + RANK, :]))
    begin = part * (width // 2)
    for piece in rows:
        size = piece.shape[0]
        copies.append((w_hbm.at[pl.ds(pl.multiple_of(begin, RANK), size), :], piece))
        begin = begin + size
    for j in range(quads):
        out = tokens_out.at[j]
        copies.append((x_hbm.at[:, j * width : (j + 1) * width], out.at[:tokens, :]))
        here = pl.ds(pl.multiple_of(core * features + j * width, width), width)
        copies.append((d_hbm.at[:, here], out.at[tokens : tokens + ranks, :]))
        for slot, first, row, col in up_places(cols, width):
            row += tokens + ranks
            up = u_hbm.at[slot * RANK : (slot + 1) * RANK, first : first + step]
            copies.append((up, out.at[row : row + RANK, col : col + step]))
    copies = [pltpu.make_async_copy(src, dst, sems.at[i]) for i, (src, dst) in enumerate(copies)]
    for copy in copies:
        copy.start()
    for copy in copies:
        copy.wait()


def up_places(cols, width):
    step = min(cols, width)
    return [
        (slot, first, (slot * cols + first) // width * RANK, (slot * cols + first) % width)
        for slot in range(2)
        for first in range(0, cols, step)
    ]


def pack(tokens, downs, ups, weights, quads):
    vmem = pl.BlockSpec(memory_space=pltpu.VMEM)
    hbm = pl.BlockSpec(memory_space=pltpu.HBM)
    ranks, cols = ups.shape
    width = weights.shape[0]
    step = min(cols, width)
    kind = tokens.dtype
    pieces = (width + cols) // step
    first = width // 4
    sizes = [(quads, tokens.shape[0] + ranks + RANK * (2 * cols // width), width)]
    sizes += [(RANK * pieces, step)] * quads + [(first, cols), (width // 2 - first, cols)]
    count = quads * (pieces + 2 + len(up_places(cols, width))) + 2
    return pl.pallas_call(
        pack_kernel,
        in_specs=[hbm] * 4,
        out_specs=[vmem] * len(sizes),
        out_shape=[jax.ShapeDtypeStruct(size, kind) for size in sizes],
        scratch_shapes=[pltpu.SemaphoreType.DMA((count,))],
        compiler_params=pltpu.CompilerParams(vmem_limit_bytes=57 * MIB),
        cost_estimate=FREE,
        name="pack",
    )(tokens, downs, ups, weights)


def near_kernel(tokens, quads, position, adapter, own_ref, *refs):
    maps_mine, maps_theirs, refs = refs[:2], refs[2:4], refs[4:]
    mine, theirs, out, ds, us = refs
    part, core = lax.axis_index("parts") % 2, lax.axis_index("tensor")
    wing, quad = lax.axis_index("wing"), lax.axis_index("quad")
    width = mine.shape[2]
    cols = own_ref.shape[1]
    ranks = 2 * RANK
    step = min(cols, width)
    for q in range(quads):
        rows = slice(q * ranks, (q + 1) * ranks)
        ds[0, rows, :] = mine[q, tokens : tokens + ranks, :]
        ds[1, rows, :] = theirs[q, tokens : tokens + ranks, :]
        for slot, first, row, col in up_places(cols, width):
            row += tokens + ranks
            place = q * ranks + slot * RANK
            us[place : place + RANK, first : first + step] = mine[q, row : row + RANK, col : col + step]
        for side in range(2):
            place = (quads + q) * ranks + side * RANK
            for i, first in enumerate(range(0, width, step)):
                row = i * RANK
                ds[0, place : place + RANK, first : first + step] = maps_mine[side][q, row : row + RANK, :]
                ds[1, place : place + RANK, first : first + step] = maps_theirs[side][q, row : row + RANK, :]
            for i, first in enumerate(range(0, cols, step)):
                row = (width // step + i) * RANK
                us[place : place + RANK, first : first + step] = maps_mine[side][q, row : row + RANK, :]

    x_mine = mine[:, :tokens, :].reshape(quads * tokens, width)
    x_theirs = theirs[:, :tokens, :].reshape(quads * tokens, width)
    shrink = dot_last(x_mine, ds[0]) + dot_last(x_theirs, ds[1])
    place = lax.broadcasted_iota(jnp.int32, (SPAN, us.shape[0]), 1)
    far = (place >= quads * ranks).astype(jnp.int32)
    index = place - far * (quads * ranks)
    group = (wing ^ far) * quads + ((far * quad) ^ (index >> 5))
    which = 2 * group + (((index >> 4) & 1) ^ (far * part))
    spans = tokens // SPAN
    masked = []
    for q in range(quads):
        for i in range(spans):
            slot = position[adapter[(wing * quads + q) * spans + i]]
            row = (q * spans + i) * SPAN
            masked.append(jnp.where(which == slot, shrink[row : row + SPAN, :], 0.0))
    shrink = (jnp.concatenate(masked, axis=0) * ADAPTER_SCALE).astype(jnp.bfloat16)
    out[...] = dot(shrink, us[...])

    @pl.when(core == wing)
    def _():
        out[...] += dot(x_mine, own_ref[...])

    @pl.when(core != wing)
    def _():
        out[...] += dot(x_theirs, own_ref[...])


def near_products(mine, theirs, maps_mine, maps_theirs, own, position, adapter, tokens):
    quads, _, width = mine.shape
    cols = own.shape[1]
    ranks = 4 * quads * RANK
    vmem = pl.BlockSpec(memory_space=pltpu.VMEM)
    smem = pl.BlockSpec(memory_space=pltpu.SMEM)
    return pl.pallas_call(
        functools.partial(near_kernel, tokens, quads),
        in_specs=[smem, smem] + [vmem] * 7,
        out_specs=vmem,
        out_shape=jax.ShapeDtypeStruct((quads * tokens, cols), jnp.float32),
        scratch_shapes=[
            pltpu.VMEM((2, ranks, width), jnp.bfloat16),
            pltpu.VMEM((ranks, cols), jnp.bfloat16),
        ],
        compiler_params=pltpu.CompilerParams(vmem_limit_bytes=48 * MIB if quads > 4 else 24 * MIB),
        cost_estimate=FREE,
        name="near_products",
    )(position, adapter, own, *maps_mine, *maps_theirs, mine, theirs)


def far_kernel(tokens, quads, near, *refs):
    weights, (mine, theirs) = refs[:4], refs[4:6]
    outs, (whole, total) = refs[6:-2], refs[-2:]
    quad = lax.axis_index("quad")
    part, core, wing = lax.axis_index("parts") % 2, lax.axis_index("tensor"), lax.axis_index("wing")
    for side in range(2):
        begin = (part if side == 0 else 1 - part) * (whole.shape[0] // 2)
        for piece in weights[2 * side : 2 * side + 2]:
            whole[pl.ds(pl.multiple_of(begin, RANK), piece.shape[0]), :] = piece[...]
            begin = begin + piece.shape[0]

    def store(blocks):
        x = blocks[:, :tokens, :].reshape(near.shape[0], -1)
        product = (near[...] + dot(x, whole[...])).astype(jnp.bfloat16)
        total[...] = product.reshape(total.shape)

    @pl.when(core == wing)
    def _():
        store(theirs)

    @pl.when(core != wing)
    def _():
        store(mine)

    for q, out in enumerate(outs):
        out[...] = total[quad ^ q]


def far_products(mine, theirs, near, weights, tokens):
    quads, _, width = mine.shape
    cols = near.shape[1]
    vmem = pl.BlockSpec(memory_space=pltpu.VMEM)
    return pl.pallas_call(
        functools.partial(far_kernel, tokens, quads),
        in_specs=[vmem] * (3 + len(weights)),
        out_specs=[vmem] * quads,
        out_shape=[jax.ShapeDtypeStruct((tokens, cols), jnp.bfloat16)] * quads,
        scratch_shapes=[
            pltpu.VMEM((width, cols), jnp.bfloat16),
            pltpu.VMEM((quads, tokens, cols), jnp.bfloat16),
        ],
        compiler_params=pltpu.CompilerParams(vmem_limit_bytes=48 * MIB if quads > 4 else 16 * MIB),
        cost_estimate=FREE,
        name="far_products",
    )(near, *weights, mine, theirs)


def finish_kernel(places, *refs):
    count = len(places)
    out_ref, values_ref = refs[-2:]
    mixed, probs, parts = refs[:count], refs[count : 2 * count], refs[2 * count : -2]
    total = parts[0][...].astype(jnp.float32)
    for part in parts[1:]:
        total = total + part[...].astype(jnp.float32)
    total = total.astype(jnp.bfloat16)
    values_ref[...] = total
    for (span, head), mix, prob in zip(places, mixed, probs):
        rows = slice(span * SPAN, (span + 1) * SPAN)
        group_size = out_ref.shape[1] // total.shape[1]
        queries = group_size * SPAN
        for k in range(prob.shape[0] // queries):
            values = total[rows, (head + k) * HD : (head + k + 1) * HD]
            fresh = dot(prob[k * queries : (k + 1) * queries, :], values)
            for h in range(group_size):
                here = slice((k * group_size + h) * HD, (k * group_size + h + 1) * HD)
                col = ((head + k) * group_size + h) * HD
                out_ref[rows, col : col + HD] = (
                    mix[:, here] + fresh[h * SPAN : (h + 1) * SPAN, :]
                ).astype(jnp.bfloat16)


def finish(places, mixed, fresh_probs, parts, q_width):
    tokens, cols = parts[0].shape
    vmem = pl.BlockSpec(memory_space=pltpu.VMEM)
    return pl.pallas_call(
        functools.partial(finish_kernel, places),
        in_specs=[vmem] * (len(parts) + 2 * len(mixed)),
        out_specs=[vmem] * 2,
        out_shape=[
            jax.ShapeDtypeStruct((tokens, q_width), jnp.bfloat16),
            jax.ShapeDtypeStruct((tokens, cols), jnp.bfloat16),
        ],
        compiler_params=pltpu.CompilerParams(vmem_limit_bytes=16 * MIB),
        cost_estimate=FREE,
        name="finish_attention",
    )(*mixed, *fresh_probs, *parts)


def on_device(
    normed_inputs,
    value_matrix,
    adapter_down_weight,
    adapter_up_weight,
    adapter_position,
    span_adapter_index,
    queries,
    incoming_keys,
    stored_keys,
    stored_values,
    cache_length,
):
    quads = lax.axis_size("quad")
    parts_swap = [(i, i ^ 1) for i in range(lax.axis_size("parts"))]
    width, cols = value_matrix.shape
    downs = adapter_down_weight.reshape(-1, adapter_down_weight.shape[2])
    ups = adapter_up_weight.reshape(-1, cols)

    kv_heads = cols // HD
    kv_heads = cols // HD
    pieces = [(0, 0, kv_heads), (1, 0, kv_heads)]

    def attention(piece, lengths):
        return cache_attention(
            *pieces[piece], False, queries, incoming_keys, stored_keys, stored_values, lengths
        )

    def after(value, *others):
        return lax.optimization_barrier((value, *others))[0]

    def to_quad(value, q):
        return lax.ppermute(value, "quad", [(j, j ^ q) for j in range(quads)])

    def to_other_wing(value, q):
        pairs = [(w * quads + j, (1 - w) * quads + (j ^ q)) for w in range(2) for j in range(quads)]
        return lax.ppermute(value, ("wing", "quad"), pairs)

    message, *maps, early, late = pack(normed_inputs, downs, ups, value_matrix, quads)
    mine = lax.all_to_all(message, "quad", 0, 0)
    maps = [to_other_wing(each, q) for q, each in enumerate(maps)]
    early = lax.ppermute(early, "wing", SWAP)

    attn = [attention(0, after(cache_length, message))]
    early, *maps = lax.optimization_barrier((early, *maps, attn[0][1]))[:-1]
    maps = jnp.stack(maps)
    late = lax.ppermute(after(late, early), "wing", SWAP)
    early_other = lax.ppermute(early, "parts", parts_swap)
    maps_other = lax.ppermute(maps, "parts", parts_swap)

    attn.append(attention(1, after(cache_length, early, maps)))
    late, mine, early_other, maps_other = lax.optimization_barrier(
        (late, mine, early_other, maps_other, attn[1][1])
    )[:-1]
    late_other = lax.ppermute(late, "parts", parts_swap)
    maps_mine = (maps, maps_other)
    maps_theirs = [lax.ppermute(each, "tensor", SWAP) for each in maps_mine]
    theirs = lax.ppermute(mine, "tensor", SWAP)

    tokens, q_width = queries.shape
    near = near_products(
        mine, theirs, maps_mine, maps_theirs, value_matrix, adapter_position, span_adapter_index, tokens
    )
    products = far_products(mine, theirs, near, (early, late, early_other, late_other), tokens)
    parts = [products[0]] + [to_quad(products[q], q) for q in range(1, quads)]
    mixed, fresh_probs = zip(*attn)
    attended, incoming_values = finish([piece[:2] for piece in pieces], mixed, fresh_probs, parts, q_width)
    return (attended, incoming_values)


def solution(mesh):
    sizes = mesh.devices.shape
    cut = Mesh(
        mesh.devices.reshape(sizes[0], 2, sizes[1] // 2, sizes[2]), ("parts", "wing", "quad", "tensor")
    )
    group = ("wing", "quad")
    home = ("parts", "wing", "quad")
    in_specs = (
        P(home, "tensor"),
        P(group, "tensor"),
        P(group, None, None),
        P(group, None, "tensor"),
        P(),
        P("parts"),
        P(home, "tensor"),
        P(home, "tensor"),
        P(home, None, "tensor"),
        P(home, None, "tensor"),
        P(home),
    )
    out_specs = (P(home, "tensor"), P(home, "tensor"))
    return jax.shard_map(
        on_device, mesh=cut, in_specs=in_specs, out_specs=out_specs, check_vma=False
    )
```

```python
import functools
import math

import jax
import jax.numpy as jnp
from jax import lax
from jax.experimental import pallas as pl
from jax.experimental.pallas import tpu as pltpu
from jax.sharding import Mesh
from jax.sharding import PartitionSpec as P

HD = 128
RANK = 16
SPAN = 64
CHUNK = 512
ONES = 16
ADAPTER_SCALE = 2.0
EXP2_SCALE = math.log2(math.e) / math.sqrt(HD)
DEAD = -1e30
MIB = 1024 * 1024
SWAP = [(0, 1), (1, 0)]
FREE = pl.CostEstimate(flops=1, bytes_accessed=1, transcendentals=0)


def dot_last(a, b):
    return lax.dot_general(a, b, (((1,), (1,)), ((), ())), preferred_element_type=jnp.float32)


def dot(a, b):
    return jnp.dot(a, b, preferred_element_type=jnp.float32)


def cache_kernel(span, first_head, kv_heads, group_size, lens, q_ref, fk_ref, k_hbm, v_hbm, out_ref, pf_ref, qs, ks, vs, m_s, acc, sems):
    length = lens[span]
    rows = group_size * SPAN
    chunks, chunk, width = ks.shape
    heads = slice(first_head * HD, first_head * HD + width)

    def copies(i):
        live = pl.ds(pl.multiple_of(i * chunk, chunk), chunk)
        return (
            pltpu.make_async_copy(k_hbm.at[span, live, heads], ks.at[i], sems.at[0, i]),
            pltpu.make_async_copy(v_hbm.at[span, live, heads], vs.at[i], sems.at[1, i]),
        )

    for i in range(chunks):

        @pl.when(i * chunk < length)
        def _():
            for copy in copies(i):
                copy.start()

    def fresh_scores(k):
        s = dot_last(fk_ref[span * SPAN : (span + 1) * SPAN, (first_head + k) * HD : (first_head + k + 1) * HD], qs[k])
        key = lax.broadcasted_iota(jnp.int32, (SPAN, rows), 0)
        token = lax.broadcasted_iota(jnp.int32, (SPAN, rows), 1) % SPAN
        return jnp.where(key <= token, s, DEAD)

    for k in range(kv_heads):
        for h in range(group_size):
            col = ((first_head + k) * group_size + h) * HD
            qs[k, h * SPAN : (h + 1) * SPAN, :] = q_ref[span * SPAN : (span + 1) * SPAN, col : col + HD]
        m_s[k] = jnp.max(fresh_scores(k), axis=0, keepdims=True)
        acc[k] = jnp.zeros((HD + ONES, rows), jnp.float32)

    ones = jnp.ones((ONES, chunk), jnp.bfloat16)

    def add_chunk(i, masked):
        for copy in copies(i):
            copy.wait()

        def scores(k):
            s = dot_last(ks[i, :, k * HD : (k + 1) * HD], qs[k])
            if masked:
                slot = i * chunk + lax.broadcasted_iota(jnp.int32, (chunk, rows), 0)
                s = jnp.where(slot < length, s, DEAD)
            return s

        s = scores(0)
        for k in range(kv_heads):
            later = scores(k + 1) if k + 1 < kv_heads else None
            before = m_s[k]
            top = jnp.maximum(before, jnp.max(s, axis=0, keepdims=True))
            m_s[k] = top
            p = jnp.exp2((s - top) * EXP2_SCALE).astype(jnp.bfloat16)
            alpha = jnp.exp2((before - top) * EXP2_SCALE)
            values = jnp.concatenate([vs[i, :, k * HD : (k + 1) * HD].T, ones], axis=0)
            acc[k] = acc[k] * alpha + dot(values, p)
            s = later

    @pl.loop(0, length // chunk)
    def _(i):
        add_chunk(i, False)

    @pl.when(length % chunk != 0)
    def _():
        add_chunk(length // chunk, True)

    for k in range(kv_heads):
        p = jnp.exp2((fresh_scores(k) - m_s[k]) * EXP2_SCALE)
        inverse = 1.0 / (acc[k, HD : HD + 1, :] + jnp.sum(p, axis=0, keepdims=True))
        pf_ref[k * rows : (k + 1) * rows, :] = (p * inverse).T.astype(jnp.bfloat16)
        mixed = (acc[k, :HD, :] * inverse).T
        for h in range(group_size):
            col = (k * group_size + h) * HD
            out_ref[:, col : col + HD] = mixed[h * SPAN : (h + 1) * SPAN, :]


def cache_attention(span, first_head, kv_heads, hides, queries, fresh_keys, keys, values, lengths):
    slots = keys.shape[1]
    group_size = queries.shape[1] // keys.shape[2]
    width = kv_heads * HD
    rows = group_size * SPAN
    chunk = min(CHUNK, slots)
    chunks = slots // chunk
    vmem = pl.BlockSpec(memory_space=pltpu.VMEM)
    hbm = pl.BlockSpec(memory_space=pltpu.HBM)
    return pl.pallas_call(
        functools.partial(cache_kernel, span, first_head, kv_heads, group_size),
        in_specs=[pl.BlockSpec(memory_space=pltpu.SMEM), vmem, vmem, hbm, hbm],
        out_specs=[vmem, vmem],
        scratch_shapes=[
            pltpu.VMEM((kv_heads, rows, HD), jnp.bfloat16),
            pltpu.VMEM((chunks, chunk, width), jnp.bfloat16),
            pltpu.VMEM((chunks, chunk, width), jnp.bfloat16),
            pltpu.VMEM((kv_heads, 1, rows), jnp.float32),
            pltpu.VMEM((kv_heads, HD + ONES, rows), jnp.float32),
            pltpu.SemaphoreType.DMA((2, chunks)),
        ],
        out_shape=[
            jax.ShapeDtypeStruct((SPAN, group_size * width), jnp.float32),
            jax.ShapeDtypeStruct((kv_heads * rows, SPAN), jnp.bfloat16),
        ],
        compiler_params=pltpu.CompilerParams(vmem_limit_bytes=57 * MIB),
        cost_estimate=pl.CostEstimate(
            flops=4 * rows * slots * width, bytes_accessed=4 * slots * width, transcendentals=0
        )
        if hides
        else FREE,
        name="cache_attention",
    )(lengths, queries, fresh_keys, keys, values)


def pack_kernel(x_hbm, d_hbm, u_hbm, w_hbm, *refs):
    quads = (len(refs) - 2) // 2
    tokens_out, (early, late, sems) = refs[:quads], refs[-3:]
    size = w_hbm.shape[0] // 2 - late.shape[0]
    maps_out = [early.at[size:, :], *refs[quads:-3]]
    part, core, quad = lax.axis_index("parts") % 2, lax.axis_index("tensor"), lax.axis_index("quad")
    tokens, features = x_hbm.shape
    width, cols = w_hbm.shape
    ranks = d_hbm.shape[0]
    step = min(cols, width)
    mine = pl.ds(pl.multiple_of(part * RANK, RANK), RANK)
    copies = []
    for q, out in enumerate(maps_out):
        begin = core * features + (quad ^ q) * width
        for i, first in enumerate(range(0, width, step)):
            here = pl.ds(pl.multiple_of(begin + first, step), step)
            copies.append((d_hbm.at[mine, here], out.at[i * RANK : (i + 1) * RANK, :step]))
        for i, first in enumerate(range(0, cols, step)):
            row = width // step * RANK + i * RANK
            copies.append((u_hbm.at[mine, first : first + step], out.at[row : row + RANK, :step]))
    begin = part * (width // 2)
    copies.append((w_hbm.at[pl.ds(pl.multiple_of(begin, RANK), size), :], early.at[:size, :]))
    begin = begin + size
    copies.append((w_hbm.at[pl.ds(pl.multiple_of(begin, RANK), late.shape[0]), :], late))
    for q, out in enumerate(tokens_out):
        here = pl.ds(pl.multiple_of((quad ^ q) * width, width), width)
        copies.append((x_hbm.at[:, here], out.at[:tokens, :]))
        here = pl.ds(pl.multiple_of(core * features + (quad ^ q) * width, width), width)
        copies.append((d_hbm.at[:, here], out.at[tokens : tokens + ranks, :]))
        for slot, first, row, col in up_places(cols, width):
            row += tokens + ranks
            up = u_hbm.at[slot * RANK : (slot + 1) * RANK, first : first + step]
            copies.append((up, out.at[row : row + RANK, col : col + step]))
    copies = [pltpu.make_async_copy(src, dst, sems.at[i]) for i, (src, dst) in enumerate(copies)]
    for copy in copies:
        copy.start()
    for copy in copies:
        copy.wait()


def up_places(cols, width):
    step = min(cols, width)
    return [
        (slot, first, (slot * cols + first) // width * RANK, (slot * cols + first) % width)
        for slot in range(2)
        for first in range(0, cols, step)
    ]


def pack(tokens, downs, ups, weights, quads):
    vmem = pl.BlockSpec(memory_space=pltpu.VMEM)
    hbm = pl.BlockSpec(memory_space=pltpu.HBM)
    ranks, cols = ups.shape
    width = weights.shape[0]
    step = min(cols, width)
    kind = tokens.dtype
    pieces = (width + cols) // step
    first = width // 4
    sizes = [(tokens.shape[0] + ranks + RANK * (2 * cols // width), width)] * quads
    sizes += [(RANK * pieces, step)] * (quads - 1)
    sizes += [(first + RANK * pieces, cols), (width // 2 - first, cols)]
    count = quads * (pieces + 2 + len(up_places(cols, width))) + 2
    return pl.pallas_call(
        pack_kernel,
        in_specs=[hbm] * 4,
        out_specs=[vmem] * len(sizes),
        out_shape=[jax.ShapeDtypeStruct(size, kind) for size in sizes],
        scratch_shapes=[pltpu.SemaphoreType.DMA((count,))],
        compiler_params=pltpu.CompilerParams(vmem_limit_bytes=57 * MIB),
        cost_estimate=FREE,
        name="pack",
    )(tokens, downs, ups, weights)


def near_kernel(tokens, quads, position, adapter, own_ref, *refs):
    maps_mine, maps_theirs, refs = refs[:2], refs[2:4], refs[4:]
    mine, theirs, out, ds, us = refs
    part, core = lax.axis_index("parts") % 2, lax.axis_index("tensor")
    wing, quad = lax.axis_index("wing"), lax.axis_index("quad")
    width = mine.shape[2]
    cols = own_ref.shape[1]
    ranks = 2 * RANK
    step = min(cols, width)
    for q in range(quads):
        rows = slice(q * ranks, (q + 1) * ranks)
        ds[0, rows, :] = mine[q, tokens : tokens + ranks, :]
        ds[1, rows, :] = theirs[q, tokens : tokens + ranks, :]
        for slot, first, row, col in up_places(cols, width):
            row += tokens + ranks
            place = q * ranks + slot * RANK
            us[place : place + RANK, first : first + step] = mine[q, row : row + RANK, col : col + step]
        for side in range(2):
            place = (quads + q) * ranks + side * RANK
            for i, first in enumerate(range(0, width, step)):
                row = i * RANK
                ds[0, place : place + RANK, first : first + step] = maps_mine[side][q, row : row + RANK, :]
                ds[1, place : place + RANK, first : first + step] = maps_theirs[side][q, row : row + RANK, :]
            for i, first in enumerate(range(0, cols, step)):
                row = (width // step + i) * RANK
                us[place : place + RANK, first : first + step] = maps_mine[side][q, row : row + RANK, :]

    x_mine = mine[:, :tokens, :].reshape(quads * tokens, width)
    x_theirs = theirs[:, :tokens, :].reshape(quads * tokens, width)
    shrink = dot_last(x_mine, ds[0]) + dot_last(x_theirs, ds[1])
    place = lax.broadcasted_iota(jnp.int32, (SPAN, us.shape[0]), 1)
    far = (place >= quads * ranks).astype(jnp.int32)
    index = place - far * (quads * ranks)
    group = (wing ^ far) * quads + (quad ^ (index >> 5))
    which = 2 * group + (((index >> 4) & 1) ^ (far * part))
    spans = tokens // SPAN
    masked = []
    for q in range(quads):
        for i in range(spans):
            slot = position[adapter[(wing * quads + (quad ^ q)) * spans + i]]
            row = (q * spans + i) * SPAN
            masked.append(jnp.where(which == slot, shrink[row : row + SPAN, :], 0.0))
    shrink = (jnp.concatenate(masked, axis=0) * ADAPTER_SCALE).astype(jnp.bfloat16)
    out[...] = dot(shrink, us[...])

    @pl.when(core == wing)
    def _():
        out[...] += dot(x_mine, own_ref[...])

    @pl.when(core != wing)
    def _():
        out[...] += dot(x_theirs, own_ref[...])


def near_products(mine, theirs, maps_mine, maps_theirs, own, position, adapter, tokens):
    quads, _, width = mine.shape
    cols = own.shape[1]
    ranks = 4 * quads * RANK
    vmem = pl.BlockSpec(memory_space=pltpu.VMEM)
    smem = pl.BlockSpec(memory_space=pltpu.SMEM)
    return pl.pallas_call(
        functools.partial(near_kernel, tokens, quads),
        in_specs=[smem, smem] + [vmem] * 7,
        out_specs=vmem,
        out_shape=jax.ShapeDtypeStruct((quads * tokens, cols), jnp.float32),
        scratch_shapes=[
            pltpu.VMEM((2, ranks, width), jnp.bfloat16),
            pltpu.VMEM((ranks, cols), jnp.bfloat16),
        ],
        compiler_params=pltpu.CompilerParams(vmem_limit_bytes=48 * MIB if quads > 4 else 24 * MIB),
        cost_estimate=FREE,
        name="near_products",
    )(position, adapter, own, *maps_mine, *maps_theirs, mine, theirs)


def far_kernel(tokens, quads, near, *refs):
    weights, (mine, theirs) = refs[:4], refs[4:6]
    outs, whole = refs[6:-1], refs[-1]
    part, core, wing = lax.axis_index("parts") % 2, lax.axis_index("tensor"), lax.axis_index("wing")
    for side in range(2):
        begin = (part if side == 0 else 1 - part) * (whole.shape[0] // 2)
        early, late = weights[2 * side : 2 * side + 2]
        size = whole.shape[0] // 2 - late.shape[0]
        whole[pl.ds(pl.multiple_of(begin, RANK), size), :] = early[:size, :]
        whole[pl.ds(pl.multiple_of(begin + size, RANK), late.shape[0]), :] = late[...]

    def store(blocks):
        x = blocks[:, :tokens, :].reshape(near.shape[0], -1)
        product = (near[...] + dot(x, whole[...])).astype(jnp.bfloat16)
        for q, out in enumerate(outs):
            out[...] = product[q * tokens : (q + 1) * tokens, :]

    @pl.when(core == wing)
    def _():
        store(theirs)

    @pl.when(core != wing)
    def _():
        store(mine)


def far_products(mine, theirs, near, weights, tokens):
    quads, _, width = mine.shape
    cols = near.shape[1]
    vmem = pl.BlockSpec(memory_space=pltpu.VMEM)
    return pl.pallas_call(
        functools.partial(far_kernel, tokens, quads),
        in_specs=[vmem] * (3 + len(weights)),
        out_specs=[vmem] * quads,
        out_shape=[jax.ShapeDtypeStruct((tokens, cols), jnp.bfloat16)] * quads,
        scratch_shapes=[pltpu.VMEM((width, cols), jnp.bfloat16)],
        compiler_params=pltpu.CompilerParams(vmem_limit_bytes=48 * MIB if quads > 4 else 16 * MIB),
        cost_estimate=FREE,
        name="far_products",
    )(near, *weights, mine, theirs)


def finish_kernel(places, *refs):
    count = len(places)
    out_ref, values_ref = refs[-2:]
    mixed, probs, parts = refs[:count], refs[count : 2 * count], refs[2 * count : -2]
    total = parts[0][...].astype(jnp.float32)
    for part in parts[1:]:
        total = total + part[...].astype(jnp.float32)
    total = total.astype(jnp.bfloat16)
    values_ref[...] = total
    for (span, head), mix, prob in zip(places, mixed, probs):
        rows = slice(span * SPAN, (span + 1) * SPAN)
        group_size = out_ref.shape[1] // total.shape[1]
        queries = group_size * SPAN
        for k in range(prob.shape[0] // queries):
            values = total[rows, (head + k) * HD : (head + k + 1) * HD]
            fresh = dot(prob[k * queries : (k + 1) * queries, :], values)
            for h in range(group_size):
                here = slice((k * group_size + h) * HD, (k * group_size + h + 1) * HD)
                col = ((head + k) * group_size + h) * HD
                out_ref[rows, col : col + HD] = (
                    mix[:, here] + fresh[h * SPAN : (h + 1) * SPAN, :]
                ).astype(jnp.bfloat16)


def finish(places, mixed, fresh_probs, parts, q_width):
    tokens, cols = parts[0].shape
    vmem = pl.BlockSpec(memory_space=pltpu.VMEM)
    return pl.pallas_call(
        functools.partial(finish_kernel, places),
        in_specs=[vmem] * (len(parts) + 2 * len(mixed)),
        out_specs=[vmem] * 2,
        out_shape=[
            jax.ShapeDtypeStruct((tokens, q_width), jnp.bfloat16),
            jax.ShapeDtypeStruct((tokens, cols), jnp.bfloat16),
        ],
        compiler_params=pltpu.CompilerParams(vmem_limit_bytes=16 * MIB),
        cost_estimate=FREE,
        name="finish_attention",
    )(*mixed, *fresh_probs, *parts)


def on_device(
    normed_inputs,
    value_matrix,
    adapter_down_weight,
    adapter_up_weight,
    adapter_position,
    span_adapter_index,
    queries,
    incoming_keys,
    stored_keys,
    stored_values,
    cache_length,
):
    quads = lax.axis_size("quad")
    parts_swap = [(i, i ^ 1) for i in range(lax.axis_size("parts"))]
    width, cols = value_matrix.shape
    downs = adapter_down_weight.reshape(-1, adapter_down_weight.shape[2])
    ups = adapter_up_weight.reshape(-1, cols)

    kv_heads = cols // HD
    kv_heads = cols // HD
    pieces = [(0, 0, kv_heads), (1, 0, kv_heads)]

    def attention(piece, lengths):
        return cache_attention(
            *pieces[piece], False, queries, incoming_keys, stored_keys, stored_values, lengths
        )

    def after(value, *others):
        return lax.optimization_barrier((value, *others))[0]

    def to_quad(value, q):
        return lax.ppermute(value, "quad", [(j, j ^ q) for j in range(quads)])

    def to_other_wing(value, q):
        pairs = [(w * quads + j, (1 - w) * quads + (j ^ q)) for w in range(2) for j in range(quads)]
        return lax.ppermute(value, ("wing", "quad"), pairs)

    *blocks, early, late = pack(normed_inputs, downs, ups, value_matrix, quads)
    mine = [to_quad(blocks[q], q) for q in range(1, quads)]
    early = lax.ppermute(early, "wing", SWAP)
    maps = [to_other_wing(blocks[quads - 1 + q], q) for q in range(1, quads)]

    attn = [attention(0, after(cache_length, blocks[0]))]
    early, *maps = lax.optimization_barrier((early, *maps, attn[0][1]))[:-1]
    step = maps[0].shape[1]
    maps = jnp.stack([early[early.shape[0] - maps[0].shape[0] :, :step], *maps])
    late = lax.ppermute(after(late, early), "wing", SWAP)
    early_other = lax.ppermute(early, "parts", parts_swap)
    maps_other = lax.ppermute(maps, "parts", parts_swap)

    attn.append(attention(1, after(cache_length, early, maps)))
    late, early_other, maps_other, *mine = lax.optimization_barrier(
        (late, early_other, maps_other, *mine, attn[1][1])
    )[:-1]
    mine = jnp.stack([blocks[0], *mine])
    late_other = lax.ppermute(late, "parts", parts_swap)
    maps_mine = (maps, maps_other)
    maps_theirs = [lax.ppermute(each, "tensor", SWAP) for each in maps_mine]
    theirs = lax.ppermute(mine, "tensor", SWAP)

    tokens, q_width = queries.shape
    near = near_products(
        mine, theirs, maps_mine, maps_theirs, value_matrix, adapter_position, span_adapter_index, tokens
    )
    products = far_products(mine, theirs, near, (early, late, early_other, late_other), tokens)
    parts = [products[0]] + [to_quad(products[q], q) for q in range(1, quads)]
    mixed, fresh_probs = zip(*attn)
    attended, incoming_values = finish([piece[:2] for piece in pieces], mixed, fresh_probs, parts, q_width)
    return (attended, incoming_values)


def solution(mesh):
    sizes = mesh.devices.shape
    cut = Mesh(
        mesh.devices.reshape(sizes[0], 2, sizes[1] // 2, sizes[2]), ("parts", "wing", "quad", "tensor")
    )
    group = ("wing", "quad")
    home = ("parts", "wing", "quad")
    in_specs = (
        P(home, "tensor"),
        P(group, "tensor"),
        P(group, None, None),
        P(group, None, "tensor"),
        P(),
        P("parts"),
        P(home, "tensor"),
        P(home, "tensor"),
        P(home, None, "tensor"),
        P(home, None, "tensor"),
        P(home),
    )
    out_specs = (P(home, "tensor"), P(home, "tensor"))
    return jax.shard_map(
        on_device, mesh=cut, in_specs=in_specs, out_specs=out_specs, check_vma=False
    )
```

```python
import functools
import math

import jax
import jax.numpy as jnp
from jax import lax
from jax.experimental import pallas as pl
from jax.experimental.pallas import tpu as pltpu
from jax.sharding import Mesh
from jax.sharding import PartitionSpec as P

HD = 128
RANK = 16
SPAN = 64
CHUNK = 512
ONES = 16
TILE = 128
ADAPTER_SCALE = 2.0
EXP2_SCALE = math.log2(math.e) / math.sqrt(HD)
DEAD = -1e30
MIB = 1024 * 1024
SWAP = [(0, 1), (1, 0)]
FREE = pl.CostEstimate(flops=1, bytes_accessed=1, transcendentals=0)


def dot_last(a, b):
    return lax.dot_general(a, b, (((1,), (1,)), ((), ())), preferred_element_type=jnp.float32)


def dot(a, b):
    return jnp.dot(a, b, preferred_element_type=jnp.float32)


def cache_kernel(span, lens, q_ref, fk_ref, k_hbm, v_hbm, out_ref, pf_ref, qs, ks, vs, live, s_s, p_s, x_s, m_s, a_s, acc, sems):
    length = lens[span]
    chunks, chunk, _ = ks.shape
    kv_heads, rows, _ = qs.shape
    group_size = rows // SPAN
    count = (length + chunk - 1) // chunk

    def copies(i):
        slots = pl.ds(pl.multiple_of(i * chunk, chunk), chunk)
        return (
            pltpu.make_async_copy(k_hbm.at[span, slots, :], ks.at[i], sems.at[0, i]),
            pltpu.make_async_copy(v_hbm.at[span, slots, :], vs.at[i], sems.at[1, i]),
        )

    for i in range(chunks):

        @pl.when(i * chunk < length)
        def _():
            for copy in copies(i):
                copy.start()

    def arrive(i):
        for copy in copies(i):
            copy.wait()
        slot = i * chunk + lax.broadcasted_iota(jnp.int32, (ONES, chunk), 1)
        live[i] = (slot < length).astype(jnp.float32).astype(jnp.bfloat16)

        @pl.when((i + 1) * chunk > length)
        def _():
            dead = i * chunk + lax.broadcasted_iota(jnp.int32, ks.shape[1:], 0) >= length
            keys = ks[i].astype(jnp.float32)
            ks[i] = jnp.where(dead, keys[:1, :], keys).astype(jnp.bfloat16)
            vs[i] = jnp.where(dead, 0.0, vs[i].astype(jnp.float32)).astype(jnp.bfloat16)

    def fresh_scores(k):
        s = dot_last(fk_ref[span * SPAN : (span + 1) * SPAN, k * HD : (k + 1) * HD], qs[k])
        key = lax.broadcasted_iota(jnp.int32, (SPAN, rows), 0)
        token = lax.broadcasted_iota(jnp.int32, (SPAN, rows), 1) % SPAN
        return jnp.where(key <= token, s, DEAD)

    def tile_max(s):
        return jnp.max(s.reshape(s.shape[0] // 8, 8, rows), axis=0)

    def tiles(k):
        return slice(k * HD, (k + 1) * HD)

    for k in range(kv_heads):
        for h in range(group_size):
            qs[k, h * SPAN : (h + 1) * SPAN, :] = q_ref[
                span * SPAN : (span + 1) * SPAN, (k * group_size + h) * HD : (k * group_size + h + 1) * HD
            ]
        m_s[k] = jnp.max(fresh_scores(k), axis=0, keepdims=True)
        a_s[k] = jnp.ones((1, rows), jnp.float32)
        acc[k] = jnp.zeros((HD + ONES, rows), jnp.float32)
    p_s[1] = jnp.zeros((chunk, rows), jnp.bfloat16)
    arrive(0)
    s = dot_last(ks[0, :, :HD], qs[0])
    s_s[0] = s
    x_s[0] = tile_max(s)

    def weighted(i, k, part, index):
        return dot(jnp.concatenate([vs[i, part, tiles(k)].T, live[i, :, part]], axis=0), p_s[index, part, :])

    @pl.loop(0, count)
    def _(i):
        @pl.when(i + 1 < count)
        def _():
            arrive(i + 1)

        for k in range(kv_heads):
            now, other = k % 2, 1 - k % 2
            next_k, next_i = (k + 1) % kv_heads, i if k + 1 < kv_heads else jnp.minimum(i + 1, count - 1)
            last_k, last_i = (k - 1) % kv_heads, i if k > 0 else jnp.maximum(i - 1, 0)
            before = m_s[k]
            top = jnp.maximum(before, jnp.max(x_s[now], axis=0, keepdims=True))
            m_s[k] = top
            highest, mixed = None, None
            for j in range(0, chunk, TILE):
                part = slice(j, j + TILE)
                s = dot_last(ks[next_i, part, tiles(next_k)], qs[next_k])
                s_s[other, part, :] = s
                high = tile_max(s)
                highest = high if highest is None else jnp.maximum(highest, high)
                p_s[now, part, :] = jnp.exp2((s_s[now, part, :] - top) * EXP2_SCALE).astype(jnp.bfloat16)
                if (j // TILE) % 2 == 1:
                    product = weighted(last_i, last_k, slice(j - TILE, j + TILE), other)
                    mixed = product if mixed is None else mixed + product
            x_s[other] = highest
            acc[last_k] = acc[last_k] * a_s[last_k] + mixed
            a_s[k] = jnp.exp2((before - top) * EXP2_SCALE)

    last = kv_heads - 1
    acc[last] = acc[last] * a_s[last] + weighted(count - 1, last, slice(0, chunk), last % 2)

    for k in range(kv_heads):
        p = jnp.exp2((fresh_scores(k) - m_s[k]) * EXP2_SCALE)
        inverse = 1.0 / (acc[k, HD : HD + 1, :] + jnp.sum(p, axis=0, keepdims=True))
        pf_ref[k * rows : (k + 1) * rows, :] = (p * inverse).T.astype(jnp.bfloat16)
        mixed = (acc[k, :HD, :] * inverse).T
        for h in range(group_size):
            col = (k * group_size + h) * HD
            out_ref[:, col : col + HD] = mixed[h * SPAN : (h + 1) * SPAN, :]


def cache_attention(span, queries, fresh_keys, keys, values, lengths):
    slots, width = keys.shape[1:]
    kv_heads = width // HD
    group_size = queries.shape[1] // width
    rows = group_size * SPAN
    chunk = min(CHUNK, slots)
    chunks = slots // chunk
    vmem = pl.BlockSpec(memory_space=pltpu.VMEM)
    hbm = pl.BlockSpec(memory_space=pltpu.HBM)
    return pl.pallas_call(
        functools.partial(cache_kernel, span),
        in_specs=[pl.BlockSpec(memory_space=pltpu.SMEM), vmem, vmem, hbm, hbm],
        out_specs=[vmem, vmem],
        scratch_shapes=[
            pltpu.VMEM((kv_heads, rows, HD), jnp.bfloat16),
            pltpu.VMEM((chunks, chunk, width), jnp.bfloat16),
            pltpu.VMEM((chunks, chunk, width), jnp.bfloat16),
            pltpu.VMEM((chunks, ONES, chunk), jnp.bfloat16),
            pltpu.VMEM((2, chunk, rows), jnp.float32),
            pltpu.VMEM((2, chunk, rows), jnp.bfloat16),
            pltpu.VMEM((2, 8, rows), jnp.float32),
            pltpu.VMEM((kv_heads, 1, rows), jnp.float32),
            pltpu.VMEM((kv_heads, 1, rows), jnp.float32),
            pltpu.VMEM((kv_heads, HD + ONES, rows), jnp.float32),
            pltpu.SemaphoreType.DMA((2, chunks)),
        ],
        out_shape=[
            jax.ShapeDtypeStruct((SPAN, queries.shape[1]), jnp.float32),
            jax.ShapeDtypeStruct((kv_heads * rows, SPAN), jnp.bfloat16),
        ],
        compiler_params=pltpu.CompilerParams(vmem_limit_bytes=57 * MIB),
        cost_estimate=FREE,
        name="cache_attention",
    )(lengths, queries, fresh_keys, keys, values)


def pack_kernel(x_hbm, d_hbm, u_hbm, w_hbm, *refs):
    quads = (len(refs) - 2) // 2
    tokens_out, (early, late, sems) = refs[:quads], refs[-3:]
    size = w_hbm.shape[0] // 2 - late.shape[0]
    maps_out = [early.at[size:, :], *refs[quads:-3]]
    part, core, quad = lax.axis_index("parts") % 2, lax.axis_index("tensor"), lax.axis_index("quad")
    tokens, features = x_hbm.shape
    width, cols = w_hbm.shape
    ranks = d_hbm.shape[0]
    step = min(cols, width)
    mine = pl.ds(pl.multiple_of(part * RANK, RANK), RANK)
    copies = []
    for q, out in enumerate(maps_out):
        begin = core * features + (quad ^ q) * width
        for i, first in enumerate(range(0, width, step)):
            here = pl.ds(pl.multiple_of(begin + first, step), step)
            copies.append((d_hbm.at[mine, here], out.at[i * RANK : (i + 1) * RANK, :step]))
        for i, first in enumerate(range(0, cols, step)):
            row = width // step * RANK + i * RANK
            copies.append((u_hbm.at[mine, first : first + step], out.at[row : row + RANK, :step]))
    begin = part * (width // 2)
    copies.append((w_hbm.at[pl.ds(pl.multiple_of(begin, RANK), size), :], early.at[:size, :]))
    begin = begin + size
    copies.append((w_hbm.at[pl.ds(pl.multiple_of(begin, RANK), late.shape[0]), :], late))
    for q, out in enumerate(tokens_out):
        here = pl.ds(pl.multiple_of((quad ^ q) * width, width), width)
        copies.append((x_hbm.at[:, here], out.at[:tokens, :]))
        here = pl.ds(pl.multiple_of(core * features + (quad ^ q) * width, width), width)
        copies.append((d_hbm.at[:, here], out.at[tokens : tokens + ranks, :]))
        for slot, first, row, col in up_places(cols, width):
            row += tokens + ranks
            up = u_hbm.at[slot * RANK : (slot + 1) * RANK, first : first + step]
            copies.append((up, out.at[row : row + RANK, col : col + step]))
    copies = [pltpu.make_async_copy(src, dst, sems.at[i]) for i, (src, dst) in enumerate(copies)]
    for copy in copies:
        copy.start()
    for copy in copies:
        copy.wait()


def up_places(cols, width):
    step = min(cols, width)
    return [
        (slot, first, (slot * cols + first) // width * RANK, (slot * cols + first) % width)
        for slot in range(2)
        for first in range(0, cols, step)
    ]


def pack(tokens, downs, ups, weights, quads):
    vmem = pl.BlockSpec(memory_space=pltpu.VMEM)
    hbm = pl.BlockSpec(memory_space=pltpu.HBM)
    ranks, cols = ups.shape
    width = weights.shape[0]
    step = min(cols, width)
    kind = tokens.dtype
    pieces = (width + cols) // step
    first = width // 4
    sizes = [(tokens.shape[0] + ranks + RANK * (2 * cols // width), width)] * quads
    sizes += [(RANK * pieces, step)] * (quads - 1)
    sizes += [(first + RANK * pieces, cols), (width // 2 - first, cols)]
    count = quads * (pieces + 2 + len(up_places(cols, width))) + 2
    return pl.pallas_call(
        pack_kernel,
        in_specs=[hbm] * 4,
        out_specs=[vmem] * len(sizes),
        out_shape=[jax.ShapeDtypeStruct(size, kind) for size in sizes],
        scratch_shapes=[pltpu.SemaphoreType.DMA((count,))],
        compiler_params=pltpu.CompilerParams(vmem_limit_bytes=57 * MIB),
        cost_estimate=FREE,
        name="pack",
    )(tokens, downs, ups, weights)


def near_kernel(tokens, quads, position, adapter, own_ref, *refs):
    maps_mine, maps_theirs, refs = refs[:2], refs[2:4], refs[4:]
    mine, theirs, out, ds, us = refs
    part, core = lax.axis_index("parts") % 2, lax.axis_index("tensor")
    wing, quad = lax.axis_index("wing"), lax.axis_index("quad")
    width = mine.shape[2]
    cols = own_ref.shape[1]
    ranks = 2 * RANK
    step = min(cols, width)
    for q in range(quads):
        rows = slice(q * ranks, (q + 1) * ranks)
        ds[0, rows, :] = mine[q, tokens : tokens + ranks, :]
        ds[1, rows, :] = theirs[q, tokens : tokens + ranks, :]
        for slot, first, row, col in up_places(cols, width):
            row += tokens + ranks
            place = q * ranks + slot * RANK
            us[place : place + RANK, first : first + step] = mine[q, row : row + RANK, col : col + step]
        for side in range(2):
            place = (quads + q) * ranks + side * RANK
            for i, first in enumerate(range(0, width, step)):
                row = i * RANK
                ds[0, place : place + RANK, first : first + step] = maps_mine[side][q, row : row + RANK, :]
                ds[1, place : place + RANK, first : first + step] = maps_theirs[side][q, row : row + RANK, :]
            for i, first in enumerate(range(0, cols, step)):
                row = (width // step + i) * RANK
                us[place : place + RANK, first : first + step] = maps_mine[side][q, row : row + RANK, :]

    x_mine = mine[:, :tokens, :].reshape(quads * tokens, width)
    x_theirs = theirs[:, :tokens, :].reshape(quads * tokens, width)
    shrink = dot_last(x_mine, ds[0]) + dot_last(x_theirs, ds[1])
    place = lax.broadcasted_iota(jnp.int32, (SPAN, us.shape[0]), 1)
    far = (place >= quads * ranks).astype(jnp.int32)
    index = place - far * (quads * ranks)
    group = (wing ^ far) * quads + (quad ^ (index >> 5))
    which = 2 * group + (((index >> 4) & 1) ^ (far * part))
    spans = tokens // SPAN
    masked = []
    for q in range(quads):
        for i in range(spans):
            slot = position[adapter[(wing * quads + (quad ^ q)) * spans + i]]
            row = (q * spans + i) * SPAN
            masked.append(jnp.where(which == slot, shrink[row : row + SPAN, :], 0.0))
    shrink = (jnp.concatenate(masked, axis=0) * ADAPTER_SCALE).astype(jnp.bfloat16)
    out[...] = dot(shrink, us[...])

    @pl.when(core == wing)
    def _():
        out[...] += dot(x_mine, own_ref[...])

    @pl.when(core != wing)
    def _():
        out[...] += dot(x_theirs, own_ref[...])


def near_products(mine, theirs, maps_mine, maps_theirs, own, position, adapter, tokens):
    quads, _, width = mine.shape
    cols = own.shape[1]
    ranks = 4 * quads * RANK
    vmem = pl.BlockSpec(memory_space=pltpu.VMEM)
    smem = pl.BlockSpec(memory_space=pltpu.SMEM)
    return pl.pallas_call(
        functools.partial(near_kernel, tokens, quads),
        in_specs=[smem, smem] + [vmem] * 7,
        out_specs=vmem,
        out_shape=jax.ShapeDtypeStruct((quads * tokens, cols), jnp.float32),
        scratch_shapes=[
            pltpu.VMEM((2, ranks, width), jnp.bfloat16),
            pltpu.VMEM((ranks, cols), jnp.bfloat16),
        ],
        compiler_params=pltpu.CompilerParams(vmem_limit_bytes=48 * MIB if quads > 4 else 24 * MIB),
        cost_estimate=FREE,
        name="near_products",
    )(position, adapter, own, *maps_mine, *maps_theirs, mine, theirs)


def far_kernel(tokens, quads, near, *refs):
    weights, (mine, theirs) = refs[:4], refs[4:6]
    outs, whole = refs[6:-1], refs[-1]
    part, core, wing = lax.axis_index("parts") % 2, lax.axis_index("tensor"), lax.axis_index("wing")
    for side in range(2):
        begin = (part if side == 0 else 1 - part) * (whole.shape[0] // 2)
        early, late = weights[2 * side : 2 * side + 2]
        size = whole.shape[0] // 2 - late.shape[0]
        whole[pl.ds(pl.multiple_of(begin, RANK), size), :] = early[:size, :]
        whole[pl.ds(pl.multiple_of(begin + size, RANK), late.shape[0]), :] = late[...]

    def store(blocks):
        x = blocks[:, :tokens, :].reshape(near.shape[0], -1)
        product = (near[...] + dot(x, whole[...])).astype(jnp.bfloat16)
        for q, out in enumerate(outs):
            out[...] = product[q * tokens : (q + 1) * tokens, :]

    @pl.when(core == wing)
    def _():
        store(theirs)

    @pl.when(core != wing)
    def _():
        store(mine)


def far_products(mine, theirs, near, weights, tokens):
    quads, _, width = mine.shape
    cols = near.shape[1]
    vmem = pl.BlockSpec(memory_space=pltpu.VMEM)
    return pl.pallas_call(
        functools.partial(far_kernel, tokens, quads),
        in_specs=[vmem] * (3 + len(weights)),
        out_specs=[vmem] * quads,
        out_shape=[jax.ShapeDtypeStruct((tokens, cols), jnp.bfloat16)] * quads,
        scratch_shapes=[pltpu.VMEM((width, cols), jnp.bfloat16)],
        compiler_params=pltpu.CompilerParams(vmem_limit_bytes=48 * MIB if quads > 4 else 16 * MIB),
        cost_estimate=FREE,
        name="far_products",
    )(near, *weights, mine, theirs)


def finish_kernel(places, *refs):
    count = len(places)
    out_ref, values_ref = refs[-2:]
    mixed, probs, parts = refs[:count], refs[count : 2 * count], refs[2 * count : -2]
    total = parts[0][...].astype(jnp.float32)
    for part in parts[1:]:
        total = total + part[...].astype(jnp.float32)
    total = total.astype(jnp.bfloat16)
    values_ref[...] = total
    for (span, head), mix, prob in zip(places, mixed, probs):
        rows = slice(span * SPAN, (span + 1) * SPAN)
        group_size = out_ref.shape[1] // total.shape[1]
        queries = group_size * SPAN
        for k in range(prob.shape[0] // queries):
            values = total[rows, (head + k) * HD : (head + k + 1) * HD]
            fresh = dot(prob[k * queries : (k + 1) * queries, :], values)
            for h in range(group_size):
                here = slice((k * group_size + h) * HD, (k * group_size + h + 1) * HD)
                col = ((head + k) * group_size + h) * HD
                out_ref[rows, col : col + HD] = (
                    mix[:, here] + fresh[h * SPAN : (h + 1) * SPAN, :]
                ).astype(jnp.bfloat16)


def finish(places, mixed, fresh_probs, parts, q_width):
    tokens, cols = parts[0].shape
    vmem = pl.BlockSpec(memory_space=pltpu.VMEM)
    return pl.pallas_call(
        functools.partial(finish_kernel, places),
        in_specs=[vmem] * (len(parts) + 2 * len(mixed)),
        out_specs=[vmem] * 2,
        out_shape=[
            jax.ShapeDtypeStruct((tokens, q_width), jnp.bfloat16),
            jax.ShapeDtypeStruct((tokens, cols), jnp.bfloat16),
        ],
        compiler_params=pltpu.CompilerParams(vmem_limit_bytes=16 * MIB),
        cost_estimate=FREE,
        name="finish_attention",
    )(*mixed, *fresh_probs, *parts)


def on_device(
    normed_inputs,
    value_matrix,
    adapter_down_weight,
    adapter_up_weight,
    adapter_position,
    span_adapter_index,
    queries,
    incoming_keys,
    stored_keys,
    stored_values,
    cache_length,
):
    quads = lax.axis_size("quad")
    parts_swap = [(i, i ^ 1) for i in range(lax.axis_size("parts"))]
    width, cols = value_matrix.shape
    downs = adapter_down_weight.reshape(-1, adapter_down_weight.shape[2])
    ups = adapter_up_weight.reshape(-1, cols)

    kv_heads = cols // HD
    def attention(span, lengths):
        return cache_attention(span, queries, incoming_keys, stored_keys, stored_values, lengths)

    def after(value, *others):
        return lax.optimization_barrier((value, *others))[0]

    def to_quad(value, q):
        return lax.ppermute(value, "quad", [(j, j ^ q) for j in range(quads)])

    def to_other_wing(value, q):
        pairs = [(w * quads + j, (1 - w) * quads + (j ^ q)) for w in range(2) for j in range(quads)]
        return lax.ppermute(value, ("wing", "quad"), pairs)

    *blocks, early, late = pack(normed_inputs, downs, ups, value_matrix, quads)
    order = [*range(quads // 2, quads), *range(1, quads // 2)]
    mine = [to_quad(blocks[q], q) for q in order]
    early = lax.ppermute(early, "wing", SWAP)
    maps = [to_other_wing(blocks[quads - 1 + q], q) for q in range(1, quads)]

    attn = [attention(0, after(cache_length, blocks[0]))]
    early, *maps = lax.optimization_barrier((early, *maps, attn[0][1]))[:-1]
    step = maps[0].shape[1]
    maps = jnp.stack([early[early.shape[0] - maps[0].shape[0] :, :step], *maps])
    late = lax.ppermute(after(late, early), "wing", SWAP)
    early_other = lax.ppermute(early, "parts", parts_swap)
    maps_other = lax.ppermute(maps, "parts", parts_swap)

    attn.append(attention(1, after(cache_length, early, maps)))
    late, early_other, maps_other, *mine = lax.optimization_barrier(
        (late, early_other, maps_other, *mine, attn[1][1])
    )[:-1]
    mine = jnp.stack([blocks[0]] + [mine[order.index(q)] for q in range(1, quads)])
    late_other = lax.ppermute(late, "parts", parts_swap)
    maps_mine = (maps, maps_other)
    maps_theirs = [lax.ppermute(each, "tensor", SWAP) for each in maps_mine]
    theirs = lax.ppermute(mine, "tensor", SWAP)

    tokens, q_width = queries.shape
    near = near_products(
        mine, theirs, maps_mine, maps_theirs, value_matrix, adapter_position, span_adapter_index, tokens
    )
    products = far_products(mine, theirs, near, (early, late, early_other, late_other), tokens)
    parts = [products[0]] + [to_quad(products[q], q) for q in range(1, quads)]
    mixed, fresh_probs = zip(*attn)
    attended, incoming_values = finish([(0, 0), (1, 0)], mixed, fresh_probs, parts, q_width)
    return (attended, incoming_values)


def solution(mesh):
    sizes = mesh.devices.shape
    cut = Mesh(
        mesh.devices.reshape(sizes[0], 2, sizes[1] // 2, sizes[2]), ("parts", "wing", "quad", "tensor")
    )
    group = ("wing", "quad")
    home = ("parts", "wing", "quad")
    in_specs = (
        P(home, "tensor"),
        P(group, "tensor"),
        P(group, None, None),
        P(group, None, "tensor"),
        P(),
        P("parts"),
        P(home, "tensor"),
        P(home, "tensor"),
        P(home, None, "tensor"),
        P(home, None, "tensor"),
        P(home),
    )
    out_specs = (P(home, "tensor"), P(home, "tensor"))
    return jax.shard_map(
        on_device, mesh=cut, in_specs=in_specs, out_specs=out_specs, check_vma=False
    )
```

```python
import functools
import math

import jax
import jax.numpy as jnp
from jax import lax
from jax.experimental import pallas as pl
from jax.experimental.pallas import tpu as pltpu
from jax.sharding import Mesh
from jax.sharding import PartitionSpec as P

HD = 128
RANK = 16
SPAN = 64
CHUNK = 512
ONES = 16
TILE = 128
ADAPTER_SCALE = 2.0
EXP2_SCALE = math.log2(math.e) / math.sqrt(HD)
DEAD = -1e30
MIB = 1024 * 1024
SWAP = [(0, 1), (1, 0)]
FREE = pl.CostEstimate(flops=1, bytes_accessed=1, transcendentals=0)


def dot_last(a, b):
    return lax.dot_general(a, b, (((1,), (1,)), ((), ())), preferred_element_type=jnp.float32)


def dot(a, b):
    return jnp.dot(a, b, preferred_element_type=jnp.float32)


def span_of(order, lens):
    longer = (lens[1] > lens[0]).astype(jnp.int32)
    return longer if order == 0 else 1 - longer


def cache_kernel(order, lens, q_hbm, fk_hbm, k_hbm, v_hbm, out_hbm, pf_hbm, qs, ks, vs, live, s_s, p_s, x_s, m_s, a_s, acc, q_s, fk_s, out_s, pf_s, sems, io_sems):
    span = span_of(order, lens)
    length = lens[span]
    chunks, chunk, _ = ks.shape
    kv_heads, rows, _ = qs.shape
    group_size = rows // SPAN
    count = (length + chunk - 1) // chunk
    mine = pl.ds(pl.multiple_of(span * SPAN, SPAN), SPAN)

    def copy_in(side, i):
        slots = pl.ds(pl.multiple_of(i * chunk, chunk), chunk)
        source, target = ((k_hbm, ks), (v_hbm, vs))[side]
        return pltpu.make_async_copy(source.at[span, slots, :], target.at[i], sems.at[side, i])

    small = [
        pltpu.make_async_copy(q_hbm.at[mine, :], q_s, io_sems.at[0]),
        pltpu.make_async_copy(fk_hbm.at[mine, :], fk_s, io_sems.at[1]),
    ]
    for copy in small:
        copy.start()
    for i in range(chunks):

        @pl.when(i * chunk < length)
        def _():
            copy_in(0, i).start()
            copy_in(1, i).start()

    def dead_slots(i):
        return i * chunk + lax.broadcasted_iota(jnp.int32, ks.shape[1:], 0) >= length

    def arrive_keys(i):
        copy_in(0, i).wait()

        @pl.when((i + 1) * chunk > length)
        def _():
            keys = ks[i].astype(jnp.float32)
            ks[i] = jnp.where(dead_slots(i), keys[:1, :], keys).astype(jnp.bfloat16)

    def arrive_values(i):
        copy_in(1, i).wait()
        slot = i * chunk + lax.broadcasted_iota(jnp.int32, (ONES, chunk), 1)
        live[i] = (slot < length).astype(jnp.float32).astype(jnp.bfloat16)

        @pl.when((i + 1) * chunk > length)
        def _():
            vs[i] = jnp.where(dead_slots(i), 0.0, vs[i].astype(jnp.float32)).astype(jnp.bfloat16)

    def fresh_scores(k):
        s = dot_last(fk_s[:, k * HD : (k + 1) * HD], qs[k])
        key = lax.broadcasted_iota(jnp.int32, (SPAN, rows), 0)
        token = lax.broadcasted_iota(jnp.int32, (SPAN, rows), 1) % SPAN
        return jnp.where(key <= token, s, DEAD)

    def tile_max(s):
        return jnp.max(s.reshape(s.shape[0] // 8, 8, rows), axis=0)

    def tiles(k):
        return slice(k * HD, (k + 1) * HD)

    for copy in small:
        copy.wait()
    for k in range(kv_heads):
        for h in range(group_size):
            qs[k, h * SPAN : (h + 1) * SPAN, :] = q_s[:, tiles(k * group_size + h)]
        m_s[k] = jnp.max(fresh_scores(k), axis=0, keepdims=True)
        a_s[k] = jnp.ones((1, rows), jnp.float32)
        acc[k] = jnp.zeros((HD + ONES, rows), jnp.float32)
    p_s[1] = jnp.zeros((chunk, rows), jnp.bfloat16)
    arrive_keys(0)
    s = dot_last(ks[0, :, :HD], qs[0])
    s_s[0] = s
    x_s[0] = tile_max(s)

    def weighted(i, k, part, index):
        return dot(jnp.concatenate([vs[i, part, tiles(k)].T, live[i, :, part]], axis=0), p_s[index, part, :])

    @pl.loop(0, count)
    def _(i):
        arrive_values(i)

        @pl.when(i + 1 < count)
        def _():
            arrive_keys(i + 1)

        for k in range(kv_heads):
            now, other = k % 2, 1 - k % 2
            next_k, next_i = (k + 1) % kv_heads, i if k + 1 < kv_heads else jnp.minimum(i + 1, count - 1)
            last_k, last_i = (k - 1) % kv_heads, i if k > 0 else jnp.maximum(i - 1, 0)
            before = m_s[k]
            top = jnp.maximum(before, jnp.max(x_s[now], axis=0, keepdims=True))
            m_s[k] = top
            highest, mixed = None, None
            for j in range(0, chunk, TILE):
                part = slice(j, j + TILE)
                s = dot_last(ks[next_i, part, tiles(next_k)], qs[next_k])
                s_s[other, part, :] = s
                high = tile_max(s)
                highest = high if highest is None else jnp.maximum(highest, high)
                p_s[now, part, :] = jnp.exp2((s_s[now, part, :] - top) * EXP2_SCALE).astype(jnp.bfloat16)
                if (j // TILE) % 2 == 1:
                    product = weighted(last_i, last_k, slice(j - TILE, j + TILE), other)
                    mixed = product if mixed is None else mixed + product
            x_s[other] = highest
            acc[last_k] = acc[last_k] * a_s[last_k] + mixed
            a_s[k] = jnp.exp2((before - top) * EXP2_SCALE)

    last = kv_heads - 1
    acc[last] = acc[last] * a_s[last] + weighted(count - 1, last, slice(0, chunk), last % 2)

    leaving = []
    for k in range(kv_heads):
        p = jnp.exp2((fresh_scores(k) - m_s[k]) * EXP2_SCALE)
        inverse = 1.0 / (acc[k, HD : HD + 1, :] + jnp.sum(p, axis=0, keepdims=True))
        p_s[0, (k % 2) * SPAN : (k % 2 + 1) * SPAN, :] = (p * inverse).astype(jnp.bfloat16)
        mixed = (acc[k, :HD, :] * inverse).T.astype(jnp.bfloat16)
        for h in range(group_size):
            out_s[:, tiles(k * group_size + h)] = mixed[h * SPAN : (h + 1) * SPAN, :]
        here = slice(k * group_size * HD, (k + 1) * group_size * HD)
        leaving.append(pltpu.make_async_copy(out_s.at[:, here], out_hbm.at[:, here], io_sems.at[2 + k]))
        leaving[-1].start()
        if k % 2 == 1:
            pf_s[k // 2] = p_s[0, : 2 * SPAN, :].T
    leaving.append(pltpu.make_async_copy(pf_s, pf_hbm, io_sems.at[2 + kv_heads]))
    leaving[-1].start()
    for copy in leaving:
        copy.wait()


def cache_attention(order, queries, fresh_keys, keys, values, lengths):
    slots, width = keys.shape[1:]
    kv_heads = width // HD
    group_size = queries.shape[1] // width
    rows = group_size * SPAN
    chunk = min(CHUNK, slots)
    chunks = slots // chunk
    hbm = pl.BlockSpec(memory_space=pltpu.HBM)
    result = (SPAN, queries.shape[1])
    weights = (kv_heads // 2, rows, 2 * SPAN)
    return pl.pallas_call(
        functools.partial(cache_kernel, order),
        in_specs=[pl.BlockSpec(memory_space=pltpu.SMEM)] + [hbm] * 4,
        out_specs=[hbm] * 2,
        scratch_shapes=[
            pltpu.VMEM((kv_heads, rows, HD), jnp.bfloat16),
            pltpu.VMEM((chunks, chunk, width), jnp.bfloat16),
            pltpu.VMEM((chunks, chunk, width), jnp.bfloat16),
            pltpu.VMEM((chunks, ONES, chunk), jnp.bfloat16),
            pltpu.VMEM((2, chunk, rows), jnp.float32),
            pltpu.VMEM((2, chunk, rows), jnp.bfloat16),
            pltpu.VMEM((2, 8, rows), jnp.float32),
            pltpu.VMEM((kv_heads, 1, rows), jnp.float32),
            pltpu.VMEM((kv_heads, 1, rows), jnp.float32),
            pltpu.VMEM((kv_heads, HD + ONES, rows), jnp.float32),
            pltpu.VMEM(result, jnp.bfloat16),
            pltpu.VMEM((SPAN, width), jnp.bfloat16),
            pltpu.VMEM(result, jnp.bfloat16),
            pltpu.VMEM(weights, jnp.bfloat16),
            pltpu.SemaphoreType.DMA((2, chunks)),
            pltpu.SemaphoreType.DMA((3 + kv_heads,)),
        ],
        out_shape=[
            jax.ShapeDtypeStruct(result, jnp.bfloat16),
            jax.ShapeDtypeStruct(weights, jnp.bfloat16),
        ],
        compiler_params=pltpu.CompilerParams(vmem_limit_bytes=57 * MIB),
        cost_estimate=FREE,
        name="cache_attention",
    )(lengths, queries, fresh_keys, keys, values)


def pack_kernel(x_hbm, d_hbm, u_hbm, w_hbm, *refs):
    quads = (len(refs) - 2) // 2
    tokens_out, (early, late, sems) = refs[:quads], refs[-3:]
    size = w_hbm.shape[0] // 2 - late.shape[0]
    maps_out = [early.at[size:, :], *refs[quads:-3]]
    part, core, quad = lax.axis_index("parts") % 2, lax.axis_index("tensor"), lax.axis_index("quad")
    tokens, features = x_hbm.shape
    width, cols = w_hbm.shape
    ranks = d_hbm.shape[0]
    step = min(cols, width)
    mine = pl.ds(pl.multiple_of(part * RANK, RANK), RANK)
    copies = []
    for q, out in enumerate(maps_out):
        begin = core * features + (quad ^ q) * width
        for i, first in enumerate(range(0, width, step)):
            here = pl.ds(pl.multiple_of(begin + first, step), step)
            copies.append((d_hbm.at[mine, here], out.at[i * RANK : (i + 1) * RANK, :step]))
        for i, first in enumerate(range(0, cols, step)):
            row = width // step * RANK + i * RANK
            copies.append((u_hbm.at[mine, first : first + step], out.at[row : row + RANK, :step]))
    begin = part * (width // 2)
    copies.append((w_hbm.at[pl.ds(pl.multiple_of(begin, RANK), size), :], early.at[:size, :]))
    begin = begin + size
    copies.append((w_hbm.at[pl.ds(pl.multiple_of(begin, RANK), late.shape[0]), :], late))
    for q, out in enumerate(tokens_out):
        here = pl.ds(pl.multiple_of((quad ^ q) * width, width), width)
        copies.append((x_hbm.at[:, here], out.at[:tokens, :]))
        here = pl.ds(pl.multiple_of(core * features + (quad ^ q) * width, width), width)
        copies.append((d_hbm.at[:, here], out.at[tokens : tokens + ranks, :]))
        for slot, first, row, col in up_places(cols, width):
            row += tokens + ranks
            up = u_hbm.at[slot * RANK : (slot + 1) * RANK, first : first + step]
            copies.append((up, out.at[row : row + RANK, col : col + step]))
    copies = [pltpu.make_async_copy(src, dst, sems.at[i]) for i, (src, dst) in enumerate(copies)]
    for copy in copies:
        copy.start()
    for copy in copies:
        copy.wait()


def up_places(cols, width):
    step = min(cols, width)
    return [
        (slot, first, (slot * cols + first) // width * RANK, (slot * cols + first) % width)
        for slot in range(2)
        for first in range(0, cols, step)
    ]


def pack(tokens, downs, ups, weights, quads):
    vmem = pl.BlockSpec(memory_space=pltpu.VMEM)
    hbm = pl.BlockSpec(memory_space=pltpu.HBM)
    ranks, cols = ups.shape
    width = weights.shape[0]
    step = min(cols, width)
    kind = tokens.dtype
    pieces = (width + cols) // step
    first = width // 4
    sizes = [(tokens.shape[0] + ranks + RANK * (2 * cols // width), width)] * quads
    sizes += [(RANK * pieces, step)] * (quads - 1)
    sizes += [(first + RANK * pieces, cols), (width // 2 - first, cols)]
    count = quads * (pieces + 2 + len(up_places(cols, width))) + 2
    return pl.pallas_call(
        pack_kernel,
        in_specs=[hbm] * 4,
        out_specs=[vmem] * len(sizes),
        out_shape=[jax.ShapeDtypeStruct(size, kind) for size in sizes],
        scratch_shapes=[pltpu.SemaphoreType.DMA((count,))],
        compiler_params=pltpu.CompilerParams(vmem_limit_bytes=57 * MIB),
        cost_estimate=FREE,
        name="pack",
    )(tokens, downs, ups, weights)


def near_kernel(tokens, quads, position, adapter, own_ref, *refs):
    maps_mine, maps_theirs, refs = refs[:2], refs[2:4], refs[4:]
    mine, theirs, out, ds, us = refs
    part, core = lax.axis_index("parts") % 2, lax.axis_index("tensor")
    wing, quad = lax.axis_index("wing"), lax.axis_index("quad")
    width = mine.shape[2]
    cols = own_ref.shape[1]
    ranks = 2 * RANK
    step = min(cols, width)
    for q in range(quads):
        rows = slice(q * ranks, (q + 1) * ranks)
        ds[0, rows, :] = mine[q, tokens : tokens + ranks, :]
        ds[1, rows, :] = theirs[q, tokens : tokens + ranks, :]
        for slot, first, row, col in up_places(cols, width):
            row += tokens + ranks
            place = q * ranks + slot * RANK
            us[place : place + RANK, first : first + step] = mine[q, row : row + RANK, col : col + step]
        for side in range(2):
            place = (quads + q) * ranks + side * RANK
            for i, first in enumerate(range(0, width, step)):
                row = i * RANK
                ds[0, place : place + RANK, first : first + step] = maps_mine[side][q, row : row + RANK, :]
                ds[1, place : place + RANK, first : first + step] = maps_theirs[side][q, row : row + RANK, :]
            for i, first in enumerate(range(0, cols, step)):
                row = (width // step + i) * RANK
                us[place : place + RANK, first : first + step] = maps_mine[side][q, row : row + RANK, :]

    x_mine = mine[:, :tokens, :].reshape(quads * tokens, width)
    x_theirs = theirs[:, :tokens, :].reshape(quads * tokens, width)
    shrink = dot_last(x_mine, ds[0]) + dot_last(x_theirs, ds[1])
    place = lax.broadcasted_iota(jnp.int32, (SPAN, us.shape[0]), 1)
    far = (place >= quads * ranks).astype(jnp.int32)
    index = place - far * (quads * ranks)
    group = (wing ^ far) * quads + (quad ^ (index >> 5))
    which = 2 * group + (((index >> 4) & 1) ^ (far * part))
    spans = tokens // SPAN
    masked = []
    for q in range(quads):
        for i in range(spans):
            slot = position[adapter[(wing * quads + (quad ^ q)) * spans + i]]
            row = (q * spans + i) * SPAN
            masked.append(jnp.where(which == slot, shrink[row : row + SPAN, :], 0.0))
    shrink = (jnp.concatenate(masked, axis=0) * ADAPTER_SCALE).astype(jnp.bfloat16)
    out[...] = dot(shrink, us[...])

    @pl.when(core == wing)
    def _():
        out[...] += dot(x_mine, own_ref[...])

    @pl.when(core != wing)
    def _():
        out[...] += dot(x_theirs, own_ref[...])


def near_products(mine, theirs, maps_mine, maps_theirs, own, position, adapter, tokens):
    quads, _, width = mine.shape
    cols = own.shape[1]
    ranks = 4 * quads * RANK
    vmem = pl.BlockSpec(memory_space=pltpu.VMEM)
    smem = pl.BlockSpec(memory_space=pltpu.SMEM)
    return pl.pallas_call(
        functools.partial(near_kernel, tokens, quads),
        in_specs=[smem, smem] + [vmem] * 7,
        out_specs=vmem,
        out_shape=jax.ShapeDtypeStruct((quads * tokens, cols), jnp.float32),
        scratch_shapes=[
            pltpu.VMEM((2, ranks, width), jnp.bfloat16),
            pltpu.VMEM((ranks, cols), jnp.bfloat16),
        ],
        compiler_params=pltpu.CompilerParams(vmem_limit_bytes=48 * MIB if quads > 4 else 24 * MIB),
        cost_estimate=FREE,
        name="near_products",
    )(position, adapter, own, *maps_mine, *maps_theirs, mine, theirs)


def far_kernel(tokens, quads, near, *refs):
    weights, (mine, theirs) = refs[:4], refs[4:6]
    outs, whole = refs[6:-1], refs[-1]
    part, core, wing = lax.axis_index("parts") % 2, lax.axis_index("tensor"), lax.axis_index("wing")
    for side in range(2):
        begin = (part if side == 0 else 1 - part) * (whole.shape[0] // 2)
        early, late = weights[2 * side : 2 * side + 2]
        size = whole.shape[0] // 2 - late.shape[0]
        whole[pl.ds(pl.multiple_of(begin, RANK), size), :] = early[:size, :]
        whole[pl.ds(pl.multiple_of(begin + size, RANK), late.shape[0]), :] = late[...]

    def store(blocks):
        x = blocks[:, :tokens, :].reshape(near.shape[0], -1)
        product = (near[...] + dot(x, whole[...])).astype(jnp.bfloat16)
        for q, out in enumerate(outs):
            out[...] = product[q * tokens : (q + 1) * tokens, :]

    @pl.when(core == wing)
    def _():
        store(theirs)

    @pl.when(core != wing)
    def _():
        store(mine)


def far_products(mine, theirs, near, weights, tokens):
    quads, _, width = mine.shape
    cols = near.shape[1]
    vmem = pl.BlockSpec(memory_space=pltpu.VMEM)
    return pl.pallas_call(
        functools.partial(far_kernel, tokens, quads),
        in_specs=[vmem] * (3 + len(weights)),
        out_specs=[vmem] * quads,
        out_shape=[jax.ShapeDtypeStruct((tokens, cols), jnp.bfloat16)] * quads,
        scratch_shapes=[pltpu.VMEM((width, cols), jnp.bfloat16)],
        compiler_params=pltpu.CompilerParams(vmem_limit_bytes=48 * MIB if quads > 4 else 16 * MIB),
        cost_estimate=FREE,
        name="far_products",
    )(near, *weights, mine, theirs)


def finish_kernel(spans, lens, *refs):
    out_ref, values_ref = refs[-2:]
    mixed, probs, parts = refs[:spans], refs[spans : 2 * spans], refs[2 * spans : -2]
    total = parts[0][...].astype(jnp.float32)
    for part in parts[1:]:
        total = total + part[...].astype(jnp.float32)
    values_ref[...] = total.astype(jnp.bfloat16)
    none = jnp.zeros((SPAN, HD), jnp.bfloat16)
    group_size = out_ref.shape[1] // values_ref.shape[1]
    for order in range(spans):
        span = span_of(order, lens)
        rows = pl.ds(pl.multiple_of(span * SPAN, SPAN), SPAN)
        for pair in range(probs[order].shape[0]):
            left = values_ref[rows, 2 * pair * HD : (2 * pair + 1) * HD]
            right = values_ref[rows, (2 * pair + 1) * HD : (2 * pair + 2) * HD]
            both = jnp.concatenate(
                [jnp.concatenate([left, none], axis=1), jnp.concatenate([none, right], axis=1)], axis=0
            )
            fresh = dot(probs[order][pair], both)
            for side in range(2):
                for h in range(group_size):
                    col = ((2 * pair + side) * group_size + h) * HD
                    added = fresh[h * SPAN : (h + 1) * SPAN, side * HD : (side + 1) * HD]
                    before = mixed[order][:, col : col + HD].astype(jnp.float32)
                    out_ref[rows, col : col + HD] = (before + added).astype(jnp.bfloat16)


def finish(lengths, mixed, fresh_probs, parts, q_width):
    tokens, cols = parts[0].shape
    vmem = pl.BlockSpec(memory_space=pltpu.VMEM)
    smem = pl.BlockSpec(memory_space=pltpu.SMEM)
    return pl.pallas_call(
        functools.partial(finish_kernel, len(mixed)),
        in_specs=[smem] + [vmem] * (len(parts) + 2 * len(mixed)),
        out_specs=[vmem] * 2,
        out_shape=[
            jax.ShapeDtypeStruct((tokens, q_width), jnp.bfloat16),
            jax.ShapeDtypeStruct((tokens, cols), jnp.bfloat16),
        ],
        compiler_params=pltpu.CompilerParams(vmem_limit_bytes=16 * MIB),
        cost_estimate=FREE,
        name="finish_attention",
    )(lengths, *mixed, *fresh_probs, *parts)


def on_device(
    normed_inputs,
    value_matrix,
    adapter_down_weight,
    adapter_up_weight,
    adapter_position,
    span_adapter_index,
    queries,
    incoming_keys,
    stored_keys,
    stored_values,
    cache_length,
):
    quads = lax.axis_size("quad")
    parts_swap = [(i, i ^ 1) for i in range(lax.axis_size("parts"))]
    width, cols = value_matrix.shape
    downs = adapter_down_weight.reshape(-1, adapter_down_weight.shape[2])
    ups = adapter_up_weight.reshape(-1, cols)

    kv_heads = cols // HD
    def attention(order, lengths):
        return cache_attention(order, queries, incoming_keys, stored_keys, stored_values, lengths)

    def after(value, *others):
        return lax.optimization_barrier((value, *others))[0]

    def to_quad(value, q):
        return lax.ppermute(value, "quad", [(j, j ^ q) for j in range(quads)])

    def to_other_wing(value, q):
        pairs = [(w * quads + j, (1 - w) * quads + (j ^ q)) for w in range(2) for j in range(quads)]
        return lax.ppermute(value, ("wing", "quad"), pairs)

    *blocks, early, late = pack(normed_inputs, downs, ups, value_matrix, quads)
    order = [*range(quads // 2, quads), *range(1, quads // 2)]
    mine = [to_quad(blocks[q], q) for q in order]
    early = lax.ppermute(early, "wing", SWAP)
    maps = [to_other_wing(blocks[quads - 1 + q], q) for q in range(1, quads)]

    attn = [attention(0, after(cache_length, blocks[0]))]
    early, *maps = lax.optimization_barrier((early, *maps, attn[0][1]))[:-1]
    step = maps[0].shape[1]
    maps = jnp.stack([early[early.shape[0] - maps[0].shape[0] :, :step], *maps])
    late = lax.ppermute(after(late, early), "wing", SWAP)
    early_other = lax.ppermute(early, "parts", parts_swap)
    maps_other = lax.ppermute(maps, "parts", parts_swap)

    attn.append(attention(1, after(cache_length, early, maps)))
    late, early_other, maps_other, *mine = lax.optimization_barrier(
        (late, early_other, maps_other, *mine, attn[1][1])
    )[:-1]
    mine = jnp.stack([blocks[0]] + [mine[order.index(q)] for q in range(1, quads)])
    late_other = lax.ppermute(late, "parts", parts_swap)
    maps_mine = (maps, maps_other)
    maps_theirs = [lax.ppermute(each, "tensor", SWAP) for each in maps_mine]
    theirs = lax.ppermute(mine, "tensor", SWAP)

    tokens, q_width = queries.shape
    near = near_products(
        mine, theirs, maps_mine, maps_theirs, value_matrix, adapter_position, span_adapter_index, tokens
    )
    products = far_products(mine, theirs, near, (early, late, early_other, late_other), tokens)
    parts = [products[0]] + [to_quad(products[q], q) for q in range(1, quads)]
    mixed, fresh_probs = zip(*attn)
    attended, incoming_values = finish(cache_length, mixed, fresh_probs, parts, q_width)
    return (attended, incoming_values)


def solution(mesh):
    sizes = mesh.devices.shape
    cut = Mesh(
        mesh.devices.reshape(sizes[0], 2, sizes[1] // 2, sizes[2]), ("parts", "wing", "quad", "tensor")
    )
    group = ("wing", "quad")
    home = ("parts", "wing", "quad")
    in_specs = (
        P(home, "tensor"),
        P(group, "tensor"),
        P(group, None, None),
        P(group, None, "tensor"),
        P(),
        P("parts"),
        P(home, "tensor"),
        P(home, "tensor"),
        P(home, None, "tensor"),
        P(home, None, "tensor"),
        P(home),
    )
    out_specs = (P(home, "tensor"), P(home, "tensor"))
    return jax.shard_map(
        on_device, mesh=cut, in_specs=in_specs, out_specs=out_specs, check_vma=False
    )
```

```python
import functools
import math

import jax
import jax.numpy as jnp
from jax import lax
from jax.experimental import pallas as pl
from jax.experimental.pallas import tpu as pltpu
from jax.sharding import Mesh
from jax.sharding import PartitionSpec as P

HD = 128
RANK = 16
SPAN = 64
CHUNK = 512
ONES = 16
TILE = 128
ADAPTER_SCALE = 2.0
EXP2_SCALE = math.log2(math.e) / math.sqrt(HD)
DEAD = -1e30
MIB = 1024 * 1024
SWAP = [(0, 1), (1, 0)]
FREE = pl.CostEstimate(flops=1, bytes_accessed=1, transcendentals=0)


def dot_last(a, b):
    return lax.dot_general(a, b, (((1,), (1,)), ((), ())), preferred_element_type=jnp.float32)


def dot(a, b):
    return jnp.dot(a, b, preferred_element_type=jnp.float32)


def span_of(order, lens):
    longer = (lens[1] > lens[0]).astype(jnp.int32)
    return longer if order == 0 else 1 - longer


def cache_kernel(order, lens, q_hbm, fk_hbm, k_hbm, v_hbm, out_hbm, pf_hbm, qs, ks, vs, live, s_s, p_s, x_s, m_s, a_s, acc, q_s, fk_s, out_s, pf_s, sems, io_sems):
    span = span_of(order, lens)
    length = lens[span]
    chunks, chunk, _ = ks.shape
    kv_heads, rows, _ = qs.shape
    group_size = rows // SPAN
    count = (length + chunk - 1) // chunk
    mine = pl.ds(pl.multiple_of(span * SPAN, SPAN), SPAN)

    def copy_in(side, i):
        slots = pl.ds(pl.multiple_of(i * chunk, chunk), chunk)
        source, target = ((k_hbm, ks), (v_hbm, vs))[side]
        return pltpu.make_async_copy(source.at[span, slots, :], target.at[i], sems.at[side, i])

    small = [
        pltpu.make_async_copy(q_hbm.at[mine, :], q_s, io_sems.at[0]),
        pltpu.make_async_copy(fk_hbm.at[mine, :], fk_s, io_sems.at[1]),
    ]
    for copy in small:
        copy.start()
    copy_in(0, 0).start()

    def dead_slots(i):
        return i * chunk + lax.broadcasted_iota(jnp.int32, ks.shape[1:], 0) >= length

    def arrive_keys(i):
        copy_in(0, i).wait()

        @pl.when((i + 1) * chunk > length)
        def _():
            keys = ks[i].astype(jnp.float32)
            ks[i] = jnp.where(dead_slots(i), keys[:1, :], keys).astype(jnp.bfloat16)

    def arrive_values(i):
        copy_in(1, i).wait()
        slot = i * chunk + lax.broadcasted_iota(jnp.int32, (ONES, chunk), 1)
        live[i] = (slot < length).astype(jnp.float32).astype(jnp.bfloat16)

        @pl.when((i + 1) * chunk > length)
        def _():
            vs[i] = jnp.where(dead_slots(i), 0.0, vs[i].astype(jnp.float32)).astype(jnp.bfloat16)

    def fresh_scores(k):
        s = dot_last(fk_s[:, k * HD : (k + 1) * HD], qs[k])
        key = lax.broadcasted_iota(jnp.int32, (SPAN, rows), 0)
        token = lax.broadcasted_iota(jnp.int32, (SPAN, rows), 1) % SPAN
        return jnp.where(key <= token, s, DEAD)

    def tile_max(s):
        return jnp.max(s.reshape(s.shape[0] // 8, 8, rows), axis=0)

    def tiles(k):
        return slice(k * HD, (k + 1) * HD)

    for copy in small:
        copy.wait()
    copy_in(1, 0).start()
    for k in range(kv_heads):
        for h in range(group_size):
            qs[k, h * SPAN : (h + 1) * SPAN, :] = q_s[:, tiles(k * group_size + h)]
        m_s[k] = jnp.max(fresh_scores(k), axis=0, keepdims=True)
        a_s[k] = jnp.ones((1, rows), jnp.float32)
        acc[k] = jnp.zeros((HD + ONES, rows), jnp.float32)
    p_s[1] = jnp.zeros((chunk, rows), jnp.bfloat16)
    arrive_keys(0)
    for i in range(1, chunks):

        @pl.when(i * chunk < length)
        def _():
            copy_in(0, i).start()
            copy_in(1, i).start()

    s = dot_last(ks[0, :, :HD], qs[0])
    s_s[0] = s
    x_s[0] = tile_max(s)

    def weighted(i, k, part, index):
        return dot(jnp.concatenate([vs[i, part, tiles(k)].T, live[i, :, part]], axis=0), p_s[index, part, :])

    @pl.loop(0, count)
    def _(i):
        arrive_values(i)

        @pl.when(i + 1 < count)
        def _():
            arrive_keys(i + 1)

        for k in range(kv_heads):
            now, other = k % 2, 1 - k % 2
            next_k, next_i = (k + 1) % kv_heads, i if k + 1 < kv_heads else jnp.minimum(i + 1, count - 1)
            last_k, last_i = (k - 1) % kv_heads, i if k > 0 else jnp.maximum(i - 1, 0)
            before = m_s[k]
            top = jnp.maximum(before, jnp.max(x_s[now], axis=0, keepdims=True))
            m_s[k] = top
            highest, mixed = None, None
            for j in range(0, chunk, TILE):
                part = slice(j, j + TILE)
                s = dot_last(ks[next_i, part, tiles(next_k)], qs[next_k])
                s_s[other, part, :] = s
                high = tile_max(s)
                highest = high if highest is None else jnp.maximum(highest, high)
                p_s[now, part, :] = jnp.exp2((s_s[now, part, :] - top) * EXP2_SCALE).astype(jnp.bfloat16)
                if (j // TILE) % 2 == 1:
                    product = weighted(last_i, last_k, slice(j - TILE, j + TILE), other)
                    mixed = product if mixed is None else mixed + product
            x_s[other] = highest
            acc[last_k] = acc[last_k] * a_s[last_k] + mixed
            a_s[k] = jnp.exp2((before - top) * EXP2_SCALE)

    last = kv_heads - 1
    acc[last] = acc[last] * a_s[last] + weighted(count - 1, last, slice(0, chunk), last % 2)

    leaving = []
    for k in range(kv_heads):
        p = jnp.exp2((fresh_scores(k) - m_s[k]) * EXP2_SCALE)
        inverse = 1.0 / (acc[k, HD : HD + 1, :] + jnp.sum(p, axis=0, keepdims=True))
        p_s[0, (k % 2) * SPAN : (k % 2 + 1) * SPAN, :] = (p * inverse).astype(jnp.bfloat16)
        mixed = (acc[k, :HD, :] * inverse).T.astype(jnp.bfloat16)
        for h in range(group_size):
            out_s[:, tiles(k * group_size + h)] = mixed[h * SPAN : (h + 1) * SPAN, :]
        here = slice(k * group_size * HD, (k + 1) * group_size * HD)
        leaving.append(pltpu.make_async_copy(out_s.at[:, here], out_hbm.at[:, here], io_sems.at[2 + k]))
        leaving[-1].start()
        if k % 2 == 1:
            pf_s[k // 2] = p_s[0, : 2 * SPAN, :].T
    leaving.append(pltpu.make_async_copy(pf_s, pf_hbm, io_sems.at[2 + kv_heads]))
    leaving[-1].start()
    for copy in leaving:
        copy.wait()


def cache_attention(order, queries, fresh_keys, keys, values, lengths):
    slots, width = keys.shape[1:]
    kv_heads = width // HD
    group_size = queries.shape[1] // width
    rows = group_size * SPAN
    chunk = min(CHUNK, slots)
    chunks = slots // chunk
    hbm = pl.BlockSpec(memory_space=pltpu.HBM)
    result = (SPAN, queries.shape[1])
    weights = (kv_heads // 2, rows, 2 * SPAN)
    return pl.pallas_call(
        functools.partial(cache_kernel, order),
        in_specs=[pl.BlockSpec(memory_space=pltpu.SMEM)] + [hbm] * 4,
        out_specs=[hbm] * 2,
        scratch_shapes=[
            pltpu.VMEM((kv_heads, rows, HD), jnp.bfloat16),
            pltpu.VMEM((chunks, chunk, width), jnp.bfloat16),
            pltpu.VMEM((chunks, chunk, width), jnp.bfloat16),
            pltpu.VMEM((chunks, ONES, chunk), jnp.bfloat16),
            pltpu.VMEM((2, chunk, rows), jnp.float32),
            pltpu.VMEM((2, chunk, rows), jnp.bfloat16),
            pltpu.VMEM((2, 8, rows), jnp.float32),
            pltpu.VMEM((kv_heads, 1, rows), jnp.float32),
            pltpu.VMEM((kv_heads, 1, rows), jnp.float32),
            pltpu.VMEM((kv_heads, HD + ONES, rows), jnp.float32),
            pltpu.VMEM(result, jnp.bfloat16),
            pltpu.VMEM((SPAN, width), jnp.bfloat16),
            pltpu.VMEM(result, jnp.bfloat16),
            pltpu.VMEM(weights, jnp.bfloat16),
            pltpu.SemaphoreType.DMA((2, chunks)),
            pltpu.SemaphoreType.DMA((3 + kv_heads,)),
        ],
        out_shape=[
            jax.ShapeDtypeStruct(result, jnp.bfloat16),
            jax.ShapeDtypeStruct(weights, jnp.bfloat16),
        ],
        compiler_params=pltpu.CompilerParams(vmem_limit_bytes=57 * MIB),
        cost_estimate=FREE,
        name="cache_attention",
    )(lengths, queries, fresh_keys, keys, values)


def run_copies(copies, sems):
    copies = [pltpu.make_async_copy(src, dst, sems.at[i]) for i, (src, dst) in enumerate(copies)]
    for copy in copies:
        copy.start()
    for copy in copies:
        copy.wait()


def cross_kernel(d_hbm, u_hbm, w_hbm, early, late, *refs):
    maps_out, sems = [early, *refs[:-1]], refs[-1]
    part, core, quad = lax.axis_index("parts") % 2, lax.axis_index("tensor"), lax.axis_index("quad")
    width, cols = w_hbm.shape
    step = min(cols, width)
    size = width // 2 - late.shape[0]
    mine = pl.ds(pl.multiple_of(part * RANK, RANK), RANK)
    begin = part * (width // 2)
    copies = [
        (w_hbm.at[pl.ds(pl.multiple_of(begin, RANK), size), :], early.at[:size, :]),
        (w_hbm.at[pl.ds(pl.multiple_of(begin + size, RANK), late.shape[0]), :], late),
    ]
    for q, out in enumerate(maps_out):
        base = size if q == 0 else 0
        begin = core * (d_hbm.shape[1] // 2) + (quad ^ q) * width
        sources = [
            d_hbm.at[mine, pl.ds(pl.multiple_of(begin + first, step), step)] for first in range(0, width, step)
        ]
        sources += [u_hbm.at[mine, first : first + step] for first in range(0, cols, step)]
        for i, source in enumerate(sources):
            copies.append((source, out.at[base + i * RANK : base + (i + 1) * RANK, :step]))
    run_copies(copies, sems)


def cross_pack(downs, ups, weights, quads):
    vmem = pl.BlockSpec(memory_space=pltpu.VMEM)
    hbm = pl.BlockSpec(memory_space=pltpu.HBM)
    width, cols = weights.shape
    step = min(cols, width)
    pieces = (width + cols) // step
    first = width // 2 * 13 // 32 // RANK * RANK
    sizes = [(first + RANK * pieces, cols), (width // 2 - first, cols)]
    sizes += [(RANK * pieces, step)] * (quads - 1)
    return pl.pallas_call(
        cross_kernel,
        in_specs=[hbm] * 3,
        out_specs=[vmem] * len(sizes),
        out_shape=[jax.ShapeDtypeStruct(size, weights.dtype) for size in sizes],
        scratch_shapes=[pltpu.SemaphoreType.DMA((quads * pieces + 2,))],
        compiler_params=pltpu.CompilerParams(vmem_limit_bytes=57 * MIB),
        cost_estimate=FREE,
        name="cross_pack",
    )(downs, ups, weights)


def quad_kernel(x_hbm, d_hbm, u_hbm, *refs):
    outs, sems = refs[:-1], refs[-1]
    core, quad = lax.axis_index("tensor"), lax.axis_index("quad")
    tokens, features = x_hbm.shape
    ranks, cols = u_hbm.shape
    width = outs[0].shape[1]
    step = min(cols, width)
    copies = []
    for q, out in enumerate(outs):
        here = pl.ds(pl.multiple_of((quad ^ q) * width, width), width)
        copies.append((x_hbm.at[:, here], out.at[:tokens, :]))
        here = pl.ds(pl.multiple_of(core * features + (quad ^ q) * width, width), width)
        copies.append((d_hbm.at[:, here], out.at[tokens : tokens + ranks, :]))
        for slot, first, row, col in up_places(cols, width):
            row += tokens + ranks
            up = u_hbm.at[slot * RANK : (slot + 1) * RANK, first : first + step]
            copies.append((up, out.at[row : row + RANK, col : col + step]))
    run_copies(copies, sems)


def up_places(cols, width):
    step = min(cols, width)
    return [
        (slot, first, (slot * cols + first) // width * RANK, (slot * cols + first) % width)
        for slot in range(2)
        for first in range(0, cols, step)
    ]


def quad_pack(tokens, downs, ups, width, quads):
    vmem = pl.BlockSpec(memory_space=pltpu.VMEM)
    hbm = pl.BlockSpec(memory_space=pltpu.HBM)
    ranks, cols = ups.shape
    block = (tokens.shape[0] + ranks + RANK * (2 * cols // width), width)
    count = quads * (2 + len(up_places(cols, width)))
    return pl.pallas_call(
        quad_kernel,
        in_specs=[hbm] * 3,
        out_specs=[vmem] * quads,
        out_shape=[jax.ShapeDtypeStruct(block, tokens.dtype)] * quads,
        scratch_shapes=[pltpu.SemaphoreType.DMA((count,))],
        compiler_params=pltpu.CompilerParams(vmem_limit_bytes=57 * MIB),
        cost_estimate=FREE,
        name="quad_pack",
    )(tokens, downs, ups)


def near_kernel(tokens, quads, position, adapter, own_ref, *refs):
    maps_mine, maps_theirs, refs = refs[:2], refs[2:4], refs[4:]
    mine, theirs, out, ds, us = refs
    part, core = lax.axis_index("parts") % 2, lax.axis_index("tensor")
    wing, quad = lax.axis_index("wing"), lax.axis_index("quad")
    width = mine.shape[2]
    cols = own_ref.shape[1]
    ranks = 2 * RANK
    step = min(cols, width)
    for q in range(quads):
        rows = slice(q * ranks, (q + 1) * ranks)
        ds[0, rows, :] = mine[q, tokens : tokens + ranks, :]
        ds[1, rows, :] = theirs[q, tokens : tokens + ranks, :]
        for slot, first, row, col in up_places(cols, width):
            row += tokens + ranks
            place = q * ranks + slot * RANK
            us[place : place + RANK, first : first + step] = mine[q, row : row + RANK, col : col + step]
        for side in range(2):
            place = (quads + q) * ranks + side * RANK
            for i, first in enumerate(range(0, width, step)):
                row = i * RANK
                ds[0, place : place + RANK, first : first + step] = maps_mine[side][q, row : row + RANK, :]
                ds[1, place : place + RANK, first : first + step] = maps_theirs[side][q, row : row + RANK, :]
            for i, first in enumerate(range(0, cols, step)):
                row = (width // step + i) * RANK
                us[place : place + RANK, first : first + step] = maps_mine[side][q, row : row + RANK, :]

    x_mine = mine[:, :tokens, :].reshape(quads * tokens, width)
    x_theirs = theirs[:, :tokens, :].reshape(quads * tokens, width)
    shrink = dot_last(x_mine, ds[0]) + dot_last(x_theirs, ds[1])
    place = lax.broadcasted_iota(jnp.int32, (SPAN, us.shape[0]), 1)
    far = (place >= quads * ranks).astype(jnp.int32)
    index = place - far * (quads * ranks)
    group = (wing ^ far) * quads + (quad ^ (index >> 5))
    which = 2 * group + (((index >> 4) & 1) ^ (far * part))
    spans = tokens // SPAN
    masked = []
    for q in range(quads):
        for i in range(spans):
            slot = position[adapter[(wing * quads + (quad ^ q)) * spans + i]]
            row = (q * spans + i) * SPAN
            masked.append(jnp.where(which == slot, shrink[row : row + SPAN, :], 0.0))
    shrink = (jnp.concatenate(masked, axis=0) * ADAPTER_SCALE).astype(jnp.bfloat16)
    out[...] = dot(shrink, us[...])

    @pl.when(core == wing)
    def _():
        out[...] += dot(x_mine, own_ref[...])

    @pl.when(core != wing)
    def _():
        out[...] += dot(x_theirs, own_ref[...])


def near_products(mine, theirs, maps_mine, maps_theirs, own, position, adapter, tokens):
    quads, _, width = mine.shape
    cols = own.shape[1]
    ranks = 4 * quads * RANK
    vmem = pl.BlockSpec(memory_space=pltpu.VMEM)
    smem = pl.BlockSpec(memory_space=pltpu.SMEM)
    return pl.pallas_call(
        functools.partial(near_kernel, tokens, quads),
        in_specs=[smem, smem] + [vmem] * 7,
        out_specs=vmem,
        out_shape=jax.ShapeDtypeStruct((quads * tokens, cols), jnp.float32),
        scratch_shapes=[
            pltpu.VMEM((2, ranks, width), jnp.bfloat16),
            pltpu.VMEM((ranks, cols), jnp.bfloat16),
        ],
        compiler_params=pltpu.CompilerParams(vmem_limit_bytes=48 * MIB if quads > 4 else 24 * MIB),
        cost_estimate=FREE,
        name="near_products",
    )(position, adapter, own, *maps_mine, *maps_theirs, mine, theirs)


def far_kernel(tokens, quads, near, *refs):
    weights, (mine, theirs) = refs[:4], refs[4:6]
    outs, whole = refs[6:-1], refs[-1]
    part, core, wing = lax.axis_index("parts") % 2, lax.axis_index("tensor"), lax.axis_index("wing")
    for side in range(2):
        begin = (part if side == 0 else 1 - part) * (whole.shape[0] // 2)
        early, late = weights[2 * side : 2 * side + 2]
        size = whole.shape[0] // 2 - late.shape[0]
        whole[pl.ds(pl.multiple_of(begin, RANK), size), :] = early[:size, :]
        whole[pl.ds(pl.multiple_of(begin + size, RANK), late.shape[0]), :] = late[...]

    def store(blocks):
        x = blocks[:, :tokens, :].reshape(near.shape[0], -1)
        product = (near[...] + dot(x, whole[...])).astype(jnp.bfloat16)
        for q, out in enumerate(outs):
            out[...] = product[q * tokens : (q + 1) * tokens, :]

    @pl.when(core == wing)
    def _():
        store(theirs)

    @pl.when(core != wing)
    def _():
        store(mine)


def far_products(mine, theirs, near, weights, tokens):
    quads, _, width = mine.shape
    cols = near.shape[1]
    vmem = pl.BlockSpec(memory_space=pltpu.VMEM)
    return pl.pallas_call(
        functools.partial(far_kernel, tokens, quads),
        in_specs=[vmem] * (3 + len(weights)),
        out_specs=[vmem] * quads,
        out_shape=[jax.ShapeDtypeStruct((tokens, cols), jnp.bfloat16)] * quads,
        scratch_shapes=[pltpu.VMEM((width, cols), jnp.bfloat16)],
        compiler_params=pltpu.CompilerParams(vmem_limit_bytes=48 * MIB if quads > 4 else 16 * MIB),
        cost_estimate=FREE,
        name="far_products",
    )(near, *weights, mine, theirs)


def finish_kernel(spans, lens, *refs):
    out_ref, values_ref = refs[-2:]
    mixed, probs, parts = refs[:spans], refs[spans : 2 * spans], refs[2 * spans : -2]
    total = parts[0][...].astype(jnp.float32)
    for part in parts[1:]:
        total = total + part[...].astype(jnp.float32)
    values_ref[...] = total.astype(jnp.bfloat16)
    none = jnp.zeros((SPAN, HD), jnp.bfloat16)
    group_size = out_ref.shape[1] // values_ref.shape[1]
    for order in range(spans):
        span = span_of(order, lens)
        rows = pl.ds(pl.multiple_of(span * SPAN, SPAN), SPAN)
        for pair in range(probs[order].shape[0]):
            left = values_ref[rows, 2 * pair * HD : (2 * pair + 1) * HD]
            right = values_ref[rows, (2 * pair + 1) * HD : (2 * pair + 2) * HD]
            both = jnp.concatenate(
                [jnp.concatenate([left, none], axis=1), jnp.concatenate([none, right], axis=1)], axis=0
            )
            fresh = dot(probs[order][pair], both)
            for side in range(2):
                for h in range(group_size):
                    col = ((2 * pair + side) * group_size + h) * HD
                    added = fresh[h * SPAN : (h + 1) * SPAN, side * HD : (side + 1) * HD]
                    before = mixed[order][:, col : col + HD].astype(jnp.float32)
                    out_ref[rows, col : col + HD] = (before + added).astype(jnp.bfloat16)


def finish(lengths, mixed, fresh_probs, parts, q_width):
    tokens, cols = parts[0].shape
    vmem = pl.BlockSpec(memory_space=pltpu.VMEM)
    smem = pl.BlockSpec(memory_space=pltpu.SMEM)
    return pl.pallas_call(
        functools.partial(finish_kernel, len(mixed)),
        in_specs=[smem] + [vmem] * (len(parts) + 2 * len(mixed)),
        out_specs=[vmem] * 2,
        out_shape=[
            jax.ShapeDtypeStruct((tokens, q_width), jnp.bfloat16),
            jax.ShapeDtypeStruct((tokens, cols), jnp.bfloat16),
        ],
        compiler_params=pltpu.CompilerParams(vmem_limit_bytes=16 * MIB),
        cost_estimate=FREE,
        name="finish_attention",
    )(lengths, *mixed, *fresh_probs, *parts)


def on_device(
    normed_inputs,
    value_matrix,
    adapter_down_weight,
    adapter_up_weight,
    adapter_position,
    span_adapter_index,
    queries,
    incoming_keys,
    stored_keys,
    stored_values,
    cache_length,
):
    quads = lax.axis_size("quad")
    parts_swap = [(i, i ^ 1) for i in range(lax.axis_size("parts"))]
    width, cols = value_matrix.shape
    downs = adapter_down_weight.reshape(-1, adapter_down_weight.shape[2])
    ups = adapter_up_weight.reshape(-1, cols)

    kv_heads = cols // HD
    def attention(order, lengths):
        return cache_attention(order, queries, incoming_keys, stored_keys, stored_values, lengths)

    def after(value, *others):
        return lax.optimization_barrier((value, *others))[0]

    def to_quad(value, q):
        return lax.ppermute(value, "quad", [(j, j ^ q) for j in range(quads)])

    def to_other_wing(value, q):
        pairs = [(w * quads + j, (1 - w) * quads + (j ^ q)) for w in range(2) for j in range(quads)]
        return lax.ppermute(value, ("wing", "quad"), pairs)

    early, late, *maps = cross_pack(downs, ups, value_matrix, quads)
    blocks = quad_pack(after(normed_inputs, early), downs, ups, width, quads)
    order = [*range(quads // 2, quads), *range(1, quads // 2)]
    mine = [to_quad(blocks[q], q) for q in order]
    early = lax.ppermute(early, "wing", SWAP)
    maps = [to_other_wing(each, q + 1) for q, each in enumerate(maps)]

    attn = [attention(0, after(cache_length, blocks[0]))]
    early, *maps = lax.optimization_barrier((early, *maps, attn[0][1]))[:-1]
    step = maps[0].shape[1]
    maps = jnp.stack([early[early.shape[0] - maps[0].shape[0] :, :step], *maps])
    late = lax.ppermute(after(late, early), "wing", SWAP)
    early_other = lax.ppermute(early, "parts", parts_swap)
    maps_other = lax.ppermute(maps, "parts", parts_swap)

    attn.append(attention(1, after(cache_length, early, maps)))
    late, early_other, maps_other, *mine = lax.optimization_barrier(
        (late, early_other, maps_other, *mine, attn[1][1])
    )[:-1]
    mine = jnp.stack([blocks[0]] + [mine[order.index(q)] for q in range(1, quads)])
    late_other = lax.ppermute(late, "parts", parts_swap)
    maps_mine = (maps, maps_other)
    maps_theirs = [lax.ppermute(each, "tensor", SWAP) for each in maps_mine]
    theirs = lax.ppermute(mine, "tensor", SWAP)

    tokens, q_width = queries.shape
    near = near_products(
        mine, theirs, maps_mine, maps_theirs, value_matrix, adapter_position, span_adapter_index, tokens
    )
    products = far_products(mine, theirs, near, (early, late, early_other, late_other), tokens)
    parts = [products[0]] + [to_quad(products[q], q) for q in range(1, quads)]
    mixed, fresh_probs = zip(*attn)
    attended, incoming_values = finish(cache_length, mixed, fresh_probs, parts, q_width)
    return (attended, incoming_values)


def solution(mesh):
    sizes = mesh.devices.shape
    cut = Mesh(
        mesh.devices.reshape(sizes[0], 2, sizes[1] // 2, sizes[2]), ("parts", "wing", "quad", "tensor")
    )
    group = ("wing", "quad")
    home = ("parts", "wing", "quad")
    in_specs = (
        P(home, "tensor"),
        P(group, "tensor"),
        P(group, None, None),
        P(group, None, "tensor"),
        P(),
        P("parts"),
        P(home, "tensor"),
        P(home, "tensor"),
        P(home, None, "tensor"),
        P(home, None, "tensor"),
        P(home),
    )
    out_specs = (P(home, "tensor"), P(home, "tensor"))
    return jax.shard_map(
        on_device, mesh=cut, in_specs=in_specs, out_specs=out_specs, check_vma=False
    )
```

```python
import functools
import math

import jax
import jax.numpy as jnp
from jax import lax
from jax.experimental import pallas as pl
from jax.experimental.pallas import tpu as pltpu
from jax.sharding import Mesh
from jax.sharding import PartitionSpec as P

HD = 128
RANK = 16
SPAN = 64
CHUNK = 512
ONES = 16
TILE = 128
ADAPTER_SCALE = 2.0
EXP2_SCALE = math.log2(math.e) / math.sqrt(HD)
DEAD = -1e30
MIB = 1024 * 1024
SWAP = [(0, 1), (1, 0)]
FREE = pl.CostEstimate(flops=1, bytes_accessed=1, transcendentals=0)


def dot_last(a, b):
    return lax.dot_general(a, b, (((1,), (1,)), ((), ())), preferred_element_type=jnp.float32)


def dot(a, b):
    return jnp.dot(a, b, preferred_element_type=jnp.float32)


def span_of(order, lens):
    longer = (lens[1] > lens[0]).astype(jnp.int32)
    return longer if order == 0 else 1 - longer


def cache_kernel(order, lens, q_hbm, fk_hbm, k_hbm, v_hbm, out_hbm, pf_hbm, qs, ks, vs, live, s_s, p_s, x_s, m_s, a_s, acc, q_s, fk_s, out_s, pf_s, sems, io_sems):
    span = span_of(order, lens)
    length = lens[span]
    chunks, chunk, _ = ks.shape
    kv_heads, rows, _ = qs.shape
    group_size = rows // SPAN
    count = (length + chunk - 1) // chunk
    mine = pl.ds(pl.multiple_of(span * SPAN, SPAN), SPAN)

    def copy_in(side, i):
        slots = pl.ds(pl.multiple_of(i * chunk, chunk), chunk)
        source, target = ((k_hbm, ks), (v_hbm, vs))[side]
        return pltpu.make_async_copy(source.at[span, slots, :], target.at[i], sems.at[side, i])

    small = [
        pltpu.make_async_copy(q_hbm.at[mine, :], q_s, io_sems.at[0]),
        pltpu.make_async_copy(fk_hbm.at[mine, :], fk_s, io_sems.at[1]),
    ]
    for copy in small:
        copy.start()
    copy_in(0, 0).start()

    def dead_slots(i):
        return i * chunk + lax.broadcasted_iota(jnp.int32, ks.shape[1:], 0) >= length

    def arrive_keys(i):
        copy_in(0, i).wait()

        @pl.when((i + 1) * chunk > length)
        def _():
            keys = ks[i].astype(jnp.float32)
            ks[i] = jnp.where(dead_slots(i), keys[:1, :], keys).astype(jnp.bfloat16)

    def arrive_values(i):
        copy_in(1, i).wait()
        slot = i * chunk + lax.broadcasted_iota(jnp.int32, (ONES, chunk), 1)
        live[i] = (slot < length).astype(jnp.float32).astype(jnp.bfloat16)

        @pl.when((i + 1) * chunk > length)
        def _():
            vs[i] = jnp.where(dead_slots(i), 0.0, vs[i].astype(jnp.float32)).astype(jnp.bfloat16)

    def fresh_scores(k):
        s = dot_last(fk_s[:, k * HD : (k + 1) * HD], qs[k])
        key = lax.broadcasted_iota(jnp.int32, (SPAN, rows), 0)
        token = lax.broadcasted_iota(jnp.int32, (SPAN, rows), 1) % SPAN
        return jnp.where(key <= token, s, DEAD)

    def tile_max(s):
        return jnp.max(s.reshape(s.shape[0] // 8, 8, rows), axis=0)

    def tiles(k):
        return slice(k * HD, (k + 1) * HD)

    for copy in small:
        copy.wait()
    copy_in(1, 0).start()
    for k in range(kv_heads):
        for h in range(group_size):
            qs[k, h * SPAN : (h + 1) * SPAN, :] = q_s[:, tiles(k * group_size + h)]
        m_s[k] = jnp.max(fresh_scores(k), axis=0, keepdims=True)
        a_s[k] = jnp.ones((1, rows), jnp.float32)
        acc[k] = jnp.zeros((HD + ONES, rows), jnp.float32)
    p_s[1] = jnp.zeros((chunk, rows), jnp.bfloat16)
    arrive_keys(0)
    for i in range(1, chunks):

        @pl.when(i * chunk < length)
        def _():
            copy_in(0, i).start()
            copy_in(1, i).start()

    s = dot_last(ks[0, :, :HD], qs[0])
    s_s[0] = s
    x_s[0] = tile_max(s)

    def weighted(i, k, part, index):
        return dot(jnp.concatenate([vs[i, part, tiles(k)].T, live[i, :, part]], axis=0), p_s[index, part, :])

    @pl.loop(0, count)
    def _(i):
        arrive_values(i)

        @pl.when(i + 1 < count)
        def _():
            arrive_keys(i + 1)

        for k in range(kv_heads):
            now, other = k % 2, 1 - k % 2
            next_k, next_i = (k + 1) % kv_heads, i if k + 1 < kv_heads else jnp.minimum(i + 1, count - 1)
            last_k, last_i = (k - 1) % kv_heads, i if k > 0 else jnp.maximum(i - 1, 0)
            before = m_s[k]
            top = jnp.maximum(before, jnp.max(x_s[now], axis=0, keepdims=True))
            m_s[k] = top
            highest, mixed = None, None
            for j in range(0, chunk, TILE):
                part = slice(j, j + TILE)
                s = dot_last(ks[next_i, part, tiles(next_k)], qs[next_k])
                s_s[other, part, :] = s
                high = tile_max(s)
                highest = high if highest is None else jnp.maximum(highest, high)
                p_s[now, part, :] = jnp.exp2((s_s[now, part, :] - top) * EXP2_SCALE).astype(jnp.bfloat16)
                if (j // TILE) % 2 == 1:
                    product = weighted(last_i, last_k, slice(j - TILE, j + TILE), other)
                    mixed = product if mixed is None else mixed + product
            x_s[other] = highest
            acc[last_k] = acc[last_k] * a_s[last_k] + mixed
            a_s[k] = jnp.exp2((before - top) * EXP2_SCALE)

    last = kv_heads - 1
    acc[last] = acc[last] * a_s[last] + weighted(count - 1, last, slice(0, chunk), last % 2)

    leaving = []
    for k in range(kv_heads):
        p = jnp.exp2((fresh_scores(k) - m_s[k]) * EXP2_SCALE)
        inverse = 1.0 / (acc[k, HD : HD + 1, :] + jnp.sum(p, axis=0, keepdims=True))
        p_s[0, (k % 2) * SPAN : (k % 2 + 1) * SPAN, :] = (p * inverse).astype(jnp.bfloat16)
        mixed = (acc[k, :HD, :] * inverse).T.astype(jnp.bfloat16)
        for h in range(group_size):
            out_s[:, tiles(k * group_size + h)] = mixed[h * SPAN : (h + 1) * SPAN, :]
        here = slice(k * group_size * HD, (k + 1) * group_size * HD)
        leaving.append(pltpu.make_async_copy(out_s.at[:, here], out_hbm.at[:, here], io_sems.at[2 + k]))
        leaving[-1].start()
        if k % 2 == 1:
            pf_s[k // 2] = p_s[0, : 2 * SPAN, :].T
    leaving.append(pltpu.make_async_copy(pf_s, pf_hbm, io_sems.at[2 + kv_heads]))
    leaving[-1].start()
    for copy in leaving:
        copy.wait()


def cache_attention(order, queries, fresh_keys, keys, values, lengths):
    slots, width = keys.shape[1:]
    kv_heads = width // HD
    group_size = queries.shape[1] // width
    rows = group_size * SPAN
    chunk = min(CHUNK, slots)
    chunks = slots // chunk
    hbm = pl.BlockSpec(memory_space=pltpu.HBM)
    result = (SPAN, queries.shape[1])
    weights = (kv_heads // 2, rows, 2 * SPAN)
    return pl.pallas_call(
        functools.partial(cache_kernel, order),
        in_specs=[pl.BlockSpec(memory_space=pltpu.SMEM)] + [hbm] * 4,
        out_specs=[hbm] * 2,
        scratch_shapes=[
            pltpu.VMEM((kv_heads, rows, HD), jnp.bfloat16),
            pltpu.VMEM((chunks, chunk, width), jnp.bfloat16),
            pltpu.VMEM((chunks, chunk, width), jnp.bfloat16),
            pltpu.VMEM((chunks, ONES, chunk), jnp.bfloat16),
            pltpu.VMEM((2, chunk, rows), jnp.float32),
            pltpu.VMEM((2, chunk, rows), jnp.bfloat16),
            pltpu.VMEM((2, 8, rows), jnp.float32),
            pltpu.VMEM((kv_heads, 1, rows), jnp.float32),
            pltpu.VMEM((kv_heads, 1, rows), jnp.float32),
            pltpu.VMEM((kv_heads, HD + ONES, rows), jnp.float32),
            pltpu.VMEM(result, jnp.bfloat16),
            pltpu.VMEM((SPAN, width), jnp.bfloat16),
            pltpu.VMEM(result, jnp.bfloat16),
            pltpu.VMEM(weights, jnp.bfloat16),
            pltpu.SemaphoreType.DMA((2, chunks)),
            pltpu.SemaphoreType.DMA((3 + kv_heads,)),
        ],
        out_shape=[
            jax.ShapeDtypeStruct(result, jnp.bfloat16),
            jax.ShapeDtypeStruct(weights, jnp.bfloat16),
        ],
        compiler_params=pltpu.CompilerParams(vmem_limit_bytes=57 * MIB),
        cost_estimate=FREE,
        name="cache_attention",
    )(lengths, queries, fresh_keys, keys, values)


def pack_kernel(x_hbm, d_hbm, u_hbm, w_hbm, early, late, *refs):
    sems = refs[-1]
    quads = len(refs) // 2
    maps_out, tokens_out = [early, *refs[: quads - 1]], refs[quads - 1 : -1]
    part, core, quad = lax.axis_index("parts") % 2, lax.axis_index("tensor"), lax.axis_index("quad")
    width, cols = w_hbm.shape
    tokens, features = x_hbm.shape
    ranks = u_hbm.shape[0]
    step = min(cols, width)
    size = width // 2 - late.shape[0]
    mine = pl.ds(pl.multiple_of(part * RANK, RANK), RANK)
    begin = part * (width // 2)
    copies = [
        (w_hbm.at[pl.ds(pl.multiple_of(begin, RANK), size), :], early.at[:size, :]),
        (w_hbm.at[pl.ds(pl.multiple_of(begin + size, RANK), late.shape[0]), :], late),
    ]
    for q, out in enumerate(tokens_out):
        here = pl.ds(pl.multiple_of((quad ^ q) * width, width), width)
        copies.append((x_hbm.at[:, here], out.at[:tokens, :]))
        here = pl.ds(pl.multiple_of(core * features + (quad ^ q) * width, width), width)
        copies.append((d_hbm.at[:, here], out.at[tokens : tokens + ranks, :]))
    for q, out in enumerate(maps_out):
        base = size if q == 0 else 0
        begin = core * features + (quad ^ q) * width
        sources = [
            d_hbm.at[mine, pl.ds(pl.multiple_of(begin + first, step), step)] for first in range(0, width, step)
        ]
        sources += [u_hbm.at[mine, first : first + step] for first in range(0, cols, step)]
        for i, source in enumerate(sources):
            copies.append((source, out.at[base + i * RANK : base + (i + 1) * RANK, :step]))
    for out in tokens_out:
        for slot, first, row, col in up_places(cols, width):
            row += tokens + ranks
            up = u_hbm.at[slot * RANK : (slot + 1) * RANK, first : first + step]
            copies.append((up, out.at[row : row + RANK, col : col + step]))
    copies = [pltpu.make_async_copy(src, dst, sems.at[i]) for i, (src, dst) in enumerate(copies)]
    for copy in copies:
        copy.start()
    for copy in copies:
        copy.wait()


def pack(tokens, downs, ups, weights, quads):
    hbm = pl.BlockSpec(memory_space=pltpu.HBM)
    ranks, cols = ups.shape
    width = weights.shape[0]
    step = min(cols, width)
    pieces = (width + cols) // step
    first = width // 2 * 9 // 32 // RANK * RANK
    sizes = [(first + RANK * pieces, cols), (width // 2 - first, cols)]
    sizes += [(RANK * pieces, step)] * (quads - 1)
    sizes += [(tokens.shape[0] + ranks + RANK * (2 * cols // width), width)] * quads
    count = 2 + quads * (2 + pieces + len(up_places(cols, width)))
    return pl.pallas_call(
        pack_kernel,
        in_specs=[hbm] * 4,
        out_specs=[hbm] * len(sizes),
        out_shape=[jax.ShapeDtypeStruct(size, tokens.dtype) for size in sizes],
        scratch_shapes=[pltpu.SemaphoreType.DMA((count,))],
        compiler_params=pltpu.CompilerParams(vmem_limit_bytes=57 * MIB),
        cost_estimate=FREE,
        name="pack",
    )(tokens, downs, ups, weights)


def up_places(cols, width):
    step = min(cols, width)
    return [
        (slot, first, (slot * cols + first) // width * RANK, (slot * cols + first) % width)
        for slot in range(2)
        for first in range(0, cols, step)
    ]


def near_kernel(tokens, quads, position, adapter, own_ref, *refs):
    maps_mine, maps_theirs, refs = refs[:2], refs[2:4], refs[4:]
    mine, theirs, out, ds, us = refs
    part, core = lax.axis_index("parts") % 2, lax.axis_index("tensor")
    wing, quad = lax.axis_index("wing"), lax.axis_index("quad")
    width = mine.shape[2]
    cols = own_ref.shape[1]
    ranks = 2 * RANK
    step = min(cols, width)
    for q in range(quads):
        rows = slice(q * ranks, (q + 1) * ranks)
        ds[0, rows, :] = mine[q, tokens : tokens + ranks, :]
        ds[1, rows, :] = theirs[q, tokens : tokens + ranks, :]
        for slot, first, row, col in up_places(cols, width):
            row += tokens + ranks
            place = q * ranks + slot * RANK
            us[place : place + RANK, first : first + step] = mine[q, row : row + RANK, col : col + step]
        for side in range(2):
            place = (quads + q) * ranks + side * RANK
            for i, first in enumerate(range(0, width, step)):
                row = i * RANK
                ds[0, place : place + RANK, first : first + step] = maps_mine[side][q, row : row + RANK, :]
                ds[1, place : place + RANK, first : first + step] = maps_theirs[side][q, row : row + RANK, :]
            for i, first in enumerate(range(0, cols, step)):
                row = (width // step + i) * RANK
                us[place : place + RANK, first : first + step] = maps_mine[side][q, row : row + RANK, :]

    x_mine = mine[:, :tokens, :].reshape(quads * tokens, width)
    x_theirs = theirs[:, :tokens, :].reshape(quads * tokens, width)
    shrink = dot_last(x_mine, ds[0]) + dot_last(x_theirs, ds[1])
    place = lax.broadcasted_iota(jnp.int32, (SPAN, us.shape[0]), 1)
    far = (place >= quads * ranks).astype(jnp.int32)
    index = place - far * (quads * ranks)
    group = (wing ^ far) * quads + (quad ^ (index >> 5))
    which = 2 * group + (((index >> 4) & 1) ^ (far * part))
    spans = tokens // SPAN
    masked = []
    for q in range(quads):
        for i in range(spans):
            slot = position[adapter[(wing * quads + (quad ^ q)) * spans + i]]
            row = (q * spans + i) * SPAN
            masked.append(jnp.where(which == slot, shrink[row : row + SPAN, :], 0.0))
    shrink = (jnp.concatenate(masked, axis=0) * ADAPTER_SCALE).astype(jnp.bfloat16)
    out[...] = dot(shrink, us[...])

    @pl.when(core == wing)
    def _():
        out[...] += dot(x_mine, own_ref[...])

    @pl.when(core != wing)
    def _():
        out[...] += dot(x_theirs, own_ref[...])


def near_products(mine, theirs, maps_mine, maps_theirs, own, position, adapter, tokens):
    quads, _, width = mine.shape
    cols = own.shape[1]
    ranks = 4 * quads * RANK
    vmem = pl.BlockSpec(memory_space=pltpu.VMEM)
    smem = pl.BlockSpec(memory_space=pltpu.SMEM)
    return pl.pallas_call(
        functools.partial(near_kernel, tokens, quads),
        in_specs=[smem, smem] + [vmem] * 7,
        out_specs=vmem,
        out_shape=jax.ShapeDtypeStruct((quads * tokens, cols), jnp.float32),
        scratch_shapes=[
            pltpu.VMEM((2, ranks, width), jnp.bfloat16),
            pltpu.VMEM((ranks, cols), jnp.bfloat16),
        ],
        compiler_params=pltpu.CompilerParams(vmem_limit_bytes=48 * MIB if quads > 4 else 24 * MIB),
        cost_estimate=FREE,
        name="near_products",
    )(position, adapter, own, *maps_mine, *maps_theirs, mine, theirs)


def far_kernel(tokens, quads, near, *refs):
    weights, (mine, theirs) = refs[:4], refs[4:6]
    outs, whole = refs[6:-1], refs[-1]
    part, core, wing = lax.axis_index("parts") % 2, lax.axis_index("tensor"), lax.axis_index("wing")
    for side in range(2):
        begin = (part if side == 0 else 1 - part) * (whole.shape[0] // 2)
        early, late = weights[2 * side : 2 * side + 2]
        size = whole.shape[0] // 2 - late.shape[0]
        whole[pl.ds(pl.multiple_of(begin, RANK), size), :] = early[:size, :]
        whole[pl.ds(pl.multiple_of(begin + size, RANK), late.shape[0]), :] = late[...]

    def store(blocks):
        x = blocks[:, :tokens, :].reshape(near.shape[0], -1)
        product = (near[...] + dot(x, whole[...])).astype(jnp.bfloat16)
        for q, out in enumerate(outs):
            out[...] = product[q * tokens : (q + 1) * tokens, :]

    @pl.when(core == wing)
    def _():
        store(theirs)

    @pl.when(core != wing)
    def _():
        store(mine)


def far_products(mine, theirs, near, weights, tokens):
    quads, _, width = mine.shape
    cols = near.shape[1]
    vmem = pl.BlockSpec(memory_space=pltpu.VMEM)
    return pl.pallas_call(
        functools.partial(far_kernel, tokens, quads),
        in_specs=[vmem] * (3 + len(weights)),
        out_specs=[vmem] * quads,
        out_shape=[jax.ShapeDtypeStruct((tokens, cols), jnp.bfloat16)] * quads,
        scratch_shapes=[pltpu.VMEM((width, cols), jnp.bfloat16)],
        compiler_params=pltpu.CompilerParams(vmem_limit_bytes=48 * MIB if quads > 4 else 16 * MIB),
        cost_estimate=FREE,
        name="far_products",
    )(near, *weights, mine, theirs)


def finish_kernel(spans, lens, *refs):
    out_ref, values_ref = refs[-2:]
    mixed, probs, parts = refs[:spans], refs[spans : 2 * spans], refs[2 * spans : -2]
    total = parts[0][...].astype(jnp.float32)
    for part in parts[1:]:
        total = total + part[...].astype(jnp.float32)
    values_ref[...] = total.astype(jnp.bfloat16)
    none = jnp.zeros((SPAN, HD), jnp.bfloat16)
    group_size = out_ref.shape[1] // values_ref.shape[1]
    for order in range(spans):
        span = span_of(order, lens)
        rows = pl.ds(pl.multiple_of(span * SPAN, SPAN), SPAN)
        for pair in range(probs[order].shape[0]):
            left = values_ref[rows, 2 * pair * HD : (2 * pair + 1) * HD]
            right = values_ref[rows, (2 * pair + 1) * HD : (2 * pair + 2) * HD]
            both = jnp.concatenate(
                [jnp.concatenate([left, none], axis=1), jnp.concatenate([none, right], axis=1)], axis=0
            )
            fresh = dot(probs[order][pair], both)
            for side in range(2):
                for h in range(group_size):
                    col = ((2 * pair + side) * group_size + h) * HD
                    added = fresh[h * SPAN : (h + 1) * SPAN, side * HD : (side + 1) * HD]
                    before = mixed[order][:, col : col + HD].astype(jnp.float32)
                    out_ref[rows, col : col + HD] = (before + added).astype(jnp.bfloat16)


def finish(lengths, mixed, fresh_probs, parts, q_width):
    tokens, cols = parts[0].shape
    vmem = pl.BlockSpec(memory_space=pltpu.VMEM)
    smem = pl.BlockSpec(memory_space=pltpu.SMEM)
    return pl.pallas_call(
        functools.partial(finish_kernel, len(mixed)),
        in_specs=[smem] + [vmem] * (len(parts) + 2 * len(mixed)),
        out_specs=[vmem] * 2,
        out_shape=[
            jax.ShapeDtypeStruct((tokens, q_width), jnp.bfloat16),
            jax.ShapeDtypeStruct((tokens, cols), jnp.bfloat16),
        ],
        compiler_params=pltpu.CompilerParams(vmem_limit_bytes=16 * MIB),
        cost_estimate=FREE,
        name="finish_attention",
    )(lengths, *mixed, *fresh_probs, *parts)


def on_device(
    normed_inputs,
    value_matrix,
    adapter_down_weight,
    adapter_up_weight,
    adapter_position,
    span_adapter_index,
    queries,
    incoming_keys,
    stored_keys,
    stored_values,
    cache_length,
):
    quads = lax.axis_size("quad")
    parts_swap = [(i, i ^ 1) for i in range(lax.axis_size("parts"))]
    width, cols = value_matrix.shape
    downs = adapter_down_weight.reshape(-1, adapter_down_weight.shape[2])
    ups = adapter_up_weight.reshape(-1, cols)

    kv_heads = cols // HD
    def attention(order, lengths):
        return cache_attention(order, queries, incoming_keys, stored_keys, stored_values, lengths)

    def after(value, *others):
        return lax.optimization_barrier((value, *others))[0]

    def to_quad(value, q):
        return lax.ppermute(value, "quad", [(j, j ^ q) for j in range(quads)])

    def to_other_wing(value, q):
        pairs = [(w * quads + j, (1 - w) * quads + (j ^ q)) for w in range(2) for j in range(quads)]
        return lax.ppermute(value, ("wing", "quad"), pairs)

    early, late, *blocks = pack(normed_inputs, downs, ups, value_matrix, quads)
    maps, blocks = blocks[: quads - 1], blocks[quads - 1 :]
    order = [*range(quads // 2, quads), *range(1, quads // 2)]
    mine = [to_quad(blocks[q], q) for q in order]
    early = lax.ppermute(early, "wing", SWAP)
    maps = [to_other_wing(each, q + 1) for q, each in enumerate(maps)]

    attn = [attention(0, after(cache_length, blocks[0]))]
    early, *maps = lax.optimization_barrier((early, *maps, attn[0][1]))[:-1]
    step = maps[0].shape[1]
    maps = jnp.stack([early[early.shape[0] - maps[0].shape[0] :, :step], *maps])
    late = lax.ppermute(after(late, attn[0][1]), "wing", SWAP)
    early_other = lax.ppermute(early, "parts", parts_swap)
    maps_other = lax.ppermute(maps, "parts", parts_swap)

    attn.append(attention(1, after(cache_length, early, maps)))
    late, early_other, maps_other, *mine = lax.optimization_barrier(
        (late, early_other, maps_other, *mine, attn[1][1])
    )[:-1]
    mine = jnp.stack([blocks[0]] + [mine[order.index(q)] for q in range(1, quads)])
    late_other = lax.ppermute(late, "parts", parts_swap)
    maps_mine = (maps, maps_other)
    maps_theirs = [lax.ppermute(each, "tensor", SWAP) for each in maps_mine]
    theirs = lax.ppermute(mine, "tensor", SWAP)

    tokens, q_width = queries.shape
    near = near_products(
        mine, theirs, maps_mine, maps_theirs, value_matrix, adapter_position, span_adapter_index, tokens
    )
    products = far_products(mine, theirs, near, (early, late, early_other, late_other), tokens)
    parts = [products[0]] + [to_quad(products[q], q) for q in range(1, quads)]
    mixed, fresh_probs = zip(*attn)
    attended, incoming_values = finish(cache_length, mixed, fresh_probs, parts, q_width)
    return (attended, incoming_values)


def solution(mesh):
    sizes = mesh.devices.shape
    cut = Mesh(
        mesh.devices.reshape(sizes[0], 2, sizes[1] // 2, sizes[2]), ("parts", "wing", "quad", "tensor")
    )
    group = ("wing", "quad")
    home = ("parts", "wing", "quad")
    in_specs = (
        P(home, "tensor"),
        P(group, "tensor"),
        P(group, None, None),
        P(group, None, "tensor"),
        P(),
        P("parts"),
        P(home, "tensor"),
        P(home, "tensor"),
        P(home, None, "tensor"),
        P(home, None, "tensor"),
        P(home),
    )
    out_specs = (P(home, "tensor"), P(home, "tensor"))
    return jax.shard_map(
        on_device, mesh=cut, in_specs=in_specs, out_specs=out_specs, check_vma=False
    )
```

```python
import functools
import math

import jax
import jax.numpy as jnp
from jax import lax
from jax.experimental import pallas as pl
from jax.experimental.pallas import tpu as pltpu
from jax.sharding import Mesh
from jax.sharding import PartitionSpec as P

HD = 128
RANK = 16
SPAN = 64
CHUNK = 512
ONES = 16
TILE = 128
ADAPTER_SCALE = 2.0
EXP2_SCALE = math.log2(math.e) / math.sqrt(HD)
DEAD = -1e30
MIB = 1024 * 1024
SWAP = [(0, 1), (1, 0)]
FREE = pl.CostEstimate(flops=1, bytes_accessed=1, transcendentals=0)


def dot_last(a, b):
    return lax.dot_general(a, b, (((1,), (1,)), ((), ())), preferred_element_type=jnp.float32)


def dot(a, b):
    return jnp.dot(a, b, preferred_element_type=jnp.float32)


def span_of(order, lens):
    longer = (lens[1] > lens[0]).astype(jnp.int32)
    return longer if order == 0 else 1 - longer


def cache_kernel(order, lens, q_hbm, fk_hbm, k_hbm, v_hbm, out_hbm, pf_hbm, qs, ks, vs, live, s_s, p_s, x_s, m_s, a_s, acc, q_s, fk_s, out_s, pf_s, sems, io_sems):
    span = span_of(order, lens)
    length = lens[span]
    chunks, chunk, _ = ks.shape
    kv_heads, rows, _ = qs.shape
    group_size = rows // SPAN
    count = (length + chunk - 1) // chunk
    mine = pl.ds(pl.multiple_of(span * SPAN, SPAN), SPAN)

    def copy_in(side, i):
        slots = pl.ds(pl.multiple_of(i * chunk, chunk), chunk)
        source, target = ((k_hbm, ks), (v_hbm, vs))[side]
        return pltpu.make_async_copy(source.at[span, slots, :], target.at[i], sems.at[side, i])

    small = [
        pltpu.make_async_copy(q_hbm.at[mine, :], q_s, io_sems.at[0]),
        pltpu.make_async_copy(fk_hbm.at[mine, :], fk_s, io_sems.at[1]),
    ]
    for copy in small:
        copy.start()
    copy_in(0, 0).start()

    def dead_slots(i):
        return i * chunk + lax.broadcasted_iota(jnp.int32, ks.shape[1:], 0) >= length

    def arrive_keys(i):
        copy_in(0, i).wait()

        @pl.when((i + 1) * chunk > length)
        def _():
            keys = ks[i].astype(jnp.float32)
            ks[i] = jnp.where(dead_slots(i), keys[:1, :], keys).astype(jnp.bfloat16)

    def arrive_values(i):
        copy_in(1, i).wait()
        slot = i * chunk + lax.broadcasted_iota(jnp.int32, (ONES, chunk), 1)
        live[i] = (slot < length).astype(jnp.float32).astype(jnp.bfloat16)

        @pl.when((i + 1) * chunk > length)
        def _():
            vs[i] = jnp.where(dead_slots(i), 0.0, vs[i].astype(jnp.float32)).astype(jnp.bfloat16)

    def fresh_scores(k):
        s = dot_last(fk_s[:, k * HD : (k + 1) * HD], qs[k])
        key = lax.broadcasted_iota(jnp.int32, (SPAN, rows), 0)
        token = lax.broadcasted_iota(jnp.int32, (SPAN, rows), 1) % SPAN
        return jnp.where(key <= token, s, DEAD)

    def tile_max(s):
        return jnp.max(s.reshape(s.shape[0] // 8, 8, rows), axis=0)

    def tiles(k):
        return slice(k * HD, (k + 1) * HD)

    for copy in small:
        copy.wait()
    copy_in(1, 0).start()
    for k in range(kv_heads):
        for h in range(group_size):
            qs[k, h * SPAN : (h + 1) * SPAN, :] = q_s[:, tiles(k * group_size + h)]
        m_s[k] = jnp.max(fresh_scores(k), axis=0, keepdims=True)
        a_s[k] = jnp.ones((1, rows), jnp.float32)
        acc[k] = jnp.zeros((HD + ONES, rows), jnp.float32)
    p_s[1] = jnp.zeros((chunk, rows), jnp.bfloat16)
    arrive_keys(0)
    for i in range(1, chunks):

        @pl.when(i * chunk < length)
        def _():
            copy_in(0, i).start()
            copy_in(1, i).start()

    s = dot_last(ks[0, :, :HD], qs[0])
    s_s[0] = s
    x_s[0] = tile_max(s)

    def weighted(i, k, part, index):
        return dot(jnp.concatenate([vs[i, part, tiles(k)].T, live[i, :, part]], axis=0), p_s[index, part, :])

    @pl.loop(0, count)
    def _(i):
        arrive_values(i)

        @pl.when(i + 1 < count)
        def _():
            arrive_keys(i + 1)

        for k in range(kv_heads):
            now, other = k % 2, 1 - k % 2
            next_k, next_i = (k + 1) % kv_heads, i if k + 1 < kv_heads else jnp.minimum(i + 1, count - 1)
            last_k, last_i = (k - 1) % kv_heads, i if k > 0 else jnp.maximum(i - 1, 0)
            before = m_s[k]
            top = jnp.maximum(before, jnp.max(x_s[now], axis=0, keepdims=True))
            m_s[k] = top
            highest, mixed = None, None
            for j in range(0, chunk, TILE):
                part = slice(j, j + TILE)
                s = dot_last(ks[next_i, part, tiles(next_k)], qs[next_k])
                s_s[other, part, :] = s
                high = tile_max(s)
                highest = high if highest is None else jnp.maximum(highest, high)
                p_s[now, part, :] = jnp.exp2((s_s[now, part, :] - top) * EXP2_SCALE).astype(jnp.bfloat16)
                if (j // TILE) % 2 == 1:
                    product = weighted(last_i, last_k, slice(j - TILE, j + TILE), other)
                    mixed = product if mixed is None else mixed + product
            x_s[other] = highest
            acc[last_k] = acc[last_k] * a_s[last_k] + mixed
            a_s[k] = jnp.exp2((before - top) * EXP2_SCALE)

    last = kv_heads - 1
    acc[last] = acc[last] * a_s[last] + weighted(count - 1, last, slice(0, chunk), last % 2)

    leaving = []
    for k in range(kv_heads):
        p = jnp.exp2((fresh_scores(k) - m_s[k]) * EXP2_SCALE)
        inverse = 1.0 / (acc[k, HD : HD + 1, :] + jnp.sum(p, axis=0, keepdims=True))
        p_s[0, (k % 2) * SPAN : (k % 2 + 1) * SPAN, :] = (p * inverse).astype(jnp.bfloat16)
        mixed = (acc[k, :HD, :] * inverse).T.astype(jnp.bfloat16)
        for h in range(group_size):
            out_s[:, tiles(k * group_size + h)] = mixed[h * SPAN : (h + 1) * SPAN, :]
        here = slice(k * group_size * HD, (k + 1) * group_size * HD)
        leaving.append(pltpu.make_async_copy(out_s.at[:, here], out_hbm.at[:, here], io_sems.at[2 + k]))
        leaving[-1].start()
        if k % 2 == 1:
            pf_s[k // 2] = p_s[0, : 2 * SPAN, :].T
    leaving.append(pltpu.make_async_copy(pf_s, pf_hbm, io_sems.at[2 + kv_heads]))
    leaving[-1].start()
    for copy in leaving:
        copy.wait()


def cache_attention(order, queries, fresh_keys, keys, values, lengths):
    slots, width = keys.shape[1:]
    kv_heads = width // HD
    group_size = queries.shape[1] // width
    rows = group_size * SPAN
    chunk = min(CHUNK, slots)
    chunks = slots // chunk
    hbm = pl.BlockSpec(memory_space=pltpu.HBM)
    result = (SPAN, queries.shape[1])
    weights = (kv_heads // 2, rows, 2 * SPAN)
    return pl.pallas_call(
        functools.partial(cache_kernel, order),
        in_specs=[pl.BlockSpec(memory_space=pltpu.SMEM)] + [hbm] * 4,
        out_specs=[hbm] * 2,
        scratch_shapes=[
            pltpu.VMEM((kv_heads, rows, HD), jnp.bfloat16),
            pltpu.VMEM((chunks, chunk, width), jnp.bfloat16),
            pltpu.VMEM((chunks, chunk, width), jnp.bfloat16),
            pltpu.VMEM((chunks, ONES, chunk), jnp.bfloat16),
            pltpu.VMEM((2, chunk, rows), jnp.float32),
            pltpu.VMEM((2, chunk, rows), jnp.bfloat16),
            pltpu.VMEM((2, 8, rows), jnp.float32),
            pltpu.VMEM((kv_heads, 1, rows), jnp.float32),
            pltpu.VMEM((kv_heads, 1, rows), jnp.float32),
            pltpu.VMEM((kv_heads, HD + ONES, rows), jnp.float32),
            pltpu.VMEM(result, jnp.bfloat16),
            pltpu.VMEM((SPAN, width), jnp.bfloat16),
            pltpu.VMEM(result, jnp.bfloat16),
            pltpu.VMEM(weights, jnp.bfloat16),
            pltpu.SemaphoreType.DMA((2, chunks)),
            pltpu.SemaphoreType.DMA((3 + kv_heads,)),
        ],
        out_shape=[
            jax.ShapeDtypeStruct(result, jnp.bfloat16),
            jax.ShapeDtypeStruct(weights, jnp.bfloat16),
        ],
        compiler_params=pltpu.CompilerParams(vmem_limit_bytes=57 * MIB),
        cost_estimate=FREE,
        name="cache_attention",
    )(lengths, queries, fresh_keys, keys, values)


def run_copies(copies, sems):
    copies = [pltpu.make_async_copy(src, dst, sems.at[i]) for i, (src, dst) in enumerate(copies)]
    for copy in copies:
        copy.start()
    for copy in copies:
        copy.wait()


def cross_kernel(d_hbm, u_hbm, w_hbm, early, late, *refs):
    maps_out, sems = [early, *refs[:-1]], refs[-1]
    part, core, quad = lax.axis_index("parts") % 2, lax.axis_index("tensor"), lax.axis_index("quad")
    width, cols = w_hbm.shape
    step = min(cols, width)
    size = width // 2 - late.shape[0]
    mine = pl.ds(pl.multiple_of(part * RANK, RANK), RANK)
    begin = part * (width // 2)
    copies = [
        (w_hbm.at[pl.ds(pl.multiple_of(begin, RANK), size), :], early.at[:size, :]),
        (w_hbm.at[pl.ds(pl.multiple_of(begin + size, RANK), late.shape[0]), :], late),
    ]
    for q, out in enumerate(maps_out):
        base = size if q == 0 else 0
        begin = core * (d_hbm.shape[1] // 2) + (quad ^ q) * width
        sources = [
            d_hbm.at[mine, pl.ds(pl.multiple_of(begin + first, step), step)] for first in range(0, width, step)
        ]
        sources += [u_hbm.at[mine, first : first + step] for first in range(0, cols, step)]
        for i, source in enumerate(sources):
            copies.append((source, out.at[base + i * RANK : base + (i + 1) * RANK, :step]))
    run_copies(copies, sems)


def cross_pack(downs, ups, weights, quads):
    vmem = pl.BlockSpec(memory_space=pltpu.VMEM)
    hbm = pl.BlockSpec(memory_space=pltpu.HBM)
    width, cols = weights.shape
    step = min(cols, width)
    pieces = (width + cols) // step
    first = width // 2 * 15 // 32 // RANK * RANK
    sizes = [(first + RANK * pieces, cols), (width // 2 - first, cols)]
    sizes += [(RANK * pieces, step)] * (quads - 1)
    return pl.pallas_call(
        cross_kernel,
        in_specs=[hbm] * 3,
        out_specs=[vmem] * len(sizes),
        out_shape=[jax.ShapeDtypeStruct(size, weights.dtype) for size in sizes],
        scratch_shapes=[pltpu.SemaphoreType.DMA((quads * pieces + 2,))],
        compiler_params=pltpu.CompilerParams(vmem_limit_bytes=57 * MIB),
        cost_estimate=FREE,
        name="cross_pack",
    )(downs, ups, weights)


def quad_kernel(x_hbm, d_hbm, u_hbm, *refs):
    outs, sems = refs[:-1], refs[-1]
    core, quad = lax.axis_index("tensor"), lax.axis_index("quad")
    tokens, features = x_hbm.shape
    ranks, cols = u_hbm.shape
    width = outs[0].shape[1]
    step = min(cols, width)
    copies = []
    for q, out in enumerate(outs):
        here = pl.ds(pl.multiple_of((quad ^ q) * width, width), width)
        copies.append((x_hbm.at[:, here], out.at[:tokens, :]))
        here = pl.ds(pl.multiple_of(core * features + (quad ^ q) * width, width), width)
        copies.append((d_hbm.at[:, here], out.at[tokens : tokens + ranks, :]))
        for slot, first, row, col in up_places(cols, width):
            row += tokens + ranks
            up = u_hbm.at[slot * RANK : (slot + 1) * RANK, first : first + step]
            copies.append((up, out.at[row : row + RANK, col : col + step]))
    run_copies(copies, sems)


def up_places(cols, width):
    step = min(cols, width)
    return [
        (slot, first, (slot * cols + first) // width * RANK, (slot * cols + first) % width)
        for slot in range(2)
        for first in range(0, cols, step)
    ]


def quad_pack(tokens, downs, ups, width, quads):
    vmem = pl.BlockSpec(memory_space=pltpu.VMEM)
    hbm = pl.BlockSpec(memory_space=pltpu.HBM)
    ranks, cols = ups.shape
    block = (tokens.shape[0] + ranks + RANK * (2 * cols // width), width)
    count = quads * (2 + len(up_places(cols, width)))
    return pl.pallas_call(
        quad_kernel,
        in_specs=[hbm] * 3,
        out_specs=[vmem] * quads,
        out_shape=[jax.ShapeDtypeStruct(block, tokens.dtype)] * quads,
        scratch_shapes=[pltpu.SemaphoreType.DMA((count,))],
        compiler_params=pltpu.CompilerParams(vmem_limit_bytes=57 * MIB),
        cost_estimate=FREE,
        name="quad_pack",
    )(tokens, downs, ups)


def near_kernel(tokens, quads, position, adapter, own_ref, *refs):
    maps_mine, maps_theirs, refs = refs[:2], refs[2:4], refs[4:]
    mine, theirs, out, ds, us = refs
    part, core = lax.axis_index("parts") % 2, lax.axis_index("tensor")
    wing, quad = lax.axis_index("wing"), lax.axis_index("quad")
    width = mine.shape[2]
    cols = own_ref.shape[1]
    ranks = 2 * RANK
    step = min(cols, width)
    for q in range(quads):
        rows = slice(q * ranks, (q + 1) * ranks)
        ds[0, rows, :] = mine[q, tokens : tokens + ranks, :]
        ds[1, rows, :] = theirs[q, tokens : tokens + ranks, :]
        for slot, first, row, col in up_places(cols, width):
            row += tokens + ranks
            place = q * ranks + slot * RANK
            us[place : place + RANK, first : first + step] = mine[q, row : row + RANK, col : col + step]
        for side in range(2):
            place = (quads + q) * ranks + side * RANK
            for i, first in enumerate(range(0, width, step)):
                row = i * RANK
                ds[0, place : place + RANK, first : first + step] = maps_mine[side][q, row : row + RANK, :]
                ds[1, place : place + RANK, first : first + step] = maps_theirs[side][q, row : row + RANK, :]
            for i, first in enumerate(range(0, cols, step)):
                row = (width // step + i) * RANK
                us[place : place + RANK, first : first + step] = maps_mine[side][q, row : row + RANK, :]

    x_mine = mine[:, :tokens, :].reshape(quads * tokens, width)
    x_theirs = theirs[:, :tokens, :].reshape(quads * tokens, width)
    shrink = dot_last(x_mine, ds[0]) + dot_last(x_theirs, ds[1])
    place = lax.broadcasted_iota(jnp.int32, (SPAN, us.shape[0]), 1)
    far = (place >= quads * ranks).astype(jnp.int32)
    index = place - far * (quads * ranks)
    group = (wing ^ far) * quads + (quad ^ (index >> 5))
    which = 2 * group + (((index >> 4) & 1) ^ (far * part))
    spans = tokens // SPAN
    masked = []
    for q in range(quads):
        for i in range(spans):
            slot = position[adapter[(wing * quads + (quad ^ q)) * spans + i]]
            row = (q * spans + i) * SPAN
            masked.append(jnp.where(which == slot, shrink[row : row + SPAN, :], 0.0))
    shrink = (jnp.concatenate(masked, axis=0) * ADAPTER_SCALE).astype(jnp.bfloat16)
    out[...] = dot(shrink, us[...])

    @pl.when(core == wing)
    def _():
        out[...] += dot(x_mine, own_ref[...])

    @pl.when(core != wing)
    def _():
        out[...] += dot(x_theirs, own_ref[...])


def near_products(mine, theirs, maps_mine, maps_theirs, own, position, adapter, tokens):
    quads, _, width = mine.shape
    cols = own.shape[1]
    ranks = 4 * quads * RANK
    vmem = pl.BlockSpec(memory_space=pltpu.VMEM)
    smem = pl.BlockSpec(memory_space=pltpu.SMEM)
    return pl.pallas_call(
        functools.partial(near_kernel, tokens, quads),
        in_specs=[smem, smem] + [vmem] * 7,
        out_specs=vmem,
        out_shape=jax.ShapeDtypeStruct((quads * tokens, cols), jnp.float32),
        scratch_shapes=[
            pltpu.VMEM((2, ranks, width), jnp.bfloat16),
            pltpu.VMEM((ranks, cols), jnp.bfloat16),
        ],
        compiler_params=pltpu.CompilerParams(vmem_limit_bytes=48 * MIB if quads > 4 else 24 * MIB),
        cost_estimate=FREE,
        name="near_products",
    )(position, adapter, own, *maps_mine, *maps_theirs, mine, theirs)


def far_kernel(tokens, quads, near, *refs):
    weights, (mine, theirs) = refs[:4], refs[4:6]
    outs, whole = refs[6:-1], refs[-1]
    part, core, wing = lax.axis_index("parts") % 2, lax.axis_index("tensor"), lax.axis_index("wing")
    for side in range(2):
        begin = (part if side == 0 else 1 - part) * (whole.shape[0] // 2)
        early, late = weights[2 * side : 2 * side + 2]
        size = whole.shape[0] // 2 - late.shape[0]
        whole[pl.ds(pl.multiple_of(begin, RANK), size), :] = early[:size, :]
        whole[pl.ds(pl.multiple_of(begin + size, RANK), late.shape[0]), :] = late[...]

    def store(blocks):
        x = blocks[:, :tokens, :].reshape(near.shape[0], -1)
        product = (near[...] + dot(x, whole[...])).astype(jnp.bfloat16)
        for q, out in enumerate(outs):
            out[...] = product[q * tokens : (q + 1) * tokens, :]

    @pl.when(core == wing)
    def _():
        store(theirs)

    @pl.when(core != wing)
    def _():
        store(mine)


def far_products(mine, theirs, near, weights, tokens):
    quads, _, width = mine.shape
    cols = near.shape[1]
    vmem = pl.BlockSpec(memory_space=pltpu.VMEM)
    return pl.pallas_call(
        functools.partial(far_kernel, tokens, quads),
        in_specs=[vmem] * (3 + len(weights)),
        out_specs=[vmem] * quads,
        out_shape=[jax.ShapeDtypeStruct((tokens, cols), jnp.bfloat16)] * quads,
        scratch_shapes=[pltpu.VMEM((width, cols), jnp.bfloat16)],
        compiler_params=pltpu.CompilerParams(vmem_limit_bytes=48 * MIB if quads > 4 else 16 * MIB),
        cost_estimate=FREE,
        name="far_products",
    )(near, *weights, mine, theirs)


def finish_kernel(spans, lens, *refs):
    out_hbm, values_ref, out_s, sems = refs[-4:]
    mixed, probs, parts = refs[:spans], refs[spans : 2 * spans], refs[2 * spans : -4]
    total = parts[0][...].astype(jnp.float32)
    for part in parts[1:]:
        total = total + part[...].astype(jnp.float32)
    values_ref[...] = total.astype(jnp.bfloat16)
    none = jnp.zeros((SPAN, HD), jnp.bfloat16)
    group_size = out_hbm.shape[1] // values_ref.shape[1]
    pair_width = 2 * group_size * HD
    leaving = []
    for order in range(spans):
        span = span_of(order, lens)
        rows = pl.ds(pl.multiple_of(span * SPAN, SPAN), SPAN)
        for pair in range(probs[order].shape[0]):
            left = values_ref[rows, 2 * pair * HD : (2 * pair + 1) * HD]
            right = values_ref[rows, (2 * pair + 1) * HD : (2 * pair + 2) * HD]
            both = jnp.concatenate(
                [jnp.concatenate([left, none], axis=1), jnp.concatenate([none, right], axis=1)], axis=0
            )
            fresh = dot(probs[order][pair], both)
            for side in range(2):
                for h in range(group_size):
                    col = ((2 * pair + side) * group_size + h) * HD
                    added = fresh[h * SPAN : (h + 1) * SPAN, side * HD : (side + 1) * HD]
                    before = mixed[order][:, col : col + HD].astype(jnp.float32)
                    out_s[order, :, col : col + HD] = (before + added).astype(jnp.bfloat16)
            here = slice(pair * pair_width, (pair + 1) * pair_width)
            leaving.append(
                pltpu.make_async_copy(out_s.at[order, :, here], out_hbm.at[rows, here], sems.at[order, pair])
            )
            leaving[-1].start()
    for copy in leaving:
        copy.wait()


def finish(lengths, mixed, fresh_probs, parts, q_width):
    tokens, cols = parts[0].shape
    vmem = pl.BlockSpec(memory_space=pltpu.VMEM)
    smem = pl.BlockSpec(memory_space=pltpu.SMEM)
    return pl.pallas_call(
        functools.partial(finish_kernel, len(mixed)),
        in_specs=[smem] + [vmem] * (len(parts) + 2 * len(mixed)),
        out_specs=[pl.BlockSpec(memory_space=pl.ANY), vmem],
        out_shape=[
            jax.ShapeDtypeStruct((tokens, q_width), jnp.bfloat16),
            jax.ShapeDtypeStruct((tokens, cols), jnp.bfloat16),
        ],
        scratch_shapes=[
            pltpu.VMEM((len(mixed), *mixed[0].shape), jnp.bfloat16),
            pltpu.SemaphoreType.DMA((len(mixed), fresh_probs[0].shape[0])),
        ],
        compiler_params=pltpu.CompilerParams(vmem_limit_bytes=16 * MIB),
        cost_estimate=FREE,
        name="finish_attention",
    )(lengths, *mixed, *fresh_probs, *parts)


def on_device(
    normed_inputs,
    value_matrix,
    adapter_down_weight,
    adapter_up_weight,
    adapter_position,
    span_adapter_index,
    queries,
    incoming_keys,
    stored_keys,
    stored_values,
    cache_length,
):
    quads = lax.axis_size("quad")
    parts_swap = [(i, i ^ 1) for i in range(lax.axis_size("parts"))]
    width, cols = value_matrix.shape
    downs = adapter_down_weight.reshape(-1, adapter_down_weight.shape[2])
    ups = adapter_up_weight.reshape(-1, cols)

    kv_heads = cols // HD
    def attention(order, lengths):
        return cache_attention(order, queries, incoming_keys, stored_keys, stored_values, lengths)

    def after(value, *others):
        return lax.optimization_barrier((value, *others))[0]

    def to_quad(value, q):
        return lax.ppermute(value, "quad", [(j, j ^ q) for j in range(quads)])

    def to_other_wing(value, q):
        pairs = [(w * quads + j, (1 - w) * quads + (j ^ q)) for w in range(2) for j in range(quads)]
        return lax.ppermute(value, ("wing", "quad"), pairs)

    early, late, *maps = cross_pack(downs, ups, value_matrix, quads)
    blocks = quad_pack(after(normed_inputs, early), downs, ups, width, quads)
    order = [*range(quads // 2, quads), *range(1, quads // 2)]
    mine = [to_quad(blocks[q], q) for q in order]
    early = lax.ppermute(early, "wing", SWAP)
    maps = [to_other_wing(each, q + 1) for q, each in enumerate(maps)]

    attn = [attention(0, after(cache_length, blocks[0]))]
    early, *maps = lax.optimization_barrier((early, *maps, attn[0][1]))[:-1]
    step = maps[0].shape[1]
    maps = jnp.stack([early[early.shape[0] - maps[0].shape[0] :, :step], *maps])
    late = lax.ppermute(after(late, early), "wing", SWAP)
    early_other = lax.ppermute(early, "parts", parts_swap)
    maps_other = lax.ppermute(maps, "parts", parts_swap)

    attn.append(attention(1, after(cache_length, early, maps)))
    late, early_other, maps_other, *mine = lax.optimization_barrier(
        (late, early_other, maps_other, *mine, attn[1][1])
    )[:-1]
    mine = jnp.stack([blocks[0]] + [mine[order.index(q)] for q in range(1, quads)])
    late_other = lax.ppermute(late, "parts", parts_swap)
    maps_mine = (maps, maps_other)
    maps_theirs = [lax.ppermute(each, "tensor", SWAP) for each in maps_mine]
    theirs = lax.ppermute(mine, "tensor", SWAP)

    tokens, q_width = queries.shape
    near = near_products(
        mine, theirs, maps_mine, maps_theirs, value_matrix, adapter_position, span_adapter_index, tokens
    )
    products = far_products(mine, theirs, near, (early, late, early_other, late_other), tokens)
    parts = [products[0]] + [to_quad(products[q], q) for q in range(1, quads)]
    mixed, fresh_probs = zip(*attn)
    attended, incoming_values = finish(cache_length, mixed, fresh_probs, parts, q_width)
    return (attended, incoming_values)


def solution(mesh):
    sizes = mesh.devices.shape
    cut = Mesh(
        mesh.devices.reshape(sizes[0], 2, sizes[1] // 2, sizes[2]), ("parts", "wing", "quad", "tensor")
    )
    group = ("wing", "quad")
    home = ("parts", "wing", "quad")
    in_specs = (
        P(home, "tensor"),
        P(group, "tensor"),
        P(group, None, None),
        P(group, None, "tensor"),
        P(),
        P("parts"),
        P(home, "tensor"),
        P(home, "tensor"),
        P(home, None, "tensor"),
        P(home, None, "tensor"),
        P(home),
    )
    out_specs = (P(home, "tensor"), P(home, "tensor"))
    return jax.shard_map(
        on_device, mesh=cut, in_specs=in_specs, out_specs=out_specs, check_vma=False
    )
```

```python
import functools
import math

import jax
import jax.numpy as jnp
from jax import lax
from jax.experimental import pallas as pl
from jax.experimental.pallas import tpu as pltpu
from jax.sharding import Mesh
from jax.sharding import PartitionSpec as P

HD = 128
RANK = 16
SPAN = 64
CHUNK = 512
ONES = 16
TILE = 128
ADAPTER_SCALE = 2.0
EXP2_SCALE = math.log2(math.e) / math.sqrt(HD)
DEAD = -1e30
MIB = 1024 * 1024
SWAP = [(0, 1), (1, 0)]
FREE = pl.CostEstimate(flops=1, bytes_accessed=1, transcendentals=0)


def dot_last(a, b):
    return lax.dot_general(a, b, (((1,), (1,)), ((), ())), preferred_element_type=jnp.float32)


def dot(a, b):
    return jnp.dot(a, b, preferred_element_type=jnp.float32)


def span_of(order, lens):
    longer = (lens[1] > lens[0]).astype(jnp.int32)
    return longer if order == 0 else 1 - longer


def cache_kernel(order, first_head, lens, q_hbm, fk_hbm, k_hbm, v_hbm, out_hbm, pf_hbm, qs, ks, vs, live, s_s, p_s, x_s, m_s, a_s, acc, q_s, fk_s, out_s, pf_s, sems, io_sems):
    span = span_of(order, lens)
    length = lens[span]
    chunks, chunk, _ = ks.shape
    kv_heads, rows, _ = qs.shape
    group_size = rows // SPAN
    count = (length + chunk - 1) // chunk
    mine = pl.ds(pl.multiple_of(span * SPAN, SPAN), SPAN)

    def copy_in(side, i):
        slots = pl.ds(pl.multiple_of(i * chunk, chunk), chunk)
        source, target = ((k_hbm, ks), (v_hbm, vs))[side]
        heads = slice(first_head * HD, (first_head + kv_heads) * HD)
        return pltpu.make_async_copy(source.at[span, slots, heads], target.at[i], sems.at[side, i])

    small = [
        pltpu.make_async_copy(
            q_hbm.at[mine, first_head * group_size * HD : (first_head + kv_heads) * group_size * HD],
            q_s,
            io_sems.at[0],
        ),
        pltpu.make_async_copy(
            fk_hbm.at[mine, first_head * HD : (first_head + kv_heads) * HD], fk_s, io_sems.at[1]
        ),
    ]
    for copy in small:
        copy.start()
    copy_in(0, 0).start()

    def dead_slots(i):
        return i * chunk + lax.broadcasted_iota(jnp.int32, ks.shape[1:], 0) >= length

    def arrive_keys(i):
        copy_in(0, i).wait()

        @pl.when((i + 1) * chunk > length)
        def _():
            keys = ks[i].astype(jnp.float32)
            ks[i] = jnp.where(dead_slots(i), keys[:1, :], keys).astype(jnp.bfloat16)

    def arrive_values(i):
        copy_in(1, i).wait()
        slot = i * chunk + lax.broadcasted_iota(jnp.int32, (ONES, chunk), 1)
        live[i] = (slot < length).astype(jnp.float32).astype(jnp.bfloat16)

        @pl.when((i + 1) * chunk > length)
        def _():
            vs[i] = jnp.where(dead_slots(i), 0.0, vs[i].astype(jnp.float32)).astype(jnp.bfloat16)

    def fresh_scores(k):
        s = dot_last(fk_s[:, k * HD : (k + 1) * HD], qs[k])
        key = lax.broadcasted_iota(jnp.int32, (SPAN, rows), 0)
        token = lax.broadcasted_iota(jnp.int32, (SPAN, rows), 1) % SPAN
        return jnp.where(key <= token, s, DEAD)

    def tile_max(s):
        return jnp.max(s.reshape(s.shape[0] // 8, 8, rows), axis=0)

    def tiles(k):
        return slice(k * HD, (k + 1) * HD)

    for copy in small:
        copy.wait()
    copy_in(1, 0).start()
    for k in range(kv_heads):
        for h in range(group_size):
            qs[k, h * SPAN : (h + 1) * SPAN, :] = q_s[:, tiles(k * group_size + h)]
        m_s[k] = jnp.max(fresh_scores(k), axis=0, keepdims=True)
        a_s[k] = jnp.ones((1, rows), jnp.float32)
        acc[k] = jnp.zeros((HD + ONES, rows), jnp.float32)
    p_s[1] = jnp.zeros((chunk, rows), jnp.bfloat16)
    arrive_keys(0)
    for i in range(1, chunks):

        @pl.when(i * chunk < length)
        def _():
            copy_in(0, i).start()
            copy_in(1, i).start()

    s = dot_last(ks[0, :, :HD], qs[0])
    s_s[0] = s
    x_s[0] = tile_max(s)

    def weighted(i, k, part, index):
        return dot(jnp.concatenate([vs[i, part, tiles(k)].T, live[i, :, part]], axis=0), p_s[index, part, :])

    @pl.loop(0, count)
    def _(i):
        arrive_values(i)

        @pl.when(i + 1 < count)
        def _():
            arrive_keys(i + 1)

        for k in range(kv_heads):
            now, other = k % 2, 1 - k % 2
            next_k, next_i = (k + 1) % kv_heads, i if k + 1 < kv_heads else jnp.minimum(i + 1, count - 1)
            last_k, last_i = (k - 1) % kv_heads, i if k > 0 else jnp.maximum(i - 1, 0)
            before = m_s[k]
            top = jnp.maximum(before, jnp.max(x_s[now], axis=0, keepdims=True))
            m_s[k] = top
            highest, mixed = None, None
            for j in range(0, chunk, TILE):
                part = slice(j, j + TILE)
                s = dot_last(ks[next_i, part, tiles(next_k)], qs[next_k])
                s_s[other, part, :] = s
                high = tile_max(s)
                highest = high if highest is None else jnp.maximum(highest, high)
                p_s[now, part, :] = jnp.exp2((s_s[now, part, :] - top) * EXP2_SCALE).astype(jnp.bfloat16)
                if (j // TILE) % 2 == 1:
                    product = weighted(last_i, last_k, slice(j - TILE, j + TILE), other)
                    mixed = product if mixed is None else mixed + product
            x_s[other] = highest
            acc[last_k] = acc[last_k] * a_s[last_k] + mixed
            a_s[k] = jnp.exp2((before - top) * EXP2_SCALE)

    last = kv_heads - 1
    acc[last] = acc[last] * a_s[last] + weighted(count - 1, last, slice(0, chunk), last % 2)

    leaving = []
    for k in range(kv_heads):
        p = jnp.exp2((fresh_scores(k) - m_s[k]) * EXP2_SCALE)
        inverse = 1.0 / (acc[k, HD : HD + 1, :] + jnp.sum(p, axis=0, keepdims=True))
        p_s[0, (k % 2) * SPAN : (k % 2 + 1) * SPAN, :] = (p * inverse).astype(jnp.bfloat16)
        mixed = (acc[k, :HD, :] * inverse).astype(jnp.bfloat16).T
        for h in range(group_size):
            out_s[:, tiles(k * group_size + h)] = mixed[h * SPAN : (h + 1) * SPAN, :]
        here = slice(k * group_size * HD, (k + 1) * group_size * HD)
        leaving.append(pltpu.make_async_copy(out_s.at[:, here], out_hbm.at[:, here], io_sems.at[2 + k]))
        leaving[-1].start()
        if k % 2 == 1:
            pf_s[k // 2] = p_s[0, : 2 * SPAN, :].T
    leaving.append(pltpu.make_async_copy(pf_s, pf_hbm, io_sems.at[2 + kv_heads]))
    leaving[-1].start()
    for copy in leaving:
        copy.wait()


def cache_attention(order, first_head, kv_heads, queries, fresh_keys, keys, values, lengths):
    slots = keys.shape[1]
    group_size = queries.shape[1] // keys.shape[2]
    width = kv_heads * HD
    rows = group_size * SPAN
    chunk = min(CHUNK, slots)
    chunks = slots // chunk
    hbm = pl.BlockSpec(memory_space=pltpu.HBM)
    result = (SPAN, group_size * width)
    weights = (kv_heads // 2, rows, 2 * SPAN)
    return pl.pallas_call(
        functools.partial(cache_kernel, order, first_head),
        in_specs=[pl.BlockSpec(memory_space=pltpu.SMEM)] + [hbm] * 4,
        out_specs=[hbm] * 2,
        scratch_shapes=[
            pltpu.VMEM((kv_heads, rows, HD), jnp.bfloat16),
            pltpu.VMEM((chunks, chunk, width), jnp.bfloat16),
            pltpu.VMEM((chunks, chunk, width), jnp.bfloat16),
            pltpu.VMEM((chunks, ONES, chunk), jnp.bfloat16),
            pltpu.VMEM((2, chunk, rows), jnp.float32),
            pltpu.VMEM((2, chunk, rows), jnp.bfloat16),
            pltpu.VMEM((2, 8, rows), jnp.float32),
            pltpu.VMEM((kv_heads, 1, rows), jnp.float32),
            pltpu.VMEM((kv_heads, 1, rows), jnp.float32),
            pltpu.VMEM((kv_heads, HD + ONES, rows), jnp.float32),
            pltpu.VMEM(result, jnp.bfloat16),
            pltpu.VMEM((SPAN, width), jnp.bfloat16),
            pltpu.VMEM(result, jnp.bfloat16),
            pltpu.VMEM(weights, jnp.bfloat16),
            pltpu.SemaphoreType.DMA((2, chunks)),
            pltpu.SemaphoreType.DMA((3 + kv_heads,)),
        ],
        out_shape=[
            jax.ShapeDtypeStruct(result, jnp.bfloat16),
            jax.ShapeDtypeStruct(weights, jnp.bfloat16),
        ],
        compiler_params=pltpu.CompilerParams(vmem_limit_bytes=57 * MIB),
        cost_estimate=FREE,
        name="cache_attention",
    )(lengths, queries, fresh_keys, keys, values)


def run_copies(copies, sems):
    copies = [pltpu.make_async_copy(src, dst, sems.at[i]) for i, (src, dst) in enumerate(copies)]
    for copy in copies:
        copy.start()
    for copy in copies:
        copy.wait()


def cross_kernel(d_hbm, u_hbm, w_hbm, early, late, *refs):
    maps_out, sems = [early, *refs[:-1]], refs[-1]
    part, core, quad = lax.axis_index("parts") % 2, lax.axis_index("tensor"), lax.axis_index("quad")
    width, cols = w_hbm.shape
    step = min(cols, width)
    size = width // 2 - late.shape[0]
    mine = pl.ds(pl.multiple_of(part * RANK, RANK), RANK)
    begin = part * (width // 2)
    copies = [
        (w_hbm.at[pl.ds(pl.multiple_of(begin, RANK), size), :], early.at[:size, :]),
        (w_hbm.at[pl.ds(pl.multiple_of(begin + size, RANK), late.shape[0]), :], late),
    ]
    for q, out in enumerate(maps_out):
        base = size if q == 0 else 0
        begin = core * (d_hbm.shape[1] // 2) + (quad ^ q) * width
        sources = [
            d_hbm.at[mine, pl.ds(pl.multiple_of(begin + first, step), step)] for first in range(0, width, step)
        ]
        sources += [u_hbm.at[mine, first : first + step] for first in range(0, cols, step)]
        for i, source in enumerate(sources):
            copies.append((source, out.at[base + i * RANK : base + (i + 1) * RANK, :step]))
    run_copies(copies, sems)


def cross_pack(downs, ups, weights, quads):
    vmem = pl.BlockSpec(memory_space=pltpu.VMEM)
    hbm = pl.BlockSpec(memory_space=pltpu.HBM)
    width, cols = weights.shape
    step = min(cols, width)
    pieces = (width + cols) // step
    first = width // 2 * 20 // 32 // RANK * RANK
    sizes = [(first + RANK * pieces, cols), (width // 2 - first, cols)]
    sizes += [(RANK * pieces, step)] * (quads - 1)
    return pl.pallas_call(
        cross_kernel,
        in_specs=[hbm] * 3,
        out_specs=[vmem] * len(sizes),
        out_shape=[jax.ShapeDtypeStruct(size, weights.dtype) for size in sizes],
        scratch_shapes=[pltpu.SemaphoreType.DMA((quads * pieces + 2,))],
        compiler_params=pltpu.CompilerParams(vmem_limit_bytes=57 * MIB),
        cost_estimate=FREE,
        name="cross_pack",
    )(downs, ups, weights)


def quad_kernel(x_hbm, d_hbm, u_hbm, *refs):
    outs, sems = refs[:-1], refs[-1]
    core, quad = lax.axis_index("tensor"), lax.axis_index("quad")
    tokens, features = x_hbm.shape
    ranks, cols = u_hbm.shape
    width = outs[0].shape[1]
    step = min(cols, width)
    copies = []
    for q, out in enumerate(outs):
        here = pl.ds(pl.multiple_of((quad ^ q) * width, width), width)
        copies.append((x_hbm.at[:, here], out.at[:tokens, :]))
        here = pl.ds(pl.multiple_of(core * features + (quad ^ q) * width, width), width)
        copies.append((d_hbm.at[:, here], out.at[tokens : tokens + ranks, :]))
        for slot, first, row, col in up_places(cols, width):
            row += tokens + ranks
            up = u_hbm.at[slot * RANK : (slot + 1) * RANK, first : first + step]
            copies.append((up, out.at[row : row + RANK, col : col + step]))
    run_copies(copies, sems)


def up_places(cols, width):
    step = min(cols, width)
    return [
        (slot, first, (slot * cols + first) // width * RANK, (slot * cols + first) % width)
        for slot in range(2)
        for first in range(0, cols, step)
    ]


def quad_pack(tokens, downs, ups, width, quads):
    vmem = pl.BlockSpec(memory_space=pltpu.VMEM)
    hbm = pl.BlockSpec(memory_space=pltpu.HBM)
    ranks, cols = ups.shape
    block = (tokens.shape[0] + ranks + RANK * (2 * cols // width), width)
    count = quads * (2 + len(up_places(cols, width)))
    return pl.pallas_call(
        quad_kernel,
        in_specs=[hbm] * 3,
        out_specs=[vmem] * quads,
        out_shape=[jax.ShapeDtypeStruct(block, tokens.dtype)] * quads,
        scratch_shapes=[pltpu.SemaphoreType.DMA((count,))],
        compiler_params=pltpu.CompilerParams(vmem_limit_bytes=57 * MIB),
        cost_estimate=FREE,
        name="quad_pack",
    )(tokens, downs, ups)


def near_kernel(tokens, quads, position, adapter, own_ref, *refs):
    maps_mine, maps_theirs, refs = refs[:2], refs[2:4], refs[4:]
    mine, theirs, out, ds, us = refs
    part, core = lax.axis_index("parts") % 2, lax.axis_index("tensor")
    wing, quad = lax.axis_index("wing"), lax.axis_index("quad")
    width = mine.shape[2]
    cols = own_ref.shape[1]
    ranks = 2 * RANK
    step = min(cols, width)
    for q in range(quads):
        rows = slice(q * ranks, (q + 1) * ranks)
        ds[0, rows, :] = mine[q, tokens : tokens + ranks, :]
        ds[1, rows, :] = theirs[q, tokens : tokens + ranks, :]
        for slot, first, row, col in up_places(cols, width):
            row += tokens + ranks
            place = q * ranks + slot * RANK
            us[place : place + RANK, first : first + step] = mine[q, row : row + RANK, col : col + step]
        for side in range(2):
            place = (quads + q) * ranks + side * RANK
            for i, first in enumerate(range(0, width, step)):
                row = i * RANK
                ds[0, place : place + RANK, first : first + step] = maps_mine[side][q, row : row + RANK, :step]
                ds[1, place : place + RANK, first : first + step] = maps_theirs[side][q, row : row + RANK, :step]
            for i, first in enumerate(range(0, cols, step)):
                row = (width // step + i) * RANK
                us[place : place + RANK, first : first + step] = maps_mine[side][q, row : row + RANK, :step]

    x_mine = mine[:, :tokens, :].reshape(quads * tokens, width)
    x_theirs = theirs[:, :tokens, :].reshape(quads * tokens, width)
    shrink = dot_last(x_mine, ds[0]) + dot_last(x_theirs, ds[1])
    place = lax.broadcasted_iota(jnp.int32, (SPAN, us.shape[0]), 1)
    far = (place >= quads * ranks).astype(jnp.int32)
    index = place - far * (quads * ranks)
    group = (wing ^ far) * quads + (quad ^ (index >> 5))
    which = 2 * group + (((index >> 4) & 1) ^ (far * part))
    spans = tokens // SPAN
    masked = []
    for q in range(quads):
        for i in range(spans):
            slot = position[adapter[(wing * quads + (quad ^ q)) * spans + i]]
            row = (q * spans + i) * SPAN
            masked.append(jnp.where(which == slot, shrink[row : row + SPAN, :], 0.0))
    shrink = (jnp.concatenate(masked, axis=0) * ADAPTER_SCALE).astype(jnp.bfloat16)
    out[...] = dot(shrink, us[...])

    @pl.when(core == wing)
    def _():
        out[...] += dot(x_mine, own_ref[...])

    @pl.when(core != wing)
    def _():
        out[...] += dot(x_theirs, own_ref[...])


def near_products(mine, theirs, maps_mine, maps_theirs, own, position, adapter, tokens):
    quads, _, width = mine.shape
    cols = own.shape[1]
    ranks = 4 * quads * RANK
    vmem = pl.BlockSpec(memory_space=pltpu.VMEM)
    smem = pl.BlockSpec(memory_space=pltpu.SMEM)
    return pl.pallas_call(
        functools.partial(near_kernel, tokens, quads),
        in_specs=[smem, smem] + [vmem] * 7,
        out_specs=vmem,
        out_shape=jax.ShapeDtypeStruct((quads * tokens, cols), jnp.float32),
        scratch_shapes=[
            pltpu.VMEM((2, ranks, width), jnp.bfloat16),
            pltpu.VMEM((ranks, cols), jnp.bfloat16),
        ],
        compiler_params=pltpu.CompilerParams(vmem_limit_bytes=48 * MIB if quads > 4 else 24 * MIB),
        cost_estimate=FREE,
        name="near_products",
    )(position, adapter, own, *maps_mine, *maps_theirs, mine, theirs)


def far_kernel(tokens, quads, near, *refs):
    weights, (mine, theirs) = refs[:4], refs[4:6]
    outs, whole = refs[6:-1], refs[-1]
    part, core, wing = lax.axis_index("parts") % 2, lax.axis_index("tensor"), lax.axis_index("wing")
    for side in range(2):
        begin = (part if side == 0 else 1 - part) * (whole.shape[0] // 2)
        early, late = weights[2 * side : 2 * side + 2]
        size = whole.shape[0] // 2 - late.shape[0]
        whole[pl.ds(pl.multiple_of(begin, RANK), size), :] = early[:size, :]
        whole[pl.ds(pl.multiple_of(begin + size, RANK), late.shape[0]), :] = late[...]

    def store(blocks):
        x = blocks[:, :tokens, :].reshape(near.shape[0], -1)
        product = (near[...] + dot(x, whole[...])).astype(jnp.bfloat16)
        for q, out in enumerate(outs):
            out[...] = product[q * tokens : (q + 1) * tokens, :]

    @pl.when(core == wing)
    def _():
        store(theirs)

    @pl.when(core != wing)
    def _():
        store(mine)


def far_products(mine, theirs, near, weights, tokens):
    quads, _, width = mine.shape
    cols = near.shape[1]
    vmem = pl.BlockSpec(memory_space=pltpu.VMEM)
    return pl.pallas_call(
        functools.partial(far_kernel, tokens, quads),
        in_specs=[vmem] * (3 + len(weights)),
        out_specs=[vmem] * quads,
        out_shape=[jax.ShapeDtypeStruct((tokens, cols), jnp.bfloat16)] * quads,
        scratch_shapes=[pltpu.VMEM((width, cols), jnp.bfloat16)],
        compiler_params=pltpu.CompilerParams(vmem_limit_bytes=48 * MIB if quads > 4 else 16 * MIB),
        cost_estimate=FREE,
        name="far_products",
    )(near, *weights, mine, theirs)


def finish_kernel(pieces, lens, *refs):
    count = len(pieces)
    out_ref, values_ref = refs[-2:]
    mixed, probs, parts = refs[:count], refs[count : 2 * count], refs[2 * count : -2]
    total = parts[0][...].astype(jnp.float32)
    for part in parts[1:]:
        total = total + part[...].astype(jnp.float32)
    values_ref[...] = total.astype(jnp.bfloat16)
    none = jnp.zeros((SPAN, HD), jnp.bfloat16)
    group_size = out_ref.shape[1] // values_ref.shape[1]
    for (order, first_head, _), mix, prob in zip(pieces, mixed, probs):
        span = span_of(order, lens)
        rows = pl.ds(pl.multiple_of(span * SPAN, SPAN), SPAN)
        for pair in range(prob.shape[0]):
            head = first_head + 2 * pair
            left = values_ref[rows, head * HD : (head + 1) * HD]
            right = values_ref[rows, (head + 1) * HD : (head + 2) * HD]
            both = jnp.concatenate(
                [jnp.concatenate([left, none], axis=1), jnp.concatenate([none, right], axis=1)], axis=0
            )
            fresh = dot(prob[pair], both)
            for side in range(2):
                for h in range(group_size):
                    here = ((2 * pair + side) * group_size + h) * HD
                    col = ((head + side) * group_size + h) * HD
                    added = fresh[h * SPAN : (h + 1) * SPAN, side * HD : (side + 1) * HD]
                    before = mix[:, here : here + HD].astype(jnp.float32)
                    out_ref[rows, col : col + HD] = (before + added).astype(jnp.bfloat16)


def finish(pieces, lengths, mixed, fresh_probs, parts, q_width):
    tokens, cols = parts[0].shape
    vmem = pl.BlockSpec(memory_space=pltpu.VMEM)
    smem = pl.BlockSpec(memory_space=pltpu.SMEM)
    return pl.pallas_call(
        functools.partial(finish_kernel, pieces),
        in_specs=[smem] + [vmem] * (len(parts) + 2 * len(mixed)),
        out_specs=[vmem] * 2,
        out_shape=[
            jax.ShapeDtypeStruct((tokens, q_width), jnp.bfloat16),
            jax.ShapeDtypeStruct((tokens, cols), jnp.bfloat16),
        ],
        compiler_params=pltpu.CompilerParams(vmem_limit_bytes=16 * MIB),
        cost_estimate=FREE,
        name="finish_attention",
    )(lengths, *mixed, *fresh_probs, *parts)


def on_device(
    normed_inputs,
    value_matrix,
    adapter_down_weight,
    adapter_up_weight,
    adapter_position,
    span_adapter_index,
    queries,
    incoming_keys,
    stored_keys,
    stored_values,
    cache_length,
):
    quads = lax.axis_size("quad")
    parts_swap = [(i, i ^ 1) for i in range(lax.axis_size("parts"))]
    width, cols = value_matrix.shape
    downs = adapter_down_weight.reshape(-1, adapter_down_weight.shape[2])
    ups = adapter_up_weight.reshape(-1, cols)

    kv_heads = cols // HD
    heads = cols // HD
    pieces = [(0, 0, heads), (1, 0, heads // 2), (1, heads // 2, heads // 2)]

    def attention(piece, lengths):
        return cache_attention(
            *pieces[piece], queries, incoming_keys, stored_keys, stored_values, lengths
        )

    def after(value, *others):
        return lax.optimization_barrier((value, *others))[0]

    def to_quad(value, q):
        return lax.ppermute(value, "quad", [(j, j ^ q) for j in range(quads)])

    def to_other_wing(value, q):
        pairs = [(w * quads + j, (1 - w) * quads + (j ^ q)) for w in range(2) for j in range(quads)]
        return lax.ppermute(value, ("wing", "quad"), pairs)

    early, late, *maps = cross_pack(downs, ups, value_matrix, quads)
    blocks = quad_pack(after(normed_inputs, early), downs, ups, width, quads)
    order = [*range(quads // 2, quads), *range(1, quads // 2)]
    mine = [to_quad(blocks[q], q) for q in order]
    early = lax.ppermute(early, "wing", SWAP)
    maps = [to_other_wing(each, q + 1) for q, each in enumerate(maps)]

    attn = [attention(0, after(cache_length, blocks[0]))]
    early, mine[0], *maps = lax.optimization_barrier((early, mine[0], *maps, attn[0][1]))[:-1]
    late = lax.ppermute(after(late, early), "wing", SWAP)
    count = maps[0].shape[0]
    early = jnp.concatenate([early] + [jnp.pad(each, ((0, 0), (0, cols - each.shape[1]))) for each in maps])
    early_other = lax.ppermute(early, "parts", parts_swap)

    attn.append(attention(1, after(cache_length, early)))
    late, early_other, *mine = lax.optimization_barrier((late, early_other, *mine, attn[1][1]))[:-1]
    mine = jnp.stack([blocks[0]] + [mine[order.index(q)] for q in range(1, quads)])
    late_other = lax.ppermute(late, "parts", parts_swap)
    maps_mine = [each[-count * quads :].reshape(quads, count, cols) for each in (early, early_other)]
    maps_theirs = [lax.ppermute(each, "tensor", SWAP) for each in maps_mine]
    theirs = lax.ppermute(mine, "tensor", SWAP)

    attn.append(attention(2, after(cache_length, late)))
    theirs, *maps_theirs = lax.optimization_barrier((theirs, *maps_theirs, attn[2][1]))[:-1]

    tokens, q_width = queries.shape
    near = near_products(
        mine, theirs, maps_mine, maps_theirs, value_matrix, adapter_position, span_adapter_index, tokens
    )
    products = far_products(mine, theirs, near, (early, late, early_other, late_other), tokens)
    parts = [products[0]] + [to_quad(products[q], q) for q in range(1, quads)]
    mixed, fresh_probs = zip(*attn)
    attended, incoming_values = finish(pieces, cache_length, mixed, fresh_probs, parts, q_width)
    return (attended, incoming_values)


def solution(mesh):
    sizes = mesh.devices.shape
    cut = Mesh(
        mesh.devices.reshape(sizes[0], 2, sizes[1] // 2, sizes[2]), ("parts", "wing", "quad", "tensor")
    )
    group = ("wing", "quad")
    home = ("parts", "wing", "quad")
    in_specs = (
        P(home, "tensor"),
        P(group, "tensor"),
        P(group, None, None),
        P(group, None, "tensor"),
        P(),
        P("parts"),
        P(home, "tensor"),
        P(home, "tensor"),
        P(home, None, "tensor"),
        P(home, None, "tensor"),
        P(home),
    )
    out_specs = (P(home, "tensor"), P(home, "tensor"))
    return jax.shard_map(
        on_device, mesh=cut, in_specs=in_specs, out_specs=out_specs, check_vma=False
    )
```

```python
import functools
import math

import jax
import jax.numpy as jnp
from jax import lax
from jax.experimental import pallas as pl
from jax.experimental.pallas import tpu as pltpu
from jax.sharding import Mesh
from jax.sharding import PartitionSpec as P

HD = 128
RANK = 16
SPAN = 64
CHUNK = 512
ONES = 16
TILE = 128
ADAPTER_SCALE = 2.0
EXP2_SCALE = math.log2(math.e) / math.sqrt(HD)
DEAD = -1e30
MIB = 1024 * 1024
SWAP = [(0, 1), (1, 0)]
FREE = pl.CostEstimate(flops=1, bytes_accessed=1, transcendentals=0)


def dot_last(a, b):
    return lax.dot_general(a, b, (((1,), (1,)), ((), ())), preferred_element_type=jnp.float32)


def dot(a, b):
    return jnp.dot(a, b, preferred_element_type=jnp.float32)


def span_of(order, lens):
    longer = (lens[1] > lens[0]).astype(jnp.int32)
    return longer if order == 0 else 1 - longer


def cache_kernel(order, lens, q_hbm, fk_hbm, k_hbm, v_hbm, out_hbm, pf_hbm, qs, ks, vs, live, s_s, p_s, x_s, m_s, a_s, acc, q_s, fk_s, out_s, pf_s, sems, io_sems):
    span = span_of(order, lens)
    length = lens[span]
    chunks, chunk, _ = ks.shape
    kv_heads, rows, _ = qs.shape
    group_size = rows // SPAN
    count = (length + chunk - 1) // chunk
    mine = pl.ds(pl.multiple_of(span * SPAN, SPAN), SPAN)

    def copy_in(side, i):
        slots = pl.ds(pl.multiple_of(i * chunk, chunk), chunk)
        source, target = ((k_hbm, ks), (v_hbm, vs))[side]
        return pltpu.make_async_copy(source.at[span, slots, :], target.at[i], sems.at[side, i])

    small = [
        pltpu.make_async_copy(q_hbm.at[mine, :], q_s, io_sems.at[0]),
        pltpu.make_async_copy(fk_hbm.at[mine, :], fk_s, io_sems.at[1]),
    ]
    for copy in small:
        copy.start()
    copy_in(0, 0).start()

    def dead_slots(i):
        return i * chunk + lax.broadcasted_iota(jnp.int32, ks.shape[1:], 0) >= length

    def arrive_keys(i):
        copy_in(0, i).wait()

        @pl.when((i + 1) * chunk > length)
        def _():
            keys = ks[i].astype(jnp.float32)
            ks[i] = jnp.where(dead_slots(i), keys[:1, :], keys).astype(jnp.bfloat16)

    def arrive_values(i):
        copy_in(1, i).wait()
        slot = i * chunk + lax.broadcasted_iota(jnp.int32, (ONES, chunk), 1)
        live[i] = (slot < length).astype(jnp.float32).astype(jnp.bfloat16)

        @pl.when((i + 1) * chunk > length)
        def _():
            vs[i] = jnp.where(dead_slots(i), 0.0, vs[i].astype(jnp.float32)).astype(jnp.bfloat16)

    def fresh_scores(k):
        s = dot_last(fk_s[:, k * HD : (k + 1) * HD], qs[k])
        key = lax.broadcasted_iota(jnp.int32, (SPAN, rows), 0)
        token = lax.broadcasted_iota(jnp.int32, (SPAN, rows), 1) % SPAN
        return jnp.where(key <= token, s, DEAD)

    def tile_max(s):
        return jnp.max(s.reshape(s.shape[0] // 8, 8, rows), axis=0)

    def tiles(k):
        return slice(k * HD, (k + 1) * HD)

    for copy in small:
        copy.wait()
    copy_in(1, 0).start()
    for k in range(kv_heads):
        for h in range(group_size):
            qs[k, h * SPAN : (h + 1) * SPAN, :] = q_s[:, tiles(k * group_size + h)]
        m_s[k] = jnp.max(fresh_scores(k), axis=0, keepdims=True)
        a_s[k] = jnp.ones((1, rows), jnp.float32)
        acc[k] = jnp.zeros((HD + ONES, rows), jnp.float32)
    p_s[1] = jnp.zeros((chunk, rows), jnp.bfloat16)
    arrive_keys(0)
    for i in range(1, chunks):

        @pl.when(i * chunk < length)
        def _():
            copy_in(0, i).start()
            copy_in(1, i).start()

    s = dot_last(ks[0, :, :HD], qs[0])
    s_s[0] = s
    x_s[0] = tile_max(s)

    def weighted(i, k, part, index):
        return dot(jnp.concatenate([vs[i, part, tiles(k)].T, live[i, :, part]], axis=0), p_s[index, part, :])

    @pl.loop(0, count)
    def _(i):
        arrive_values(i)

        @pl.when(i + 1 < count)
        def _():
            arrive_keys(i + 1)

        for k in range(kv_heads):
            now, other = k % 2, 1 - k % 2
            next_k, next_i = (k + 1) % kv_heads, i if k + 1 < kv_heads else jnp.minimum(i + 1, count - 1)
            last_k, last_i = (k - 1) % kv_heads, i if k > 0 else jnp.maximum(i - 1, 0)
            before = m_s[k]
            top = jnp.maximum(before, jnp.max(x_s[now], axis=0, keepdims=True))
            m_s[k] = top
            highest, mixed = None, None
            for j in range(0, chunk, TILE):
                part = slice(j, j + TILE)
                s = dot_last(ks[next_i, part, tiles(next_k)], qs[next_k])
                s_s[other, part, :] = s
                high = tile_max(s)
                highest = high if highest is None else jnp.maximum(highest, high)
                p_s[now, part, :] = jnp.exp2((s_s[now, part, :] - top) * EXP2_SCALE).astype(jnp.bfloat16)
                if (j // TILE) % 2 == 1:
                    product = weighted(last_i, last_k, slice(j - TILE, j + TILE), other)
                    mixed = product if mixed is None else mixed + product
            x_s[other] = highest
            acc[last_k] = acc[last_k] * a_s[last_k] + mixed
            a_s[k] = jnp.exp2((before - top) * EXP2_SCALE)

    last = kv_heads - 1
    acc[last] = acc[last] * a_s[last] + weighted(count - 1, last, slice(0, chunk), last % 2)

    leaving = []
    for k in range(kv_heads):
        p = jnp.exp2((fresh_scores(k) - m_s[k]) * EXP2_SCALE)
        inverse = 1.0 / (acc[k, HD : HD + 1, :] + jnp.sum(p, axis=0, keepdims=True))
        p_s[0, (k % 2) * SPAN : (k % 2 + 1) * SPAN, :] = (p * inverse).astype(jnp.bfloat16)
        mixed = (acc[k, :HD, :] * inverse).astype(jnp.bfloat16).T
        for h in range(group_size):
            out_s[:, tiles(k * group_size + h)] = mixed[h * SPAN : (h + 1) * SPAN, :]
        here = slice(k * group_size * HD, (k + 1) * group_size * HD)
        leaving.append(pltpu.make_async_copy(out_s.at[:, here], out_hbm.at[:, here], io_sems.at[2 + k]))
        leaving[-1].start()
        if k % 2 == 1:
            pf_s[k // 2] = p_s[0, : 2 * SPAN, :].T
    leaving.append(pltpu.make_async_copy(pf_s, pf_hbm, io_sems.at[2 + kv_heads]))
    leaving[-1].start()
    for copy in leaving:
        copy.wait()


def cache_attention(order, queries, fresh_keys, keys, values, lengths):
    slots, width = keys.shape[1:]
    kv_heads = width // HD
    group_size = queries.shape[1] // width
    rows = group_size * SPAN
    chunk = min(CHUNK, slots)
    chunks = slots // chunk
    hbm = pl.BlockSpec(memory_space=pltpu.HBM)
    result = (SPAN, queries.shape[1])
    weights = (kv_heads // 2, rows, 2 * SPAN)
    return pl.pallas_call(
        functools.partial(cache_kernel, order),
        in_specs=[pl.BlockSpec(memory_space=pltpu.SMEM)] + [hbm] * 4,
        out_specs=[hbm] * 2,
        scratch_shapes=[
            pltpu.VMEM((kv_heads, rows, HD), jnp.bfloat16),
            pltpu.VMEM((chunks, chunk, width), jnp.bfloat16),
            pltpu.VMEM((chunks, chunk, width), jnp.bfloat16),
            pltpu.VMEM((chunks, ONES, chunk), jnp.bfloat16),
            pltpu.VMEM((2, chunk, rows), jnp.float32),
            pltpu.VMEM((2, chunk, rows), jnp.bfloat16),
            pltpu.VMEM((2, 8, rows), jnp.float32),
            pltpu.VMEM((kv_heads, 1, rows), jnp.float32),
            pltpu.VMEM((kv_heads, 1, rows), jnp.float32),
            pltpu.VMEM((kv_heads, HD + ONES, rows), jnp.float32),
            pltpu.VMEM(result, jnp.bfloat16),
            pltpu.VMEM((SPAN, width), jnp.bfloat16),
            pltpu.VMEM(result, jnp.bfloat16),
            pltpu.VMEM(weights, jnp.bfloat16),
            pltpu.SemaphoreType.DMA((2, chunks)),
            pltpu.SemaphoreType.DMA((3 + kv_heads,)),
        ],
        out_shape=[
            jax.ShapeDtypeStruct(result, jnp.bfloat16),
            jax.ShapeDtypeStruct(weights, jnp.bfloat16),
        ],
        compiler_params=pltpu.CompilerParams(vmem_limit_bytes=57 * MIB),
        cost_estimate=FREE,
        name="cache_attention",
    )(lengths, queries, fresh_keys, keys, values)


def run_copies(copies, sems):
    copies = [pltpu.make_async_copy(src, dst, sems.at[i]) for i, (src, dst) in enumerate(copies)]
    for copy in copies:
        copy.start()
    for copy in copies:
        copy.wait()


def cross_kernel(d_hbm, u_hbm, w_hbm, early, late, *refs):
    maps_out, sems = [early, *refs[:-1]], refs[-1]
    part, core, quad = lax.axis_index("parts") % 2, lax.axis_index("tensor"), lax.axis_index("quad")
    width, cols = w_hbm.shape
    step = min(cols, width)
    size = width // 2 - late.shape[0]
    mine = pl.ds(pl.multiple_of(part * RANK, RANK), RANK)
    begin = part * (width // 2)
    copies = [
        (w_hbm.at[pl.ds(pl.multiple_of(begin, RANK), size), :], early.at[:size, :]),
        (w_hbm.at[pl.ds(pl.multiple_of(begin + size, RANK), late.shape[0]), :], late),
    ]
    for q, out in enumerate(maps_out):
        base = size if q == 0 else 0
        begin = core * (d_hbm.shape[1] // 2) + (quad ^ q) * width
        sources = [
            d_hbm.at[mine, pl.ds(pl.multiple_of(begin + first, step), step)] for first in range(0, width, step)
        ]
        sources += [u_hbm.at[mine, first : first + step] for first in range(0, cols, step)]
        for i, source in enumerate(sources):
            copies.append((source, out.at[base + i * RANK : base + (i + 1) * RANK, :step]))
    run_copies(copies, sems)


def cross_pack(downs, ups, weights, quads):
    vmem = pl.BlockSpec(memory_space=pltpu.VMEM)
    hbm = pl.BlockSpec(memory_space=pltpu.HBM)
    width, cols = weights.shape
    step = min(cols, width)
    pieces = (width + cols) // step
    first = width // 2 * 13 // 32 // RANK * RANK
    sizes = [(first + RANK * pieces, cols), (width // 2 - first, cols)]
    sizes += [(RANK * pieces, step)] * (quads - 1)
    return pl.pallas_call(
        cross_kernel,
        in_specs=[hbm] * 3,
        out_specs=[vmem] * len(sizes),
        out_shape=[jax.ShapeDtypeStruct(size, weights.dtype) for size in sizes],
        scratch_shapes=[pltpu.SemaphoreType.DMA((quads * pieces + 2,))],
        compiler_params=pltpu.CompilerParams(vmem_limit_bytes=57 * MIB),
        cost_estimate=FREE,
        name="cross_pack",
    )(downs, ups, weights)


def quad_kernel(x_hbm, d_hbm, u_hbm, *refs):
    outs, sems = refs[:-1], refs[-1]
    core, quad = lax.axis_index("tensor"), lax.axis_index("quad")
    tokens, features = x_hbm.shape
    ranks, cols = u_hbm.shape
    width = outs[0].shape[1]
    step = min(cols, width)
    copies = []
    for q, out in enumerate(outs):
        here = pl.ds(pl.multiple_of((quad ^ q) * width, width), width)
        copies.append((x_hbm.at[:, here], out.at[:tokens, :]))
        here = pl.ds(pl.multiple_of(core * features + (quad ^ q) * width, width), width)
        copies.append((d_hbm.at[:, here], out.at[tokens : tokens + ranks, :]))
        for slot, first, row, col in up_places(cols, width):
            row += tokens + ranks
            up = u_hbm.at[slot * RANK : (slot + 1) * RANK, first : first + step]
            copies.append((up, out.at[row : row + RANK, col : col + step]))
    run_copies(copies, sems)


def up_places(cols, width):
    step = min(cols, width)
    return [
        (slot, first, (slot * cols + first) // width * RANK, (slot * cols + first) % width)
        for slot in range(2)
        for first in range(0, cols, step)
    ]


def quad_pack(tokens, downs, ups, width, quads):
    vmem = pl.BlockSpec(memory_space=pltpu.VMEM)
    hbm = pl.BlockSpec(memory_space=pltpu.HBM)
    ranks, cols = ups.shape
    block = (tokens.shape[0] + ranks + RANK * (2 * cols // width), width)
    count = quads * (2 + len(up_places(cols, width)))
    return pl.pallas_call(
        quad_kernel,
        in_specs=[hbm] * 3,
        out_specs=[vmem] * quads,
        out_shape=[jax.ShapeDtypeStruct(block, tokens.dtype)] * quads,
        scratch_shapes=[pltpu.SemaphoreType.DMA((count,))],
        compiler_params=pltpu.CompilerParams(vmem_limit_bytes=57 * MIB),
        cost_estimate=FREE,
        name="quad_pack",
    )(tokens, downs, ups)


def near_kernel(tokens, quads, position, adapter, own_ref, *refs):
    maps_mine, maps_theirs, refs = refs[:2], refs[2:4], refs[4:]
    mine, theirs, out, ds, us = refs
    part, core = lax.axis_index("parts") % 2, lax.axis_index("tensor")
    wing, quad = lax.axis_index("wing"), lax.axis_index("quad")
    width = mine.shape[2]
    cols = own_ref.shape[1]
    ranks = 2 * RANK
    step = min(cols, width)
    for q in range(quads):
        rows = slice(q * ranks, (q + 1) * ranks)
        ds[0, rows, :] = mine[q, tokens : tokens + ranks, :]
        ds[1, rows, :] = theirs[q, tokens : tokens + ranks, :]
        for slot, first, row, col in up_places(cols, width):
            row += tokens + ranks
            place = q * ranks + slot * RANK
            us[place : place + RANK, first : first + step] = mine[q, row : row + RANK, col : col + step]
        for side in range(2):
            place = (quads + q) * ranks + side * RANK
            for i, first in enumerate(range(0, width, step)):
                row = i * RANK
                ds[0, place : place + RANK, first : first + step] = maps_mine[side][q, row : row + RANK, :]
                ds[1, place : place + RANK, first : first + step] = maps_theirs[side][q, row : row + RANK, :]
            for i, first in enumerate(range(0, cols, step)):
                row = (width // step + i) * RANK
                us[place : place + RANK, first : first + step] = maps_mine[side][q, row : row + RANK, :]

    x_mine = mine[:, :tokens, :].reshape(quads * tokens, width)
    x_theirs = theirs[:, :tokens, :].reshape(quads * tokens, width)
    shrink = dot_last(x_mine, ds[0]) + dot_last(x_theirs, ds[1])
    place = lax.broadcasted_iota(jnp.int32, (SPAN, us.shape[0]), 1)
    far = (place >= quads * ranks).astype(jnp.int32)
    index = place - far * (quads * ranks)
    group = (wing ^ far) * quads + (quad ^ (index >> 5))
    which = 2 * group + (((index >> 4) & 1) ^ (far * part))
    spans = tokens // SPAN
    masked = []
    for q in range(quads):
        for i in range(spans):
            slot = position[adapter[(wing * quads + (quad ^ q)) * spans + i]]
            row = (q * spans + i) * SPAN
            masked.append(jnp.where(which == slot, shrink[row : row + SPAN, :], 0.0))
    shrink = (jnp.concatenate(masked, axis=0) * ADAPTER_SCALE).astype(jnp.bfloat16)
    out[...] = dot(shrink, us[...])

    @pl.when(core == wing)
    def _():
        out[...] += dot(x_mine, own_ref[...])

    @pl.when(core != wing)
    def _():
        out[...] += dot(x_theirs, own_ref[...])


def near_products(mine, theirs, maps_mine, maps_theirs, own, position, adapter, tokens):
    quads, _, width = mine.shape
    cols = own.shape[1]
    ranks = 4 * quads * RANK
    vmem = pl.BlockSpec(memory_space=pltpu.VMEM)
    smem = pl.BlockSpec(memory_space=pltpu.SMEM)
    return pl.pallas_call(
        functools.partial(near_kernel, tokens, quads),
        in_specs=[smem, smem] + [vmem] * 7,
        out_specs=vmem,
        out_shape=jax.ShapeDtypeStruct((quads * tokens, cols), jnp.float32),
        scratch_shapes=[
            pltpu.VMEM((2, ranks, width), jnp.bfloat16),
            pltpu.VMEM((ranks, cols), jnp.bfloat16),
        ],
        compiler_params=pltpu.CompilerParams(vmem_limit_bytes=48 * MIB if quads > 4 else 24 * MIB),
        cost_estimate=FREE,
        name="near_products",
    )(position, adapter, own, *maps_mine, *maps_theirs, mine, theirs)


def far_kernel(tokens, quads, near, *refs):
    weights, (mine, theirs) = refs[:4], refs[4:6]
    outs, whole = refs[6:-1], refs[-1]
    part, core, wing = lax.axis_index("parts") % 2, lax.axis_index("tensor"), lax.axis_index("wing")
    for side in range(2):
        begin = (part if side == 0 else 1 - part) * (whole.shape[0] // 2)
        early, late = weights[2 * side : 2 * side + 2]
        size = whole.shape[0] // 2 - late.shape[0]
        whole[pl.ds(pl.multiple_of(begin, RANK), size), :] = early[:size, :]
        whole[pl.ds(pl.multiple_of(begin + size, RANK), late.shape[0]), :] = late[...]

    def store(blocks):
        x = blocks[:, :tokens, :].reshape(near.shape[0], -1)
        product = (near[...] + dot(x, whole[...])).astype(jnp.bfloat16)
        for q, out in enumerate(outs):
            out[...] = product[q * tokens : (q + 1) * tokens, :]

    @pl.when(core == wing)
    def _():
        store(theirs)

    @pl.when(core != wing)
    def _():
        store(mine)


def far_products(mine, theirs, near, weights, tokens):
    quads, _, width = mine.shape
    cols = near.shape[1]
    vmem = pl.BlockSpec(memory_space=pltpu.VMEM)
    return pl.pallas_call(
        functools.partial(far_kernel, tokens, quads),
        in_specs=[vmem] * (3 + len(weights)),
        out_specs=[vmem] * quads,
        out_shape=[jax.ShapeDtypeStruct((tokens, cols), jnp.bfloat16)] * quads,
        scratch_shapes=[pltpu.VMEM((width, cols), jnp.bfloat16)],
        compiler_params=pltpu.CompilerParams(vmem_limit_bytes=48 * MIB if quads > 4 else 16 * MIB),
        cost_estimate=FREE,
        name="far_products",
    )(near, *weights, mine, theirs)


def finish_kernel(spans, lens, *refs):
    out_ref, values_ref = refs[-2:]
    mixed, probs, parts = refs[:spans], refs[spans : 2 * spans], refs[2 * spans : -2]
    total = parts[0][...].astype(jnp.float32)
    for part in parts[1:]:
        total = total + part[...].astype(jnp.float32)
    values_ref[...] = total.astype(jnp.bfloat16)
    none = jnp.zeros((SPAN, HD), jnp.bfloat16)
    group_size = out_ref.shape[1] // values_ref.shape[1]
    for order in range(spans):
        span = span_of(order, lens)
        rows = pl.ds(pl.multiple_of(span * SPAN, SPAN), SPAN)
        for pair in range(probs[order].shape[0]):
            left = values_ref[rows, 2 * pair * HD : (2 * pair + 1) * HD]
            right = values_ref[rows, (2 * pair + 1) * HD : (2 * pair + 2) * HD]
            both = jnp.concatenate(
                [jnp.concatenate([left, none], axis=1), jnp.concatenate([none, right], axis=1)], axis=0
            )
            fresh = dot(probs[order][pair], both)
            for side in range(2):
                for h in range(group_size):
                    col = ((2 * pair + side) * group_size + h) * HD
                    added = fresh[h * SPAN : (h + 1) * SPAN, side * HD : (side + 1) * HD]
                    before = mixed[order][:, col : col + HD].astype(jnp.float32)
                    out_ref[rows, col : col + HD] = (before + added).astype(jnp.bfloat16)


def finish(lengths, mixed, fresh_probs, parts, q_width):
    tokens, cols = parts[0].shape
    vmem = pl.BlockSpec(memory_space=pltpu.VMEM)
    smem = pl.BlockSpec(memory_space=pltpu.SMEM)
    return pl.pallas_call(
        functools.partial(finish_kernel, len(mixed)),
        in_specs=[smem] + [vmem] * (len(parts) + 2 * len(mixed)),
        out_specs=[vmem] * 2,
        out_shape=[
            jax.ShapeDtypeStruct((tokens, q_width), jnp.bfloat16),
            jax.ShapeDtypeStruct((tokens, cols), jnp.bfloat16),
        ],
        compiler_params=pltpu.CompilerParams(vmem_limit_bytes=16 * MIB),
        cost_estimate=FREE,
        name="finish_attention",
    )(lengths, *mixed, *fresh_probs, *parts)


def on_device(
    normed_inputs,
    value_matrix,
    adapter_down_weight,
    adapter_up_weight,
    adapter_position,
    span_adapter_index,
    queries,
    incoming_keys,
    stored_keys,
    stored_values,
    cache_length,
):
    quads = lax.axis_size("quad")
    parts_swap = [(i, i ^ 1) for i in range(lax.axis_size("parts"))]
    width, cols = value_matrix.shape
    downs = adapter_down_weight.reshape(-1, adapter_down_weight.shape[2])
    ups = adapter_up_weight.reshape(-1, cols)

    kv_heads = cols // HD
    def attention(order, lengths):
        return cache_attention(order, queries, incoming_keys, stored_keys, stored_values, lengths)

    def after(value, *others):
        return lax.optimization_barrier((value, *others))[0]

    def to_quad(value, q):
        return lax.ppermute(value, "quad", [(j, j ^ q) for j in range(quads)])

    def to_other_wing(value, q):
        pairs = [(w * quads + j, (1 - w) * quads + (j ^ q)) for w in range(2) for j in range(quads)]
        return lax.ppermute(value, ("wing", "quad"), pairs)

    early, late, *maps = cross_pack(downs, ups, value_matrix, quads)
    blocks = quad_pack(after(normed_inputs, early), downs, ups, width, quads)
    order = [*range(quads // 2, quads), *range(1, quads // 2)]
    mine = [to_quad(blocks[q], q) for q in order]
    early = lax.ppermute(early, "wing", SWAP)
    maps = [to_other_wing(each, q + 1) for q, each in enumerate(maps)]

    attn = [attention(0, after(cache_length, blocks[0]))]
    early, *maps = lax.optimization_barrier((early, *maps, attn[0][1]))[:-1]
    step = maps[0].shape[1]
    maps = jnp.stack([early[early.shape[0] - maps[0].shape[0] :, :step], *maps])
    late = lax.ppermute(after(late, early), "wing", SWAP)
    early_other = lax.ppermute(early, "parts", parts_swap)
    maps_other = lax.ppermute(maps, "parts", parts_swap)

    attn.append(attention(1, after(cache_length, early, maps)))
    late, early_other, maps_other, *mine = lax.optimization_barrier(
        (late, early_other, maps_other, *mine, attn[1][1])
    )[:-1]
    mine = jnp.stack([blocks[0]] + [mine[order.index(q)] for q in range(1, quads)])
    late_other = lax.ppermute(late, "parts", parts_swap)
    maps_mine = (maps, maps_other)
    maps_theirs = [lax.ppermute(each, "tensor", SWAP) for each in maps_mine]
    theirs = lax.ppermute(mine, "tensor", SWAP)

    tokens, q_width = queries.shape
    near = near_products(
        mine, theirs, maps_mine, maps_theirs, value_matrix, adapter_position, span_adapter_index, tokens
    )
    products = far_products(mine, theirs, near, (early, late, early_other, late_other), tokens)
    parts = [products[0]] + [to_quad(products[q], q) for q in range(quads - 1, 0, -1)]
    mixed, fresh_probs = zip(*attn)
    attended, incoming_values = finish(cache_length, mixed, fresh_probs, parts, q_width)
    return (attended, incoming_values)


def solution(mesh):
    sizes = mesh.devices.shape
    cut = Mesh(
        mesh.devices.reshape(sizes[0], 2, sizes[1] // 2, sizes[2]), ("parts", "wing", "quad", "tensor")
    )
    group = ("wing", "quad")
    home = ("parts", "wing", "quad")
    in_specs = (
        P(home, "tensor"),
        P(group, "tensor"),
        P(group, None, None),
        P(group, None, "tensor"),
        P(),
        P("parts"),
        P(home, "tensor"),
        P(home, "tensor"),
        P(home, None, "tensor"),
        P(home, None, "tensor"),
        P(home),
    )
    out_specs = (P(home, "tensor"), P(home, "tensor"))
    return jax.shard_map(
        on_device, mesh=cut, in_specs=in_specs, out_specs=out_specs, check_vma=False
    )
```

```python
import functools
import math

import jax
import jax.numpy as jnp
from jax import lax
from jax.experimental import pallas as pl
from jax.experimental.pallas import tpu as pltpu
from jax.sharding import Mesh
from jax.sharding import PartitionSpec as P

HD = 128
RANK = 16
SPAN = 64
CHUNK = 512
ONES = 16
TILE = 128
ADAPTER_SCALE = 2.0
EXP2_SCALE = math.log2(math.e) / math.sqrt(HD)
DEAD = -1e30
MIB = 1024 * 1024
SWAP = [(0, 1), (1, 0)]
FREE = pl.CostEstimate(flops=1, bytes_accessed=1, transcendentals=0)


def dot_last(a, b):
    return lax.dot_general(a, b, (((1,), (1,)), ((), ())), preferred_element_type=jnp.float32)


def dot(a, b):
    return jnp.dot(a, b, preferred_element_type=jnp.float32)


def span_of(order, lens):
    longer = (lens[1] > lens[0]).astype(jnp.int32)
    return longer if order == 0 else 1 - longer


def cache_kernel(order, lens, q_hbm, fk_hbm, k_hbm, v_hbm, out_hbm, pf_hbm, qs, ks, vs, live, s_s, p_s, x_s, m_s, a_s, acc, q_s, fk_s, out_s, pf_s, sems, io_sems):
    span = span_of(order, lens)
    length = lens[span]
    chunks, chunk, _ = ks.shape
    kv_heads, rows, _ = qs.shape
    group_size = rows // SPAN
    count = (length + chunk - 1) // chunk
    mine = pl.ds(pl.multiple_of(span * SPAN, SPAN), SPAN)

    def copy_in(side, i):
        slots = pl.ds(pl.multiple_of(i * chunk, chunk), chunk)
        source, target = ((k_hbm, ks), (v_hbm, vs))[side]
        return pltpu.make_async_copy(source.at[span, slots, :], target.at[i], sems.at[side, i])

    small = [
        pltpu.make_async_copy(q_hbm.at[mine, :], q_s, io_sems.at[0]),
        pltpu.make_async_copy(fk_hbm.at[mine, :], fk_s, io_sems.at[1]),
    ]
    for copy in small:
        copy.start()
    copy_in(0, 0).start()

    def dead_slots(i):
        return i * chunk + lax.broadcasted_iota(jnp.int32, ks.shape[1:], 0) >= length

    def arrive_keys(i):
        copy_in(0, i).wait()

        @pl.when((i + 1) * chunk > length)
        def _():
            keys = ks[i].astype(jnp.float32)
            ks[i] = jnp.where(dead_slots(i), keys[:1, :], keys).astype(jnp.bfloat16)

    def arrive_values(i):
        copy_in(1, i).wait()
        slot = i * chunk + lax.broadcasted_iota(jnp.int32, (ONES, chunk), 1)
        live[i] = (slot < length).astype(jnp.float32).astype(jnp.bfloat16)

        @pl.when((i + 1) * chunk > length)
        def _():
            vs[i] = jnp.where(dead_slots(i), 0.0, vs[i].astype(jnp.float32)).astype(jnp.bfloat16)

    def fresh_scores(k):
        s = dot_last(fk_s[:, k * HD : (k + 1) * HD], qs[k])
        key = lax.broadcasted_iota(jnp.int32, (SPAN, rows), 0)
        token = lax.broadcasted_iota(jnp.int32, (SPAN, rows), 1) % SPAN
        return jnp.where(key <= token, s, DEAD)

    def tile_max(s):
        return jnp.max(s.reshape(s.shape[0] // 8, 8, rows), axis=0)

    def tiles(k):
        return slice(k * HD, (k + 1) * HD)

    for copy in small:
        copy.wait()
    copy_in(1, 0).start()
    for k in range(kv_heads):
        for h in range(group_size):
            qs[k, h * SPAN : (h + 1) * SPAN, :] = q_s[:, tiles(k * group_size + h)]
        m_s[k] = jnp.max(fresh_scores(k), axis=0, keepdims=True)
        a_s[k] = jnp.ones((1, rows), jnp.float32)
        acc[k] = jnp.zeros((HD + ONES, rows), jnp.float32)
    p_s[1] = jnp.zeros((chunk, rows), jnp.bfloat16)
    arrive_keys(0)
    for i in range(1, chunks):

        @pl.when(i * chunk < length)
        def _():
            copy_in(0, i).start()
            copy_in(1, i).start()

    s = dot_last(ks[0, :, :HD], qs[0])
    s_s[0] = s
    x_s[0] = tile_max(s)

    def weighted(i, k, part, index):
        return dot(jnp.concatenate([vs[i, part, tiles(k)].T, live[i, :, part]], axis=0), p_s[index, part, :])

    @pl.loop(0, count)
    def _(i):
        arrive_values(i)

        @pl.when(i + 1 < count)
        def _():
            arrive_keys(i + 1)

        for k in range(kv_heads):
            now, other = k % 2, 1 - k % 2
            next_k, next_i = (k + 1) % kv_heads, i if k + 1 < kv_heads else jnp.minimum(i + 1, count - 1)
            last_k, last_i = (k - 1) % kv_heads, i if k > 0 else jnp.maximum(i - 1, 0)
            before = m_s[k]
            top = jnp.maximum(before, jnp.max(x_s[now], axis=0, keepdims=True))
            m_s[k] = top
            highest, mixed = None, None
            for j in range(0, chunk, TILE):
                part = slice(j, j + TILE)
                s = dot_last(ks[next_i, part, tiles(next_k)], qs[next_k])
                s_s[other, part, :] = s
                high = tile_max(s)
                highest = high if highest is None else jnp.maximum(highest, high)
                p_s[now, part, :] = jnp.exp2((s_s[now, part, :] - top) * EXP2_SCALE).astype(jnp.bfloat16)
                if (j // TILE) % 2 == 1:
                    product = weighted(last_i, last_k, slice(j - TILE, j + TILE), other)
                    mixed = product if mixed is None else mixed + product
            x_s[other] = highest
            acc[last_k] = acc[last_k] * a_s[last_k] + mixed
            a_s[k] = jnp.exp2((before - top) * EXP2_SCALE)

    last = kv_heads - 1
    acc[last] = acc[last] * a_s[last] + weighted(count - 1, last, slice(0, chunk), last % 2)

    leaving = []
    for k in range(kv_heads):
        p = jnp.exp2((fresh_scores(k) - m_s[k]) * EXP2_SCALE)
        inverse = 1.0 / (acc[k, HD : HD + 1, :] + jnp.sum(p, axis=0, keepdims=True))
        p_s[0, (k % 2) * SPAN : (k % 2 + 1) * SPAN, :] = (p * inverse).astype(jnp.bfloat16)
        mixed = (acc[k, :HD, :] * inverse).astype(jnp.bfloat16).T
        for h in range(group_size):
            out_s[:, tiles(k * group_size + h)] = mixed[h * SPAN : (h + 1) * SPAN, :]
        here = slice(k * group_size * HD, (k + 1) * group_size * HD)
        leaving.append(pltpu.make_async_copy(out_s.at[:, here], out_hbm.at[:, here], io_sems.at[2 + k]))
        leaving[-1].start()
        if k % 2 == 1:
            pf_s[k // 2] = p_s[0, : 2 * SPAN, :].T
    leaving.append(pltpu.make_async_copy(pf_s, pf_hbm, io_sems.at[2 + kv_heads]))
    leaving[-1].start()
    for copy in leaving:
        copy.wait()


def cache_attention(order, queries, fresh_keys, keys, values, lengths):
    slots, width = keys.shape[1:]
    kv_heads = width // HD
    group_size = queries.shape[1] // width
    rows = group_size * SPAN
    chunk = min(CHUNK, slots)
    chunks = slots // chunk
    hbm = pl.BlockSpec(memory_space=pltpu.HBM)
    result = (SPAN, queries.shape[1])
    weights = (kv_heads // 2, rows, 2 * SPAN)
    return pl.pallas_call(
        functools.partial(cache_kernel, order),
        in_specs=[pl.BlockSpec(memory_space=pltpu.SMEM)] + [hbm] * 4,
        out_specs=[hbm] * 2,
        scratch_shapes=[
            pltpu.VMEM((kv_heads, rows, HD), jnp.bfloat16),
            pltpu.VMEM((chunks, chunk, width), jnp.bfloat16),
            pltpu.VMEM((chunks, chunk, width), jnp.bfloat16),
            pltpu.VMEM((chunks, ONES, chunk), jnp.bfloat16),
            pltpu.VMEM((2, chunk, rows), jnp.float32),
            pltpu.VMEM((2, chunk, rows), jnp.bfloat16),
            pltpu.VMEM((2, 8, rows), jnp.float32),
            pltpu.VMEM((kv_heads, 1, rows), jnp.float32),
            pltpu.VMEM((kv_heads, 1, rows), jnp.float32),
            pltpu.VMEM((kv_heads, HD + ONES, rows), jnp.float32),
            pltpu.VMEM(result, jnp.bfloat16),
            pltpu.VMEM((SPAN, width), jnp.bfloat16),
            pltpu.VMEM(result, jnp.bfloat16),
            pltpu.VMEM(weights, jnp.bfloat16),
            pltpu.SemaphoreType.DMA((2, chunks)),
            pltpu.SemaphoreType.DMA((3 + kv_heads,)),
        ],
        out_shape=[
            jax.ShapeDtypeStruct(result, jnp.bfloat16),
            jax.ShapeDtypeStruct(weights, jnp.bfloat16),
        ],
        compiler_params=pltpu.CompilerParams(vmem_limit_bytes=57 * MIB),
        cost_estimate=FREE,
        name="cache_attention",
    )(lengths, queries, fresh_keys, keys, values)


def run_copies(copies, sems):
    copies = [pltpu.make_async_copy(src, dst, sems.at[i]) for i, (src, dst) in enumerate(copies)]
    for copy in copies:
        copy.start()
    for copy in copies:
        copy.wait()


def cross_kernel(d_hbm, u_hbm, w_hbm, early, late, *refs):
    maps_out, sems = [early, *refs[:-1]], refs[-1]
    part, core, quad = lax.axis_index("parts") % 2, lax.axis_index("tensor"), lax.axis_index("quad")
    width, cols = w_hbm.shape
    step = min(cols, width)
    size = width // 2 - late.shape[0]
    mine = pl.ds(pl.multiple_of(part * RANK, RANK), RANK)
    begin = part * (width // 2)
    copies = [
        (w_hbm.at[pl.ds(pl.multiple_of(begin, RANK), size), :], early.at[:size, :]),
        (w_hbm.at[pl.ds(pl.multiple_of(begin + size, RANK), late.shape[0]), :], late),
    ]
    for q, out in enumerate(maps_out):
        base = size if q == 0 else 0
        begin = core * (d_hbm.shape[1] // 2) + (quad ^ q) * width
        sources = [
            d_hbm.at[mine, pl.ds(pl.multiple_of(begin + first, step), step)] for first in range(0, width, step)
        ]
        sources += [u_hbm.at[mine, first : first + step] for first in range(0, cols, step)]
        for i, source in enumerate(sources):
            copies.append((source, out.at[base + i * RANK : base + (i + 1) * RANK, :step]))
    run_copies(copies, sems)


def cross_pack(downs, ups, weights, quads):
    vmem = pl.BlockSpec(memory_space=pltpu.VMEM)
    hbm = pl.BlockSpec(memory_space=pltpu.HBM)
    width, cols = weights.shape
    step = min(cols, width)
    pieces = (width + cols) // step
    first = width // 2 * 14 // 32 // RANK * RANK
    sizes = [(first + RANK * pieces, cols), (width // 2 - first, cols)]
    sizes += [(RANK * pieces, step)] * (quads - 1)
    return pl.pallas_call(
        cross_kernel,
        in_specs=[hbm] * 3,
        out_specs=[vmem] * len(sizes),
        out_shape=[jax.ShapeDtypeStruct(size, weights.dtype) for size in sizes],
        scratch_shapes=[pltpu.SemaphoreType.DMA((quads * pieces + 2,))],
        compiler_params=pltpu.CompilerParams(vmem_limit_bytes=57 * MIB),
        cost_estimate=FREE,
        name="cross_pack",
    )(downs, ups, weights)


def quad_kernel(x_hbm, d_hbm, u_hbm, *refs):
    outs, sems = refs[:-1], refs[-1]
    core, quad = lax.axis_index("tensor"), lax.axis_index("quad")
    tokens, features = x_hbm.shape
    ranks, cols = u_hbm.shape
    width = outs[0].shape[1]
    step = min(cols, width)
    copies = []
    for q, out in enumerate(outs):
        here = pl.ds(pl.multiple_of((quad ^ q) * width, width), width)
        copies.append((x_hbm.at[:, here], out.at[:tokens, :]))
        here = pl.ds(pl.multiple_of(core * features + (quad ^ q) * width, width), width)
        copies.append((d_hbm.at[:, here], out.at[tokens : tokens + ranks, :]))
        for slot, first, row, col in up_places(cols, width):
            row += tokens + ranks
            up = u_hbm.at[slot * RANK : (slot + 1) * RANK, first : first + step]
            copies.append((up, out.at[row : row + RANK, col : col + step]))
    run_copies(copies, sems)


def up_places(cols, width):
    step = min(cols, width)
    return [
        (slot, first, (slot * cols + first) // width * RANK, (slot * cols + first) % width)
        for slot in range(2)
        for first in range(0, cols, step)
    ]


def quad_pack(tokens, downs, ups, width, quads):
    vmem = pl.BlockSpec(memory_space=pltpu.VMEM)
    hbm = pl.BlockSpec(memory_space=pltpu.HBM)
    ranks, cols = ups.shape
    block = (tokens.shape[0] + ranks + RANK * (2 * cols // width), width)
    count = quads * (2 + len(up_places(cols, width)))
    return pl.pallas_call(
        quad_kernel,
        in_specs=[hbm] * 3,
        out_specs=[vmem] * quads,
        out_shape=[jax.ShapeDtypeStruct(block, tokens.dtype)] * quads,
        scratch_shapes=[pltpu.SemaphoreType.DMA((count,))],
        compiler_params=pltpu.CompilerParams(vmem_limit_bytes=57 * MIB),
        cost_estimate=FREE,
        name="quad_pack",
    )(tokens, downs, ups)


def near_kernel(tokens, quads, position, adapter, own_ref, *refs):
    maps_mine, maps_theirs, refs = refs[:2], refs[2:4], refs[4:]
    mine, theirs, out, ds, us = refs
    part, core = lax.axis_index("parts") % 2, lax.axis_index("tensor")
    wing, quad = lax.axis_index("wing"), lax.axis_index("quad")
    width = mine.shape[2]
    cols = own_ref.shape[1]
    ranks = 2 * RANK
    step = min(cols, width)
    for q in range(quads):
        rows = slice(q * ranks, (q + 1) * ranks)
        ds[0, rows, :] = mine[q, tokens : tokens + ranks, :]
        ds[1, rows, :] = theirs[q, tokens : tokens + ranks, :]
        for slot, first, row, col in up_places(cols, width):
            row += tokens + ranks
            place = q * ranks + slot * RANK
            us[place : place + RANK, first : first + step] = mine[q, row : row + RANK, col : col + step]
        for side in range(2):
            place = (quads + q) * ranks + side * RANK
            for i, first in enumerate(range(0, width, step)):
                row = i * RANK
                ds[0, place : place + RANK, first : first + step] = maps_mine[side][q, row : row + RANK, :]
                ds[1, place : place + RANK, first : first + step] = maps_theirs[side][q, row : row + RANK, :]
            for i, first in enumerate(range(0, cols, step)):
                row = (width // step + i) * RANK
                us[place : place + RANK, first : first + step] = maps_mine[side][q, row : row + RANK, :]

    x_mine = mine[:, :tokens, :].reshape(quads * tokens, width)
    x_theirs = theirs[:, :tokens, :].reshape(quads * tokens, width)
    shrink = dot_last(x_mine, ds[0]) + dot_last(x_theirs, ds[1])
    place = lax.broadcasted_iota(jnp.int32, (SPAN, us.shape[0]), 1)
    far = (place >= quads * ranks).astype(jnp.int32)
    index = place - far * (quads * ranks)
    group = (wing ^ far) * quads + (quad ^ (index >> 5))
    which = 2 * group + (((index >> 4) & 1) ^ (far * part))
    spans = tokens // SPAN
    masked = []
    for q in range(quads):
        for i in range(spans):
            slot = position[adapter[(wing * quads + (quad ^ q)) * spans + i]]
            row = (q * spans + i) * SPAN
            masked.append(jnp.where(which == slot, shrink[row : row + SPAN, :], 0.0))
    shrink = (jnp.concatenate(masked, axis=0) * ADAPTER_SCALE).astype(jnp.bfloat16)
    out[...] = dot(shrink, us[...])

    @pl.when(core == wing)
    def _():
        out[...] += dot(x_mine, own_ref[...])

    @pl.when(core != wing)
    def _():
        out[...] += dot(x_theirs, own_ref[...])


def near_products(mine, theirs, maps_mine, maps_theirs, own, position, adapter, tokens):
    quads, _, width = mine.shape
    cols = own.shape[1]
    ranks = 4 * quads * RANK
    vmem = pl.BlockSpec(memory_space=pltpu.VMEM)
    smem = pl.BlockSpec(memory_space=pltpu.SMEM)
    return pl.pallas_call(
        functools.partial(near_kernel, tokens, quads),
        in_specs=[smem, smem] + [vmem] * 7,
        out_specs=vmem,
        out_shape=jax.ShapeDtypeStruct((quads * tokens, cols), jnp.float32),
        scratch_shapes=[
            pltpu.VMEM((2, ranks, width), jnp.bfloat16),
            pltpu.VMEM((ranks, cols), jnp.bfloat16),
        ],
        compiler_params=pltpu.CompilerParams(vmem_limit_bytes=48 * MIB if quads > 4 else 24 * MIB),
        cost_estimate=FREE,
        name="near_products",
    )(position, adapter, own, *maps_mine, *maps_theirs, mine, theirs)


def far_kernel(tokens, quads, near, *refs):
    weights, (mine, theirs) = refs[:4], refs[4:6]
    outs, whole = refs[6:-1], refs[-1]
    part, core, wing = lax.axis_index("parts") % 2, lax.axis_index("tensor"), lax.axis_index("wing")
    for side in range(2):
        begin = (part if side == 0 else 1 - part) * (whole.shape[0] // 2)
        early, late = weights[2 * side : 2 * side + 2]
        size = whole.shape[0] // 2 - late.shape[0]
        whole[pl.ds(pl.multiple_of(begin, RANK), size), :] = early[:size, :]
        whole[pl.ds(pl.multiple_of(begin + size, RANK), late.shape[0]), :] = late[...]

    def store(blocks):
        x = blocks[:, :tokens, :].reshape(near.shape[0], -1)
        product = (near[...] + dot(x, whole[...])).astype(jnp.bfloat16)
        for q, out in enumerate(outs):
            out[...] = product[q * tokens : (q + 1) * tokens, :]

    @pl.when(core == wing)
    def _():
        store(theirs)

    @pl.when(core != wing)
    def _():
        store(mine)


def far_products(mine, theirs, near, weights, tokens):
    quads, _, width = mine.shape
    cols = near.shape[1]
    vmem = pl.BlockSpec(memory_space=pltpu.VMEM)
    return pl.pallas_call(
        functools.partial(far_kernel, tokens, quads),
        in_specs=[vmem] * (3 + len(weights)),
        out_specs=[vmem] * quads,
        out_shape=[jax.ShapeDtypeStruct((tokens, cols), jnp.bfloat16)] * quads,
        scratch_shapes=[pltpu.VMEM((width, cols), jnp.bfloat16)],
        compiler_params=pltpu.CompilerParams(vmem_limit_bytes=48 * MIB if quads > 4 else 16 * MIB),
        cost_estimate=FREE,
        name="far_products",
    )(near, *weights, mine, theirs)


def finish_kernel(spans, lens, *refs):
    out_ref, values_ref = refs[-2:]
    mixed, probs, parts = refs[:spans], refs[spans : 2 * spans], refs[2 * spans : -2]
    total = parts[0][...].astype(jnp.float32)
    for part in parts[1:]:
        total = total + part[...].astype(jnp.float32)
    values_ref[...] = total.astype(jnp.bfloat16)
    none = jnp.zeros((SPAN, HD), jnp.bfloat16)
    group_size = out_ref.shape[1] // values_ref.shape[1]
    for order in range(spans):
        span = span_of(order, lens)
        rows = pl.ds(pl.multiple_of(span * SPAN, SPAN), SPAN)
        for pair in range(probs[order].shape[0]):
            left = values_ref[rows, 2 * pair * HD : (2 * pair + 1) * HD]
            right = values_ref[rows, (2 * pair + 1) * HD : (2 * pair + 2) * HD]
            both = jnp.concatenate(
                [jnp.concatenate([left, none], axis=1), jnp.concatenate([none, right], axis=1)], axis=0
            )
            fresh = dot(probs[order][pair], both)
            for side in range(2):
                for h in range(group_size):
                    col = ((2 * pair + side) * group_size + h) * HD
                    added = fresh[h * SPAN : (h + 1) * SPAN, side * HD : (side + 1) * HD]
                    before = mixed[order][:, col : col + HD].astype(jnp.float32)
                    out_ref[rows, col : col + HD] = (before + added).astype(jnp.bfloat16)


def finish(lengths, mixed, fresh_probs, parts, q_width):
    tokens, cols = parts[0].shape
    vmem = pl.BlockSpec(memory_space=pltpu.VMEM)
    smem = pl.BlockSpec(memory_space=pltpu.SMEM)
    return pl.pallas_call(
        functools.partial(finish_kernel, len(mixed)),
        in_specs=[smem] + [vmem] * (len(parts) + 2 * len(mixed)),
        out_specs=[vmem] * 2,
        out_shape=[
            jax.ShapeDtypeStruct((tokens, q_width), jnp.bfloat16),
            jax.ShapeDtypeStruct((tokens, cols), jnp.bfloat16),
        ],
        compiler_params=pltpu.CompilerParams(vmem_limit_bytes=16 * MIB),
        cost_estimate=FREE,
        name="finish_attention",
    )(lengths, *mixed, *fresh_probs, *parts)


def on_device(
    normed_inputs,
    value_matrix,
    adapter_down_weight,
    adapter_up_weight,
    adapter_position,
    span_adapter_index,
    queries,
    incoming_keys,
    stored_keys,
    stored_values,
    cache_length,
):
    quads = lax.axis_size("quad")
    parts_swap = [(i, i ^ 1) for i in range(lax.axis_size("parts"))]
    width, cols = value_matrix.shape
    downs = adapter_down_weight.reshape(-1, adapter_down_weight.shape[2])
    ups = adapter_up_weight.reshape(-1, cols)

    kv_heads = cols // HD
    def attention(order, lengths):
        return cache_attention(order, queries, incoming_keys, stored_keys, stored_values, lengths)

    def after(value, *others):
        return lax.optimization_barrier((value, *others))[0]

    def to_quad(value, q):
        return lax.ppermute(value, "quad", [(j, j ^ q) for j in range(quads)])

    def to_other_wing(value, q):
        pairs = [(w * quads + j, (1 - w) * quads + (j ^ q)) for w in range(2) for j in range(quads)]
        return lax.ppermute(value, ("wing", "quad"), pairs)

    early, late, *maps = cross_pack(downs, ups, value_matrix, quads)
    blocks = quad_pack(after(normed_inputs, early), downs, ups, width, quads)
    order = list(range(quads - 1, 0, -1))
    mine = [to_quad(blocks[q], q) for q in order]
    early = lax.ppermute(early, "wing", SWAP)
    maps = [to_other_wing(each, q + 1) for q, each in enumerate(maps)]

    attn = [attention(0, after(cache_length, blocks[0]))]
    early, *maps = lax.optimization_barrier((early, *maps, attn[0][1]))[:-1]
    step = maps[0].shape[1]
    maps = jnp.stack([early[early.shape[0] - maps[0].shape[0] :, :step], *maps])
    late = lax.ppermute(after(late, early), "wing", SWAP)
    early_other = lax.ppermute(early, "parts", parts_swap)
    maps_other = lax.ppermute(maps, "parts", parts_swap)

    attn.append(attention(1, after(cache_length, early, maps)))
    late, early_other, maps_other, *mine = lax.optimization_barrier(
        (late, early_other, maps_other, *mine, attn[1][1])
    )[:-1]
    mine = jnp.stack([blocks[0]] + [mine[order.index(q)] for q in range(1, quads)])
    late_other = lax.ppermute(late, "parts", parts_swap)
    maps_mine = (maps, maps_other)
    maps_theirs = [lax.ppermute(each, "tensor", SWAP) for each in maps_mine]
    theirs = lax.ppermute(mine, "tensor", SWAP)

    tokens, q_width = queries.shape
    near = near_products(
        mine, theirs, maps_mine, maps_theirs, value_matrix, adapter_position, span_adapter_index, tokens
    )
    products = far_products(mine, theirs, near, (early, late, early_other, late_other), tokens)
    parts = [products[0]] + [to_quad(products[q], q) for q in range(quads - 1, 0, -1)]
    mixed, fresh_probs = zip(*attn)
    attended, incoming_values = finish(cache_length, mixed, fresh_probs, parts, q_width)
    return (attended, incoming_values)


def solution(mesh):
    sizes = mesh.devices.shape
    cut = Mesh(
        mesh.devices.reshape(sizes[0], 2, sizes[1] // 2, sizes[2]), ("parts", "wing", "quad", "tensor")
    )
    group = ("wing", "quad")
    home = ("parts", "wing", "quad")
    in_specs = (
        P(home, "tensor"),
        P(group, "tensor"),
        P(group, None, None),
        P(group, None, "tensor"),
        P(),
        P("parts"),
        P(home, "tensor"),
        P(home, "tensor"),
        P(home, None, "tensor"),
        P(home, None, "tensor"),
        P(home),
    )
    out_specs = (P(home, "tensor"), P(home, "tensor"))
    return jax.shard_map(
        on_device, mesh=cut, in_specs=in_specs, out_specs=out_specs, check_vma=False
    )
```
